32 devices in a mesh: dp: 8 (over y, x, core), seq: 4 (over z).
Axes of the slice: x: 2, y: 2, z: 4, core: 2. Of those that a mesh axis runs over, the one named last changes fastest.
Arguments:
- tokens: bfloat16 [8, 1024, 1152], P('dp', 'seq'), may hold values from -4 to 4, as said below
- conditions: bfloat16 [8, 4, 1152], P('dp'), may hold values from -4 to 4, as said below
- segment_ids: int32 [8, 1024], P('dp'), may hold values from 0 to 3, never falling along the last dimension, each value on 1 to 770 neighbouring positions
- padding: int32 [8, 1024], P('dp'), may hold values 0 or 1
- targets: bfloat16 [8, 1024, 768], P('dp', 'seq'), may hold values from -6 to 6
- cotangent: float32 [8, 1024, 1152], P('dp', 'seq'), may hold values from -0.01953125 to 0.01953125
- tile_counts: int32 [32], replicated, may hold values from 1 to 612, as said below
- master: float32 [19584, 2048], P(('dp', 'seq')), may hold values from -2 to 2, as said below
- first_moment: float32 [19584, 2048], P(('dp', 'seq')), may hold values from -1.75 to 1.75
- second_moment: float32 [19584, 2048], P(('dp', 'seq')), may hold values from 0.013888889 to 0.055555556
Outputs:
- output: bfloat16 [8, 1024, 1152], P('dp', 'seq')
- grad_tokens: float32 [8, 1024, 1152], P('dp', 'seq')
- grad_conditions: float32 [8, 4, 1152], P('dp')
- new_master: float32 [19584, 2048], P(('dp', 'seq'))
- new_first: float32 [19584, 2048], P(('dp', 'seq'))
- new_second: float32 [19584, 2048], P(('dp', 'seq'))
The draws below stay inside these ranges and needn't reach their ends.
Inputs may be any that keep to these rules, and one draw needn't show every extreme that they name: `tile_counts`: the counts sum to 15643 and one device owns exactly 612 tiles. `master`: each weight's entries of order its fan-in to the minus one half. `segment_ids`: in each row the ids never fall, each of the 4 images has 1 to 770 tokens, and one has exactly that many. `tokens`: entries of order one. `conditions`: entries of order one.
All inputs are finite; a program needn't handle non-finite values. No bound on the sum of `padding` on one device may be relied on, other than what follows from the above.
Results may differ from the reference program's by a relative error of at most 0.017.
Values may be sent and summed in bfloat16 or wider, within the bound.
A program may use at most 512 MiB of HBM per device.

```python
import math
from functools import partial
import jax
import jax.numpy as jnp
import numpy as np
from jax import lax

HEADS = 16
HEAD_DIM = 72
D = 1152
FF = 4608
PROJ = 2048
TARGET = 768
LEN = 1024
SEGS = 4
ROWS = 8
TE = 2048
STEP = 10
TILES = 15643
OWNERS = 32
CAP = 612


def count_layout(key):
    inner = jax.random.fold_in(key, 17)
    base_share = TILES // OWNERS
    leftover = TILES % OWNERS
    order = jax.random.permutation(jax.random.fold_in(inner, 1), OWNERS).astype(jnp.int32)
    ranks = jnp.zeros((OWNERS,), jnp.int32).at[order].set(jnp.arange(OWNERS, dtype=jnp.int32))
    positions = jnp.arange(OWNERS, dtype=jnp.int32)
    base = base_share + (positions < leftover).astype(jnp.int32)
    shifts = jax.random.randint(jax.random.fold_in(inner, 2), (OWNERS // 2,), 0, CAP - base_share - 1).astype(jnp.int32)
    shifts = shifts.at[0].set(CAP - base[0])
    signs = jnp.where(positions % 2 == 0, 1, -1).astype(jnp.int32)
    by_rank = base + signs * jnp.repeat(shifts, 2)
    return jnp.take(by_rank, ranks).astype(jnp.int32)


def draw_tile_counts(key, part):
    return count_layout(key)


def region_scales():
    spread = 0.3
    inner_scale = D ** (-0.5)
    return [(D * 6 * D, inner_scale), (6 * D, spread), (D * 3 * D, inner_scale), (D, spread), (D, spread), (D * D, 4.0 * inner_scale), (D, spread), (D * FF, inner_scale), (FF, spread), (FF * D, FF ** (-0.5)), (D, spread), (D * PROJ, inner_scale), (PROJ, spread), (PROJ * PROJ, PROJ ** (-0.5)), (PROJ, spread), (PROJ * TARGET, PROJ ** (-0.5)), (TARGET, spread)]


def draw_master(key, part):
    counts = count_layout(key)
    key = jax.random.fold_in(key, 5)
    ends = jnp.cumsum(counts).astype(jnp.int32)
    starts = ends - counts
    slots = jnp.arange(OWNERS * CAP, dtype=jnp.int32)
    device = slots // CAP
    within = slots % CAP
    valid = within < jnp.take(counts, device)
    tile = jnp.take(starts, device) + within
    bounds = []
    scales = []
    running = 0
    for extent, factor in region_scales():
        running = running + extent
        bounds.append(running)
        scales.append(factor)
    scales.append(0.3)
    entry = tile[:, None] * TE + jnp.arange(TE, dtype=jnp.int32)[None, :]
    region = jnp.zeros(entry.shape, jnp.int32)
    for bound in bounds:
        region = region + (entry >= bound).astype(jnp.int32)
    factors = jnp.take(jnp.asarray(scales, jnp.float32), region)
    factors = jnp.where(valid[:, None], factors, 0.3)
    values = jax.random.truncated_normal(key, -4.0, 4.0, (OWNERS * CAP, TE), jnp.float32)
    return values * factors


def unit_field(key, shape):
    return jax.random.truncated_normal(key, -4.0, 4.0, shape, jnp.float32)


def draw_tokens(key, part):
    key = jax.random.fold_in(key, 23)
    return unit_field(key, (ROWS, LEN, D)).astype(jnp.bfloat16)


def draw_conditions(key, part):
    key = jax.random.fold_in(key, 29)
    return unit_field(key, (ROWS, SEGS, D)).astype(jnp.bfloat16)


def place_ends(entries, rng, smallest, largest):
    shape = entries.shape
    place = [jax.random.randint(jax.random.fold_in(rng, axis), (), 0, shape[axis]) for axis in range(len(shape))]
    entries = entries.at[tuple(place)].set(smallest)
    longest = shape.index(max(shape))
    place[longest] = (place[longest] + 1) % shape[longest]
    return entries.at[tuple(place)].set(largest)


def level_of(rng, shape, cuts, smallest, top_value):
    factor_of = 1.0
    for position, parts in cuts:
        draws = jax.random.uniform(jax.random.fold_in(jax.random.fold_in(rng, 6), position), (parts,), jnp.float32, smallest / len(cuts), top_value / len(cuts))
        factor_of = factor_of * jnp.repeat(jnp.exp(draws), shape[position] // parts).reshape((-1,) + (1,) * (len(shape) - 1 - position))
    return factor_of


def split_up(count, total, limit, slope):
    loads = [(1 << 20) // math.isqrt(standing ** slope) + 1 for standing in range(2, count + 1)]
    surplus, holding = total - limit - (count - 1), [1] * (count - 1)
    while surplus > 0:
        free = [i for i in range(count - 1) if holding[i] < limit]
        mass, budget = sum([loads[i] for i in free]), surplus
        for i in free:
            addition = min(limit - holding[i], max(1, budget * loads[i] // mass), surplus)
            holding[i] = holding[i] + addition
            surplus = surplus - addition
    return np.array([limit] + holding)


def ragged_sizes(key, number_of, total, most, lean):
    if number_of == 2:
        one = jax.random.randint(key, (), max(1, total - most), min(most, total - 1) + 1)
        return jnp.stack([one, total - one])
    sizes = jnp.asarray(split_up(number_of, total, most, lean), jnp.int32)
    twos = (number_of - 1) // 2
    giver, receiver = sizes[1:1 + 2 * twos:2], sizes[2:2 + 2 * twos:2]
    margin = jnp.minimum(giver - 1, most - receiver)
    moved = jax.random.randint(jax.random.fold_in(key, 1), (twos,), 0, 1 << 20) % (margin + 1)
    sizes = sizes.at[1:1 + 2 * twos:2].set(giver - moved).at[2:2 + 2 * twos:2].set(receiver + moved)
    return sizes[jax.random.permutation(jax.random.fold_in(key, 2), number_of)]


def bell_draw(stream_key, shape, scale, reach, shards=(), kind=jnp.bfloat16):
    drawn = jax.random.normal(stream_key, shape, jnp.float32) * scale
    if len(shards) > 0:
        drawn = level_of(stream_key, shape, shards, -0.22, 0.18) * drawn
    return jnp.clip(drawn, min=-reach, max=reach).astype(kind)


def setup_inputs(seed: int = 0) -> dict:
    seeds = jax.random.split(jax.random.key(seed), 11)
    tokens = draw_tokens(jax.random.fold_in(seeds[10], 71), 0)
    conditions = draw_conditions(jax.random.fold_in(seeds[10], 71), 0)
    segment_ids = jax.vmap(lambda own: jnp.searchsorted(jnp.cumsum(ragged_sizes(own, SEGS, LEN, 3 * LEN // 4 + 2, 2)), jnp.arange(LEN), side="right"))(jax.random.split(seeds[2], ROWS)).reshape((ROWS, LEN)).astype(jnp.int32)
    padding = place_ends((jax.random.randint(seeds[3], (ROWS, LEN), 0, 8) < 7).astype(jnp.int32), jax.random.fold_in(seeds[3], 1), 0, 1)
    targets = bell_draw(seeds[4], (ROWS, LEN, TARGET), 1.0, 6.0, ((0, 8), (1, 4)))
    cotangent = bell_draw(seeds[5], (ROWS, LEN, D), (1 / TARGET), 0.01953125, ((0, 8), (1, 4)), jnp.float32)
    tile_counts = draw_tile_counts(jax.random.fold_in(seeds[10], 71), 0)
    master = draw_master(jax.random.fold_in(seeds[10], 71), 0)
    first_moment = bell_draw(seeds[8], (OWNERS * CAP, TE), ((ROWS * LEN) ** 0.5 / TARGET), 1.75, ((0, 32),), jnp.float32)
    second_moment = jnp.clip(0.013888889 + 0.041666667 * jax.random.uniform(seeds[9], (OWNERS * CAP, TE), jnp.float32) ** level_of(seeds[9], (OWNERS * CAP, TE), ((0, 32),), -0.2, 0.2), 0.013888889, 0.055555556)
    return {"tokens": tokens, "conditions": conditions, "segment_ids": segment_ids, "padding": padding, "targets": targets, "cotangent": cotangent, "tile_counts": tile_counts, "master": master, "first_moment": first_moment, "second_moment": second_moment}


@jax.custom_vjp
def low(v):
    return lax.optimization_barrier(v.astype(jnp.bfloat16)).astype(jnp.float32)

@jax.custom_vjp
def low_back(v):
    return v

def low_keep(v):
    return (low(v), None)

def low_pass(kept, grad):
    return (grad,)

def back_keep(v):
    return (v, None)

def back_low(kept, grad):
    return (low(grad),)
low.defvjp(low_keep, low_pass)
low_back.defvjp(back_keep, back_low)
ln_eps = 1e-06
cos_eps = 1e-06
repa_weight = 0.5
beta_one = 0.5
beta_two = 0.5
learn_rate = 0.02
weight_decay = 0.01
adam_eps = 1e-08
highest = lax.Precision.HIGHEST

def param_shapes():
    return [(D, 6 * D), (6 * D,), (D, 3 * D), (D,), (D,), (D, D), (D,), (D, FF), (FF,), (FF, D), (D,), (D, PROJ), (PROJ,), (PROJ, PROJ), (PROJ,), (PROJ, TARGET), (TARGET,)]

def unpack(flat):
    pieces = []
    offset = 0
    for dims in param_shapes():
        extent = math.prod(dims)
        pieces.append(flat[offset:offset + extent].reshape(dims))
        offset = offset + extent
    return pieces

def held_rows(tile_counts):
    ends = jnp.cumsum(tile_counts).astype(jnp.int32)
    starts = (ends - tile_counts).astype(jnp.int32)
    tiles = jnp.arange(TILES, dtype=jnp.int32)
    owner = lax.optimization_barrier(jnp.sum((tiles[:, None] >= ends[None, :]).astype(jnp.int32), axis=1)).astype(jnp.int32)
    return (owner * CAP + tiles - jnp.take(starts, owner)).astype(jnp.int32)

def normalize(values):
    centred = values - lax.optimization_barrier(jnp.mean(values, axis=-1, keepdims=True))
    spread = lax.optimization_barrier(jnp.mean(centred * centred, axis=-1, keepdims=True))
    return centred * lax.rsqrt(spread + ln_eps)

def cosine_of(target, projected):
    inner_mean = lax.optimization_barrier(jnp.mean(projected * target, axis=-1))
    return inner_mean * lax.rsqrt(lax.optimization_barrier(jnp.mean(projected * projected, axis=-1)) + cos_eps) * lax.rsqrt(lax.optimization_barrier(jnp.mean(target * target, axis=-1)) + cos_eps)

def row_forward(params, row_tokens, row_cond, row_seg, row_pad, row_target):
    mod_weight, mod_bias, attend_weight, query_bias, value_bias, output_weight, output_bias, hidden_weight, hidden_bias, return_weight, return_bias, proj_one, proj_bias_one, proj_two, proj_bias_two, proj_three, proj_bias_three = params
    cond_act = low(jax.nn.silu(row_cond))
    modulation = low_back(jnp.dot(cond_act, mod_weight, precision=highest) + mod_bias)
    per_token = jnp.take(modulation, row_seg, axis=0)
    shift_one, scale_one, gate_one, shift_two, scale_two, gate_two = jnp.split(per_token, 6, axis=-1)
    attend_in = low(normalize(row_tokens) * (1.0 + scale_one) + shift_one)
    triple_bias = jnp.concatenate([query_bias, jnp.zeros_like(query_bias), value_bias])
    triple = low_back(low(jnp.dot(attend_in, attend_weight, precision=highest) + triple_bias))
    triple_view = triple.reshape(LEN, 3, HEADS, HEAD_DIM)
    queries = triple_view[:, 0]
    key_rows = triple_view[:, 1]
    values = triple_view[:, 2]
    scores = low_back(jnp.einsum('qhe,khe->hqk', queries, key_rows, precision=highest) * HEAD_DIM ** (-0.5))
    positions = jnp.arange(LEN, dtype=jnp.int32)
    allowed = (row_seg[:, None] == row_seg[None, :]) & ((row_pad[None, :] == 1) | (positions[:, None] == positions[None, :]))
    scores = jnp.where(allowed[None], scores, -1e+30)
    probs = low(jax.nn.softmax(scores, axis=-1))
    attended = low_back(low(jnp.einsum('hqk,khe->qhe', probs, values, precision=highest).reshape(LEN, D)))
    branch_one = low_back(jnp.dot(attended, output_weight, precision=highest) + output_bias)
    middle = row_tokens + gate_one * branch_one
    mlp_in = low(normalize(middle) * (1.0 + scale_two) + shift_two)
    hidden = low_back(jnp.dot(mlp_in, hidden_weight, precision=highest) + hidden_bias)
    activated = low(jax.nn.gelu(hidden, approximate=True))
    branch_two = low_back(jnp.dot(activated, return_weight, precision=highest) + return_bias)
    result = middle + gate_two * branch_two
    feature = low(result)
    first = low(jax.nn.silu(low_back(jnp.dot(feature, proj_one, precision=highest) + proj_bias_one)))
    second = low(jax.nn.silu(low_back(jnp.dot(first, proj_two, precision=highest) + proj_bias_two)))
    projected = low_back(jnp.dot(second, proj_three, precision=highest) + proj_bias_three)
    cosine = cosine_of(row_target, projected)
    row_loss = -jnp.sum(row_pad.astype(jnp.float32) * cosine)
    return (result, row_loss)

def reference(tokens, conditions, segment_ids, padding, targets, cotangent, tile_counts, master, first_moment, second_moment):
    token_f = tokens.astype(jnp.float32)
    cond_f = conditions.astype(jnp.float32)
    target_f = targets.astype(jnp.float32)
    rows_for = held_rows(tile_counts)

    def forward(token_in, cond_in, master_in):
        natural = jnp.take(master_in, rows_for, axis=0)
        params = unpack(low(natural).reshape(-1))
        row_step = jax.checkpoint(partial(row_forward, params))

        def one_row(inputs):
            return row_step(*inputs)
        results, losses = lax.map(one_row, (token_in, cond_in, segment_ids, padding, target_f))
        return (results, jnp.sum(losses))
    (result, total_loss), pullback = jax.vjp(forward, token_f, cond_f, master)
    grad_tokens, grad_conditions, grad_master = pullback((cotangent, jnp.ones((), jnp.float32) * repa_weight))
    new_first = beta_one * first_moment + (1.0 - beta_one) * grad_master
    new_second = beta_two * second_moment + (1.0 - beta_two) * grad_master * grad_master
    corr_one = 1.0 - beta_one ** STEP
    corr_two = 1.0 - beta_two ** STEP
    new_master = master - learn_rate * (new_first / corr_one / (jnp.sqrt(new_second / corr_two) + adam_eps) + weight_decay * master)
    return (result.astype(jnp.bfloat16), grad_tokens, grad_conditions, new_master, new_first, new_second)
```

```python
from functools import partial
import math

import jax
import jax.numpy as jnp
from jax import lax
from jax.experimental import pallas as pl
from jax.experimental.pallas import tpu as pltpu
from jax.sharding import PartitionSpec as P

HEADS = 16
HEAD_DIM = 72
D = 1152
FF = 4608
PROJ = 2048
TARGET = 768
SEGS = 4
STEP = 10
TILES = 15643


ln_eps = 1e-06
cos_eps = 1e-06
repa_weight = 0.5
beta_one = 0.5
beta_two = 0.5
learn_rate = 0.02
weight_decay = 0.01
adam_eps = 1e-08
highest = lax.Precision.HIGHEST


LANES = 128
SUBS = 16
MOD_ROWS = (D + 1) * 6 * D // LANES
VMEM_LIMIT = 56 * 1024 * 1024
MESH = pl.DeviceIdType.MESH


def param_shapes():
    return [
        (D, 6 * D),
        (6 * D,),
        (D, 3 * D),
        (D,),
        (D,),
        (D, D),
        (D,),
        (D, FF),
        (FF,),
        (FF, D),
        (D,),
        (D, PROJ),
        (PROJ,),
        (PROJ, PROJ),
        (PROJ,),
        (PROJ, TARGET),
        (TARGET,),
    ]


def param_rows():
    starts = []
    row = 0
    for dims in param_shapes():
        starts.append(row)
        row = row + math.prod(dims) // LANES
    return starts


CHUNK = {0: 128, 2: 128, 5: 384, 7: 128, 9: 512, 11: 384, 13: 256, 15: 1024}
EDGE_TILES = [3888, 3889, 3890, 3891, 5835, 5836, 6484, 6485, 9077, 9078, 9079, 11671, 12823, 12824, 14872, 14873, 15641, 15642]


def chunk_spans():
    spans = []
    base = {}
    rows = param_rows()
    for index, chunk in CHUNK.items():
        depth, width = param_shapes()[index]
        per_chunk = chunk * width // LANES // SUBS
        extra = 1 if rows[index] % SUBS else 0
        base[index] = len(spans)
        for step in range(depth // chunk):
            first = rows[index] // SUBS + step * per_chunk
            spans.append((first, first + per_chunk + extra - 1))
    return spans, base


def unpack_body(base, first_tile, per_chunk, tiles, shift, chunk, col_blocks, slots,
                first_ref, last_ref, starts_ref, packed, out_ref, landed, wide, sems):
    step = pl.program_id(0)

    def fetch(which, slot):
        low_tile = first_tile + which * per_chunk

        def one(owner, carry):
            begin = jnp.maximum(starts_ref[owner], low_tile)
            end = jnp.minimum(starts_ref[owner + 1], low_tile + tiles)
            size = pl.multiple_of((end - begin) * SUBS, SUBS)
            origin = pl.multiple_of((owner * slots + begin - starts_ref[owner]) * SUBS, SUBS)
            target = pl.multiple_of((begin - low_tile) * SUBS, SUBS)
            pltpu.make_async_copy(
                packed.at[pl.ds(origin, size)], landed.at[slot, pl.ds(target, size)], sems.at[slot]
            ).start()
            return carry

        lax.fori_loop(first_ref[base + which], last_ref[base + which] + 1, one, 0)

    @pl.when(step == 0)
    def _():
        fetch(0, 0)

    slot = step % 2

    @pl.when(step + 1 < pl.num_programs(0))
    def _():
        fetch(step + 1, (step + 1) % 2)

    pltpu.make_async_copy(packed.at[pl.ds(0, tiles * SUBS)], landed.at[slot], sems.at[slot]).wait()
    wide[...] = landed[slot].astype(jnp.float32)
    for block in range(col_blocks):
        out_ref[:, block * LANES : (block + 1) * LANES] = wide[
            pl.ds(shift + block, chunk, stride=col_blocks), :
        ].astype(jnp.bfloat16)


def unpack_weight(index, packed, slots, firsts, lasts, starts):
    depth, width = param_shapes()[index]
    chunk = CHUNK[index]
    col_blocks = width // LANES
    row = param_rows()[index]
    shift = row % SUBS
    per_chunk = chunk * col_blocks // SUBS
    tiles = per_chunk + (1 if shift else 0)
    base = chunk_spans()[1][index]
    return pl.pallas_call(
        partial(unpack_body, base, row // SUBS, per_chunk, tiles, shift, chunk, col_blocks, slots),
        out_shape=jax.ShapeDtypeStruct((depth, width), jnp.bfloat16),
        grid_spec=pltpu.PrefetchScalarGridSpec(
            num_scalar_prefetch=3,
            grid=(depth // chunk,),
            in_specs=[pl.BlockSpec(memory_space=pl.ANY)],
            out_specs=pl.BlockSpec((chunk, width), lambda i, *_: (i, 0)),
            scratch_shapes=[
                pltpu.VMEM((2, tiles * SUBS, LANES), jnp.bfloat16),
                pltpu.VMEM((tiles * SUBS, LANES), jnp.float32),
                pltpu.SemaphoreType.DMA((2,)),
            ],
        ),
        compiler_params=pltpu.CompilerParams(vmem_limit_bytes=VMEM_LIMIT),
        cost_estimate=pl.CostEstimate(flops=0, bytes_accessed=depth * width * 4, transcendentals=0),
        name="unpack_%d" % index,
    )(firsts, lasts, starts, packed)


def edge_read_body(table_ref, packed, out_ref, sem):
    count = out_ref.shape[0] // SUBS

    def one(i, carry):
        origin = pl.multiple_of(table_ref[i] * SUBS, SUBS)
        target = pl.multiple_of(i * SUBS, SUBS)
        pltpu.make_async_copy(packed.at[pl.ds(origin, SUBS)], out_ref.at[pl.ds(target, SUBS)], sem).start()
        return carry

    lax.fori_loop(0, count, one, 0)
    pltpu.make_async_copy(packed.at[pl.ds(0, count * SUBS)], out_ref, sem).wait()


def edge_read(packed, table):
    return pl.pallas_call(
        edge_read_body,
        out_shape=jax.ShapeDtypeStruct((len(EDGE_TILES) * SUBS, LANES), jnp.bfloat16),
        grid_spec=pltpu.PrefetchScalarGridSpec(
            num_scalar_prefetch=1,
            grid=(1,),
            in_specs=[pl.BlockSpec(memory_space=pl.ANY)],
            out_specs=pl.BlockSpec(memory_space=pltpu.VMEM),
            scratch_shapes=[pltpu.SemaphoreType.DMA],
        ),
        name="edge_read",
    )(table, packed)


def edge_write_body(layout, table_ref, *refs):
    pieces = refs[: len(layout)]
    out, wide, narrow, sem = refs[len(layout) + 1 :]
    wide[...] = jnp.zeros_like(wide)
    at = 0
    for piece, (skip, low, high) in zip(pieces, layout):
        at = at + skip
        wide[at : at + high - low, :] = piece[low:high, :]
        at = at + high - low
    narrow[...] = wide[...].astype(jnp.bfloat16)
    count = narrow.shape[0] // SUBS

    def one(i, carry):
        origin = pl.multiple_of(i * SUBS, SUBS)
        target = pl.multiple_of(table_ref[i] * SUBS, SUBS)
        pltpu.make_async_copy(narrow.at[pl.ds(origin, SUBS)], out.at[pl.ds(target, SUBS)], sem).start()
        return carry

    lax.fori_loop(0, count, one, 0)
    pltpu.make_async_copy(narrow, out.at[pl.ds(0, count * SUBS)], sem).wait()


def edge_write(pieces, buffer, table):
    count = table.shape[0]
    layout = [(skip, low, high) for skip, _, low, high in pieces]
    arrays = [array for _, array, _, _ in pieces]
    return pl.pallas_call(
        partial(edge_write_body, layout),
        out_shape=jax.ShapeDtypeStruct(buffer.shape, buffer.dtype),
        grid_spec=pltpu.PrefetchScalarGridSpec(
            num_scalar_prefetch=1,
            grid=(1,),
            in_specs=[pl.BlockSpec(memory_space=pltpu.VMEM)] * len(arrays)
            + [pl.BlockSpec(memory_space=pl.ANY)],
            out_specs=pl.BlockSpec(memory_space=pl.ANY),
            scratch_shapes=[
                pltpu.VMEM((count * SUBS, LANES), jnp.float32),
                pltpu.VMEM((count * SUBS, LANES), jnp.bfloat16),
                pltpu.SemaphoreType.DMA,
            ],
        ),
        input_output_aliases={1 + len(arrays): 0},
        name="edge_write",
    )(table, *arrays, buffer)


def weight_grad_body(base, first_tile, per_chunk, shift, chunk, col_blocks, slots, piece, chained,
                     first_ref, last_ref, starts_ref, x_ref, dy_ref, *rest):
    if chained:
        rest = rest[1:]
    out, ends_ref, wide, narrow, sems = rest
    step = pl.program_id(0)
    steps = pl.num_programs(0)
    slot = step % 2
    rows = chunk * col_blocks

    def drain(which):
        pltpu.make_async_copy(narrow.at[which], out.at[pl.ds(0, rows)], sems.at[which]).wait()

    @pl.when(step == 0)
    def _():
        wide[...] = jnp.zeros_like(wide)

    if shift:
        @pl.when(step > 0)
        def _():
            wide[0:SUBS, :] = wide[rows : rows + SUBS, :]

    left = x_ref[...].T
    for start in range(0, col_blocks, piece):
        part = jnp.dot(
            left, dy_ref[:, start * LANES : (start + piece) * LANES], preferred_element_type=jnp.float32
        )
        for block in range(piece):
            wide[pl.ds(shift + start + block, chunk, stride=col_blocks), :] = part[
                :, block * LANES : (block + 1) * LANES
            ]

    @pl.when(step >= 2)
    def _():
        drain(slot)

    narrow[slot] = wide[0:rows, :].astype(jnp.bfloat16)

    @pl.when(step == 0)
    def _():
        ends_ref[0:SUBS, :] = wide[0:SUBS, :]

    if shift:
        @pl.when(step == steps - 1)
        def _():
            ends_ref[SUBS : 2 * SUBS, :] = wide[rows : rows + SUBS, :]
    else:
        ends_ref[SUBS : 2 * SUBS, :] = jnp.zeros((SUBS, LANES), jnp.float32)

    low_tile = first_tile + step * per_chunk

    def one(owner, carry):
        begin = jnp.maximum(starts_ref[owner], low_tile)
        end = jnp.minimum(starts_ref[owner + 1], low_tile + per_chunk)
        size = pl.multiple_of(jnp.maximum(end - begin, 0) * SUBS, SUBS)
        target = pl.multiple_of((owner * slots + begin - starts_ref[owner]) * SUBS, SUBS)
        origin = pl.multiple_of((begin - low_tile) * SUBS, SUBS)

        @pl.when(end > begin)
        def _():
            pltpu.make_async_copy(
                narrow.at[slot, pl.ds(origin, size)], out.at[pl.ds(target, size)], sems.at[slot]
            ).start()

        return carry

    lax.fori_loop(first_ref[base + step], last_ref[base + step] + 1, one, 0)

    @pl.when(step == steps - 1)
    def _():
        drain(slot)

        @pl.when(steps > 1)
        def _():
            drain(1 - slot)


def weight_grad(index, left, right, buffer, owners, slots, firsts, lasts, starts):
    depth, width = param_shapes()[index]
    tokens = left.shape[0]
    chunk = CHUNK[index]
    col_blocks = width // LANES
    piece = next(p for p in (9, 8, 6) if col_blocks % p == 0)
    row = param_rows()[index]
    shift = row % SUBS
    per_chunk = chunk * col_blocks // SUBS
    base = chunk_spans()[1][index]
    shape = (owners * slots * SUBS, LANES)
    in_specs = [
        pl.BlockSpec((tokens, chunk), lambda i, *_: (0, i)),
        pl.BlockSpec((tokens, width), lambda i, *_: (0, 0)),
    ]
    operands = [firsts, lasts, starts, left, right]
    aliases = {}
    if buffer is not None:
        in_specs.append(pl.BlockSpec(memory_space=pl.ANY))
        operands.append(buffer)
        aliases = {5: 0}
    return pl.pallas_call(
        partial(weight_grad_body, base, row // SUBS, per_chunk, shift, chunk, col_blocks, slots, piece,
                buffer is not None),
        out_shape=(
            jax.ShapeDtypeStruct(shape, jnp.bfloat16),
            jax.ShapeDtypeStruct((2 * SUBS, LANES), jnp.float32),
        ),
        grid_spec=pltpu.PrefetchScalarGridSpec(
            num_scalar_prefetch=3,
            grid=(depth // chunk,),
            in_specs=in_specs,
            out_specs=(
                pl.BlockSpec(memory_space=pl.ANY),
                pl.BlockSpec((2 * SUBS, LANES), lambda i, *_: (0, 0)),
            ),
            scratch_shapes=[
                pltpu.VMEM((chunk * col_blocks + SUBS, LANES), jnp.float32),
                pltpu.VMEM((2, chunk * col_blocks, LANES), jnp.bfloat16),
                pltpu.SemaphoreType.DMA((2,)),
            ],
        ),
        input_output_aliases=aliases,
        compiler_params=pltpu.CompilerParams(vmem_limit_bytes=VMEM_LIMIT),
        cost_estimate=pl.CostEstimate(
            flops=2 * tokens * depth * width, bytes_accessed=depth * width * 2, transcendentals=0
        ),
        name="weight_grad_%d" % index,
    )(*operands)


class Grid:
    def __init__(self, side, depth):
        self.side = side
        self.sizes = {"u": side, "v": side, "z": depth}
        self.place = lax.axis_index("dp")
        self.core = self.place % 2
        outer = self.place // 2 // side
        inner = self.place // 2 % side
        self.mine = {
            "u": jnp.where(self.core == 0, outer, inner),
            "v": jnp.where(self.core == 0, inner, outer),
            "z": lax.axis_index("seq"),
        }
        self.sibling = (
            self.place + 1 - 2 * self.core,
            self.mine["z"],
        )

    def dp_of(self, first, second, core):
        outer = jnp.where(core == 0, first, second)
        inner = jnp.where(core == 0, second, first)
        return (outer * self.side + inner) * 2 + core

    def device(self, axis, other):
        at = dict(self.mine)
        at[axis] = other
        return (self.dp_of(at["u"], at["v"], self.core), at["z"])

    def other(self, axis, k):
        return k + (k >= self.mine[axis]).astype(jnp.int32)

    def seat(self, axis, other):
        mine = self.mine[axis]
        return mine - (mine > other).astype(jnp.int32)

    def partners(self):
        found = [self.sibling]
        for axis in ("u", "v", "z"):
            for k in range(self.sizes[axis] - 1):
                found.append(self.device(axis, self.other(axis, k)))
        return found

    def greet(self):
        barrier = pltpu.get_barrier_semaphore()
        partners = self.partners()
        for partner in partners:
            pl.semaphore_signal(barrier, inc=1, device_id=partner, device_id_type=MESH)
        pl.semaphore_wait(barrier, len(partners))


def split_slots(slots, shards):
    room = 32 * 1024 * 1024 // ((HELD + 2 * SLOTS) * shards * SUBS * LANES * 2)
    part = max(p for p in range(2, 19) if slots % p == 0 and p <= max(room, 2))
    late = max(1, round(part * 0.37))
    return slots // part, (part - late, late)


ORDERS = (("u", "v", "z"), ("u", "z", "v"))
LAG = 2
SLOTS = 4
HELD = 4 * LAG + 1


def gather_stream(grid, order, first_row, span, steps, own_ref, out_ref, sems):
    (send_a, recv_a, send_b, recv_b, send_c, recv_c, send_d, recv_d) = sems
    mine = grid.mine
    side = grid.side
    near, mid, far = order[2], order[1], order[0]

    def rows(q):
        return pl.ds(pl.multiple_of(first_row + q * span, SUBS), span)

    def copy(source, target, send, recv, device):
        return pltpu.make_async_remote_copy(
            src_ref=source, dst_ref=target, send_sem=send, recv_sem=recv, device_id=device,
            device_id_type=MESH,
        )

    def one_a(q, axis, k):
        other = grid.other(axis, k)
        mine_dp = grid.dp_of(mine["u"], mine["v"], grid.core)
        return copy(
            own_ref.at[rows(q)], out_ref.at[mine_dp, mine["z"], rows(q)],
            send_a.at[q % 4, k], recv_a.at[q, grid.seat(axis, other)],
            grid.device(axis, other),
        )

    def wait_a(q, axis, k):
        dp = grid.dp_of(mine["u"], mine["v"], grid.core)
        copy(
            own_ref.at[rows(q)], out_ref.at[dp, mine["z"], rows(q)],
            send_a.at[q % 4, k], recv_a.at[q, k], grid.device(axis, grid.other(axis, k)),
        ).wait_recv()

    def many_b(q, axis, k):
        other = grid.other(axis, k)
        seat = grid.seat(axis, other)
        if axis == "v":
            at = out_ref.at[grid.dp_of(mine["u"], mine["v"], grid.core), :, rows(q)]
            return [copy(at, at, send_b.at[q % 4, k], recv_b.at[q, seat], grid.device(axis, other))]
        found = []
        for v in range(side):
            at = out_ref.at[grid.dp_of(mine["u"], v, grid.core), mine["z"], rows(q)]
            found.append(copy(at, at, send_b.at[q % 4, k], recv_b.at[q, seat], grid.device(axis, other)))
        return found

    def many_c(q, k):
        other = grid.other("u", k)
        seat = grid.seat("u", other)
        found = []
        for v in range(side):
            at = out_ref.at[grid.dp_of(mine["u"], v, grid.core), :, rows(q)]
            found.append(copy(at, at, send_c.at[q % 4, k], recv_c.at[q, seat], grid.device("u", other)))
        return found

    def many_d(q):
        found = []
        for u in range(side):
            for v in range(side):
                at = out_ref.at[grid.dp_of(u, v, grid.core), :, rows(q)]
                found.append(copy(at, at, send_d.at[q % 4], recv_d.at[q], grid.sibling))
        return found

    def bulk(q, count, send, recv, device):
        at = out_ref.at[pl.ds(0, count), :, rows(q)]
        return copy(at, at, send, recv, device)

    def bulk_b(q, axis, send, recv):
        if axis == "v":
            at = out_ref.at[0, :, rows(q)]
        else:
            at = out_ref.at[pl.ds(0, side), 0, rows(q)]
        return copy(at, at, send, recv, grid.sibling)

    far_count = grid.sizes[near] - 1
    mid_count = grid.sizes[mid] - 1

    def stage_d(q):
        bulk(q, side, send_c.at[q % 4, 0], recv_c.at[q, 0], grid.sibling).wait_recv()
        for k in range(1, side - 1):
            bulk(q, side, send_c.at[q % 4, k], recv_c.at[q, k], grid.sibling).wait_recv()
        for k in range(side - 1):
            bulk(q, side, send_c.at[q % 4, k], recv_c.at[q, k], grid.sibling).wait_send()
        for one in many_d(q):
            one.start()

    def stage_c(q):
        for k in range(mid_count):
            bulk_b(q, mid, send_b.at[q % 4, k], recv_b.at[q, k]).wait_recv()
        for k in range(mid_count):
            bulk_b(q, mid, send_b.at[q % 4, k], recv_b.at[q, k]).wait_send()
        for k in range(side - 1):
            for one in many_c(q, k):
                one.start()

    def stage_b(q):
        for k in range(far_count):
            wait_a(q, near, k)
        for k in range(far_count):
            one_a(q, near, k).wait_send()
        for k in range(mid_count):
            for one in many_b(q, mid, k):
                one.start()

    def stage_a(q):
        for k in range(far_count):
            one_a(q, near, k).start()

    def finish(q):
        whole = bulk(q, side * side, send_d.at[q % 4], recv_d.at[q], grid.sibling)
        whole.wait_recv()
        whole.wait_send()

    return (stage_a, stage_b, stage_c, stage_d, finish)


def gather_body(side, depth, steps, parts, own_ref, out_ref, own_sem, *sems):
    grid = Grid(side, depth)
    keep = pltpu.make_async_copy(
        own_ref, out_ref.at[grid.dp_of(grid.mine["u"], grid.mine["v"], grid.core), grid.mine["z"]], own_sem
    )
    keep.start()
    grid.greet()
    streams = []
    first = 0
    for number, (order, part) in enumerate(zip(ORDERS, parts)):
        span = part * SUBS
        streams.append(
            gather_stream(grid, order, first, span, steps, own_ref, out_ref, sems[8 * number : 8 * number + 8])
        )
        first = first + steps * span
    keep.wait()

    def round_trip(s, carry):
        for late in range(4, -1, -1):
            q = s - LAG * late

            @pl.when((q >= 0) & (q < steps))
            def _(late=late, q=q):
                for stream in streams:
                    stream[late](q)

        return carry

    lax.fori_loop(0, steps + 4 * LAG, round_trip, 0)


def gather_slots(own, slots, data_count, seq_count):
    side = math.isqrt(data_count // 2)
    steps, parts = split_slots(slots, side * side * seq_count)
    dma = pltpu.SemaphoreType.DMA
    sems = []
    for order in ORDERS:
        sizes = {"u": side - 1, "v": side - 1, "z": seq_count - 1}
        for axis in (order[2], order[1], order[0]):
            sems.append(dma((4, sizes[axis])))
            sems.append(dma((steps, sizes[axis])))
        sems.append(dma((4,)))
        sems.append(dma((steps,)))
    return pl.pallas_call(
        partial(gather_body, side, seq_count, steps, parts),
        out_shape=jax.ShapeDtypeStruct((data_count, seq_count, slots * SUBS, LANES), jnp.bfloat16),
        in_specs=[pl.BlockSpec(memory_space=pl.ANY)],
        out_specs=pl.BlockSpec(memory_space=pl.ANY),
        scratch_shapes=[dma] + sems,
        compiler_params=pltpu.CompilerParams(
            collective_id=2, has_side_effects=True, vmem_limit_bytes=VMEM_LIMIT
        ),
        name="gather_slots",
    )(own).reshape(data_count * seq_count * slots * SUBS, LANES)


def reduce_stream(grid, order, first_row, span, steps, parts_ref, out_ref, refs):
    (own, rc, r1, r2, r3, outs, own_sem, out_sem, c_send, c_recv, s1, v1, s2, v2, s3, v3,
     c_credit, k1, k2, k3) = refs
    mine = grid.mine
    side = grid.side
    held = own.shape[0]
    mu, mv, mz = mine["u"], mine["v"], mine["z"]

    def rows(q):
        return pl.ds(pl.multiple_of(first_row + q * span, SUBS), span)

    def load(q, u, v):
        return pltpu.make_async_copy(
            parts_ref.at[grid.dp_of(u, v, grid.core), :, rows(q)], own.at[q % held, u, v], own_sem.at[q % held, u, v]
        )

    def give(q, u, v):
        return pltpu.make_async_remote_copy(
            src_ref=parts_ref.at[grid.dp_of(u, v, 1 - grid.core), :, rows(q)],
            dst_ref=rc.at[q % SLOTS, u, v],
            send_sem=c_send.at[q % SLOTS, u, v],
            recv_sem=c_recv.at[q % SLOTS, u, v],
            device_id=grid.sibling,
            device_id_type=MESH,
        )

    def block(q, stage, other):
        if stage == 0:
            return own.at[q % held, other]
        if order[1] == "v":
            return own.at[q % held, mu, other] if stage == 1 else own.at[q % held, mu, mv, other]
        return own.at[q % held, mu, :, other] if stage == 1 else own.at[q % held, mu, other, mz]

    landing = (r1, r2, r3)
    sends = (s1, s2, s3)
    arrivals = (v1, v2, v3)
    credits = (k1, k2, k3)

    def send(q, stage, k):
        axis = order[stage]
        other = grid.other(axis, k)
        seat = grid.seat(axis, other)
        return pltpu.make_async_remote_copy(
            src_ref=block(q, stage, other),
            dst_ref=landing[stage].at[q % SLOTS, seat],
            send_sem=sends[stage].at[q % SLOTS, k],
            recv_sem=arrivals[stage].at[q % SLOTS, seat],
            device_id=grid.device(axis, other),
            device_id_type=MESH,
        )

    def receive(q, stage, k):
        axis = order[stage]
        return pltpu.make_async_remote_copy(
            src_ref=block(q, stage, 0),
            dst_ref=landing[stage].at[q % SLOTS, k],
            send_sem=sends[stage].at[q % SLOTS, k],
            recv_sem=arrivals[stage].at[q % SLOTS, k],
            device_id=grid.device(axis, grid.other(axis, k)),
            device_id_type=MESH,
        )

    def write(q):
        return pltpu.make_async_copy(outs.at[q % 2], out_ref.at[rows(q)], out_sem.at[q % 2])

    def collect(q, stage):
        axis = order[stage]
        count = grid.sizes[axis] - 1
        for k in range(count):
            receive(q, stage, k).wait_recv()
        kept = block(q, stage, mine[axis])
        total = kept[...].astype(jnp.float32)
        for k in range(count):
            total = total + landing[stage][q % SLOTS, k].astype(jnp.float32)
        if stage < 2:
            kept[...] = total.astype(jnp.bfloat16)
        else:
            @pl.when(q >= 2)
            def _():
                write(q - 2).wait()

            outs[q % 2] = total.astype(jnp.bfloat16)
            write(q).start()
        for k in range(count):
            send(q, stage, k).wait_send()

        @pl.when(q + SLOTS < steps)
        def _():
            for k in range(count):
                pl.semaphore_signal(
                    credits[stage].at[mine[axis]], inc=1, device_id=grid.device(axis, grid.other(axis, k)),
                    device_id_type=MESH,
                )

    def launch(q, stage):
        axis = order[stage]
        count = grid.sizes[axis] - 1

        @pl.when(q >= SLOTS)
        def _():
            for k in range(count):
                pl.semaphore_wait(credits[stage].at[grid.other(axis, k)], 1)

        for k in range(count):
            send(q, stage, k).start()

    def begin(q):
        @pl.when(q >= SLOTS)
        def _():
            pl.semaphore_wait(c_credit, 1)

        for u in range(side):
            for v in range(side):
                give(q, u, v).start()
                load(q, u, v).start()

    def stage_c(q):
        for u in range(side):
            for v in range(side):
                load(q, u, v).wait()
                give(q, u, v).wait_recv()
                own[q % held, u, v] = (
                    own[q % held, u, v].astype(jnp.float32) + rc[q % SLOTS, u, v].astype(jnp.float32)
                ).astype(jnp.bfloat16)
        for u in range(side):
            for v in range(side):
                give(q, u, v).wait_send()

        @pl.when(q + SLOTS < steps)
        def _():
            pl.semaphore_signal(c_credit, inc=1, device_id=grid.sibling, device_id_type=MESH)

        launch(q, 0)

    def stage_one(q):
        collect(q, 0)
        launch(q, 1)

    def stage_two(q):
        collect(q, 1)
        launch(q, 2)

    def stage_three(q):
        collect(q, 2)

    return (begin, stage_c, stage_one, stage_two, stage_three), write


REDUCE_REFS = 20


def reduce_body(side, depth, steps, parts, parts_ref, out_ref, *refs):
    grid = Grid(side, depth)
    grid.greet()
    streams = []
    writes = []
    first = 0
    for number, (order, part) in enumerate(zip(ORDERS, parts)):
        span = part * SUBS
        stages, write = reduce_stream(
            grid, order, first, span, steps, parts_ref, out_ref,
            refs[REDUCE_REFS * number : REDUCE_REFS * (number + 1)],
        )
        streams.append(stages)
        writes.append(write)
        first = first + steps * span

    def round_trip(s, carry):
        for late in range(4, -1, -1):
            q = s - LAG * late

            @pl.when((q >= 0) & (q < steps))
            def _(late=late, q=q):
                for stream in streams:
                    stream[late](q)

        return carry

    lax.fori_loop(0, steps + 4 * LAG, round_trip, 0)
    for write in writes:
        for q in range(max(steps - 2, 0), steps):
            write(q).wait()


def reduce_slots(grads, slots, data_count, seq_count):
    side = math.isqrt(data_count // 2)
    steps, parts = split_slots(slots, side * side * seq_count)
    held = HELD
    dma = pltpu.SemaphoreType.DMA
    regular = pltpu.SemaphoreType.REGULAR
    bf16 = jnp.bfloat16
    scratch = []
    for order, part in zip(ORDERS, parts):
        span = part * SUBS
        sizes = {"u": side, "v": side, "z": seq_count}
        left = dict(sizes)
        scratch.append(pltpu.VMEM((held, side, side, seq_count, span, LANES), bf16))
        scratch.append(pltpu.VMEM((SLOTS, side, side, seq_count, span, LANES), bf16))
        for axis in order:
            del left[axis]
            rest = tuple(left[name] for name in ("u", "v", "z") if name in left)
            scratch.append(pltpu.VMEM((SLOTS, sizes[axis] - 1) + rest + (span, LANES), bf16))
        scratch.append(pltpu.VMEM((2, span, LANES), bf16))
        scratch.append(dma((held, side, side)))
        scratch.append(dma((2,)))
        scratch.append(dma((SLOTS, side, side)))
        scratch.append(dma((SLOTS, side, side)))
        for axis in order:
            scratch.append(dma((SLOTS, sizes[axis] - 1)))
            scratch.append(dma((SLOTS, sizes[axis] - 1)))
        scratch.append(regular)
        for axis in order:
            scratch.append(regular((sizes[axis],)))
    return pl.pallas_call(
        partial(reduce_body, side, seq_count, steps, parts),
        out_shape=jax.ShapeDtypeStruct((slots * SUBS, LANES), bf16),
        in_specs=[pl.BlockSpec(memory_space=pl.ANY)],
        out_specs=pl.BlockSpec(memory_space=pl.ANY),
        scratch_shapes=scratch,
        compiler_params=pltpu.CompilerParams(
            collective_id=1, has_side_effects=True, vmem_limit_bytes=VMEM_LIMIT
        ),
        name="reduce_slots",
    )(grads.reshape(data_count, seq_count, slots * SUBS, LANES))


UPDATE_TILES = 72


def update_body(mod_depth, own_ref, reduced, cond_ref, mod_ref, master, first, second,
                new_master, new_first, new_second, mod_rows, wide):
    step = pl.program_id(0)
    mod_blocks = 6 * D // LANES
    start_row = own_ref[0] * SUBS
    shift = lax.rem(start_row, mod_blocks)
    tiles = UPDATE_TILES
    piece = 9

    @pl.when((step == 0) & (start_row < MOD_ROWS))
    def _():
        for begin in range(0, mod_blocks, piece):
            part = jnp.dot(
                cond_ref[...], mod_ref[:, begin * LANES : (begin + piece) * LANES],
                preferred_element_type=jnp.float32,
            )
            for block in range(piece):
                mod_rows[pl.ds(begin + block, mod_depth, stride=mod_blocks), :] = part[
                    :, block * LANES : (block + 1) * LANES
                ]

    wide[...] = reduced[...].astype(jnp.float32)
    corr_one = 1.0 - beta_one**STEP
    corr_two = 1.0 - beta_two**STEP
    local = step * tiles + lax.broadcasted_iota(jnp.int32, (tiles, LANES), 0)
    used = local < own_ref[1]
    for sub in range(SUBS):
        columns = pl.ds(sub * LANES, LANES)
        from_mod = mod_rows[pl.ds(shift + step * tiles * SUBS + sub, tiles, stride=SUBS), :]
        is_mod = start_row + local * SUBS + sub < MOD_ROWS
        grad = jnp.where(is_mod, from_mod, wide[pl.ds(sub, tiles, stride=SUBS), :])
        grad = jnp.where(used, grad, 0.0)
        one = beta_one * first[:, columns] + (1.0 - beta_one) * grad
        two = beta_two * second[:, columns] + (1.0 - beta_two) * grad * grad
        held = master[:, columns]
        new_first[:, columns] = one
        new_second[:, columns] = two
        new_master[:, columns] = held - learn_rate * (
            one / corr_one / (jnp.sqrt(two / corr_two) + adam_eps) + weight_decay * held
        )


def update(reduced, cond_all, mod_all, own_first, master, first, second):
    slots, tile_len = master.shape
    images = cond_all.shape[0]
    tiles = UPDATE_TILES
    steps = -(-slots // tiles)
    mod_blocks = 6 * D // LANES
    mod_depth = -(-(steps * tiles * SUBS + mod_blocks) // mod_blocks)
    mod_depth = -(-mod_depth // 8) * 8
    extended = jnp.concatenate(
        [
            cond_all.T,
            jnp.ones((1, images), jnp.bfloat16),
            jnp.zeros((mod_depth, images), jnp.bfloat16),
        ],
        axis=0,
    )
    cond_own = lax.dynamic_slice_in_dim(
        extended, jnp.minimum(own_first[0] * SUBS // mod_blocks, D + 1), mod_depth, 0
    )
    wide_block = pl.BlockSpec((tiles, tile_len), lambda i, *_: (i, 0))
    return pl.pallas_call(
        partial(update_body, mod_depth),
        out_shape=(jax.ShapeDtypeStruct(master.shape, jnp.float32),) * 3,
        grid_spec=pltpu.PrefetchScalarGridSpec(
            num_scalar_prefetch=1,
            grid=(steps,),
            in_specs=[
                pl.BlockSpec((tiles * SUBS, LANES), lambda i, *_: (i, 0)),
                pl.BlockSpec((mod_depth, images), lambda i, *_: (0, 0)),
                pl.BlockSpec((images, 6 * D), lambda i, *_: (0, 0)),
                wide_block,
                wide_block,
                wide_block,
            ],
            out_specs=(wide_block,) * 3,
            scratch_shapes=[
                pltpu.VMEM((mod_depth * mod_blocks, LANES), jnp.float32),
                pltpu.VMEM((tiles * SUBS, LANES), jnp.float32),
            ],
        ),
        compiler_params=pltpu.CompilerParams(vmem_limit_bytes=VMEM_LIMIT),
        name="update",
    )(own_first, reduced, cond_own, mod_all, master, first, second)


def normalize(values):
    centred = values - jnp.mean(values, axis=-1, keepdims=True)
    spread = jnp.mean(centred * centred, axis=-1, keepdims=True)
    return centred * lax.rsqrt(spread + ln_eps)


def cosine_of(target, projected):
    inner_mean = jnp.mean(projected * target, axis=-1)
    return (
        inner_mean
        * lax.rsqrt(jnp.mean(projected * projected, axis=-1) + cos_eps)
        * lax.rsqrt(jnp.mean(target * target, axis=-1) + cos_eps)
    )


def gelu_tanh(values):
    return jax.nn.gelu(values, approximate=True)


def block_mask(seg_row, pad_row, start_row, block_len):
    full_len = seg_row.shape[0]
    query_seg = seg_row[start_row : start_row + block_len]
    query_pos = start_row + jnp.arange(block_len, dtype=jnp.int32)
    key_pos = jnp.arange(full_len, dtype=jnp.int32)
    same_image = query_seg[:, None] == seg_row[None, :]
    usable = (pad_row[None, :] == 1) | (query_pos[:, None] == key_pos[None, :])
    return same_image & usable


def attend_forward(queries, key_rows, values, seg_row, pad_row, block_len, scaling):
    out_parts = []
    lse_parts = []
    for start_row in range(0, queries.shape[0], block_len):
        allowed = block_mask(seg_row, pad_row, start_row, block_len)
        scores = (
            jnp.einsum(
                "qhe,khe->hqk",
                queries[start_row : start_row + block_len],
                key_rows,
                preferred_element_type=jnp.float32,
            )
            * scaling
        )
        scores = jnp.where(allowed[None], scores, -1e30)
        row_max = jnp.max(scores, axis=-1, keepdims=True)
        shifted = jnp.exp(scores - row_max)
        row_sum = jnp.sum(shifted, axis=-1, keepdims=True)
        probs_low = (shifted / row_sum).astype(jnp.bfloat16)
        out_parts.append(
            jnp.einsum("hqk,khe->qhe", probs_low, values, preferred_element_type=jnp.float32)
        )
        lse_parts.append(row_max[..., 0] + jnp.log(row_sum[..., 0]))
    return (jnp.concatenate(out_parts, 0), jnp.concatenate(lse_parts, 1))


def attend_backward(
    queries, key_rows, values, grad_out, row_lse, seg_row, pad_row, block_len, scaling
):
    grad_keys = jnp.zeros(key_rows.shape, jnp.float32)
    grad_values = jnp.zeros(values.shape, jnp.float32)
    query_parts = []
    for start_row in range(0, queries.shape[0], block_len):
        allowed = block_mask(seg_row, pad_row, start_row, block_len)
        query_block = queries[start_row : start_row + block_len]
        grad_block = grad_out[start_row : start_row + block_len]
        scores = (
            jnp.einsum("qhe,khe->hqk", query_block, key_rows, preferred_element_type=jnp.float32)
            * scaling
        )
        scores = jnp.where(allowed[None], scores, -1e30)
        probs = jnp.exp(scores - row_lse[:, start_row : start_row + block_len, None])
        probs_low = probs.astype(jnp.bfloat16)
        grad_probs = jnp.einsum(
            "qhe,khe->hqk", grad_block, values, preferred_element_type=jnp.float32
        )
        inner_sum = jnp.sum(probs * grad_probs, axis=-1, keepdims=True)
        grad_scores = (probs * (grad_probs - inner_sum)).astype(jnp.bfloat16)
        query_parts.append(
            jnp.einsum("hqk,khe->qhe", grad_scores, key_rows, preferred_element_type=jnp.float32)
            * scaling
        )
        grad_keys = (
            grad_keys
            + jnp.einsum(
                "hqk,qhe->khe", grad_scores, query_block, preferred_element_type=jnp.float32
            )
            * scaling
        )
        grad_values = grad_values + jnp.einsum(
            "hqk,qhe->khe", probs_low, grad_block, preferred_element_type=jnp.float32
        )
    return (jnp.concatenate(query_parts, 0), grad_keys, grad_values)


def shards(
    tokens,
    conditions,
    segment_ids,
    padding,
    targets,
    cotangent,
    tile_counts,
    master,
    first_moment,
    second_moment,
):
    seq_count = lax.axis_size("seq")
    data_count = lax.axis_size("dp")
    seq_place = lax.axis_index("seq")
    data_place = lax.axis_index("dp")
    owners = data_count * seq_count
    slot_count, tile_len = master.shape
    own_rows = slot_count * SUBS
    tile_ends = jnp.cumsum(tile_counts)
    starts = jnp.concatenate([jnp.zeros((1,), jnp.int32), tile_ends.astype(jnp.int32)])
    spans = jnp.asarray(chunk_spans()[0], jnp.int32)
    firsts = jnp.sum((tile_ends[None, :] <= spans[:, :1]).astype(jnp.int32), axis=1)
    lasts = jnp.sum((tile_ends[None, :] <= spans[:, 1:]).astype(jnp.int32), axis=1)
    edge_ids = jnp.asarray(EDGE_TILES, jnp.int32)
    edge_owner = jnp.sum((tile_ends[None, :] <= edge_ids[:, None]).astype(jnp.int32), axis=1)
    edge_slots = edge_owner * slot_count + edge_ids - jnp.take(starts, edge_owner)
    own_place = data_place * seq_count + seq_place
    own_start = lax.dynamic_index_in_dim(starts, own_place, 0, False)
    own_count = lax.dynamic_index_in_dim(tile_counts, own_place, 0, False)
    own_low = master.astype(jnp.bfloat16).reshape(own_rows, LANES)
    packed = gather_slots(own_low, slot_count, data_count, seq_count)

    mod_blocks = 6 * D // LANES
    own_first = jnp.stack([own_start, own_count])
    cond_f = conditions.astype(jnp.float32)
    cond_act, silu_cond_back = jax.vjp(jax.nn.silu, cond_f)
    cond_low = cond_act.astype(jnp.bfloat16)
    cond_all = lax.all_gather(cond_low, "dp", axis=0, tiled=True)
    image_rows = cond_all.shape[0]
    cond_all = cond_all.reshape(image_rows * SEGS, D)

    weights = {
        index: unpack_weight(index, packed, slot_count, firsts, lasts, starts) for index in CHUNK
    }
    mod_weight, attend_weight, output_weight, hidden_weight, return_weight, proj_one, proj_two, proj_three = (
        weights[index] for index in (0, 2, 5, 7, 9, 11, 13, 15)
    )
    edges = edge_read(packed, edge_slots)
    edge_flat = edges.reshape(-1)

    def bias(index):
        row = param_rows()[index]
        at = EDGE_TILES.index(row // SUBS) * SUBS + row % SUBS
        return edge_flat[at * LANES : at * LANES + param_shapes()[index][0]]

    mod_bias = bias(1)
    modulation = (
        jnp.einsum("rsd,dc->rsc", cond_low, mod_weight, preferred_element_type=jnp.float32) + mod_bias
    )
    query_bias, value_bias, output_bias, hidden_bias, return_bias = (bias(i) for i in (3, 4, 6, 8, 10))
    proj_bias_one, proj_bias_two, proj_bias_three = (bias(i) for i in (12, 14, 16))
    rows_dev, local_len, model_width = tokens.shape
    full_len = segment_ids.shape[1]
    heads_local = HEADS // seq_count
    group_width = model_width // seq_count
    scaling = HEAD_DIM ** (-0.5)
    block_len = min(512, full_len)
    token_start = seq_place * local_len
    local_seg = lax.dynamic_slice_in_dim(segment_ids, token_start, local_len, 1)
    local_pad = lax.dynamic_slice_in_dim(padding, token_start, local_len, 1).astype(jnp.float32)
    onehot = (local_seg[:, :, None] == jnp.arange(SEGS, dtype=jnp.int32)).astype(jnp.float32)
    per_token = jnp.einsum("rts,rsc->rtc", onehot, modulation, precision=highest)
    shift_one, scale_one, gate_one, shift_two, scale_two, gate_two = jnp.split(
        per_token, 6, axis=-1
    )
    token_f = tokens.astype(jnp.float32)
    normed_one, norm_back_one = jax.vjp(normalize, token_f)
    attend_in = (normed_one * (1.0 + scale_one) + shift_one).astype(jnp.bfloat16)
    triple_bias = jnp.concatenate([query_bias, jnp.zeros_like(query_bias), value_bias])
    triple = (
        jnp.einsum("rtd,dc->rtc", attend_in, attend_weight, preferred_element_type=jnp.float32)
        + triple_bias
    )
    triple_low = triple.astype(jnp.bfloat16).reshape(rows_dev, local_len, 3, model_width)
    head_rows = lax.all_to_all(triple_low, "seq", split_axis=3, concat_axis=1, tiled=True)
    (head_rows, output_weight, hidden_weight, return_weight, proj_one, proj_two, proj_three) = (
        lax.optimization_barrier(
            (head_rows, output_weight, hidden_weight, return_weight, proj_one, proj_two, proj_three)
        )
    )
    head_view = head_rows.reshape(rows_dev, full_len, 3, heads_local, HEAD_DIM)
    row_index = 0
    head_out, head_lse = attend_forward(
        head_view[row_index, :, 0],
        head_view[row_index, :, 1],
        head_view[row_index, :, 2],
        segment_ids[row_index],
        padding[row_index],
        block_len,
        scaling,
    )
    attended_parts = [head_out.astype(jnp.bfloat16).reshape(full_len, group_width)]
    lse_rows = [head_lse]
    head_attended = jnp.stack(attended_parts)
    attended = lax.all_to_all(head_attended, "seq", split_axis=1, concat_axis=2, tiled=True)
    branch_one = (
        jnp.einsum("rtd,dc->rtc", attended, output_weight, preferred_element_type=jnp.float32)
        + output_bias
    )
    middle = token_f + gate_one * branch_one
    normed_two, norm_back_two = jax.vjp(normalize, middle)
    mlp_in = (normed_two * (1.0 + scale_two) + shift_two).astype(jnp.bfloat16)
    hidden = (
        jnp.einsum("rtd,df->rtf", mlp_in, hidden_weight, preferred_element_type=jnp.float32)
        + hidden_bias
    )
    activated_f, gelu_back = jax.vjp(gelu_tanh, hidden)
    activated = activated_f.astype(jnp.bfloat16)
    branch_two = (
        jnp.einsum("rtf,fd->rtd", activated, return_weight, preferred_element_type=jnp.float32)
        + return_bias
    )
    result = middle + gate_two * branch_two
    feature = result.astype(jnp.bfloat16)
    first_pre = (
        jnp.einsum("rtd,dp->rtp", feature, proj_one, preferred_element_type=jnp.float32)
        + proj_bias_one
    )
    first_act, first_back = jax.vjp(jax.nn.silu, first_pre)
    first_low = first_act.astype(jnp.bfloat16)
    second_pre = (
        jnp.einsum("rtp,pc->rtc", first_low, proj_two, preferred_element_type=jnp.float32)
        + proj_bias_two
    )
    second_act, second_back = jax.vjp(jax.nn.silu, second_pre)
    second_low = second_act.astype(jnp.bfloat16)
    projected = (
        jnp.einsum("rtc,co->rto", second_low, proj_three, preferred_element_type=jnp.float32)
        + proj_bias_three
    )
    target_f = targets.astype(jnp.float32)
    cosine, cosine_back = jax.vjp(partial(cosine_of, target_f), projected)
    ends = {}

    def put(buffer, index, left, right):
        buffer, ends[index] = weight_grad(
            index,
            left.reshape(-1, left.shape[-1]),
            right.reshape(-1, right.shape[-1]),
            buffer,
            owners,
            slot_count,
            firsts,
            lasts,
            starts,
        )
        return buffer

    def summed(grad):
        return jnp.sum(grad.astype(jnp.float32), axis=(0, 1))

    (grad_projected,) = cosine_back(local_pad * -repa_weight)
    grad_projected = grad_projected.astype(jnp.bfloat16)
    grad_buffer = put(None, 15, second_low, grad_projected)
    sum_sixteen = summed(grad_projected)
    (grad_second,) = second_back(
        jnp.einsum("rto,co->rtc", grad_projected, proj_three, preferred_element_type=jnp.float32)
    )
    grad_second = grad_second.astype(jnp.bfloat16)
    grad_buffer = put(grad_buffer, 13, first_low, grad_second)
    sum_fourteen = summed(grad_second)
    (grad_first,) = first_back(
        jnp.einsum("rtc,pc->rtp", grad_second, proj_two, preferred_element_type=jnp.float32)
    )
    grad_first = grad_first.astype(jnp.bfloat16)
    grad_buffer = put(grad_buffer, 11, feature, grad_first)
    sum_twelve = summed(grad_first)
    grad_result = cotangent + jnp.einsum(
        "rtp,dp->rtd", grad_first, proj_one, preferred_element_type=jnp.float32
    )
    grad_gate_two = grad_result * branch_two
    grad_branch_two = (grad_result * gate_two).astype(jnp.bfloat16)
    grad_buffer = put(grad_buffer, 9, activated, grad_branch_two)
    sum_ten = summed(grad_branch_two)
    (grad_hidden,) = gelu_back(
        jnp.einsum(
            "rtd,fd->rtf", grad_branch_two, return_weight, preferred_element_type=jnp.float32
        )
    )
    grad_hidden = grad_hidden.astype(jnp.bfloat16)
    grad_buffer = put(grad_buffer, 7, mlp_in, grad_hidden)
    sum_eight = summed(grad_hidden)
    grad_mlp_in = jnp.einsum(
        "rtf,df->rtd", grad_hidden, hidden_weight, preferred_element_type=jnp.float32
    )
    grad_scale_two = grad_mlp_in * normed_two
    (grad_through_two,) = norm_back_two(grad_mlp_in * (1.0 + scale_two))
    grad_middle = grad_result + grad_through_two
    grad_gate_one = grad_middle * branch_one
    grad_branch_one = (grad_middle * gate_one).astype(jnp.bfloat16)
    grad_buffer = put(grad_buffer, 5, attended, grad_branch_one)
    sum_six = summed(grad_branch_one)
    grad_attended = jnp.einsum(
        "rtc,dc->rtd", grad_branch_one, output_weight, preferred_element_type=jnp.float32
    ).astype(jnp.bfloat16)
    head_grad = lax.all_to_all(grad_attended, "seq", split_axis=2, concat_axis=1, tiled=True)
    row_index = 0
    grad_query, grad_key, grad_value = attend_backward(
        head_view[row_index, :, 0],
        head_view[row_index, :, 1],
        head_view[row_index, :, 2],
        head_grad[row_index].reshape(full_len, heads_local, HEAD_DIM),
        lse_rows[row_index],
        segment_ids[row_index],
        padding[row_index],
        block_len,
        scaling,
    )
    triple_parts = [
        jnp.stack([grad_query, grad_key, grad_value], 1).reshape(full_len, 3, group_width)
    ]
    grad_triple_heads = jnp.stack(triple_parts).astype(jnp.bfloat16)
    grad_triple = lax.all_to_all(
        grad_triple_heads, "seq", split_axis=1, concat_axis=3, tiled=True
    ).reshape(rows_dev, local_len, 3 * model_width)
    grad_buffer = put(grad_buffer, 2, attend_in, grad_triple)
    triple_sums = summed(grad_triple)
    grad_attend_in = jnp.einsum(
        "rtc,dc->rtd", grad_triple, attend_weight, preferred_element_type=jnp.float32
    )
    grad_scale_one = grad_attend_in * normed_one
    (grad_through_one,) = norm_back_one(grad_attend_in * (1.0 + scale_one))
    grad_tokens = grad_middle + grad_through_one
    token_mod_grad = jnp.concatenate(
        [grad_attend_in, grad_scale_one, grad_gate_one, grad_mlp_in, grad_scale_two, grad_gate_two],
        axis=-1,
    )
    mod_part = jnp.einsum("rts,rtc->rsc", onehot, token_mod_grad, precision=highest)
    mod_grad = lax.psum(mod_part.astype(jnp.bfloat16), "seq")
    mod_all = lax.all_gather(mod_grad, "dp", axis=0, tiled=True).reshape(image_rows * SEGS, 6 * D)
    (grad_conditions,) = silu_cond_back(
        jnp.einsum("rsc,dc->rsd", mod_grad, mod_weight, preferred_element_type=jnp.float32)
    )

    def rows(vector):
        return vector.reshape(-1, LANES)

    rows_at = param_rows()

    def head(index):
        return (0, ends[index], rows_at[index] % SUBS, SUBS)

    def tail(index):
        return (0, ends[index], SUBS, SUBS + rows_at[index] % SUBS)

    def whole(vector):
        return (0, rows(vector), 0, vector.shape[0] // LANES)

    pieces = [
        (6,) + head(2)[1:],
        tail(2),
        whole(triple_sums[:model_width]),
        whole(triple_sums[2 * model_width :]),
        head(5),
        tail(5),
        whole(sum_six),
        head(7),
        tail(7),
        whole(sum_eight),
        head(9),
        tail(9),
        whole(sum_ten),
        head(11),
        tail(11),
        whole(sum_twelve),
        head(13),
        tail(13),
        whole(sum_fourteen),
        head(15),
        tail(15),
        whole(sum_sixteen),
    ]
    grad_buffer = edge_write(pieces, grad_buffer, edge_slots[EDGE_TILES.index(3891) :])
    reduced = reduce_slots(grad_buffer, slot_count, data_count, seq_count)
    new_master, new_first, new_second = update(
        reduced, cond_all, mod_all, own_first, master, first_moment, second_moment
    )
    return (
        result.astype(jnp.bfloat16),
        grad_tokens,
        grad_conditions,
        new_master,
        new_first,
        new_second,
    )


def solution(mesh):
    return jax.shard_map(
        shards,
        mesh=mesh,
        in_specs=(
            P("dp", "seq", None),
            P("dp", None, None),
            P("dp", None),
            P("dp", None),
            P("dp", "seq", None),
            P("dp", "seq", None),
            P(),
            P(("dp", "seq"), None),
            P(("dp", "seq"), None),
            P(("dp", "seq"), None),
        ),
        out_specs=(
            P("dp", "seq", None),
            P("dp", "seq", None),
            P("dp", None, None),
            P(("dp", "seq"), None),
            P(("dp", "seq"), None),
            P(("dp", "seq"), None),
        ),
        check_vma=False,
    )
```

```python
from functools import partial
import math

import jax
import jax.numpy as jnp
from jax import lax
from jax.experimental import pallas as pl
from jax.experimental.pallas import tpu as pltpu
from jax.sharding import PartitionSpec as P

HEADS = 16
HEAD_DIM = 72
D = 1152
FF = 4608
PROJ = 2048
TARGET = 768
SEGS = 4
STEP = 10
TILES = 15643


ln_eps = 1e-06
cos_eps = 1e-06
repa_weight = 0.5
beta_one = 0.5
beta_two = 0.5
learn_rate = 0.02
weight_decay = 0.01
adam_eps = 1e-08
highest = lax.Precision.HIGHEST


LANES = 128
SUBS = 16
MOD_ROWS = (D + 1) * 6 * D // LANES
VMEM_LIMIT = 56 * 1024 * 1024
MESH = pl.DeviceIdType.MESH


def param_shapes():
    return [
        (D, 6 * D),
        (6 * D,),
        (D, 3 * D),
        (D,),
        (D,),
        (D, D),
        (D,),
        (D, FF),
        (FF,),
        (FF, D),
        (D,),
        (D, PROJ),
        (PROJ,),
        (PROJ, PROJ),
        (PROJ,),
        (PROJ, TARGET),
        (TARGET,),
    ]


def param_rows():
    starts = []
    row = 0
    for dims in param_shapes():
        starts.append(row)
        row = row + math.prod(dims) // LANES
    return starts


CHUNK = {0: 128, 2: 128, 5: 384, 7: 128, 9: 512, 11: 384, 13: 256, 15: 1024}
EDGE_TILES = [3888, 3889, 3890, 3891, 5835, 5836, 6484, 6485, 9077, 9078, 9079, 11671, 12823, 12824, 14872, 14873, 15641, 15642]


def chunk_spans():
    spans = []
    base = {}
    rows = param_rows()
    for index, chunk in CHUNK.items():
        depth, width = param_shapes()[index]
        per_chunk = chunk * width // LANES // SUBS
        extra = 1 if rows[index] % SUBS else 0
        base[index] = len(spans)
        for step in range(depth // chunk):
            first = rows[index] // SUBS + step * per_chunk
            spans.append((first, first + per_chunk + extra - 1))
    return spans, base


def unpack_body(base, first_tile, per_chunk, tiles, shift, chunk, col_blocks, slots,
                first_ref, last_ref, starts_ref, packed, out_ref, landed, wide, sems):
    step = pl.program_id(0)

    def fetch(which, slot):
        low_tile = first_tile + which * per_chunk

        def one(owner, carry):
            begin = jnp.maximum(starts_ref[owner], low_tile)
            end = jnp.minimum(starts_ref[owner + 1], low_tile + tiles)
            size = pl.multiple_of((end - begin) * SUBS, SUBS)
            origin = pl.multiple_of((owner * slots + begin - starts_ref[owner]) * SUBS, SUBS)
            target = pl.multiple_of((begin - low_tile) * SUBS, SUBS)
            pltpu.make_async_copy(
                packed.at[pl.ds(origin, size)], landed.at[slot, pl.ds(target, size)], sems.at[slot]
            ).start()
            return carry

        lax.fori_loop(first_ref[base + which], last_ref[base + which] + 1, one, 0)

    @pl.when(step == 0)
    def _():
        fetch(0, 0)

    slot = step % 2

    @pl.when(step + 1 < pl.num_programs(0))
    def _():
        fetch(step + 1, (step + 1) % 2)

    pltpu.make_async_copy(packed.at[pl.ds(0, tiles * SUBS)], landed.at[slot], sems.at[slot]).wait()
    wide[...] = landed[slot].astype(jnp.float32)
    for block in range(col_blocks):
        out_ref[:, block * LANES : (block + 1) * LANES] = wide[
            pl.ds(shift + block, chunk, stride=col_blocks), :
        ].astype(jnp.bfloat16)


def unpack_weight(index, packed, slots, firsts, lasts, starts):
    depth, width = param_shapes()[index]
    chunk = CHUNK[index]
    col_blocks = width // LANES
    row = param_rows()[index]
    shift = row % SUBS
    per_chunk = chunk * col_blocks // SUBS
    tiles = per_chunk + (1 if shift else 0)
    base = chunk_spans()[1][index]
    return pl.pallas_call(
        partial(unpack_body, base, row // SUBS, per_chunk, tiles, shift, chunk, col_blocks, slots),
        out_shape=jax.ShapeDtypeStruct((depth, width), jnp.bfloat16),
        grid_spec=pltpu.PrefetchScalarGridSpec(
            num_scalar_prefetch=3,
            grid=(depth // chunk,),
            in_specs=[pl.BlockSpec(memory_space=pl.ANY)],
            out_specs=pl.BlockSpec((chunk, width), lambda i, *_: (i, 0)),
            scratch_shapes=[
                pltpu.VMEM((2, tiles * SUBS, LANES), jnp.bfloat16),
                pltpu.VMEM((tiles * SUBS, LANES), jnp.float32),
                pltpu.SemaphoreType.DMA((2,)),
            ],
        ),
        compiler_params=pltpu.CompilerParams(vmem_limit_bytes=VMEM_LIMIT),
        cost_estimate=pl.CostEstimate(flops=0, bytes_accessed=depth * width * 4, transcendentals=0),
        name="unpack_%d" % index,
    )(firsts, lasts, starts, packed)


def edge_read_body(table_ref, packed, out_ref, sem):
    count = out_ref.shape[0] // SUBS

    def one(i, carry):
        origin = pl.multiple_of(table_ref[i] * SUBS, SUBS)
        target = pl.multiple_of(i * SUBS, SUBS)
        pltpu.make_async_copy(packed.at[pl.ds(origin, SUBS)], out_ref.at[pl.ds(target, SUBS)], sem).start()
        return carry

    lax.fori_loop(0, count, one, 0)
    pltpu.make_async_copy(packed.at[pl.ds(0, count * SUBS)], out_ref, sem).wait()


def edge_read(packed, table):
    return pl.pallas_call(
        edge_read_body,
        out_shape=jax.ShapeDtypeStruct((len(EDGE_TILES) * SUBS, LANES), jnp.bfloat16),
        grid_spec=pltpu.PrefetchScalarGridSpec(
            num_scalar_prefetch=1,
            grid=(1,),
            in_specs=[pl.BlockSpec(memory_space=pl.ANY)],
            out_specs=pl.BlockSpec(memory_space=pltpu.VMEM),
            scratch_shapes=[pltpu.SemaphoreType.DMA],
        ),
        name="edge_read",
    )(table, packed)


def edge_write_body(layout, table_ref, *refs):
    pieces = refs[: len(layout)]
    out, wide, narrow, sem = refs[len(layout) + 1 :]
    wide[...] = jnp.zeros_like(wide)
    at = 0
    for piece, (skip, low, high) in zip(pieces, layout):
        at = at + skip
        wide[at : at + high - low, :] = piece[low:high, :]
        at = at + high - low
    narrow[...] = wide[...].astype(jnp.bfloat16)
    count = narrow.shape[0] // SUBS

    def one(i, carry):
        origin = pl.multiple_of(i * SUBS, SUBS)
        target = pl.multiple_of(table_ref[i] * SUBS, SUBS)
        pltpu.make_async_copy(narrow.at[pl.ds(origin, SUBS)], out.at[pl.ds(target, SUBS)], sem).start()
        return carry

    lax.fori_loop(0, count, one, 0)
    pltpu.make_async_copy(narrow, out.at[pl.ds(0, count * SUBS)], sem).wait()


def edge_write(pieces, buffer, table):
    count = table.shape[0]
    layout = [(skip, low, high) for skip, _, low, high in pieces]
    arrays = [array for _, array, _, _ in pieces]
    return pl.pallas_call(
        partial(edge_write_body, layout),
        out_shape=jax.ShapeDtypeStruct(buffer.shape, buffer.dtype),
        grid_spec=pltpu.PrefetchScalarGridSpec(
            num_scalar_prefetch=1,
            grid=(1,),
            in_specs=[pl.BlockSpec(memory_space=pltpu.VMEM)] * len(arrays)
            + [pl.BlockSpec(memory_space=pl.ANY)],
            out_specs=pl.BlockSpec(memory_space=pl.ANY),
            scratch_shapes=[
                pltpu.VMEM((count * SUBS, LANES), jnp.float32),
                pltpu.VMEM((count * SUBS, LANES), jnp.bfloat16),
                pltpu.SemaphoreType.DMA,
            ],
        ),
        input_output_aliases={1 + len(arrays): 0},
        name="edge_write",
    )(table, *arrays, buffer)


def weight_grad_body(base, first_tile, per_chunk, shift, chunk, col_blocks, slots, piece, chained,
                     first_ref, last_ref, starts_ref, x_ref, dy_ref, *rest):
    if chained:
        rest = rest[1:]
    out, ends_ref, wide, narrow, sems = rest
    step = pl.program_id(0)
    steps = pl.num_programs(0)
    slot = step % 2
    rows = chunk * col_blocks

    def drain(which):
        pltpu.make_async_copy(narrow.at[which], out.at[pl.ds(0, rows)], sems.at[which]).wait()

    @pl.when(step == 0)
    def _():
        wide[...] = jnp.zeros_like(wide)

    if shift:
        @pl.when(step > 0)
        def _():
            wide[0:SUBS, :] = wide[rows : rows + SUBS, :]

    left = x_ref[...].T
    for start in range(0, col_blocks, piece):
        part = jnp.dot(
            left, dy_ref[:, start * LANES : (start + piece) * LANES], preferred_element_type=jnp.float32
        )
        for block in range(piece):
            wide[pl.ds(shift + start + block, chunk, stride=col_blocks), :] = part[
                :, block * LANES : (block + 1) * LANES
            ]

    @pl.when(step >= 2)
    def _():
        drain(slot)

    narrow[slot] = wide[0:rows, :].astype(jnp.bfloat16)

    @pl.when(step == 0)
    def _():
        ends_ref[0:SUBS, :] = wide[0:SUBS, :]

    if shift:
        @pl.when(step == steps - 1)
        def _():
            ends_ref[SUBS : 2 * SUBS, :] = wide[rows : rows + SUBS, :]
    else:
        ends_ref[SUBS : 2 * SUBS, :] = jnp.zeros((SUBS, LANES), jnp.float32)

    low_tile = first_tile + step * per_chunk

    def one(owner, carry):
        begin = jnp.maximum(starts_ref[owner], low_tile)
        end = jnp.minimum(starts_ref[owner + 1], low_tile + per_chunk)
        size = pl.multiple_of(jnp.maximum(end - begin, 0) * SUBS, SUBS)
        target = pl.multiple_of((owner * slots + begin - starts_ref[owner]) * SUBS, SUBS)
        origin = pl.multiple_of((begin - low_tile) * SUBS, SUBS)

        @pl.when(end > begin)
        def _():
            pltpu.make_async_copy(
                narrow.at[slot, pl.ds(origin, size)], out.at[pl.ds(target, size)], sems.at[slot]
            ).start()

        return carry

    lax.fori_loop(first_ref[base + step], last_ref[base + step] + 1, one, 0)

    @pl.when(step == steps - 1)
    def _():
        drain(slot)

        @pl.when(steps > 1)
        def _():
            drain(1 - slot)


def weight_grad(index, left, right, buffer, owners, slots, firsts, lasts, starts):
    depth, width = param_shapes()[index]
    tokens = left.shape[0]
    chunk = CHUNK[index]
    col_blocks = width // LANES
    piece = next(p for p in (9, 8, 6) if col_blocks % p == 0)
    row = param_rows()[index]
    shift = row % SUBS
    per_chunk = chunk * col_blocks // SUBS
    base = chunk_spans()[1][index]
    shape = (owners * slots * SUBS, LANES)
    in_specs = [
        pl.BlockSpec((tokens, chunk), lambda i, *_: (0, i)),
        pl.BlockSpec((tokens, width), lambda i, *_: (0, 0)),
    ]
    operands = [firsts, lasts, starts, left, right]
    aliases = {}
    if buffer is not None:
        in_specs.append(pl.BlockSpec(memory_space=pl.ANY))
        operands.append(buffer)
        aliases = {5: 0}
    return pl.pallas_call(
        partial(weight_grad_body, base, row // SUBS, per_chunk, shift, chunk, col_blocks, slots, piece,
                buffer is not None),
        out_shape=(
            jax.ShapeDtypeStruct(shape, jnp.bfloat16),
            jax.ShapeDtypeStruct((2 * SUBS, LANES), jnp.float32),
        ),
        grid_spec=pltpu.PrefetchScalarGridSpec(
            num_scalar_prefetch=3,
            grid=(depth // chunk,),
            in_specs=in_specs,
            out_specs=(
                pl.BlockSpec(memory_space=pl.ANY),
                pl.BlockSpec((2 * SUBS, LANES), lambda i, *_: (0, 0)),
            ),
            scratch_shapes=[
                pltpu.VMEM((chunk * col_blocks + SUBS, LANES), jnp.float32),
                pltpu.VMEM((2, chunk * col_blocks, LANES), jnp.bfloat16),
                pltpu.SemaphoreType.DMA((2,)),
            ],
        ),
        input_output_aliases=aliases,
        compiler_params=pltpu.CompilerParams(vmem_limit_bytes=VMEM_LIMIT),
        cost_estimate=pl.CostEstimate(
            flops=2 * tokens * depth * width, bytes_accessed=depth * width * 2, transcendentals=0
        ),
        name="weight_grad_%d" % index,
    )(*operands)


class Grid:
    def __init__(self, side, depth):
        self.side = side
        self.sizes = {"u": side, "v": side, "z": depth}
        self.place = lax.axis_index("dp")
        self.core = self.place % 2
        outer = self.place // 2 // side
        inner = self.place // 2 % side
        self.mine = {
            "u": jnp.where(self.core == 0, outer, inner),
            "v": jnp.where(self.core == 0, inner, outer),
            "z": lax.axis_index("seq"),
        }
        self.sibling = (
            self.place + 1 - 2 * self.core,
            self.mine["z"],
        )

    def dp_of(self, first, second, core):
        outer = jnp.where(core == 0, first, second)
        inner = jnp.where(core == 0, second, first)
        return (outer * self.side + inner) * 2 + core

    def device(self, axis, other):
        at = dict(self.mine)
        at[axis] = other
        return (self.dp_of(at["u"], at["v"], self.core), at["z"])

    def other(self, axis, k):
        return k + (k >= self.mine[axis]).astype(jnp.int32)

    def seat(self, axis, other):
        mine = self.mine[axis]
        return mine - (mine > other).astype(jnp.int32)

    def partners(self):
        found = [self.sibling]
        for axis in ("u", "v", "z"):
            for k in range(self.sizes[axis] - 1):
                found.append(self.device(axis, self.other(axis, k)))
        return found

    def greet(self):
        barrier = pltpu.get_barrier_semaphore()
        partners = self.partners()
        for partner in partners:
            pl.semaphore_signal(barrier, inc=1, device_id=partner, device_id_type=MESH)
        pl.semaphore_wait(barrier, len(partners))


def split_slots(slots, shards):
    room = 32 * 1024 * 1024 // ((HELD + 2 * SLOTS) * shards * SUBS * LANES * 2)
    part = max(p for p in range(2, 13) if slots % p == 0 and p <= max(room, 2))
    late = max(1, round(part * 0.34))
    return slots // part, (part - late, late)


ORDERS = (("u", "v", "z"), ("u", "z", "v"))
LAG = 2
SLOTS = 4
HELD = 4 * LAG + 1


def gather_stream(grid, order, first_row, span, steps, own_ref, out_ref, sems):
    (send_a, recv_a, send_b, recv_b, send_c, recv_c, send_d, recv_d) = sems
    mine = grid.mine
    side = grid.side
    near, mid, far = order[2], order[1], order[0]

    def rows(q):
        return pl.ds(pl.multiple_of(first_row + q * span, SUBS), span)

    def copy(source, target, send, recv, device):
        return pltpu.make_async_remote_copy(
            src_ref=source, dst_ref=target, send_sem=send, recv_sem=recv, device_id=device,
            device_id_type=MESH,
        )

    def one_a(q, axis, k):
        other = grid.other(axis, k)
        mine_dp = grid.dp_of(mine["u"], mine["v"], grid.core)
        return copy(
            own_ref.at[rows(q)], out_ref.at[mine_dp, mine["z"], rows(q)],
            send_a.at[q % 4, k], recv_a.at[q, grid.seat(axis, other)],
            grid.device(axis, other),
        )

    def wait_a(q, axis, k):
        dp = grid.dp_of(mine["u"], mine["v"], grid.core)
        copy(
            own_ref.at[rows(q)], out_ref.at[dp, mine["z"], rows(q)],
            send_a.at[q % 4, k], recv_a.at[q, k], grid.device(axis, grid.other(axis, k)),
        ).wait_recv()

    def many_b(q, axis, k):
        other = grid.other(axis, k)
        seat = grid.seat(axis, other)
        if axis == "v":
            at = out_ref.at[grid.dp_of(mine["u"], mine["v"], grid.core), :, rows(q)]
            return [copy(at, at, send_b.at[q % 4, k], recv_b.at[q, seat], grid.device(axis, other))]
        found = []
        for v in range(side):
            at = out_ref.at[grid.dp_of(mine["u"], v, grid.core), mine["z"], rows(q)]
            found.append(copy(at, at, send_b.at[q % 4, k], recv_b.at[q, seat], grid.device(axis, other)))
        return found

    def many_c(q, k):
        other = grid.other("u", k)
        seat = grid.seat("u", other)
        found = []
        for v in range(side):
            at = out_ref.at[grid.dp_of(mine["u"], v, grid.core), :, rows(q)]
            found.append(copy(at, at, send_c.at[q % 4, k], recv_c.at[q, seat], grid.device("u", other)))
        return found

    def many_d(q):
        found = []
        for u in range(side):
            for v in range(side):
                at = out_ref.at[grid.dp_of(u, v, grid.core), :, rows(q)]
                found.append(copy(at, at, send_d.at[q % 4], recv_d.at[q], grid.sibling))
        return found

    def bulk(q, count, send, recv, device):
        at = out_ref.at[pl.ds(0, count), :, rows(q)]
        return copy(at, at, send, recv, device)

    def bulk_b(q, axis, send, recv):
        if axis == "v":
            at = out_ref.at[0, :, rows(q)]
        else:
            at = out_ref.at[pl.ds(0, side), 0, rows(q)]
        return copy(at, at, send, recv, grid.sibling)

    far_count = grid.sizes[near] - 1
    mid_count = grid.sizes[mid] - 1

    def stage_d(q):
        bulk(q, side, send_c.at[q % 4, 0], recv_c.at[q, 0], grid.sibling).wait_recv()
        for k in range(1, side - 1):
            bulk(q, side, send_c.at[q % 4, k], recv_c.at[q, k], grid.sibling).wait_recv()
        for k in range(side - 1):
            bulk(q, side, send_c.at[q % 4, k], recv_c.at[q, k], grid.sibling).wait_send()
        for one in many_d(q):
            one.start()

    def stage_c(q):
        for k in range(mid_count):
            bulk_b(q, mid, send_b.at[q % 4, k], recv_b.at[q, k]).wait_recv()
        for k in range(mid_count):
            bulk_b(q, mid, send_b.at[q % 4, k], recv_b.at[q, k]).wait_send()
        for k in range(side - 1):
            for one in many_c(q, k):
                one.start()

    def stage_b(q):
        for k in range(far_count):
            wait_a(q, near, k)
        for k in range(far_count):
            one_a(q, near, k).wait_send()
        for k in range(mid_count):
            for one in many_b(q, mid, k):
                one.start()

    def stage_a(q):
        for k in range(far_count):
            one_a(q, near, k).start()

    def finish(q):
        whole = bulk(q, side * side, send_d.at[q % 4], recv_d.at[q], grid.sibling)
        whole.wait_recv()
        whole.wait_send()

    return (stage_a, stage_b, stage_c, stage_d, finish)


def gather_body(side, depth, steps, parts, own_ref, out_ref, own_sem, *sems):
    grid = Grid(side, depth)
    keep = pltpu.make_async_copy(
        own_ref, out_ref.at[grid.dp_of(grid.mine["u"], grid.mine["v"], grid.core), grid.mine["z"]], own_sem
    )
    keep.start()
    grid.greet()
    streams = []
    first = 0
    for number, (order, part) in enumerate(zip(ORDERS, parts)):
        span = part * SUBS
        streams.append(
            gather_stream(grid, order, first, span, steps, own_ref, out_ref, sems[8 * number : 8 * number + 8])
        )
        first = first + steps * span
    keep.wait()

    def round_trip(s, carry):
        for late in range(4, -1, -1):
            q = s - LAG * late

            @pl.when((q >= 0) & (q < steps))
            def _(late=late, q=q):
                for stream in streams:
                    stream[late](q)

        return carry

    lax.fori_loop(0, steps + 4 * LAG, round_trip, 0)


def gather_slots(own, slots, data_count, seq_count):
    side = math.isqrt(data_count // 2)
    steps, parts = split_slots(slots, side * side * seq_count)
    dma = pltpu.SemaphoreType.DMA
    sems = []
    for order in ORDERS:
        sizes = {"u": side - 1, "v": side - 1, "z": seq_count - 1}
        for axis in (order[2], order[1], order[0]):
            sems.append(dma((4, sizes[axis])))
            sems.append(dma((steps, sizes[axis])))
        sems.append(dma((4,)))
        sems.append(dma((steps,)))
    return pl.pallas_call(
        partial(gather_body, side, seq_count, steps, parts),
        out_shape=jax.ShapeDtypeStruct((data_count, seq_count, slots * SUBS, LANES), jnp.bfloat16),
        in_specs=[pl.BlockSpec(memory_space=pltpu.VMEM)],
        out_specs=pl.BlockSpec(memory_space=pl.ANY),
        scratch_shapes=[dma] + sems,
        compiler_params=pltpu.CompilerParams(
            collective_id=2, has_side_effects=True, vmem_limit_bytes=VMEM_LIMIT
        ),
        name="gather_slots",
    )(own).reshape(data_count * seq_count * slots * SUBS, LANES)


def reduce_stream(grid, order, first_row, span, steps, parts_ref, out_ref, refs):
    (own, rc, r1, r2, r3, outs, own_sem, out_sem, c_send, c_recv, s1, v1, s2, v2, s3, v3,
     c_credit, k1, k2, k3) = refs
    mine = grid.mine
    side = grid.side
    held = own.shape[0]
    mu, mv, mz = mine["u"], mine["v"], mine["z"]

    def rows(q):
        return pl.ds(pl.multiple_of(first_row + q * span, SUBS), span)

    def load(q, u, v):
        return pltpu.make_async_copy(
            parts_ref.at[grid.dp_of(u, v, grid.core), :, rows(q)], own.at[q % held, u, v], own_sem.at[q % held, u, v]
        )

    def give(q, u, v):
        return pltpu.make_async_remote_copy(
            src_ref=parts_ref.at[grid.dp_of(u, v, 1 - grid.core), :, rows(q)],
            dst_ref=rc.at[q % SLOTS, u, v],
            send_sem=c_send.at[q % SLOTS, u, v],
            recv_sem=c_recv.at[q % SLOTS, u, v],
            device_id=grid.sibling,
            device_id_type=MESH,
        )

    def block(q, stage, other):
        if stage == 0:
            return own.at[q % held, other]
        if order[1] == "v":
            return own.at[q % held, mu, other] if stage == 1 else own.at[q % held, mu, mv, other]
        return own.at[q % held, mu, :, other] if stage == 1 else own.at[q % held, mu, other, mz]

    landing = (r1, r2, r3)
    sends = (s1, s2, s3)
    arrivals = (v1, v2, v3)
    credits = (k1, k2, k3)

    def send(q, stage, k):
        axis = order[stage]
        other = grid.other(axis, k)
        seat = grid.seat(axis, other)
        return pltpu.make_async_remote_copy(
            src_ref=block(q, stage, other),
            dst_ref=landing[stage].at[q % SLOTS, seat],
            send_sem=sends[stage].at[q % SLOTS, k],
            recv_sem=arrivals[stage].at[q % SLOTS, seat],
            device_id=grid.device(axis, other),
            device_id_type=MESH,
        )

    def receive(q, stage, k):
        axis = order[stage]
        return pltpu.make_async_remote_copy(
            src_ref=block(q, stage, 0),
            dst_ref=landing[stage].at[q % SLOTS, k],
            send_sem=sends[stage].at[q % SLOTS, k],
            recv_sem=arrivals[stage].at[q % SLOTS, k],
            device_id=grid.device(axis, grid.other(axis, k)),
            device_id_type=MESH,
        )

    def write(q):
        return pltpu.make_async_copy(outs.at[q % 2], out_ref.at[rows(q)], out_sem.at[q % 2])

    def collect(q, stage):
        axis = order[stage]
        count = grid.sizes[axis] - 1
        for k in range(count):
            receive(q, stage, k).wait_recv()
        kept = block(q, stage, mine[axis])
        total = kept[...].astype(jnp.float32)
        for k in range(count):
            total = total + landing[stage][q % SLOTS, k].astype(jnp.float32)
        if stage < 2:
            kept[...] = total.astype(jnp.bfloat16)
        else:
            @pl.when(q >= 2)
            def _():
                write(q - 2).wait()

            outs[q % 2] = total.astype(jnp.bfloat16)
            write(q).start()
        for k in range(count):
            send(q, stage, k).wait_send()

        @pl.when(q + SLOTS < steps)
        def _():
            for k in range(count):
                pl.semaphore_signal(
                    credits[stage].at[mine[axis]], inc=1, device_id=grid.device(axis, grid.other(axis, k)),
                    device_id_type=MESH,
                )

    def launch(q, stage):
        axis = order[stage]
        count = grid.sizes[axis] - 1

        @pl.when(q >= SLOTS)
        def _():
            for k in range(count):
                pl.semaphore_wait(credits[stage].at[grid.other(axis, k)], 1)

        for k in range(count):
            send(q, stage, k).start()

    def begin(q):
        @pl.when(q >= SLOTS)
        def _():
            pl.semaphore_wait(c_credit, 1)

        for u in range(side):
            for v in range(side):
                give(q, u, v).start()
                load(q, u, v).start()

    def stage_c(q):
        for u in range(side):
            for v in range(side):
                load(q, u, v).wait()
                give(q, u, v).wait_recv()
                own[q % held, u, v] = (
                    own[q % held, u, v].astype(jnp.float32) + rc[q % SLOTS, u, v].astype(jnp.float32)
                ).astype(jnp.bfloat16)
        for u in range(side):
            for v in range(side):
                give(q, u, v).wait_send()

        @pl.when(q + SLOTS < steps)
        def _():
            pl.semaphore_signal(c_credit, inc=1, device_id=grid.sibling, device_id_type=MESH)

        launch(q, 0)

    def stage_one(q):
        collect(q, 0)
        launch(q, 1)

    def stage_two(q):
        collect(q, 1)
        launch(q, 2)

    def stage_three(q):
        collect(q, 2)

    return (begin, stage_c, stage_one, stage_two, stage_three), write


REDUCE_REFS = 20


MOD_BLOCKS = 6 * D // LANES
IMAGE_ROWS = SEGS * MOD_BLOCKS
SENT_ROWS = -(-IMAGE_ROWS // SUBS) * SUBS
COND_CHUNK = 128
MOD_REFS = 14
MOD_STEPS = 11 + D // COND_CHUNK


def modulation_stages(grid, part_ref, weight_ref, all_ref, cond_ref, refs):
    (arrived, dense, held, send_z, recv_z, send_v, recv_v, send_u, recv_u, send_c, recv_c, loads,
     done_sem, summed) = refs
    mine = grid.mine
    side = grid.side
    depth = grid.sizes["z"]
    here = grid.dp_of(mine["u"], mine["v"], grid.core)
    chunks = D // COND_CHUNK

    def to_z(k, seat):
        return pltpu.make_async_remote_copy(
            src_ref=part_ref, dst_ref=arrived.at[seat], send_sem=send_z.at[k], recv_sem=recv_z.at[seat],
            device_id=grid.device("z", grid.other("z", k)), device_id_type=MESH,
        )

    def rows_of(dp):
        return summed.at[dp]

    def one(dp, send, recv, device):
        return pltpu.make_async_remote_copy(
            src_ref=rows_of(dp), dst_ref=rows_of(dp), send_sem=send, recv_sem=recv, device_id=device,
            device_id_type=MESH,
        )

    def load(i):
        return pltpu.make_async_copy(
            weight_ref.at[pl.ds(pl.multiple_of(i * COND_CHUNK, COND_CHUNK), COND_CHUNK)],
            held.at[i % 2], loads.at[i % 2],
        )

    def v_copies():
        return [
            one(here, send_v.at[k], recv_v.at[grid.seat("v", grid.other("v", k))], grid.device("v", grid.other("v", k)))
            for k in range(side - 1)
        ]

    def u_copies():
        return [
            one(grid.dp_of(mine["u"], v, grid.core), send_u.at[k, v],
                recv_u.at[grid.seat("u", grid.other("u", k)), v], grid.device("u", grid.other("u", k)))
            for k in range(side - 1)
            for v in range(side)
        ]

    def c_copies():
        return [
            one(grid.dp_of(u, v, grid.core), send_c.at[u, v], recv_c.at[u, v], grid.sibling)
            for u in range(side)
            for v in range(side)
        ]

    def run(s):
        @pl.when(s == 0)
        def _():
            for k in range(depth - 1):
                to_z(k, grid.seat("z", grid.other("z", k))).start()

        @pl.when(s == 2)
        def _():
            for k in range(depth - 1):
                to_z(k, k).wait_recv()
            total = part_ref[...].astype(jnp.float32)
            for k in range(depth - 1):
                total = total + arrived[k].astype(jnp.float32)
            total = total.astype(jnp.bfloat16).astype(jnp.float32)
            summed[here] = total[:IMAGE_ROWS]
            for k in range(depth - 1):
                to_z(k, 0).wait_send()
            for copy in v_copies():
                copy.start()
            load(0).start()
            load(1).start()
            dense[...] = jnp.zeros_like(dense)
            for block in range(MOD_BLOCKS):
                dense[0:SEGS, block * LANES : (block + 1) * LANES] = summed[
                    here, pl.ds(block, SEGS, stride=MOD_BLOCKS), :
                ]

        @pl.when(s == 4)
        def _():
            for k in range(side - 1):
                one(here, send_v.at[k], recv_v.at[k], grid.sibling).wait_recv()
            for copy in v_copies():
                copy.wait_send()
            for copy in u_copies():
                copy.start()

        @pl.when(s == 6)
        def _():
            for k in range(side - 1):
                for v in range(side):
                    one(here, send_u.at[k, v], recv_u.at[k, v], grid.sibling).wait_recv()
            for copy in u_copies():
                copy.wait_send()
            for copy in c_copies():
                copy.start()

        @pl.when(s == 9)
        def _():
            for copy in c_copies():
                copy.wait_recv()
            for copy in c_copies():
                copy.wait_send()
            pltpu.make_async_copy(summed, all_ref, done_sem).start()

        i = s - 10

        @pl.when((i >= 0) & (i < chunks))
        def _():
            load(i).wait()
            cond_ref[:, pl.ds(pl.multiple_of(i * COND_CHUNK, COND_CHUNK), COND_CHUNK)] = lax.dot_general(
                dense[...].astype(jnp.bfloat16), held[i % 2], (((1,), (1,)), ((), ())),
                preferred_element_type=jnp.float32,
            )

            @pl.when(i + 2 < chunks)
            def _():
                load(i + 2).start()

        @pl.when(s == 10 + chunks)
        def _():
            pltpu.make_async_copy(summed, all_ref, done_sem).wait()

    return run


def reduce_body(side, depth, steps, parts, parts_ref, part_ref, weight_ref, out_ref, all_ref, cond_ref, *refs):
    grid = Grid(side, depth)
    grid.greet()
    modulation_step = modulation_stages(grid, part_ref, weight_ref, all_ref, cond_ref, refs[:MOD_REFS])
    refs = refs[MOD_REFS:]
    streams = []
    writes = []
    first = 0
    for number, (order, part) in enumerate(zip(ORDERS, parts)):
        span = part * SUBS
        stages, write = reduce_stream(
            grid, order, first, span, steps, parts_ref, out_ref,
            refs[REDUCE_REFS * number : REDUCE_REFS * (number + 1)],
        )
        streams.append(stages)
        writes.append(write)
        first = first + steps * span

    def round_trip(s, carry):
        for late in range(4, -1, -1):
            q = s - LAG * late

            @pl.when((q >= 0) & (q < steps))
            def _(late=late, q=q):
                for stream in streams:
                    stream[late](q)

        modulation_step(s)
        return carry

    lax.fori_loop(0, max(steps + 4 * LAG, MOD_STEPS), round_trip, 0)
    for write in writes:
        for q in range(max(steps - 2, 0), steps):
            write(q).wait()


def reduce_slots(grads, mod_part, mod_weight, slots, data_count, seq_count):
    side = math.isqrt(data_count // 2)
    steps, parts = split_slots(slots, side * side * seq_count)
    held = HELD
    dma = pltpu.SemaphoreType.DMA
    regular = pltpu.SemaphoreType.REGULAR
    bf16 = jnp.bfloat16
    f32 = jnp.float32
    scratch = [
        pltpu.VMEM((seq_count - 1, SENT_ROWS, LANES), bf16),
        pltpu.VMEM((8, 6 * D), f32),
        pltpu.VMEM((2, COND_CHUNK, 6 * D), bf16),
        dma((seq_count - 1,)),
        dma((seq_count - 1,)),
        dma((side - 1,)),
        dma((side - 1,)),
        dma((side - 1, side)),
        dma((side - 1, side)),
        dma((side, side)),
        dma((side, side)),
        dma((2,)),
        dma,
        pltpu.VMEM((data_count, IMAGE_ROWS, LANES), f32),
    ]
    for order, part in zip(ORDERS, parts):
        span = part * SUBS
        sizes = {"u": side, "v": side, "z": seq_count}
        left = dict(sizes)
        scratch.append(pltpu.VMEM((held, side, side, seq_count, span, LANES), bf16))
        scratch.append(pltpu.VMEM((SLOTS, side, side, seq_count, span, LANES), bf16))
        for axis in order:
            del left[axis]
            rest = tuple(left[name] for name in ("u", "v", "z") if name in left)
            scratch.append(pltpu.VMEM((SLOTS, sizes[axis] - 1) + rest + (span, LANES), bf16))
        scratch.append(pltpu.VMEM((2, span, LANES), bf16))
        scratch.append(dma((held, side, side)))
        scratch.append(dma((2,)))
        scratch.append(dma((SLOTS, side, side)))
        scratch.append(dma((SLOTS, side, side)))
        for axis in order:
            scratch.append(dma((SLOTS, sizes[axis] - 1)))
            scratch.append(dma((SLOTS, sizes[axis] - 1)))
        scratch.append(regular)
        for axis in order:
            scratch.append(regular((sizes[axis],)))
    return pl.pallas_call(
        partial(reduce_body, side, seq_count, steps, parts),
        out_shape=(
            jax.ShapeDtypeStruct((slots * SUBS, LANES), bf16),
            jax.ShapeDtypeStruct((data_count, IMAGE_ROWS, LANES), f32),
            jax.ShapeDtypeStruct((8, D), f32),
        ),
        in_specs=[
            pl.BlockSpec(memory_space=pl.ANY),
            pl.BlockSpec(memory_space=pltpu.VMEM),
            pl.BlockSpec(memory_space=pl.ANY),
        ],
        out_specs=(
            pl.BlockSpec(memory_space=pl.ANY),
            pl.BlockSpec(memory_space=pl.ANY),
            pl.BlockSpec(memory_space=pltpu.VMEM),
        ),
        scratch_shapes=scratch,
        compiler_params=pltpu.CompilerParams(
            collective_id=1, has_side_effects=True, vmem_limit_bytes=VMEM_LIMIT
        ),
        name="reduce_slots",
    )(grads.reshape(data_count, seq_count, slots * SUBS, LANES), mod_part, mod_weight)


UPDATE_TILES = 72


def update_body(mod_depth, own_ref, reduced, cond_ref, mod_ref, master, first, second,
                new_master, new_first, new_second, mod_rows, wide):
    step = pl.program_id(0)
    mod_blocks = 6 * D // LANES
    start_row = own_ref[0] * SUBS
    shift = lax.rem(start_row, mod_blocks)
    tiles = UPDATE_TILES
    piece = 9

    @pl.when((step == 0) & (start_row < MOD_ROWS))
    def _():
        images = cond_ref.shape[1]
        for begin in range(0, mod_blocks, piece):
            grads = [
                mod_ref[pl.ds(begin + block, images, stride=mod_blocks), :].astype(jnp.bfloat16)
                for block in range(piece)
            ]
            part = jnp.dot(
                cond_ref[...], jnp.concatenate(grads, axis=1), preferred_element_type=jnp.float32
            )
            for block in range(piece):
                mod_rows[pl.ds(begin + block, mod_depth, stride=mod_blocks), :] = part[
                    :, block * LANES : (block + 1) * LANES
                ]

    wide[...] = reduced[...].astype(jnp.float32)
    corr_one = 1.0 - beta_one**STEP
    corr_two = 1.0 - beta_two**STEP
    local = step * tiles + lax.broadcasted_iota(jnp.int32, (tiles, LANES), 0)
    used = local < own_ref[1]
    for sub in range(SUBS):
        columns = pl.ds(sub * LANES, LANES)
        from_mod = mod_rows[pl.ds(shift + step * tiles * SUBS + sub, tiles, stride=SUBS), :]
        is_mod = start_row + local * SUBS + sub < MOD_ROWS
        grad = jnp.where(is_mod, from_mod, wide[pl.ds(sub, tiles, stride=SUBS), :])
        grad = jnp.where(used, grad, 0.0)
        one = beta_one * first[:, columns] + (1.0 - beta_one) * grad
        two = beta_two * second[:, columns] + (1.0 - beta_two) * grad * grad
        held = master[:, columns]
        new_first[:, columns] = one
        new_second[:, columns] = two
        new_master[:, columns] = held - learn_rate * (
            one / corr_one / (jnp.sqrt(two / corr_two) + adam_eps) + weight_decay * held
        )


def own_conditions(cond_all, own_first, slots):
    images = cond_all.shape[0]
    steps = -(-slots // UPDATE_TILES)
    depth = -(-(steps * UPDATE_TILES * SUBS + MOD_BLOCKS) // MOD_BLOCKS)
    depth = -(-depth // 8) * 8
    extended = jnp.concatenate(
        [cond_all.T, jnp.ones((1, images), jnp.bfloat16), jnp.zeros((depth, images), jnp.bfloat16)],
        axis=0,
    )
    return lax.dynamic_slice_in_dim(
        extended, jnp.minimum(own_first[0] * SUBS // MOD_BLOCKS, D + 1), depth, 0
    )


def update(reduced, cond_own, mod_all, own_first, master, first, second):
    slots, tile_len = master.shape
    mod_depth, images = cond_own.shape
    tiles = UPDATE_TILES
    steps = -(-slots // tiles)
    wide_block = pl.BlockSpec((tiles, tile_len), lambda i, *_: (i, 0))
    return pl.pallas_call(
        partial(update_body, mod_depth),
        out_shape=(jax.ShapeDtypeStruct(master.shape, jnp.float32),) * 3,
        grid_spec=pltpu.PrefetchScalarGridSpec(
            num_scalar_prefetch=1,
            grid=(steps,),
            in_specs=[
                pl.BlockSpec((tiles * SUBS, LANES), lambda i, *_: (i, 0)),
                pl.BlockSpec((mod_depth, images), lambda i, *_: (0, 0)),
                pl.BlockSpec(mod_all.shape, lambda i, *_: (0, 0)),
                wide_block,
                wide_block,
                wide_block,
            ],
            out_specs=(wide_block,) * 3,
            scratch_shapes=[
                pltpu.VMEM((mod_depth * MOD_BLOCKS, LANES), jnp.float32),
                pltpu.VMEM((tiles * SUBS, LANES), jnp.float32),
            ],
        ),
        compiler_params=pltpu.CompilerParams(vmem_limit_bytes=VMEM_LIMIT),
        name="update",
    )(own_first, reduced, cond_own, mod_all, master, first, second)


def normalize(values):
    centred = values - jnp.mean(values, axis=-1, keepdims=True)
    spread = jnp.mean(centred * centred, axis=-1, keepdims=True)
    return centred * lax.rsqrt(spread + ln_eps)


def cosine_of(target, projected):
    inner_mean = jnp.mean(projected * target, axis=-1)
    return (
        inner_mean
        * lax.rsqrt(jnp.mean(projected * projected, axis=-1) + cos_eps)
        * lax.rsqrt(jnp.mean(target * target, axis=-1) + cos_eps)
    )


def gelu_tanh(values):
    return jax.nn.gelu(values, approximate=True)


def block_mask(seg_row, pad_row, start_row, block_len):
    full_len = seg_row.shape[0]
    query_seg = seg_row[start_row : start_row + block_len]
    query_pos = start_row + jnp.arange(block_len, dtype=jnp.int32)
    key_pos = jnp.arange(full_len, dtype=jnp.int32)
    same_image = query_seg[:, None] == seg_row[None, :]
    usable = (pad_row[None, :] == 1) | (query_pos[:, None] == key_pos[None, :])
    return same_image & usable


def attend_forward(queries, key_rows, values, seg_row, pad_row, block_len, scaling):
    out_parts = []
    lse_parts = []
    for start_row in range(0, queries.shape[0], block_len):
        allowed = block_mask(seg_row, pad_row, start_row, block_len)
        scores = (
            jnp.einsum(
                "qhe,khe->hqk",
                queries[start_row : start_row + block_len],
                key_rows,
                preferred_element_type=jnp.float32,
            )
            * scaling
        )
        scores = jnp.where(allowed[None], scores, -1e30)
        row_max = jnp.max(scores, axis=-1, keepdims=True)
        shifted = jnp.exp(scores - row_max)
        row_sum = jnp.sum(shifted, axis=-1, keepdims=True)
        probs_low = (shifted / row_sum).astype(jnp.bfloat16)
        out_parts.append(
            jnp.einsum("hqk,khe->qhe", probs_low, values, preferred_element_type=jnp.float32)
        )
        lse_parts.append(row_max[..., 0] + jnp.log(row_sum[..., 0]))
    return (jnp.concatenate(out_parts, 0), jnp.concatenate(lse_parts, 1))


def attend_backward(
    queries, key_rows, values, grad_out, row_lse, seg_row, pad_row, block_len, scaling
):
    grad_keys = jnp.zeros(key_rows.shape, jnp.float32)
    grad_values = jnp.zeros(values.shape, jnp.float32)
    query_parts = []
    for start_row in range(0, queries.shape[0], block_len):
        allowed = block_mask(seg_row, pad_row, start_row, block_len)
        query_block = queries[start_row : start_row + block_len]
        grad_block = grad_out[start_row : start_row + block_len]
        scores = (
            jnp.einsum("qhe,khe->hqk", query_block, key_rows, preferred_element_type=jnp.float32)
            * scaling
        )
        scores = jnp.where(allowed[None], scores, -1e30)
        probs = jnp.exp(scores - row_lse[:, start_row : start_row + block_len, None])
        probs_low = probs.astype(jnp.bfloat16)
        grad_probs = jnp.einsum(
            "qhe,khe->hqk", grad_block, values, preferred_element_type=jnp.float32
        )
        inner_sum = jnp.sum(probs * grad_probs, axis=-1, keepdims=True)
        grad_scores = (probs * (grad_probs - inner_sum)).astype(jnp.bfloat16)
        query_parts.append(
            jnp.einsum("hqk,khe->qhe", grad_scores, key_rows, preferred_element_type=jnp.float32)
            * scaling
        )
        grad_keys = (
            grad_keys
            + jnp.einsum(
                "hqk,qhe->khe", grad_scores, query_block, preferred_element_type=jnp.float32
            )
            * scaling
        )
        grad_values = grad_values + jnp.einsum(
            "hqk,qhe->khe", probs_low, grad_block, preferred_element_type=jnp.float32
        )
    return (jnp.concatenate(query_parts, 0), grad_keys, grad_values)


def shards(
    tokens,
    conditions,
    segment_ids,
    padding,
    targets,
    cotangent,
    tile_counts,
    master,
    first_moment,
    second_moment,
):
    seq_count = lax.axis_size("seq")
    data_count = lax.axis_size("dp")
    seq_place = lax.axis_index("seq")
    data_place = lax.axis_index("dp")
    owners = data_count * seq_count
    slot_count, tile_len = master.shape
    own_rows = slot_count * SUBS
    tile_ends = jnp.cumsum(tile_counts)
    starts = jnp.concatenate([jnp.zeros((1,), jnp.int32), tile_ends.astype(jnp.int32)])
    spans = jnp.asarray(chunk_spans()[0], jnp.int32)
    firsts = jnp.sum((tile_ends[None, :] <= spans[:, :1]).astype(jnp.int32), axis=1)
    lasts = jnp.sum((tile_ends[None, :] <= spans[:, 1:]).astype(jnp.int32), axis=1)
    edge_ids = jnp.asarray(EDGE_TILES, jnp.int32)
    edge_owner = jnp.sum((tile_ends[None, :] <= edge_ids[:, None]).astype(jnp.int32), axis=1)
    edge_slots = edge_owner * slot_count + edge_ids - jnp.take(starts, edge_owner)
    own_place = data_place * seq_count + seq_place
    own_start = lax.dynamic_index_in_dim(starts, own_place, 0, False)
    own_count = lax.dynamic_index_in_dim(tile_counts, own_place, 0, False)
    own_low = master.astype(jnp.bfloat16).reshape(own_rows, LANES)
    packed = gather_slots(own_low, slot_count, data_count, seq_count)

    own_first = jnp.stack([own_start, own_count])
    cond_f = conditions.astype(jnp.float32)
    cond_act, silu_cond_back = jax.vjp(jax.nn.silu, cond_f)
    cond_low = cond_act.astype(jnp.bfloat16)
    weights = {
        index: unpack_weight(index, packed, slot_count, firsts, lasts, starts)
        for index in (0, 2, 5, 7, 9, 15)
    }
    mod_weight, attend_weight, output_weight, hidden_weight, return_weight, proj_three = (
        weights[index] for index in (0, 2, 5, 7, 9, 15)
    )
    edges = edge_read(packed, edge_slots)
    edge_flat = edges.reshape(-1)

    def bias(index):
        row = param_rows()[index]
        at = EDGE_TILES.index(row // SUBS) * SUBS + row % SUBS
        return edge_flat[at * LANES : at * LANES + param_shapes()[index][0]]

    mod_bias = bias(1)
    modulation = (
        jnp.einsum("rsd,dc->rsc", cond_low, mod_weight, preferred_element_type=jnp.float32) + mod_bias
    )
    query_bias, value_bias, output_bias, hidden_bias, return_bias = (bias(i) for i in (3, 4, 6, 8, 10))
    proj_bias_one, proj_bias_two, proj_bias_three = (bias(i) for i in (12, 14, 16))
    rows_dev, local_len, model_width = tokens.shape
    full_len = segment_ids.shape[1]
    heads_local = HEADS // seq_count
    group_width = model_width // seq_count
    scaling = HEAD_DIM ** (-0.5)
    block_len = min(512, full_len)
    token_start = seq_place * local_len
    local_seg = lax.dynamic_slice_in_dim(segment_ids, token_start, local_len, 1)
    local_pad = lax.dynamic_slice_in_dim(padding, token_start, local_len, 1).astype(jnp.float32)
    onehot = (local_seg[:, :, None] == jnp.arange(SEGS, dtype=jnp.int32)).astype(jnp.float32)
    per_token = jnp.einsum("rts,rsc->rtc", onehot, modulation, precision=highest)
    shift_one, scale_one, gate_one, shift_two, scale_two, gate_two = jnp.split(
        per_token, 6, axis=-1
    )
    token_f = tokens.astype(jnp.float32)
    normed_one, norm_back_one = jax.vjp(normalize, token_f)
    attend_in = (normed_one * (1.0 + scale_one) + shift_one).astype(jnp.bfloat16)
    triple_bias = jnp.concatenate([query_bias, jnp.zeros_like(query_bias), value_bias])
    triple = (
        jnp.einsum("rtd,dc->rtc", attend_in, attend_weight, preferred_element_type=jnp.float32)
        + triple_bias
    )
    triple_low = triple.astype(jnp.bfloat16).reshape(rows_dev, local_len, 3, model_width)
    head_rows = lax.all_to_all(triple_low, "seq", split_axis=3, concat_axis=1, tiled=True)
    (head_rows, output_weight, hidden_weight, return_weight, proj_three) = lax.optimization_barrier(
        (head_rows, output_weight, hidden_weight, return_weight, proj_three)
    )
    head_view = head_rows.reshape(rows_dev, full_len, 3, heads_local, HEAD_DIM)
    row_index = 0
    head_out, head_lse = attend_forward(
        head_view[row_index, :, 0],
        head_view[row_index, :, 1],
        head_view[row_index, :, 2],
        segment_ids[row_index],
        padding[row_index],
        block_len,
        scaling,
    )
    attended_parts = [head_out.astype(jnp.bfloat16).reshape(full_len, group_width)]
    lse_rows = [head_lse]
    head_attended = jnp.stack(attended_parts)
    head_attended, packed = lax.optimization_barrier((head_attended, packed))
    proj_one, proj_two = (unpack_weight(index, packed, slot_count, firsts, lasts, starts) for index in (11, 13))
    attended = lax.all_to_all(head_attended, "seq", split_axis=1, concat_axis=2, tiled=True)
    attended, proj_one, proj_two = lax.optimization_barrier((attended, proj_one, proj_two))
    branch_one = (
        jnp.einsum("rtd,dc->rtc", attended, output_weight, preferred_element_type=jnp.float32)
        + output_bias
    )
    middle = token_f + gate_one * branch_one
    normed_two, norm_back_two = jax.vjp(normalize, middle)
    mlp_in = (normed_two * (1.0 + scale_two) + shift_two).astype(jnp.bfloat16)
    hidden = (
        jnp.einsum("rtd,df->rtf", mlp_in, hidden_weight, preferred_element_type=jnp.float32)
        + hidden_bias
    )
    activated_f, gelu_back = jax.vjp(gelu_tanh, hidden)
    activated = activated_f.astype(jnp.bfloat16)
    branch_two = (
        jnp.einsum("rtf,fd->rtd", activated, return_weight, preferred_element_type=jnp.float32)
        + return_bias
    )
    result = middle + gate_two * branch_two
    feature = result.astype(jnp.bfloat16)
    first_pre = (
        jnp.einsum("rtd,dp->rtp", feature, proj_one, preferred_element_type=jnp.float32)
        + proj_bias_one
    )
    first_act, first_back = jax.vjp(jax.nn.silu, first_pre)
    first_low = first_act.astype(jnp.bfloat16)
    second_pre = (
        jnp.einsum("rtp,pc->rtc", first_low, proj_two, preferred_element_type=jnp.float32)
        + proj_bias_two
    )
    second_act, second_back = jax.vjp(jax.nn.silu, second_pre)
    second_low = second_act.astype(jnp.bfloat16)
    projected = (
        jnp.einsum("rtc,co->rto", second_low, proj_three, preferred_element_type=jnp.float32)
        + proj_bias_three
    )
    target_f = targets.astype(jnp.float32)
    cosine, cosine_back = jax.vjp(partial(cosine_of, target_f), projected)
    ends = {}

    def put(buffer, index, left, right):
        buffer, ends[index] = weight_grad(
            index,
            left.reshape(-1, left.shape[-1]),
            right.reshape(-1, right.shape[-1]),
            buffer,
            owners,
            slot_count,
            firsts,
            lasts,
            starts,
        )
        return buffer

    def summed(grad):
        return jnp.sum(grad.astype(jnp.float32), axis=(0, 1))

    (grad_projected,) = cosine_back(local_pad * -repa_weight)
    grad_projected = grad_projected.astype(jnp.bfloat16)
    sum_sixteen = summed(grad_projected)
    (grad_second,) = second_back(
        jnp.einsum("rto,co->rtc", grad_projected, proj_three, preferred_element_type=jnp.float32)
    )
    grad_second = grad_second.astype(jnp.bfloat16)
    sum_fourteen = summed(grad_second)
    (grad_first,) = first_back(
        jnp.einsum("rtc,pc->rtp", grad_second, proj_two, preferred_element_type=jnp.float32)
    )
    grad_first = grad_first.astype(jnp.bfloat16)
    sum_twelve = summed(grad_first)
    grad_result = cotangent + jnp.einsum(
        "rtp,dp->rtd", grad_first, proj_one, preferred_element_type=jnp.float32
    )
    grad_gate_two = grad_result * branch_two
    grad_branch_two = (grad_result * gate_two).astype(jnp.bfloat16)
    sum_ten = summed(grad_branch_two)
    (grad_hidden,) = gelu_back(
        jnp.einsum(
            "rtd,fd->rtf", grad_branch_two, return_weight, preferred_element_type=jnp.float32
        )
    )
    grad_hidden = grad_hidden.astype(jnp.bfloat16)
    sum_eight = summed(grad_hidden)
    grad_mlp_in = jnp.einsum(
        "rtf,df->rtd", grad_hidden, hidden_weight, preferred_element_type=jnp.float32
    )
    grad_scale_two = grad_mlp_in * normed_two
    (grad_through_two,) = norm_back_two(grad_mlp_in * (1.0 + scale_two))
    grad_middle = grad_result + grad_through_two
    grad_gate_one = grad_middle * branch_one
    grad_branch_one = (grad_middle * gate_one).astype(jnp.bfloat16)
    sum_six = summed(grad_branch_one)
    grad_attended = jnp.einsum(
        "rtc,dc->rtd", grad_branch_one, output_weight, preferred_element_type=jnp.float32
    ).astype(jnp.bfloat16)
    grad_attended, second_low = lax.optimization_barrier((grad_attended, second_low))
    head_grad = lax.all_to_all(grad_attended, "seq", split_axis=2, concat_axis=1, tiled=True)
    grad_buffer = put(None, 15, second_low, grad_projected)
    grad_buffer = put(grad_buffer, 11, feature, grad_first)
    head_grad, grad_buffer = lax.optimization_barrier((head_grad, grad_buffer))
    row_index = 0
    grad_query, grad_key, grad_value = attend_backward(
        head_view[row_index, :, 0],
        head_view[row_index, :, 1],
        head_view[row_index, :, 2],
        head_grad[row_index].reshape(full_len, heads_local, HEAD_DIM),
        lse_rows[row_index],
        segment_ids[row_index],
        padding[row_index],
        block_len,
        scaling,
    )
    triple_parts = [
        jnp.stack([grad_query, grad_key, grad_value], 1).reshape(full_len, 3, group_width)
    ]
    grad_triple_heads = jnp.stack(triple_parts).astype(jnp.bfloat16)
    grad_triple_heads, grad_buffer, cond_low = lax.optimization_barrier(
        (grad_triple_heads, grad_buffer, cond_low)
    )
    grad_triple = lax.all_to_all(
        grad_triple_heads, "seq", split_axis=1, concat_axis=3, tiled=True
    ).reshape(rows_dev, local_len, 3 * model_width)
    grad_buffer = put(grad_buffer, 13, first_low, grad_second)
    grad_buffer = put(grad_buffer, 9, activated, grad_branch_two)
    grad_buffer = put(grad_buffer, 7, mlp_in, grad_hidden)
    grad_buffer = put(grad_buffer, 5, attended, grad_branch_one)
    cond_all = lax.all_gather(cond_low, "dp", axis=0, tiled=True)
    image_rows = cond_all.shape[0]
    cond_own = own_conditions(cond_all.reshape(image_rows * SEGS, D), own_first, slot_count)
    grad_triple, grad_buffer, cond_own = lax.optimization_barrier((grad_triple, grad_buffer, cond_own))
    grad_buffer = put(grad_buffer, 2, attend_in, grad_triple)
    triple_sums = summed(grad_triple)
    grad_attend_in = jnp.einsum(
        "rtc,dc->rtd", grad_triple, attend_weight, preferred_element_type=jnp.float32
    )
    grad_scale_one = grad_attend_in * normed_one
    (grad_through_one,) = norm_back_one(grad_attend_in * (1.0 + scale_one))
    grad_tokens = grad_middle + grad_through_one
    token_mod_grad = jnp.concatenate(
        [grad_attend_in, grad_scale_one, grad_gate_one, grad_mlp_in, grad_scale_two, grad_gate_two],
        axis=-1,
    )
    mod_part = jnp.einsum("rts,rtc->rsc", onehot, token_mod_grad, precision=highest)
    mod_sent = jnp.pad(
        mod_part.astype(jnp.bfloat16).reshape(IMAGE_ROWS, LANES), ((0, SENT_ROWS - IMAGE_ROWS), (0, 0))
    )
    rows_at = param_rows()

    def rows(vector):
        return vector.reshape(-1, LANES)


    def head(index):
        return (0, ends[index], rows_at[index] % SUBS, SUBS)

    def tail(index):
        return (0, ends[index], SUBS, SUBS + rows_at[index] % SUBS)

    def whole(vector):
        return (0, rows(vector), 0, vector.shape[0] // LANES)

    pieces = [
        (6,) + head(2)[1:],
        tail(2),
        whole(triple_sums[:model_width]),
        whole(triple_sums[2 * model_width :]),
        head(5),
        tail(5),
        whole(sum_six),
        head(7),
        tail(7),
        whole(sum_eight),
        head(9),
        tail(9),
        whole(sum_ten),
        head(11),
        tail(11),
        whole(sum_twelve),
        head(13),
        tail(13),
        whole(sum_fourteen),
        head(15),
        tail(15),
        whole(sum_sixteen),
    ]
    grad_buffer = edge_write(pieces, grad_buffer, edge_slots[EDGE_TILES.index(3891) :])
    reduced, mod_all, cond_grad = reduce_slots(
        grad_buffer, mod_sent, mod_weight, slot_count, data_count, seq_count
    )
    (grad_conditions,) = silu_cond_back(cond_grad[None, :SEGS])
    mod_all = mod_all.reshape(image_rows * IMAGE_ROWS, LANES)
    new_master, new_first, new_second = update(
        reduced, cond_own, mod_all, own_first, master, first_moment, second_moment
    )
    return (
        result.astype(jnp.bfloat16),
        grad_tokens,
        grad_conditions,
        new_master,
        new_first,
        new_second,
    )


def solution(mesh):
    return jax.shard_map(
        shards,
        mesh=mesh,
        in_specs=(
            P("dp", "seq", None),
            P("dp", None, None),
            P("dp", None),
            P("dp", None),
            P("dp", "seq", None),
            P("dp", "seq", None),
            P(),
            P(("dp", "seq"), None),
            P(("dp", "seq"), None),
            P(("dp", "seq"), None),
        ),
        out_specs=(
            P("dp", "seq", None),
            P("dp", "seq", None),
            P("dp", None, None),
            P(("dp", "seq"), None),
            P(("dp", "seq"), None),
            P(("dp", "seq"), None),
        ),
        check_vma=False,
    )
```

```python
from functools import partial
import math

import jax
import jax.numpy as jnp
from jax import lax
from jax.experimental import pallas as pl
from jax.experimental.pallas import tpu as pltpu
from jax.sharding import PartitionSpec as P

HEADS = 16
HEAD_DIM = 72
D = 1152
FF = 4608
PROJ = 2048
TARGET = 768
SEGS = 4
STEP = 10
TILES = 15643


ln_eps = 1e-06
cos_eps = 1e-06
repa_weight = 0.5
beta_one = 0.5
beta_two = 0.5
learn_rate = 0.02
weight_decay = 0.01
adam_eps = 1e-08
highest = lax.Precision.HIGHEST


LANES = 128
SUBS = 16
MOD_ROWS = (D + 1) * 6 * D // LANES
VMEM_LIMIT = 56 * 1024 * 1024
MESH = pl.DeviceIdType.MESH


def param_shapes():
    return [
        (D, 6 * D),
        (6 * D,),
        (D, 3 * D),
        (D,),
        (D,),
        (D, D),
        (D,),
        (D, FF),
        (FF,),
        (FF, D),
        (D,),
        (D, PROJ),
        (PROJ,),
        (PROJ, PROJ),
        (PROJ,),
        (PROJ, TARGET),
        (TARGET,),
    ]


def param_rows():
    starts = []
    row = 0
    for dims in param_shapes():
        starts.append(row)
        row = row + math.prod(dims) // LANES
    return starts


CHUNK = {0: 128, 2: 128, 5: 384, 7: 128, 9: 512, 11: 384, 13: 256, 15: 1024}
EDGE_TILES = [3888, 3889, 3890, 3891, 5835, 5836, 6484, 6485, 9077, 9078, 9079, 11671, 12823, 12824, 14872, 14873, 15641, 15642]


def chunk_spans():
    spans = []
    base = {}
    rows = param_rows()
    for index, chunk in CHUNK.items():
        depth, width = param_shapes()[index]
        per_chunk = chunk * width // LANES // SUBS
        extra = 1 if rows[index] % SUBS else 0
        base[index] = len(spans)
        for step in range(depth // chunk):
            first = rows[index] // SUBS + step * per_chunk
            spans.append((first, first + per_chunk + extra - 1))
    return spans, base


def unpack_body(base, first_tile, per_chunk, tiles, shift, chunk, col_blocks, slots,
                first_ref, last_ref, starts_ref, packed, out_ref, landed, wide, sems):
    step = pl.program_id(0)

    def fetch(which, slot):
        low_tile = first_tile + which * per_chunk

        def one(owner, carry):
            begin = jnp.maximum(starts_ref[owner], low_tile)
            end = jnp.minimum(starts_ref[owner + 1], low_tile + tiles)
            size = pl.multiple_of((end - begin) * SUBS, SUBS)
            origin = pl.multiple_of((owner * slots + begin - starts_ref[owner]) * SUBS, SUBS)
            target = pl.multiple_of((begin - low_tile) * SUBS, SUBS)
            pltpu.make_async_copy(
                packed.at[pl.ds(origin, size)], landed.at[slot, pl.ds(target, size)], sems.at[slot]
            ).start()
            return carry

        lax.fori_loop(first_ref[base + which], last_ref[base + which] + 1, one, 0)

    @pl.when(step == 0)
    def _():
        fetch(0, 0)

    slot = step % 2

    @pl.when(step + 1 < pl.num_programs(0))
    def _():
        fetch(step + 1, (step + 1) % 2)

    pltpu.make_async_copy(packed.at[pl.ds(0, tiles * SUBS)], landed.at[slot], sems.at[slot]).wait()
    wide[...] = landed[slot].astype(jnp.float32)
    for block in range(col_blocks):
        out_ref[:, block * LANES : (block + 1) * LANES] = wide[
            pl.ds(shift + block, chunk, stride=col_blocks), :
        ].astype(jnp.bfloat16)


def unpack_weight(index, packed, slots, firsts, lasts, starts):
    depth, width = param_shapes()[index]
    chunk = CHUNK[index]
    col_blocks = width // LANES
    row = param_rows()[index]
    shift = row % SUBS
    per_chunk = chunk * col_blocks // SUBS
    tiles = per_chunk + (1 if shift else 0)
    base = chunk_spans()[1][index]
    return pl.pallas_call(
        partial(unpack_body, base, row // SUBS, per_chunk, tiles, shift, chunk, col_blocks, slots),
        out_shape=jax.ShapeDtypeStruct((depth, width), jnp.bfloat16),
        grid_spec=pltpu.PrefetchScalarGridSpec(
            num_scalar_prefetch=3,
            grid=(depth // chunk,),
            in_specs=[pl.BlockSpec(memory_space=pl.ANY)],
            out_specs=pl.BlockSpec((chunk, width), lambda i, *_: (i, 0)),
            scratch_shapes=[
                pltpu.VMEM((2, tiles * SUBS, LANES), jnp.bfloat16),
                pltpu.VMEM((tiles * SUBS, LANES), jnp.float32),
                pltpu.SemaphoreType.DMA((2,)),
            ],
        ),
        compiler_params=pltpu.CompilerParams(vmem_limit_bytes=VMEM_LIMIT),
        cost_estimate=pl.CostEstimate(flops=0, bytes_accessed=depth * width * 4, transcendentals=0),
        name="unpack_%d" % index,
    )(firsts, lasts, starts, packed)


def edge_read_body(table_ref, packed, out_ref, sem):
    count = out_ref.shape[0] // SUBS

    def one(i, carry):
        origin = pl.multiple_of(table_ref[i] * SUBS, SUBS)
        target = pl.multiple_of(i * SUBS, SUBS)
        pltpu.make_async_copy(packed.at[pl.ds(origin, SUBS)], out_ref.at[pl.ds(target, SUBS)], sem).start()
        return carry

    lax.fori_loop(0, count, one, 0)
    pltpu.make_async_copy(packed.at[pl.ds(0, count * SUBS)], out_ref, sem).wait()


def edge_read(packed, table):
    return pl.pallas_call(
        edge_read_body,
        out_shape=jax.ShapeDtypeStruct((len(EDGE_TILES) * SUBS, LANES), jnp.bfloat16),
        grid_spec=pltpu.PrefetchScalarGridSpec(
            num_scalar_prefetch=1,
            grid=(1,),
            in_specs=[pl.BlockSpec(memory_space=pl.ANY)],
            out_specs=pl.BlockSpec(memory_space=pltpu.VMEM),
            scratch_shapes=[pltpu.SemaphoreType.DMA],
        ),
        name="edge_read",
    )(table, packed)


def edge_write_body(layout, table_ref, *refs):
    pieces = refs[: len(layout)]
    out, wide, narrow, sem = refs[len(layout) + 1 :]
    wide[...] = jnp.zeros_like(wide)
    at = 0
    for piece, (skip, low, high) in zip(pieces, layout):
        at = at + skip
        wide[at : at + high - low, :] = piece[low:high, :]
        at = at + high - low
    narrow[...] = wide[...].astype(jnp.bfloat16)
    count = narrow.shape[0] // SUBS

    def one(i, carry):
        origin = pl.multiple_of(i * SUBS, SUBS)
        target = pl.multiple_of(table_ref[i] * SUBS, SUBS)
        pltpu.make_async_copy(narrow.at[pl.ds(origin, SUBS)], out.at[pl.ds(target, SUBS)], sem).start()
        return carry

    lax.fori_loop(0, count, one, 0)
    pltpu.make_async_copy(narrow, out.at[pl.ds(0, count * SUBS)], sem).wait()


def edge_write(pieces, buffer, table):
    count = table.shape[0]
    layout = [(skip, low, high) for skip, _, low, high in pieces]
    arrays = [array for _, array, _, _ in pieces]
    return pl.pallas_call(
        partial(edge_write_body, layout),
        out_shape=jax.ShapeDtypeStruct(buffer.shape, buffer.dtype),
        grid_spec=pltpu.PrefetchScalarGridSpec(
            num_scalar_prefetch=1,
            grid=(1,),
            in_specs=[pl.BlockSpec(memory_space=pltpu.VMEM)] * len(arrays)
            + [pl.BlockSpec(memory_space=pl.ANY)],
            out_specs=pl.BlockSpec(memory_space=pl.ANY),
            scratch_shapes=[
                pltpu.VMEM((count * SUBS, LANES), jnp.float32),
                pltpu.VMEM((count * SUBS, LANES), jnp.bfloat16),
                pltpu.SemaphoreType.DMA,
            ],
        ),
        input_output_aliases={1 + len(arrays): 0},
        name="edge_write",
    )(table, *arrays, buffer)


def weight_grad_body(base, first_tile, per_chunk, shift, chunk, col_blocks, slots, piece, chained,
                     first_ref, last_ref, starts_ref, x_ref, dy_ref, *rest):
    if chained:
        rest = rest[1:]
    out, ends_ref, wide, narrow, sems = rest
    step = pl.program_id(0)
    steps = pl.num_programs(0)
    slot = step % 2
    rows = chunk * col_blocks

    def drain(which):
        pltpu.make_async_copy(narrow.at[which], out.at[pl.ds(0, rows)], sems.at[which]).wait()

    @pl.when(step == 0)
    def _():
        wide[...] = jnp.zeros_like(wide)

    if shift:
        @pl.when(step > 0)
        def _():
            wide[0:SUBS, :] = wide[rows : rows + SUBS, :]

    left = x_ref[...].T
    for start in range(0, col_blocks, piece):
        part = jnp.dot(
            left, dy_ref[:, start * LANES : (start + piece) * LANES], preferred_element_type=jnp.float32
        )
        for block in range(piece):
            wide[pl.ds(shift + start + block, chunk, stride=col_blocks), :] = part[
                :, block * LANES : (block + 1) * LANES
            ]

    @pl.when(step >= 2)
    def _():
        drain(slot)

    narrow[slot] = wide[0:rows, :].astype(jnp.bfloat16)

    @pl.when(step == 0)
    def _():
        ends_ref[0:SUBS, :] = wide[0:SUBS, :]

    if shift:
        @pl.when(step == steps - 1)
        def _():
            ends_ref[SUBS : 2 * SUBS, :] = wide[rows : rows + SUBS, :]
    else:
        ends_ref[SUBS : 2 * SUBS, :] = jnp.zeros((SUBS, LANES), jnp.float32)

    low_tile = first_tile + step * per_chunk

    def one(owner, carry):
        begin = jnp.maximum(starts_ref[owner], low_tile)
        end = jnp.minimum(starts_ref[owner + 1], low_tile + per_chunk)
        size = pl.multiple_of(jnp.maximum(end - begin, 0) * SUBS, SUBS)
        target = pl.multiple_of((owner * slots + begin - starts_ref[owner]) * SUBS, SUBS)
        origin = pl.multiple_of((begin - low_tile) * SUBS, SUBS)

        @pl.when(end > begin)
        def _():
            pltpu.make_async_copy(
                narrow.at[slot, pl.ds(origin, size)], out.at[pl.ds(target, size)], sems.at[slot]
            ).start()

        return carry

    lax.fori_loop(first_ref[base + step], last_ref[base + step] + 1, one, 0)

    @pl.when(step == steps - 1)
    def _():
        drain(slot)

        @pl.when(steps > 1)
        def _():
            drain(1 - slot)


def weight_grad(index, left, right, buffer, owners, slots, firsts, lasts, starts):
    depth, width = param_shapes()[index]
    tokens = left.shape[0]
    chunk = CHUNK[index]
    col_blocks = width // LANES
    piece = next(p for p in (9, 8, 6) if col_blocks % p == 0)
    row = param_rows()[index]
    shift = row % SUBS
    per_chunk = chunk * col_blocks // SUBS
    base = chunk_spans()[1][index]
    shape = (owners * slots * SUBS, LANES)
    in_specs = [
        pl.BlockSpec((tokens, chunk), lambda i, *_: (0, i)),
        pl.BlockSpec((tokens, width), lambda i, *_: (0, 0)),
    ]
    operands = [firsts, lasts, starts, left, right]
    aliases = {}
    if buffer is not None:
        in_specs.append(pl.BlockSpec(memory_space=pl.ANY))
        operands.append(buffer)
        aliases = {5: 0}
    return pl.pallas_call(
        partial(weight_grad_body, base, row // SUBS, per_chunk, shift, chunk, col_blocks, slots, piece,
                buffer is not None),
        out_shape=(
            jax.ShapeDtypeStruct(shape, jnp.bfloat16),
            jax.ShapeDtypeStruct((2 * SUBS, LANES), jnp.float32),
        ),
        grid_spec=pltpu.PrefetchScalarGridSpec(
            num_scalar_prefetch=3,
            grid=(depth // chunk,),
            in_specs=in_specs,
            out_specs=(
                pl.BlockSpec(memory_space=pl.ANY),
                pl.BlockSpec((2 * SUBS, LANES), lambda i, *_: (0, 0)),
            ),
            scratch_shapes=[
                pltpu.VMEM((chunk * col_blocks + SUBS, LANES), jnp.float32),
                pltpu.VMEM((2, chunk * col_blocks, LANES), jnp.bfloat16),
                pltpu.SemaphoreType.DMA((2,)),
            ],
        ),
        input_output_aliases=aliases,
        compiler_params=pltpu.CompilerParams(vmem_limit_bytes=VMEM_LIMIT),
        cost_estimate=pl.CostEstimate(
            flops=2 * tokens * depth * width, bytes_accessed=depth * width * 2, transcendentals=0
        ),
        name="weight_grad_%d" % index,
    )(*operands)


class Grid:
    def __init__(self, side, depth):
        self.side = side
        self.sizes = {"u": side, "v": side, "z": depth}
        self.place = lax.axis_index("dp")
        self.core = self.place % 2
        outer = self.place // 2 // side
        inner = self.place // 2 % side
        self.mine = {
            "u": jnp.where(self.core == 0, outer, inner),
            "v": jnp.where(self.core == 0, inner, outer),
            "z": lax.axis_index("seq"),
        }
        self.sibling = (
            self.place + 1 - 2 * self.core,
            self.mine["z"],
        )

    def dp_of(self, first, second, core):
        outer = jnp.where(core == 0, first, second)
        inner = jnp.where(core == 0, second, first)
        return (outer * self.side + inner) * 2 + core

    def device(self, axis, other):
        at = dict(self.mine)
        at[axis] = other
        return (self.dp_of(at["u"], at["v"], self.core), at["z"])

    def other(self, axis, k):
        return k + (k >= self.mine[axis]).astype(jnp.int32)

    def seat(self, axis, other):
        mine = self.mine[axis]
        return mine - (mine > other).astype(jnp.int32)

    def partners(self):
        found = [self.sibling]
        for axis in ("u", "v", "z"):
            for k in range(self.sizes[axis] - 1):
                found.append(self.device(axis, self.other(axis, k)))
        return found

    def greet(self):
        barrier = pltpu.get_barrier_semaphore()
        partners = self.partners()
        for partner in partners:
            pl.semaphore_signal(barrier, inc=1, device_id=partner, device_id_type=MESH)
        pl.semaphore_wait(barrier, len(partners))


def split_slots(slots, shards):
    room = 32 * 1024 * 1024 // ((HELD + 2 * SLOTS) * shards * SUBS * LANES * 2)
    part = max(p for p in range(2, 13) if slots % p == 0 and p <= max(room, 2))
    late = max(1, round(part * 0.34))
    return slots // part, (part - late, late)


ORDERS = (("u", "v", "z"), ("u", "z", "v"))
LAG = 2
SLOTS = 4
HELD = 4 * LAG + 1


def gather_stream(grid, order, first_row, span, steps, own_ref, out_ref, sems):
    (send_a, recv_a, send_b, recv_b, send_c, recv_c, send_d, recv_d) = sems
    mine = grid.mine
    side = grid.side
    near, mid, far = order[2], order[1], order[0]

    def rows(q):
        return pl.ds(pl.multiple_of(first_row + q * span, SUBS), span)

    def copy(source, target, send, recv, device):
        return pltpu.make_async_remote_copy(
            src_ref=source, dst_ref=target, send_sem=send, recv_sem=recv, device_id=device,
            device_id_type=MESH,
        )

    def one_a(q, axis, k):
        other = grid.other(axis, k)
        mine_dp = grid.dp_of(mine["u"], mine["v"], grid.core)
        return copy(
            own_ref.at[rows(q)], out_ref.at[mine_dp, mine["z"], rows(q)],
            send_a.at[q % 4, k], recv_a.at[q, grid.seat(axis, other)],
            grid.device(axis, other),
        )

    def wait_a(q, axis, k):
        dp = grid.dp_of(mine["u"], mine["v"], grid.core)
        copy(
            own_ref.at[rows(q)], out_ref.at[dp, mine["z"], rows(q)],
            send_a.at[q % 4, k], recv_a.at[q, k], grid.device(axis, grid.other(axis, k)),
        ).wait_recv()

    def many_b(q, axis, k):
        other = grid.other(axis, k)
        seat = grid.seat(axis, other)
        if axis == "v":
            at = out_ref.at[grid.dp_of(mine["u"], mine["v"], grid.core), :, rows(q)]
            return [copy(at, at, send_b.at[q % 4, k], recv_b.at[q, seat], grid.device(axis, other))]
        found = []
        for v in range(side):
            at = out_ref.at[grid.dp_of(mine["u"], v, grid.core), mine["z"], rows(q)]
            found.append(copy(at, at, send_b.at[q % 4, k], recv_b.at[q, seat], grid.device(axis, other)))
        return found

    def many_c(q, k):
        other = grid.other("u", k)
        seat = grid.seat("u", other)
        found = []
        for v in range(side):
            at = out_ref.at[grid.dp_of(mine["u"], v, grid.core), :, rows(q)]
            found.append(copy(at, at, send_c.at[q % 4, k], recv_c.at[q, seat], grid.device("u", other)))
        return found

    def many_d(q):
        found = []
        for u in range(side):
            for v in range(side):
                at = out_ref.at[grid.dp_of(u, v, grid.core), :, rows(q)]
                found.append(copy(at, at, send_d.at[q % 4], recv_d.at[q], grid.sibling))
        return found

    def bulk(q, count, send, recv, device):
        at = out_ref.at[pl.ds(0, count), :, rows(q)]
        return copy(at, at, send, recv, device)

    def bulk_b(q, axis, send, recv):
        if axis == "v":
            at = out_ref.at[0, :, rows(q)]
        else:
            at = out_ref.at[pl.ds(0, side), 0, rows(q)]
        return copy(at, at, send, recv, grid.sibling)

    far_count = grid.sizes[near] - 1
    mid_count = grid.sizes[mid] - 1

    def stage_d(q):
        bulk(q, side, send_c.at[q % 4, 0], recv_c.at[q, 0], grid.sibling).wait_recv()
        for k in range(1, side - 1):
            bulk(q, side, send_c.at[q % 4, k], recv_c.at[q, k], grid.sibling).wait_recv()
        for k in range(side - 1):
            bulk(q, side, send_c.at[q % 4, k], recv_c.at[q, k], grid.sibling).wait_send()
        for one in many_d(q):
            one.start()

    def stage_c(q):
        for k in range(mid_count):
            bulk_b(q, mid, send_b.at[q % 4, k], recv_b.at[q, k]).wait_recv()
        for k in range(mid_count):
            bulk_b(q, mid, send_b.at[q % 4, k], recv_b.at[q, k]).wait_send()
        for k in range(side - 1):
            for one in many_c(q, k):
                one.start()

    def stage_b(q):
        for k in range(far_count):
            wait_a(q, near, k)
        for k in range(far_count):
            one_a(q, near, k).wait_send()
        for k in range(mid_count):
            for one in many_b(q, mid, k):
                one.start()

    def stage_a(q):
        for k in range(far_count):
            one_a(q, near, k).start()

    def finish(q):
        whole = bulk(q, side * side, send_d.at[q % 4], recv_d.at[q], grid.sibling)
        whole.wait_recv()
        whole.wait_send()

    return (stage_a, stage_b, stage_c, stage_d, finish)


def gather_body(side, depth, steps, parts, own_ref, out_ref, own_sem, *sems):
    grid = Grid(side, depth)
    keep = pltpu.make_async_copy(
        own_ref, out_ref.at[grid.dp_of(grid.mine["u"], grid.mine["v"], grid.core), grid.mine["z"]], own_sem
    )
    keep.start()
    grid.greet()
    streams = []
    first = 0
    for number, (order, part) in enumerate(zip(ORDERS, parts)):
        span = part * SUBS
        streams.append(
            gather_stream(grid, order, first, span, steps, own_ref, out_ref, sems[8 * number : 8 * number + 8])
        )
        first = first + steps * span
    keep.wait()

    def round_trip(s, carry):
        for late in range(4, -1, -1):
            q = s - LAG * late

            @pl.when((q >= 0) & (q < steps))
            def _(late=late, q=q):
                for stream in streams:
                    stream[late](q)

        return carry

    lax.fori_loop(0, steps + 4 * LAG, round_trip, 0)


def gather_slots(own, slots, data_count, seq_count):
    side = math.isqrt(data_count // 2)
    steps, parts = split_slots(slots, side * side * seq_count)
    dma = pltpu.SemaphoreType.DMA
    sems = []
    for order in ORDERS:
        sizes = {"u": side - 1, "v": side - 1, "z": seq_count - 1}
        for axis in (order[2], order[1], order[0]):
            sems.append(dma((4, sizes[axis])))
            sems.append(dma((steps, sizes[axis])))
        sems.append(dma((4,)))
        sems.append(dma((steps,)))
    return pl.pallas_call(
        partial(gather_body, side, seq_count, steps, parts),
        out_shape=jax.ShapeDtypeStruct((data_count, seq_count, slots * SUBS, LANES), jnp.bfloat16),
        in_specs=[pl.BlockSpec(memory_space=pltpu.VMEM)],
        out_specs=pl.BlockSpec(memory_space=pl.ANY),
        scratch_shapes=[dma] + sems,
        compiler_params=pltpu.CompilerParams(
            collective_id=2, has_side_effects=True, vmem_limit_bytes=VMEM_LIMIT
        ),
        name="gather_slots",
    )(own).reshape(data_count * seq_count * slots * SUBS, LANES)


def reduce_stream(grid, order, first_row, span, steps, parts_ref, out_ref, refs):
    (own, rc, r1, r2, r3, outs, own_sem, out_sem, c_send, c_recv, s1, v1, s2, v2, s3, v3,
     c_credit, k1, k2, k3) = refs
    mine = grid.mine
    side = grid.side
    held = own.shape[0]
    mu, mv, mz = mine["u"], mine["v"], mine["z"]

    def rows(q):
        return pl.ds(pl.multiple_of(first_row + q * span, SUBS), span)

    def load(q, u, v):
        return pltpu.make_async_copy(
            parts_ref.at[grid.dp_of(u, v, grid.core), :, rows(q)], own.at[q % held, u, v], own_sem.at[q % held, u, v]
        )

    def give(q, u, v):
        return pltpu.make_async_remote_copy(
            src_ref=parts_ref.at[grid.dp_of(u, v, 1 - grid.core), :, rows(q)],
            dst_ref=rc.at[q % SLOTS, u, v],
            send_sem=c_send.at[q % SLOTS, u, v],
            recv_sem=c_recv.at[q % SLOTS, u, v],
            device_id=grid.sibling,
            device_id_type=MESH,
        )

    def block(q, stage, other):
        if stage == 0:
            return own.at[q % held, other]
        if order[1] == "v":
            return own.at[q % held, mu, other] if stage == 1 else own.at[q % held, mu, mv, other]
        return own.at[q % held, mu, :, other] if stage == 1 else own.at[q % held, mu, other, mz]

    landing = (r1, r2, r3)
    sends = (s1, s2, s3)
    arrivals = (v1, v2, v3)
    credits = (k1, k2, k3)

    def send(q, stage, k):
        axis = order[stage]
        other = grid.other(axis, k)
        seat = grid.seat(axis, other)
        return pltpu.make_async_remote_copy(
            src_ref=block(q, stage, other),
            dst_ref=landing[stage].at[q % SLOTS, seat],
            send_sem=sends[stage].at[q % SLOTS, k],
            recv_sem=arrivals[stage].at[q % SLOTS, seat],
            device_id=grid.device(axis, other),
            device_id_type=MESH,
        )

    def receive(q, stage, k):
        axis = order[stage]
        return pltpu.make_async_remote_copy(
            src_ref=block(q, stage, 0),
            dst_ref=landing[stage].at[q % SLOTS, k],
            send_sem=sends[stage].at[q % SLOTS, k],
            recv_sem=arrivals[stage].at[q % SLOTS, k],
            device_id=grid.device(axis, grid.other(axis, k)),
            device_id_type=MESH,
        )

    def write(q):
        return pltpu.make_async_copy(outs.at[q % 2], out_ref.at[rows(q)], out_sem.at[q % 2])

    def collect(q, stage):
        axis = order[stage]
        count = grid.sizes[axis] - 1
        for k in range(count):
            receive(q, stage, k).wait_recv()
        kept = block(q, stage, mine[axis])
        total = kept[...].astype(jnp.float32)
        for k in range(count):
            total = total + landing[stage][q % SLOTS, k].astype(jnp.float32)
        if stage < 2:
            kept[...] = total.astype(jnp.bfloat16)
        else:
            @pl.when(q >= 2)
            def _():
                write(q - 2).wait()

            outs[q % 2] = total.astype(jnp.bfloat16)
            write(q).start()
        for k in range(count):
            send(q, stage, k).wait_send()

        @pl.when(q + SLOTS < steps)
        def _():
            for k in range(count):
                pl.semaphore_signal(
                    credits[stage].at[mine[axis]], inc=1, device_id=grid.device(axis, grid.other(axis, k)),
                    device_id_type=MESH,
                )

    def launch(q, stage):
        axis = order[stage]
        count = grid.sizes[axis] - 1

        @pl.when(q >= SLOTS)
        def _():
            for k in range(count):
                pl.semaphore_wait(credits[stage].at[grid.other(axis, k)], 1)

        for k in range(count):
            send(q, stage, k).start()

    def begin(q):
        @pl.when(q >= SLOTS)
        def _():
            pl.semaphore_wait(c_credit, 1)

        for u in range(side):
            for v in range(side):
                give(q, u, v).start()
                load(q, u, v).start()

    def stage_c(q):
        for u in range(side):
            for v in range(side):
                load(q, u, v).wait()
                give(q, u, v).wait_recv()
                own[q % held, u, v] = (
                    own[q % held, u, v].astype(jnp.float32) + rc[q % SLOTS, u, v].astype(jnp.float32)
                ).astype(jnp.bfloat16)
        for u in range(side):
            for v in range(side):
                give(q, u, v).wait_send()

        @pl.when(q + SLOTS < steps)
        def _():
            pl.semaphore_signal(c_credit, inc=1, device_id=grid.sibling, device_id_type=MESH)

        launch(q, 0)

    def stage_one(q):
        collect(q, 0)
        launch(q, 1)

    def stage_two(q):
        collect(q, 1)
        launch(q, 2)

    def stage_three(q):
        collect(q, 2)

    return (begin, stage_c, stage_one, stage_two, stage_three), write


REDUCE_REFS = 20


MOD_BLOCKS = 6 * D // LANES
IMAGE_ROWS = SEGS * MOD_BLOCKS
SENT_ROWS = -(-IMAGE_ROWS // SUBS) * SUBS
COND_CHUNK = 128
MOD_REFS = 14
MOD_STEPS = 11 + D // COND_CHUNK


def modulation_stages(grid, part_ref, weight_ref, all_ref, cond_ref, refs):
    (arrived, dense, held, send_z, recv_z, send_v, recv_v, send_u, recv_u, send_c, recv_c, loads,
     done_sem, summed) = refs
    mine = grid.mine
    side = grid.side
    depth = grid.sizes["z"]
    here = grid.dp_of(mine["u"], mine["v"], grid.core)
    chunks = D // COND_CHUNK

    def to_z(k, seat):
        return pltpu.make_async_remote_copy(
            src_ref=part_ref, dst_ref=arrived.at[seat], send_sem=send_z.at[k], recv_sem=recv_z.at[seat],
            device_id=grid.device("z", grid.other("z", k)), device_id_type=MESH,
        )

    def rows_of(dp):
        return summed.at[dp]

    def one(dp, send, recv, device):
        return pltpu.make_async_remote_copy(
            src_ref=rows_of(dp), dst_ref=rows_of(dp), send_sem=send, recv_sem=recv, device_id=device,
            device_id_type=MESH,
        )

    def load(i):
        return pltpu.make_async_copy(
            weight_ref.at[pl.ds(pl.multiple_of(i * COND_CHUNK, COND_CHUNK), COND_CHUNK)],
            held.at[i % 2], loads.at[i % 2],
        )

    def v_copies():
        return [
            one(here, send_v.at[k], recv_v.at[grid.seat("v", grid.other("v", k))], grid.device("v", grid.other("v", k)))
            for k in range(side - 1)
        ]

    def u_copies():
        return [
            one(grid.dp_of(mine["u"], v, grid.core), send_u.at[k, v],
                recv_u.at[grid.seat("u", grid.other("u", k)), v], grid.device("u", grid.other("u", k)))
            for k in range(side - 1)
            for v in range(side)
        ]

    def c_copies():
        return [
            one(grid.dp_of(u, v, grid.core), send_c.at[u, v], recv_c.at[u, v], grid.sibling)
            for u in range(side)
            for v in range(side)
        ]

    def run(s):
        @pl.when(s == 0)
        def _():
            for k in range(depth - 1):
                to_z(k, grid.seat("z", grid.other("z", k))).start()

        @pl.when(s == 2)
        def _():
            for k in range(depth - 1):
                to_z(k, k).wait_recv()
            total = part_ref[...].astype(jnp.float32)
            for k in range(depth - 1):
                total = total + arrived[k].astype(jnp.float32)
            total = total.astype(jnp.bfloat16).astype(jnp.float32)
            summed[here] = total[:IMAGE_ROWS]
            for k in range(depth - 1):
                to_z(k, 0).wait_send()
            for copy in v_copies():
                copy.start()
            load(0).start()
            load(1).start()
            dense[...] = jnp.zeros_like(dense)
            for block in range(MOD_BLOCKS):
                dense[0:SEGS, block * LANES : (block + 1) * LANES] = summed[
                    here, pl.ds(block, SEGS, stride=MOD_BLOCKS), :
                ]

        @pl.when(s == 4)
        def _():
            for k in range(side - 1):
                one(here, send_v.at[k], recv_v.at[k], grid.sibling).wait_recv()
            for copy in v_copies():
                copy.wait_send()
            for copy in u_copies():
                copy.start()

        @pl.when(s == 6)
        def _():
            for k in range(side - 1):
                for v in range(side):
                    one(here, send_u.at[k, v], recv_u.at[k, v], grid.sibling).wait_recv()
            for copy in u_copies():
                copy.wait_send()
            for copy in c_copies():
                copy.start()

        @pl.when(s == 9)
        def _():
            for copy in c_copies():
                copy.wait_recv()
            for copy in c_copies():
                copy.wait_send()
            pltpu.make_async_copy(summed, all_ref, done_sem).start()

        i = s - 10

        @pl.when((i >= 0) & (i < chunks))
        def _():
            load(i).wait()
            cond_ref[:, pl.ds(pl.multiple_of(i * COND_CHUNK, COND_CHUNK), COND_CHUNK)] = lax.dot_general(
                dense[...].astype(jnp.bfloat16), held[i % 2], (((1,), (1,)), ((), ())),
                preferred_element_type=jnp.float32,
            )

            @pl.when(i + 2 < chunks)
            def _():
                load(i + 2).start()

        @pl.when(s == 10 + chunks)
        def _():
            pltpu.make_async_copy(summed, all_ref, done_sem).wait()

    return run


def reduce_body(side, depth, steps, parts, parts_ref, part_ref, weight_ref, out_ref, all_ref, cond_ref, *refs):
    grid = Grid(side, depth)
    grid.greet()
    modulation_step = modulation_stages(grid, part_ref, weight_ref, all_ref, cond_ref, refs[:MOD_REFS])
    refs = refs[MOD_REFS:]
    streams = []
    writes = []
    first = 0
    for number, (order, part) in enumerate(zip(ORDERS, parts)):
        span = part * SUBS
        stages, write = reduce_stream(
            grid, order, first, span, steps, parts_ref, out_ref,
            refs[REDUCE_REFS * number : REDUCE_REFS * (number + 1)],
        )
        streams.append(stages)
        writes.append(write)
        first = first + steps * span

    def round_trip(s, carry):
        for late in range(4, -1, -1):
            q = s - LAG * late

            @pl.when((q >= 0) & (q < steps))
            def _(late=late, q=q):
                for stream in streams:
                    stream[late](q)

        modulation_step(s)
        return carry

    lax.fori_loop(0, max(steps + 4 * LAG, MOD_STEPS), round_trip, 0)
    for write in writes:
        for q in range(max(steps - 2, 0), steps):
            write(q).wait()


def reduce_slots(grads, mod_part, mod_weight, slots, data_count, seq_count):
    side = math.isqrt(data_count // 2)
    steps, parts = split_slots(slots, side * side * seq_count)
    held = HELD
    dma = pltpu.SemaphoreType.DMA
    regular = pltpu.SemaphoreType.REGULAR
    bf16 = jnp.bfloat16
    f32 = jnp.float32
    scratch = [
        pltpu.VMEM((seq_count - 1, SENT_ROWS, LANES), bf16),
        pltpu.VMEM((8, 6 * D), f32),
        pltpu.VMEM((2, COND_CHUNK, 6 * D), bf16),
        dma((seq_count - 1,)),
        dma((seq_count - 1,)),
        dma((side - 1,)),
        dma((side - 1,)),
        dma((side - 1, side)),
        dma((side - 1, side)),
        dma((side, side)),
        dma((side, side)),
        dma((2,)),
        dma,
        pltpu.VMEM((data_count, IMAGE_ROWS, LANES), f32),
    ]
    for order, part in zip(ORDERS, parts):
        span = part * SUBS
        sizes = {"u": side, "v": side, "z": seq_count}
        left = dict(sizes)
        scratch.append(pltpu.VMEM((held, side, side, seq_count, span, LANES), bf16))
        scratch.append(pltpu.VMEM((SLOTS, side, side, seq_count, span, LANES), bf16))
        for axis in order:
            del left[axis]
            rest = tuple(left[name] for name in ("u", "v", "z") if name in left)
            scratch.append(pltpu.VMEM((SLOTS, sizes[axis] - 1) + rest + (span, LANES), bf16))
        scratch.append(pltpu.VMEM((2, span, LANES), bf16))
        scratch.append(dma((held, side, side)))
        scratch.append(dma((2,)))
        scratch.append(dma((SLOTS, side, side)))
        scratch.append(dma((SLOTS, side, side)))
        for axis in order:
            scratch.append(dma((SLOTS, sizes[axis] - 1)))
            scratch.append(dma((SLOTS, sizes[axis] - 1)))
        scratch.append(regular)
        for axis in order:
            scratch.append(regular((sizes[axis],)))
    return pl.pallas_call(
        partial(reduce_body, side, seq_count, steps, parts),
        out_shape=(
            jax.ShapeDtypeStruct((slots * SUBS, LANES), bf16),
            jax.ShapeDtypeStruct((data_count, IMAGE_ROWS, LANES), f32),
            jax.ShapeDtypeStruct((8, D), f32),
        ),
        in_specs=[
            pl.BlockSpec(memory_space=pl.ANY),
            pl.BlockSpec(memory_space=pltpu.VMEM),
            pl.BlockSpec(memory_space=pl.ANY),
        ],
        out_specs=(
            pl.BlockSpec(memory_space=pl.ANY),
            pl.BlockSpec(memory_space=pl.ANY),
            pl.BlockSpec(memory_space=pltpu.VMEM),
        ),
        scratch_shapes=scratch,
        compiler_params=pltpu.CompilerParams(
            collective_id=1, has_side_effects=True, vmem_limit_bytes=VMEM_LIMIT
        ),
        name="reduce_slots",
    )(grads.reshape(data_count, seq_count, slots * SUBS, LANES), mod_part, mod_weight)


UPDATE_TILES = 72


def update_body(mod_depth, own_ref, reduced, cond_ref, mod_ref, master, first, second,
                new_master, new_first, new_second, mod_rows, wide):
    step = pl.program_id(0)
    mod_blocks = 6 * D // LANES
    start_row = own_ref[0] * SUBS
    shift = lax.rem(start_row, mod_blocks)
    tiles = UPDATE_TILES
    piece = 9

    @pl.when((step == 0) & (start_row < MOD_ROWS))
    def _():
        images = cond_ref.shape[1]
        for begin in range(0, mod_blocks, piece):
            grads = [
                mod_ref[pl.ds(begin + block, images, stride=mod_blocks), :].astype(jnp.bfloat16)
                for block in range(piece)
            ]
            part = jnp.dot(
                cond_ref[...], jnp.concatenate(grads, axis=1), preferred_element_type=jnp.float32
            )
            for block in range(piece):
                mod_rows[pl.ds(begin + block, mod_depth, stride=mod_blocks), :] = part[
                    :, block * LANES : (block + 1) * LANES
                ]

    wide[...] = reduced[...].astype(jnp.float32)
    corr_one = 1.0 - beta_one**STEP
    corr_two = 1.0 - beta_two**STEP
    local = step * tiles + lax.broadcasted_iota(jnp.int32, (tiles, LANES), 0)
    used = local < own_ref[1]
    for sub in range(SUBS):
        columns = pl.ds(sub * LANES, LANES)
        from_mod = mod_rows[pl.ds(shift + step * tiles * SUBS + sub, tiles, stride=SUBS), :]
        is_mod = start_row + local * SUBS + sub < MOD_ROWS
        grad = jnp.where(is_mod, from_mod, wide[pl.ds(sub, tiles, stride=SUBS), :])
        grad = jnp.where(used, grad, 0.0)
        one = beta_one * first[:, columns] + (1.0 - beta_one) * grad
        two = beta_two * second[:, columns] + (1.0 - beta_two) * grad * grad
        held = master[:, columns]
        new_first[:, columns] = one
        new_second[:, columns] = two
        new_master[:, columns] = held - learn_rate * (
            one / corr_one / (jnp.sqrt(two / corr_two) + adam_eps) + weight_decay * held
        )


def own_conditions(cond_all, own_first, slots):
    images = cond_all.shape[0]
    steps = -(-slots // UPDATE_TILES)
    depth = -(-(steps * UPDATE_TILES * SUBS + MOD_BLOCKS) // MOD_BLOCKS)
    depth = -(-depth // 8) * 8
    extended = jnp.concatenate(
        [cond_all.T, jnp.ones((1, images), jnp.bfloat16), jnp.zeros((depth, images), jnp.bfloat16)],
        axis=0,
    )
    return lax.dynamic_slice_in_dim(
        extended, jnp.minimum(own_first[0] * SUBS // MOD_BLOCKS, D + 1), depth, 0
    )


def update(reduced, cond_own, mod_all, own_first, master, first, second):
    slots, tile_len = master.shape
    mod_depth, images = cond_own.shape
    tiles = UPDATE_TILES
    steps = -(-slots // tiles)
    wide_block = pl.BlockSpec((tiles, tile_len), lambda i, *_: (i, 0))
    return pl.pallas_call(
        partial(update_body, mod_depth),
        out_shape=(jax.ShapeDtypeStruct(master.shape, jnp.float32),) * 3,
        grid_spec=pltpu.PrefetchScalarGridSpec(
            num_scalar_prefetch=1,
            grid=(steps,),
            in_specs=[
                pl.BlockSpec((tiles * SUBS, LANES), lambda i, *_: (i, 0)),
                pl.BlockSpec((mod_depth, images), lambda i, *_: (0, 0)),
                pl.BlockSpec(mod_all.shape, lambda i, *_: (0, 0)),
                wide_block,
                wide_block,
                wide_block,
            ],
            out_specs=(wide_block,) * 3,
            scratch_shapes=[
                pltpu.VMEM((mod_depth * MOD_BLOCKS, LANES), jnp.float32),
                pltpu.VMEM((tiles * SUBS, LANES), jnp.float32),
            ],
        ),
        compiler_params=pltpu.CompilerParams(vmem_limit_bytes=VMEM_LIMIT),
        name="update",
    )(own_first, reduced, cond_own, mod_all, master, first, second)


def normalize(values):
    centred = values - jnp.mean(values, axis=-1, keepdims=True)
    spread = jnp.mean(centred * centred, axis=-1, keepdims=True)
    return centred * lax.rsqrt(spread + ln_eps)


def cosine_of(target, projected):
    inner_mean = jnp.mean(projected * target, axis=-1)
    return (
        inner_mean
        * lax.rsqrt(jnp.mean(projected * projected, axis=-1) + cos_eps)
        * lax.rsqrt(jnp.mean(target * target, axis=-1) + cos_eps)
    )


def gelu_tanh(values):
    return jax.nn.gelu(values, approximate=True)


def lane_pad(width):
    return -(-width // LANES) * LANES


def regroup_body(moves, fill, x_ref, out_ref):
    if fill is not None:
        start, width = fill
        for group in range(out_ref.shape[0]):
            out_ref[group, :, start : start + width] = jnp.zeros((out_ref.shape[1], width), out_ref.dtype)
    for from_group, start, to_group, target, width in moves:
        if from_group is None:
            values = x_ref[:, start : start + width]
        else:
            values = x_ref[from_group, :, start : start + width]
        if to_group is None:
            out_ref[:, target : target + width] = values
        else:
            out_ref[to_group, :, target : target + width] = values


def split_groups(x, parts, groups):
    tokens, total = x.shape
    width = total // parts // groups
    padded = lane_pad(parts * width) if parts > 1 else width
    moves = [
        (None, (part * groups + group) * width, group, part * width, width)
        for group in range(groups)
        for part in range(parts)
    ]
    fill = (parts * width, padded - parts * width) if padded > parts * width and parts > 1 else None
    return pl.pallas_call(
        partial(regroup_body, moves, fill),
        out_shape=jax.ShapeDtypeStruct((groups, tokens, padded), x.dtype),
        compiler_params=pltpu.CompilerParams(vmem_limit_bytes=VMEM_LIMIT),
        name="split_groups_%d" % parts,
    )(x)


def join_groups(x, parts, width):
    groups, tokens, _ = x.shape
    moves = [
        (group, part * width, None, (part * groups + group) * width, width)
        for group in range(groups)
        for part in range(parts)
    ]
    return pl.pallas_call(
        partial(regroup_body, moves, None),
        out_shape=jax.ShapeDtypeStruct((tokens, parts * groups * width), x.dtype),
        compiler_params=pltpu.CompilerParams(vmem_limit_bytes=VMEM_LIMIT),
        name="join_groups_%d" % parts,
    )(x)


QUERY_BLOCK = 256


def key_bias(seg_col, pad_col, seg_row, first):
    keys = seg_col.shape[0]
    queries = seg_row.shape[1]
    key_at = lax.broadcasted_iota(jnp.int32, (keys, queries), 0)
    query_at = first + lax.broadcasted_iota(jnp.int32, (keys, queries), 1)
    allowed = (seg_col == seg_row) & ((pad_col == 1) | (key_at == query_at))
    return jnp.where(allowed, 0.0, -1e30)


def spread_heads(rows_ref, held, heads):
    held[...] = jnp.zeros_like(held)
    for part in range(held.shape[0]):
        for head in range(heads):
            start = (part * heads + head) * HEAD_DIM
            held[part, head, :, 0:HEAD_DIM] = rows_ref[:, start : start + HEAD_DIM]


def probabilities(held, head, block, bias):
    scores = lax.dot_general(
        held[1, head], held[0, head, block, :], (((1,), (1,)), ((), ())), preferred_element_type=jnp.float32
    )
    scores = scores * (HEAD_DIM ** (-0.5)) + bias
    shifted = jnp.exp(scores - jnp.max(scores, axis=0, keepdims=True))
    return shifted * (1.0 / jnp.sum(shifted, axis=0, keepdims=True))


def attention_body(heads, rows_ref, seg_col, pad_col, seg_row, out_ref, held):
    step = pl.program_id(0)

    @pl.when(step == 0)
    def _():
        spread_heads(rows_ref, held, heads)

    first = pl.multiple_of(step * QUERY_BLOCK, QUERY_BLOCK)
    block = pl.ds(first, QUERY_BLOCK)
    bias = key_bias(seg_col[...], pad_col[...], seg_row[...], first)
    for head in range(heads):
        probs = probabilities(held, head, block, bias).astype(jnp.bfloat16)
        result = lax.dot_general(
            held[2, head], probs, (((0,), (0,)), ((), ())), preferred_element_type=jnp.float32
        )
        out_ref[:, head * HEAD_DIM : (head + 1) * HEAD_DIM] = result.T[:, :HEAD_DIM].astype(jnp.bfloat16)


def attention(rows, segments, padding, heads):
    length = rows.shape[0]
    whole = pl.BlockSpec((length, 1), lambda i: (0, 0))
    return pl.pallas_call(
        partial(attention_body, heads),
        out_shape=jax.ShapeDtypeStruct((length, heads * HEAD_DIM), jnp.bfloat16),
        grid=(length // QUERY_BLOCK,),
        in_specs=[
            pl.BlockSpec(rows.shape, lambda i: (0, 0)),
            whole,
            whole,
            pl.BlockSpec((1, QUERY_BLOCK), lambda i: (0, i)),
        ],
        out_specs=pl.BlockSpec((QUERY_BLOCK, heads * HEAD_DIM), lambda i: (i, 0)),
        scratch_shapes=[pltpu.VMEM((3, heads, length, LANES), jnp.bfloat16)],
        compiler_params=pltpu.CompilerParams(vmem_limit_bytes=VMEM_LIMIT),
        name="attention",
    )(rows, segments.reshape(length, 1), padding.reshape(length, 1), segments.reshape(1, length))


def attention_grad_body(heads, rows_ref, grad_ref, seg_col, pad_col, seg_row, out_ref, held, given, grad_k, grad_v):
    step = pl.program_id(0)
    scaling = HEAD_DIM ** (-0.5)

    @pl.when(step == 0)
    def _():
        spread_heads(rows_ref, held, heads)
        given[...] = jnp.zeros_like(given)
        grad_k[...] = jnp.zeros_like(grad_k)
        grad_v[...] = jnp.zeros_like(grad_v)
        out_ref[...] = jnp.zeros_like(out_ref)

    first = pl.multiple_of(step * QUERY_BLOCK, QUERY_BLOCK)
    block = pl.ds(first, QUERY_BLOCK)
    bias = key_bias(seg_col[...], pad_col[...], seg_row[...], first)
    for head in range(heads):
        given[:, 0:HEAD_DIM] = grad_ref[:, head * HEAD_DIM : (head + 1) * HEAD_DIM]
        upstream = given[...]
        probs = probabilities(held, head, block, bias)
        grad_v[head] += jnp.dot(probs.astype(jnp.bfloat16), upstream, preferred_element_type=jnp.float32)
        grad_probs = lax.dot_general(
            held[2, head], upstream, (((1,), (1,)), ((), ())), preferred_element_type=jnp.float32
        )
        inner = jnp.sum(probs * grad_probs, axis=0, keepdims=True)
        grad_scores = (probs * (grad_probs - inner)).astype(jnp.bfloat16)
        grad_k[head] += jnp.dot(grad_scores, held[0, head, block, :], preferred_element_type=jnp.float32)
        grad_q = lax.dot_general(
            held[1, head], grad_scores, (((0,), (0,)), ((), ())), preferred_element_type=jnp.float32
        )
        out_ref[block, head * HEAD_DIM : (head + 1) * HEAD_DIM] = (
            grad_q.T[:, :HEAD_DIM] * scaling
        ).astype(jnp.bfloat16)

    @pl.when(step == pl.num_programs(0) - 1)
    def _():
        for head in range(heads):
            start = (heads + head) * HEAD_DIM
            out_ref[:, start : start + HEAD_DIM] = (grad_k[head][:, :HEAD_DIM] * scaling).astype(jnp.bfloat16)
            start = (2 * heads + head) * HEAD_DIM
            out_ref[:, start : start + HEAD_DIM] = grad_v[head][:, :HEAD_DIM].astype(jnp.bfloat16)


def attention_grad(rows, grad, segments, padding, heads):
    length = rows.shape[0]
    whole = pl.BlockSpec((length, 1), lambda i: (0, 0))
    return pl.pallas_call(
        partial(attention_grad_body, heads),
        out_shape=jax.ShapeDtypeStruct(rows.shape, jnp.bfloat16),
        grid=(length // QUERY_BLOCK,),
        in_specs=[
            pl.BlockSpec(rows.shape, lambda i: (0, 0)),
            pl.BlockSpec((QUERY_BLOCK, grad.shape[1]), lambda i: (i, 0)),
            whole,
            whole,
            pl.BlockSpec((1, QUERY_BLOCK), lambda i: (0, i)),
        ],
        out_specs=pl.BlockSpec(rows.shape, lambda i: (0, 0)),
        scratch_shapes=[
            pltpu.VMEM((3, heads, length, LANES), jnp.bfloat16),
            pltpu.VMEM((QUERY_BLOCK, LANES), jnp.bfloat16),
            pltpu.VMEM((heads, length, LANES), jnp.float32),
            pltpu.VMEM((heads, length, LANES), jnp.float32),
        ],
        compiler_params=pltpu.CompilerParams(vmem_limit_bytes=VMEM_LIMIT),
        name="attention_grad",
    )(rows, grad, segments.reshape(length, 1), padding.reshape(length, 1), segments.reshape(1, length))


def shards(
    tokens,
    conditions,
    segment_ids,
    padding,
    targets,
    cotangent,
    tile_counts,
    master,
    first_moment,
    second_moment,
):
    seq_count = lax.axis_size("seq")
    data_count = lax.axis_size("dp")
    seq_place = lax.axis_index("seq")
    data_place = lax.axis_index("dp")
    owners = data_count * seq_count
    slot_count, tile_len = master.shape
    own_rows = slot_count * SUBS
    tile_ends = jnp.cumsum(tile_counts)
    starts = jnp.concatenate([jnp.zeros((1,), jnp.int32), tile_ends.astype(jnp.int32)])
    spans = jnp.asarray(chunk_spans()[0], jnp.int32)
    firsts = jnp.sum((tile_ends[None, :] <= spans[:, :1]).astype(jnp.int32), axis=1)
    lasts = jnp.sum((tile_ends[None, :] <= spans[:, 1:]).astype(jnp.int32), axis=1)
    edge_ids = jnp.asarray(EDGE_TILES, jnp.int32)
    edge_owner = jnp.sum((tile_ends[None, :] <= edge_ids[:, None]).astype(jnp.int32), axis=1)
    edge_slots = edge_owner * slot_count + edge_ids - jnp.take(starts, edge_owner)
    own_place = data_place * seq_count + seq_place
    own_start = lax.dynamic_index_in_dim(starts, own_place, 0, False)
    own_count = lax.dynamic_index_in_dim(tile_counts, own_place, 0, False)
    own_low = master.astype(jnp.bfloat16).reshape(own_rows, LANES)
    packed = gather_slots(own_low, slot_count, data_count, seq_count)

    own_first = jnp.stack([own_start, own_count])
    cond_f = conditions.astype(jnp.float32)
    cond_act, silu_cond_back = jax.vjp(jax.nn.silu, cond_f)
    cond_low = cond_act.astype(jnp.bfloat16)
    weights = {
        index: unpack_weight(index, packed, slot_count, firsts, lasts, starts)
        for index in (0, 2, 5, 7, 9, 15)
    }
    mod_weight, attend_weight, output_weight, hidden_weight, return_weight, proj_three = (
        weights[index] for index in (0, 2, 5, 7, 9, 15)
    )
    edges = edge_read(packed, edge_slots)
    edge_flat = edges.reshape(-1)

    def bias(index):
        row = param_rows()[index]
        at = EDGE_TILES.index(row // SUBS) * SUBS + row % SUBS
        return edge_flat[at * LANES : at * LANES + param_shapes()[index][0]]

    mod_bias = bias(1)
    modulation = (
        jnp.einsum("rsd,dc->rsc", cond_low, mod_weight, preferred_element_type=jnp.float32) + mod_bias
    )
    query_bias, value_bias, output_bias, hidden_bias, return_bias = (bias(i) for i in (3, 4, 6, 8, 10))
    proj_bias_one, proj_bias_two, proj_bias_three = (bias(i) for i in (12, 14, 16))
    rows_dev, local_len, model_width = tokens.shape
    full_len = segment_ids.shape[1]
    heads_local = HEADS // seq_count
    group_width = model_width // seq_count
    token_start = seq_place * local_len
    local_seg = lax.dynamic_slice_in_dim(segment_ids, token_start, local_len, 1)
    local_pad = lax.dynamic_slice_in_dim(padding, token_start, local_len, 1).astype(jnp.float32)
    onehot = (local_seg[:, :, None] == jnp.arange(SEGS, dtype=jnp.int32)).astype(jnp.float32)
    per_token = jnp.einsum("rts,rsc->rtc", onehot, modulation, precision=highest)
    shift_one, scale_one, gate_one, shift_two, scale_two, gate_two = jnp.split(
        per_token, 6, axis=-1
    )
    token_f = tokens.astype(jnp.float32)
    normed_one, norm_back_one = jax.vjp(normalize, token_f)
    attend_in = (normed_one * (1.0 + scale_one) + shift_one).astype(jnp.bfloat16)
    triple_bias = jnp.concatenate([query_bias, jnp.zeros_like(query_bias), value_bias])
    triple = (
        jnp.einsum("rtd,dc->rtc", attend_in, attend_weight, preferred_element_type=jnp.float32)
        + triple_bias
    )
    triple_low = split_groups(triple[0].astype(jnp.bfloat16), 3, seq_count)
    head_rows = lax.all_to_all(triple_low, "seq", split_axis=0, concat_axis=0, tiled=True)
    (head_rows, output_weight, hidden_weight, return_weight, proj_three) = lax.optimization_barrier(
        (head_rows, output_weight, hidden_weight, return_weight, proj_three)
    )
    head_rows = head_rows.reshape(full_len, head_rows.shape[-1])
    head_attended = attention(head_rows, segment_ids[0], padding[0], heads_local)
    head_attended = head_attended.reshape(seq_count, local_len, group_width)
    head_attended, packed = lax.optimization_barrier((head_attended, packed))
    proj_one, proj_two = (unpack_weight(index, packed, slot_count, firsts, lasts, starts) for index in (11, 13))
    attended = lax.all_to_all(head_attended, "seq", split_axis=0, concat_axis=0, tiled=True)
    attended, proj_one, proj_two = lax.optimization_barrier((attended, proj_one, proj_two))
    attended = join_groups(attended, 1, group_width)[None]
    branch_one = (
        jnp.einsum("rtd,dc->rtc", attended, output_weight, preferred_element_type=jnp.float32)
        + output_bias
    )
    middle = token_f + gate_one * branch_one
    normed_two, norm_back_two = jax.vjp(normalize, middle)
    mlp_in = (normed_two * (1.0 + scale_two) + shift_two).astype(jnp.bfloat16)
    hidden = (
        jnp.einsum("rtd,df->rtf", mlp_in, hidden_weight, preferred_element_type=jnp.float32)
        + hidden_bias
    )
    activated_f, gelu_back = jax.vjp(gelu_tanh, hidden)
    activated = activated_f.astype(jnp.bfloat16)
    branch_two = (
        jnp.einsum("rtf,fd->rtd", activated, return_weight, preferred_element_type=jnp.float32)
        + return_bias
    )
    result = middle + gate_two * branch_two
    feature = result.astype(jnp.bfloat16)
    first_pre = (
        jnp.einsum("rtd,dp->rtp", feature, proj_one, preferred_element_type=jnp.float32)
        + proj_bias_one
    )
    first_act, first_back = jax.vjp(jax.nn.silu, first_pre)
    first_low = first_act.astype(jnp.bfloat16)
    second_pre = (
        jnp.einsum("rtp,pc->rtc", first_low, proj_two, preferred_element_type=jnp.float32)
        + proj_bias_two
    )
    second_act, second_back = jax.vjp(jax.nn.silu, second_pre)
    second_low = second_act.astype(jnp.bfloat16)
    projected = (
        jnp.einsum("rtc,co->rto", second_low, proj_three, preferred_element_type=jnp.float32)
        + proj_bias_three
    )
    target_f = targets.astype(jnp.float32)
    cosine, cosine_back = jax.vjp(partial(cosine_of, target_f), projected)
    ends = {}

    def put(buffer, index, left, right):
        buffer, ends[index] = weight_grad(
            index,
            left.reshape(-1, left.shape[-1]),
            right.reshape(-1, right.shape[-1]),
            buffer,
            owners,
            slot_count,
            firsts,
            lasts,
            starts,
        )
        return buffer

    def summed(grad):
        return jnp.sum(grad.astype(jnp.float32), axis=(0, 1))

    (grad_projected,) = cosine_back(local_pad * -repa_weight)
    grad_projected = grad_projected.astype(jnp.bfloat16)
    sum_sixteen = summed(grad_projected)
    (grad_second,) = second_back(
        jnp.einsum("rto,co->rtc", grad_projected, proj_three, preferred_element_type=jnp.float32)
    )
    grad_second = grad_second.astype(jnp.bfloat16)
    sum_fourteen = summed(grad_second)
    (grad_first,) = first_back(
        jnp.einsum("rtc,pc->rtp", grad_second, proj_two, preferred_element_type=jnp.float32)
    )
    grad_first = grad_first.astype(jnp.bfloat16)
    sum_twelve = summed(grad_first)
    grad_result = cotangent + jnp.einsum(
        "rtp,dp->rtd", grad_first, proj_one, preferred_element_type=jnp.float32
    )
    grad_gate_two = grad_result * branch_two
    grad_branch_two = (grad_result * gate_two).astype(jnp.bfloat16)
    sum_ten = summed(grad_branch_two)
    (grad_hidden,) = gelu_back(
        jnp.einsum(
            "rtd,fd->rtf", grad_branch_two, return_weight, preferred_element_type=jnp.float32
        )
    )
    grad_hidden = grad_hidden.astype(jnp.bfloat16)
    sum_eight = summed(grad_hidden)
    grad_mlp_in = jnp.einsum(
        "rtf,df->rtd", grad_hidden, hidden_weight, preferred_element_type=jnp.float32
    )
    grad_scale_two = grad_mlp_in * normed_two
    (grad_through_two,) = norm_back_two(grad_mlp_in * (1.0 + scale_two))
    grad_middle = grad_result + grad_through_two
    grad_gate_one = grad_middle * branch_one
    grad_branch_one = (grad_middle * gate_one).astype(jnp.bfloat16)
    sum_six = summed(grad_branch_one)
    grad_attended = jnp.einsum(
        "rtc,dc->rtd", grad_branch_one, output_weight, preferred_element_type=jnp.float32
    ).astype(jnp.bfloat16)
    grad_attended = split_groups(grad_attended[0], 1, seq_count)
    grad_attended, second_low = lax.optimization_barrier((grad_attended, second_low))
    head_grad = lax.all_to_all(grad_attended, "seq", split_axis=0, concat_axis=0, tiled=True)
    grad_buffer = put(None, 15, second_low, grad_projected)
    grad_buffer = put(grad_buffer, 11, feature, grad_first)
    head_grad, grad_buffer = lax.optimization_barrier((head_grad, grad_buffer))
    grad_triple_heads = attention_grad(
        head_rows, head_grad.reshape(full_len, group_width), segment_ids[0], padding[0], heads_local
    ).reshape(seq_count, local_len, head_rows.shape[-1])
    grad_triple_heads, grad_buffer, cond_low = lax.optimization_barrier(
        (grad_triple_heads, grad_buffer, cond_low)
    )
    grad_triple = lax.all_to_all(grad_triple_heads, "seq", split_axis=0, concat_axis=0, tiled=True)
    grad_buffer = put(grad_buffer, 13, first_low, grad_second)
    grad_buffer = put(grad_buffer, 9, activated, grad_branch_two)
    grad_buffer = put(grad_buffer, 7, mlp_in, grad_hidden)
    grad_buffer = put(grad_buffer, 5, attended, grad_branch_one)
    cond_all = lax.all_gather(cond_low, "dp", axis=0, tiled=True)
    image_rows = cond_all.shape[0]
    cond_own = own_conditions(cond_all.reshape(image_rows * SEGS, D), own_first, slot_count)
    grad_triple, grad_buffer, cond_own = lax.optimization_barrier((grad_triple, grad_buffer, cond_own))
    grad_triple = join_groups(grad_triple, 3, group_width)[None]
    grad_buffer = put(grad_buffer, 2, attend_in, grad_triple)
    triple_sums = summed(grad_triple)
    grad_attend_in = jnp.einsum(
        "rtc,dc->rtd", grad_triple, attend_weight, preferred_element_type=jnp.float32
    )
    grad_scale_one = grad_attend_in * normed_one
    (grad_through_one,) = norm_back_one(grad_attend_in * (1.0 + scale_one))
    grad_tokens = grad_middle + grad_through_one
    token_mod_grad = jnp.concatenate(
        [grad_attend_in, grad_scale_one, grad_gate_one, grad_mlp_in, grad_scale_two, grad_gate_two],
        axis=-1,
    )
    mod_part = jnp.einsum("rts,rtc->rsc", onehot, token_mod_grad, precision=highest)
    mod_sent = jnp.pad(
        mod_part.astype(jnp.bfloat16).reshape(IMAGE_ROWS, LANES), ((0, SENT_ROWS - IMAGE_ROWS), (0, 0))
    )
    rows_at = param_rows()

    def rows(vector):
        return vector.reshape(-1, LANES)


    def head(index):
        return (0, ends[index], rows_at[index] % SUBS, SUBS)

    def tail(index):
        return (0, ends[index], SUBS, SUBS + rows_at[index] % SUBS)

    def whole(vector):
        return (0, rows(vector), 0, vector.shape[0] // LANES)

    pieces = [
        (6,) + head(2)[1:],
        tail(2),
        whole(triple_sums[:model_width]),
        whole(triple_sums[2 * model_width :]),
        head(5),
        tail(5),
        whole(sum_six),
        head(7),
        tail(7),
        whole(sum_eight),
        head(9),
        tail(9),
        whole(sum_ten),
        head(11),
        tail(11),
        whole(sum_twelve),
        head(13),
        tail(13),
        whole(sum_fourteen),
        head(15),
        tail(15),
        whole(sum_sixteen),
    ]
    grad_buffer = edge_write(pieces, grad_buffer, edge_slots[EDGE_TILES.index(3891) :])
    reduced, mod_all, cond_grad = reduce_slots(
        grad_buffer, mod_sent, mod_weight, slot_count, data_count, seq_count
    )
    (grad_conditions,) = silu_cond_back(cond_grad[None, :SEGS])
    mod_all = mod_all.reshape(image_rows * IMAGE_ROWS, LANES)
    new_master, new_first, new_second = update(
        reduced, cond_own, mod_all, own_first, master, first_moment, second_moment
    )
    return (
        result.astype(jnp.bfloat16),
        grad_tokens,
        grad_conditions,
        new_master,
        new_first,
        new_second,
    )


def solution(mesh):
    return jax.shard_map(
        shards,
        mesh=mesh,
        in_specs=(
            P("dp", "seq", None),
            P("dp", None, None),
            P("dp", None),
            P("dp", None),
            P("dp", "seq", None),
            P("dp", "seq", None),
            P(),
            P(("dp", "seq"), None),
            P(("dp", "seq"), None),
            P(("dp", "seq"), None),
        ),
        out_specs=(
            P("dp", "seq", None),
            P("dp", "seq", None),
            P("dp", None, None),
            P(("dp", "seq"), None),
            P(("dp", "seq"), None),
            P(("dp", "seq"), None),
        ),
        check_vma=False,
    )
```

```python
from functools import partial
import math

import jax
import jax.numpy as jnp
from jax import lax
from jax.experimental import pallas as pl
from jax.experimental.pallas import tpu as pltpu
from jax.sharding import PartitionSpec as P

HEADS = 16
HEAD_DIM = 72
D = 1152
FF = 4608
PROJ = 2048
TARGET = 768
SEGS = 4
STEP = 10
TILES = 15643


ln_eps = 1e-06
cos_eps = 1e-06
repa_weight = 0.5
beta_one = 0.5
beta_two = 0.5
learn_rate = 0.02
weight_decay = 0.01
adam_eps = 1e-08
highest = lax.Precision.HIGHEST


LANES = 128
SUBS = 16
MOD_ROWS = (D + 1) * 6 * D // LANES
VMEM_LIMIT = 56 * 1024 * 1024
MESH = pl.DeviceIdType.MESH


def param_shapes():
    return [
        (D, 6 * D),
        (6 * D,),
        (D, 3 * D),
        (D,),
        (D,),
        (D, D),
        (D,),
        (D, FF),
        (FF,),
        (FF, D),
        (D,),
        (D, PROJ),
        (PROJ,),
        (PROJ, PROJ),
        (PROJ,),
        (PROJ, TARGET),
        (TARGET,),
    ]


def param_rows():
    starts = []
    row = 0
    for dims in param_shapes():
        starts.append(row)
        row = row + math.prod(dims) // LANES
    return starts


CHUNK = {0: 128, 2: 128, 5: 384, 7: 128, 9: 512, 11: 384, 13: 256, 15: 1024}
EDGE_TILES = [3888, 3889, 3890, 3891, 5835, 5836, 6484, 6485, 9077, 9078, 9079, 11671, 12823, 12824, 14872, 14873, 15641, 15642]


def chunk_spans():
    spans = []
    base = {}
    rows = param_rows()
    for index, chunk in CHUNK.items():
        depth, width = param_shapes()[index]
        per_chunk = chunk * width // LANES // SUBS
        extra = 1 if rows[index] % SUBS else 0
        base[index] = len(spans)
        for step in range(depth // chunk):
            first = rows[index] // SUBS + step * per_chunk
            spans.append((first, first + per_chunk + extra - 1))
    return spans, base


def unpack_body(base, first_tile, per_chunk, tiles, shift, chunk, col_blocks, slots,
                first_ref, last_ref, starts_ref, packed, out_ref, landed, wide, sems):
    step = pl.program_id(0)

    def fetch(which, slot):
        low_tile = first_tile + which * per_chunk

        def one(owner, carry):
            begin = jnp.maximum(starts_ref[owner], low_tile)
            end = jnp.minimum(starts_ref[owner + 1], low_tile + tiles)
            size = pl.multiple_of((end - begin) * SUBS, SUBS)
            origin = pl.multiple_of((owner * slots + begin - starts_ref[owner]) * SUBS, SUBS)
            target = pl.multiple_of((begin - low_tile) * SUBS, SUBS)
            pltpu.make_async_copy(
                packed.at[pl.ds(origin, size)], landed.at[slot, pl.ds(target, size)], sems.at[slot]
            ).start()
            return carry

        lax.fori_loop(first_ref[base + which], last_ref[base + which] + 1, one, 0)

    @pl.when(step == 0)
    def _():
        fetch(0, 0)

    slot = step % 2

    @pl.when(step + 1 < pl.num_programs(0))
    def _():
        fetch(step + 1, (step + 1) % 2)

    pltpu.make_async_copy(packed.at[pl.ds(0, tiles * SUBS)], landed.at[slot], sems.at[slot]).wait()
    wide[...] = landed[slot].astype(jnp.float32)
    for block in range(col_blocks):
        out_ref[:, block * LANES : (block + 1) * LANES] = wide[
            pl.ds(shift + block, chunk, stride=col_blocks), :
        ].astype(jnp.bfloat16)


def unpack_weight(index, packed, slots, firsts, lasts, starts):
    depth, width = param_shapes()[index]
    chunk = CHUNK[index]
    col_blocks = width // LANES
    row = param_rows()[index]
    shift = row % SUBS
    per_chunk = chunk * col_blocks // SUBS
    tiles = per_chunk + (1 if shift else 0)
    base = chunk_spans()[1][index]
    return pl.pallas_call(
        partial(unpack_body, base, row // SUBS, per_chunk, tiles, shift, chunk, col_blocks, slots),
        out_shape=jax.ShapeDtypeStruct((depth, width), jnp.bfloat16),
        grid_spec=pltpu.PrefetchScalarGridSpec(
            num_scalar_prefetch=3,
            grid=(depth // chunk,),
            in_specs=[pl.BlockSpec(memory_space=pl.ANY)],
            out_specs=pl.BlockSpec((chunk, width), lambda i, *_: (i, 0)),
            scratch_shapes=[
                pltpu.VMEM((2, tiles * SUBS, LANES), jnp.bfloat16),
                pltpu.VMEM((tiles * SUBS, LANES), jnp.float32),
                pltpu.SemaphoreType.DMA((2,)),
            ],
        ),
        compiler_params=pltpu.CompilerParams(vmem_limit_bytes=VMEM_LIMIT),
        cost_estimate=pl.CostEstimate(flops=0, bytes_accessed=depth * width * 4, transcendentals=0),
        name="unpack_%d" % index,
    )(firsts, lasts, starts, packed)


def edge_read_body(table_ref, packed, out_ref, sem):
    count = out_ref.shape[0] // SUBS

    def one(i, carry):
        origin = pl.multiple_of(table_ref[i] * SUBS, SUBS)
        target = pl.multiple_of(i * SUBS, SUBS)
        pltpu.make_async_copy(packed.at[pl.ds(origin, SUBS)], out_ref.at[pl.ds(target, SUBS)], sem).start()
        return carry

    lax.fori_loop(0, count, one, 0)
    pltpu.make_async_copy(packed.at[pl.ds(0, count * SUBS)], out_ref, sem).wait()


def edge_read(packed, table):
    return pl.pallas_call(
        edge_read_body,
        out_shape=jax.ShapeDtypeStruct((len(EDGE_TILES) * SUBS, LANES), jnp.bfloat16),
        grid_spec=pltpu.PrefetchScalarGridSpec(
            num_scalar_prefetch=1,
            grid=(1,),
            in_specs=[pl.BlockSpec(memory_space=pl.ANY)],
            out_specs=pl.BlockSpec(memory_space=pltpu.VMEM),
            scratch_shapes=[pltpu.SemaphoreType.DMA],
        ),
        name="edge_read",
    )(table, packed)


def edge_write_body(layout, table_ref, *refs):
    pieces = refs[: len(layout)]
    out, wide, narrow, sem = refs[len(layout) + 1 :]
    wide[...] = jnp.zeros_like(wide)
    at = 0
    for piece, (skip, low, high) in zip(pieces, layout):
        at = at + skip
        wide[at : at + high - low, :] = piece[low:high, :]
        at = at + high - low
    narrow[...] = wide[...].astype(jnp.bfloat16)
    count = narrow.shape[0] // SUBS

    def one(i, carry):
        origin = pl.multiple_of(i * SUBS, SUBS)
        target = pl.multiple_of(table_ref[i] * SUBS, SUBS)
        pltpu.make_async_copy(narrow.at[pl.ds(origin, SUBS)], out.at[pl.ds(target, SUBS)], sem).start()
        return carry

    lax.fori_loop(0, count, one, 0)
    pltpu.make_async_copy(narrow, out.at[pl.ds(0, count * SUBS)], sem).wait()


def edge_write(pieces, buffer, table):
    count = table.shape[0]
    layout = [(skip, low, high) for skip, _, low, high in pieces]
    arrays = [array for _, array, _, _ in pieces]
    return pl.pallas_call(
        partial(edge_write_body, layout),
        out_shape=jax.ShapeDtypeStruct(buffer.shape, buffer.dtype),
        grid_spec=pltpu.PrefetchScalarGridSpec(
            num_scalar_prefetch=1,
            grid=(1,),
            in_specs=[pl.BlockSpec(memory_space=pltpu.VMEM)] * len(arrays)
            + [pl.BlockSpec(memory_space=pl.ANY)],
            out_specs=pl.BlockSpec(memory_space=pl.ANY),
            scratch_shapes=[
                pltpu.VMEM((count * SUBS, LANES), jnp.float32),
                pltpu.VMEM((count * SUBS, LANES), jnp.bfloat16),
                pltpu.SemaphoreType.DMA,
            ],
        ),
        input_output_aliases={1 + len(arrays): 0},
        name="edge_write",
    )(table, *arrays, buffer)


def weight_grad_body(base, first_tile, per_chunk, shift, chunk, col_blocks, slots, plan, piece, chained,
                     first_ref, last_ref, starts_ref, guests_ref, x_ref, dy_ref, *rest):
    if chained:
        rest = rest[1:]
    out, ends_ref, wide, narrow, sems = rest
    hosts, kept = plan
    step = pl.program_id(0)
    steps = pl.num_programs(0)
    slot = step % 2
    rows = chunk * col_blocks

    def drain(which):
        pltpu.make_async_copy(narrow.at[which], out.at[pl.ds(0, rows)], sems.at[which]).wait()

    @pl.when(step == 0)
    def _():
        wide[...] = jnp.zeros_like(wide)

    if shift:
        @pl.when(step > 0)
        def _():
            wide[0:SUBS, :] = wide[rows : rows + SUBS, :]

    left = x_ref[...].T
    for start in range(0, col_blocks, piece):
        part = jnp.dot(
            left, dy_ref[:, start * LANES : (start + piece) * LANES], preferred_element_type=jnp.float32
        )
        for block in range(piece):
            wide[pl.ds(shift + start + block, chunk, stride=col_blocks), :] = part[
                :, block * LANES : (block + 1) * LANES
            ]

    @pl.when(step >= 2)
    def _():
        drain(slot)

    narrow[slot] = wide[0:rows, :].astype(jnp.bfloat16)

    @pl.when(step == 0)
    def _():
        ends_ref[0:SUBS, :] = wide[0:SUBS, :]

    if shift:
        @pl.when(step == steps - 1)
        def _():
            ends_ref[SUBS : 2 * SUBS, :] = wide[rows : rows + SUBS, :]
    else:
        ends_ref[SUBS : 2 * SUBS, :] = jnp.zeros((SUBS, LANES), jnp.float32)

    low_tile = first_tile + step * per_chunk

    def run(begin, end, place):
        size = pl.multiple_of(jnp.maximum(end - begin, 0) * SUBS, SUBS)
        target = pl.multiple_of(place * SUBS, SUBS)
        origin = pl.multiple_of((begin - low_tile) * SUBS, SUBS)

        @pl.when(end > begin)
        def _():
            pltpu.make_async_copy(
                narrow.at[slot, pl.ds(origin, size)], out.at[pl.ds(target, size)], sems.at[slot]
            ).start()

    def one(owner, carry):
        begin = jnp.maximum(starts_ref[owner], low_tile)
        end = jnp.minimum(starts_ref[owner + 1], low_tile + per_chunk)
        turn = starts_ref[owner] + kept
        run(begin, jnp.minimum(end, turn), owner * kept + begin - starts_ref[owner])
        if hosts:
            begin = jnp.maximum(begin, turn)
            run(begin, end, guests_ref[owner] + begin - turn)
        return carry

    lax.fori_loop(first_ref[base + step], last_ref[base + step] + 1, one, 0)

    @pl.when(step == steps - 1)
    def _():
        drain(slot)

        @pl.when(steps > 1)
        def _():
            drain(1 - slot)


def weight_grad(index, left, right, buffer, owners, slots, firsts, lasts, starts, guests, plan):
    depth, width = param_shapes()[index]
    tokens = left.shape[0]
    chunk = CHUNK[index]
    col_blocks = width // LANES
    piece = next(p for p in (9, 8, 6) if col_blocks % p == 0)
    row = param_rows()[index]
    shift = row % SUBS
    per_chunk = chunk * col_blocks // SUBS
    base = chunk_spans()[1][index]
    shape = (owners * plan[1] * SUBS, LANES)
    in_specs = [
        pl.BlockSpec((tokens, chunk), lambda i, *_: (0, i)),
        pl.BlockSpec((tokens, width), lambda i, *_: (0, 0)),
    ]
    operands = [firsts, lasts, starts, guests, left, right]
    aliases = {}
    if buffer is not None:
        in_specs.append(pl.BlockSpec(memory_space=pl.ANY))
        operands.append(buffer)
        aliases = {6: 0}
    return pl.pallas_call(
        partial(weight_grad_body, base, row // SUBS, per_chunk, shift, chunk, col_blocks, slots, plan, piece,
                buffer is not None),
        out_shape=(
            jax.ShapeDtypeStruct(shape, jnp.bfloat16),
            jax.ShapeDtypeStruct((2 * SUBS, LANES), jnp.float32),
        ),
        grid_spec=pltpu.PrefetchScalarGridSpec(
            num_scalar_prefetch=4,
            grid=(depth // chunk,),
            in_specs=in_specs,
            out_specs=(
                pl.BlockSpec(memory_space=pl.ANY),
                pl.BlockSpec((2 * SUBS, LANES), lambda i, *_: (0, 0)),
            ),
            scratch_shapes=[
                pltpu.VMEM((chunk * col_blocks + SUBS, LANES), jnp.float32),
                pltpu.VMEM((2, chunk * col_blocks, LANES), jnp.bfloat16),
                pltpu.SemaphoreType.DMA((2,)),
            ],
        ),
        input_output_aliases=aliases,
        compiler_params=pltpu.CompilerParams(vmem_limit_bytes=VMEM_LIMIT),
        cost_estimate=pl.CostEstimate(
            flops=2 * tokens * depth * width, bytes_accessed=depth * width * 2, transcendentals=0
        ),
        name="weight_grad_%d" % index,
    )(*operands)


class Grid:
    def __init__(self, side, depth):
        self.side = side
        self.sizes = {"u": side, "v": side, "z": depth}
        self.place = lax.axis_index("dp")
        self.core = self.place % 2
        outer = self.place // 2 // side
        inner = self.place // 2 % side
        self.mine = {
            "u": jnp.where(self.core == 0, outer, inner),
            "v": jnp.where(self.core == 0, inner, outer),
            "z": lax.axis_index("seq"),
        }
        self.sibling = (
            self.place + 1 - 2 * self.core,
            self.mine["z"],
        )

    def dp_of(self, first, second, core):
        outer = jnp.where(core == 0, first, second)
        inner = jnp.where(core == 0, second, first)
        return (outer * self.side + inner) * 2 + core

    def device(self, axis, other):
        at = dict(self.mine)
        at[axis] = other
        return (self.dp_of(at["u"], at["v"], self.core), at["z"])

    def other(self, axis, k):
        return k + (k >= self.mine[axis]).astype(jnp.int32)

    def seat(self, axis, other):
        mine = self.mine[axis]
        return mine - (mine > other).astype(jnp.int32)

    def partners(self):
        found = [self.sibling]
        for axis in ("u", "v", "z"):
            for k in range(self.sizes[axis] - 1):
                found.append(self.device(axis, self.other(axis, k)))
        return found

    def greet(self, hosting=None):
        barrier = pltpu.get_barrier_semaphore()
        partners = self.partners()
        for partner in partners:
            pl.semaphore_signal(barrier, inc=1, device_id=partner, device_id_type=MESH)
        expected = len(partners)
        if hosting is not None:
            @pl.when(jnp.logical_not(hosting.is_host))
            def _():
                pl.semaphore_signal(barrier, inc=1, device_id=hosting.host, device_id_type=MESH)

            expected = expected + hosting.guests
        pl.semaphore_wait(barrier, expected)


class Hosting:
    def __init__(self, grid, owners, hosts, share, kept, left):
        depth = grid.sizes["z"]
        z = grid.mine["z"]
        self.grid, self.depth, self.hosts, self.share, self.kept, self.left = grid, depth, hosts, share, kept, left
        self.places = owners // depth
        self.is_host = grid.place * depth + z < hosts
        here, _, room = level_counts(hosts, share, self.places, depth, z)
        index = grid.place - here
        back_here, _, back_room = level_counts(hosts, share, self.places, depth, z - depth // 2)
        own = index < room
        spot = jnp.maximum(jnp.where(own, index, back_room - 1 - (index - room)), 0)
        self.host = (spot // share, jnp.where(own | self.is_host, z, z - depth // 2))
        count = jnp.int32(0)
        for piece in range(share):
            count = count + self.guest_at(piece)[1].astype(jnp.int32)
        self.guests = jnp.where(self.is_host, count, 0)

    def guest_at(self, piece):
        there, near, over = guest_of(
            self.hosts, self.share, self.places, self.depth, self.grid.place, self.grid.mine["z"], piece
        )
        device = (jnp.where(near[0], near[1], over[1]), jnp.where(near[0], near[2], over[2]))
        return device, there & (piece < self.share)

    def guest(self, tile):
        piece = tile // self.left
        device, there = self.guest_at(piece)
        return device, there, self.kept + tile - piece * self.left


def split_slots(slots, shards):
    room = 32 * 1024 * 1024 // ((HELD + 2 * SLOTS) * shards * SUBS * LANES * 2)
    part = max(p for p in range(2, 13) if slots % p == 0 and p <= max(room, 2))
    late = max(1, round(part * 0.34))
    return slots // part, (part - late, late)


def level_counts(hosts, share, places, depth, z):
    here = (hosts - z + depth - 1) // depth
    return here, places - here, share * here


def guest_of(hosts, share, places, depth, place, z, piece):
    here, guests, room = level_counts(hosts, share, places, depth, z)
    index = place * share + piece
    far = z + depth // 2
    far_here, far_guests, far_room = level_counts(hosts, share, places, depth, far)
    back = room - 1 - index
    near = index < guests
    over = (far < depth) & (far_room + back < far_guests)
    return near | over, (near, here + index, z), (over, far_here + far_room + back, far)


def guest_places(plan, owners, depth):
    hosts, share, kept, left = plan
    places = [0] * owners
    for host in range(hosts):
        for piece in range(share):
            there, near, over = guest_of(hosts, share, owners // depth, depth, host // depth, host % depth, piece)
            if there:
                _, place, z = near if near[0] else over
                places[place * depth + z] = host * kept + piece * left
    return places


def host_plan(slots, owners, depth):
    hosts = MOD_ROWS // (slots * SUBS)
    shards = owners // 2
    room = 32 * 1024 * 1024 // ((HELD + 2 * SLOTS) * shards * SUBS * LANES * 2)
    share = -(-(owners - hosts) // hosts) if hosts else 0
    levels = [level_counts(hosts, share, owners // depth, depth, z) for z in range(depth)]
    for z, (_, guests, room_here) in enumerate(levels):
        if guests > room_here and (
            z < depth // 2
            or guests - room_here > levels[z - depth // 2][2] - levels[z - depth // 2][1]
        ):
            hosts = 0
    for kept in range(1, slots) if hosts else ():
        left = slots - kept
        if share * left > kept:
            continue
        for step in range(min(12, max(room, 2)), 5, -1):
            for late in (round(step * 0.34), step // 3, -(-step // 3)):
                early = step - late
                if kept % step or left % early:
                    continue
                middle = kept // step * early
                if all((i * left - middle) % late == 0 for i in range(share + 1) if i * left > middle):
                    return hosts, share, kept, kept // step, (early, late)
    steps, parts = split_slots(slots, shards)
    return 0, 0, slots, steps, parts


ORDERS = (("u", "v", "z"), ("u", "z", "v"))
LAG = 2
SLOTS = 4
OUTS = 8
HELD = 4 * LAG + 1


def gather_stream(grid, order, first_row, span, steps, own_ref, out_ref, sems):
    (send_a, recv_a, send_b, recv_b, send_c, recv_c, send_d, recv_d) = sems
    mine = grid.mine
    side = grid.side
    near, mid, far = order[2], order[1], order[0]

    def rows(q):
        return pl.ds(pl.multiple_of(first_row + q * span, SUBS), span)

    def copy(source, target, send, recv, device):
        return pltpu.make_async_remote_copy(
            src_ref=source, dst_ref=target, send_sem=send, recv_sem=recv, device_id=device,
            device_id_type=MESH,
        )

    def one_a(q, axis, k):
        other = grid.other(axis, k)
        mine_dp = grid.dp_of(mine["u"], mine["v"], grid.core)
        return copy(
            own_ref.at[rows(q)], out_ref.at[mine_dp, mine["z"], rows(q)],
            send_a.at[q % 4, k], recv_a.at[q, grid.seat(axis, other)],
            grid.device(axis, other),
        )

    def wait_a(q, axis, k):
        dp = grid.dp_of(mine["u"], mine["v"], grid.core)
        copy(
            own_ref.at[rows(q)], out_ref.at[dp, mine["z"], rows(q)],
            send_a.at[q % 4, k], recv_a.at[q, k], grid.device(axis, grid.other(axis, k)),
        ).wait_recv()

    def many_b(q, axis, k):
        other = grid.other(axis, k)
        seat = grid.seat(axis, other)
        if axis == "v":
            at = out_ref.at[grid.dp_of(mine["u"], mine["v"], grid.core), :, rows(q)]
            return [copy(at, at, send_b.at[q % 4, k], recv_b.at[q, seat], grid.device(axis, other))]
        found = []
        for v in range(side):
            at = out_ref.at[grid.dp_of(mine["u"], v, grid.core), mine["z"], rows(q)]
            found.append(copy(at, at, send_b.at[q % 4, k], recv_b.at[q, seat], grid.device(axis, other)))
        return found

    def many_c(q, k):
        other = grid.other("u", k)
        seat = grid.seat("u", other)
        found = []
        for v in range(side):
            at = out_ref.at[grid.dp_of(mine["u"], v, grid.core), :, rows(q)]
            found.append(copy(at, at, send_c.at[q % 4, k], recv_c.at[q, seat], grid.device("u", other)))
        return found

    def many_d(q):
        found = []
        for u in range(side):
            for v in range(side):
                at = out_ref.at[grid.dp_of(u, v, grid.core), :, rows(q)]
                found.append(copy(at, at, send_d.at[q % 4], recv_d.at[q], grid.sibling))
        return found

    def bulk(q, count, send, recv, device):
        at = out_ref.at[pl.ds(0, count), :, rows(q)]
        return copy(at, at, send, recv, device)

    def bulk_b(q, axis, send, recv):
        if axis == "v":
            at = out_ref.at[0, :, rows(q)]
        else:
            at = out_ref.at[pl.ds(0, side), 0, rows(q)]
        return copy(at, at, send, recv, grid.sibling)

    far_count = grid.sizes[near] - 1
    mid_count = grid.sizes[mid] - 1

    def stage_d(q):
        bulk(q, side, send_c.at[q % 4, 0], recv_c.at[q, 0], grid.sibling).wait_recv()
        for k in range(1, side - 1):
            bulk(q, side, send_c.at[q % 4, k], recv_c.at[q, k], grid.sibling).wait_recv()
        for k in range(side - 1):
            bulk(q, side, send_c.at[q % 4, k], recv_c.at[q, k], grid.sibling).wait_send()
        for one in many_d(q):
            one.start()

    def stage_c(q):
        for k in range(mid_count):
            bulk_b(q, mid, send_b.at[q % 4, k], recv_b.at[q, k]).wait_recv()
        for k in range(mid_count):
            bulk_b(q, mid, send_b.at[q % 4, k], recv_b.at[q, k]).wait_send()
        for k in range(side - 1):
            for one in many_c(q, k):
                one.start()

    def stage_b(q):
        for k in range(far_count):
            wait_a(q, near, k)
        for k in range(far_count):
            one_a(q, near, k).wait_send()
        for k in range(mid_count):
            for one in many_b(q, mid, k):
                one.start()

    def stage_a(q):
        for k in range(far_count):
            one_a(q, near, k).start()

    def finish(q):
        whole = bulk(q, side * side, send_d.at[q % 4], recv_d.at[q], grid.sibling)
        whole.wait_recv()
        whole.wait_send()

    return (stage_a, stage_b, stage_c, stage_d, finish)


def gather_body(side, depth, steps, parts, own_ref, out_ref, own_sem, *sems):
    grid = Grid(side, depth)
    keep = pltpu.make_async_copy(
        own_ref, out_ref.at[grid.dp_of(grid.mine["u"], grid.mine["v"], grid.core), grid.mine["z"]], own_sem
    )
    keep.start()
    grid.greet()
    streams = []
    first = 0
    for number, (order, part) in enumerate(zip(ORDERS, parts)):
        span = part * SUBS
        streams.append(
            gather_stream(grid, order, first, span, steps, own_ref, out_ref, sems[8 * number : 8 * number + 8])
        )
        first = first + steps * span
    keep.wait()

    def round_trip(s, carry):
        for late in range(4, -1, -1):
            q = s - LAG * late

            @pl.when((q >= 0) & (q < steps))
            def _(late=late, q=q):
                for stream in streams:
                    stream[late](q)

        return carry

    lax.fori_loop(0, steps + 4 * LAG, round_trip, 0)


def gather_slots(own, slots, data_count, seq_count):
    side = math.isqrt(data_count // 2)
    steps, parts = split_slots(slots, side * side * seq_count)
    dma = pltpu.SemaphoreType.DMA
    sems = []
    for order in ORDERS:
        sizes = {"u": side - 1, "v": side - 1, "z": seq_count - 1}
        for axis in (order[2], order[1], order[0]):
            sems.append(dma((4, sizes[axis])))
            sems.append(dma((steps, sizes[axis])))
        sems.append(dma((4,)))
        sems.append(dma((steps,)))
    return pl.pallas_call(
        partial(gather_body, side, seq_count, steps, parts),
        out_shape=jax.ShapeDtypeStruct((data_count, seq_count, slots * SUBS, LANES), jnp.bfloat16),
        in_specs=[pl.BlockSpec(memory_space=pltpu.VMEM)],
        out_specs=pl.BlockSpec(memory_space=pl.ANY),
        scratch_shapes=[dma] + sems,
        compiler_params=pltpu.CompilerParams(
            collective_id=2, has_side_effects=True, vmem_limit_bytes=VMEM_LIMIT
        ),
        name="gather_slots",
    )(own).reshape(data_count * seq_count * slots * SUBS, LANES)


def reduce_stream(grid, order, first_row, span, steps, parts_ref, out_ref, refs, hosting, passed):
    (own, rc, r1, r2, r3, outs, own_sem, out_sem, hand_sem, c_send, c_recv, s1, v1, s2, v2, s3, v3,
     c_credit, k1, k2, k3) = refs
    mine = grid.mine
    side = grid.side
    held = own.shape[0]
    mu, mv, mz = mine["u"], mine["v"], mine["z"]

    def rows(q):
        return pl.ds(pl.multiple_of(first_row + q * span, SUBS), span)

    def load(q, u, v):
        return pltpu.make_async_copy(
            parts_ref.at[grid.dp_of(u, v, grid.core), :, rows(q)], own.at[q % held, u, v], own_sem.at[q % held, u, v]
        )

    def give(q, u, v):
        return pltpu.make_async_remote_copy(
            src_ref=parts_ref.at[grid.dp_of(u, v, 1 - grid.core), :, rows(q)],
            dst_ref=rc.at[q % SLOTS, u, v],
            send_sem=c_send.at[q % SLOTS, u, v],
            recv_sem=c_recv.at[q % SLOTS, u, v],
            device_id=grid.sibling,
            device_id_type=MESH,
        )

    def block(q, stage, other):
        if stage == 0:
            return own.at[q % held, other]
        if order[1] == "v":
            return own.at[q % held, mu, other] if stage == 1 else own.at[q % held, mu, mv, other]
        return own.at[q % held, mu, :, other] if stage == 1 else own.at[q % held, mu, other, mz]

    landing = (r1, r2, r3)
    sends = (s1, s2, s3)
    arrivals = (v1, v2, v3)
    credits = (k1, k2, k3)

    def send(q, stage, k):
        axis = order[stage]
        other = grid.other(axis, k)
        seat = grid.seat(axis, other)
        return pltpu.make_async_remote_copy(
            src_ref=block(q, stage, other),
            dst_ref=landing[stage].at[q % SLOTS, seat],
            send_sem=sends[stage].at[q % SLOTS, k],
            recv_sem=arrivals[stage].at[q % SLOTS, seat],
            device_id=grid.device(axis, other),
            device_id_type=MESH,
        )

    def receive(q, stage, k):
        axis = order[stage]
        return pltpu.make_async_remote_copy(
            src_ref=block(q, stage, 0),
            dst_ref=landing[stage].at[q % SLOTS, k],
            send_sem=sends[stage].at[q % SLOTS, k],
            recv_sem=arrivals[stage].at[q % SLOTS, k],
            device_id=grid.device(axis, grid.other(axis, k)),
            device_id_type=MESH,
        )

    def keep(q):
        return pltpu.make_async_copy(outs.at[q % OUTS], out_ref.at[rows(q)], out_sem.at[q % OUTS])

    def hand_over(q):
        device, there, slot = hosting.guest((first_row + q * span) // SUBS)
        copy = pltpu.make_async_remote_copy(
            src_ref=outs.at[q % OUTS],
            dst_ref=out_ref.at[pl.ds(pl.multiple_of(slot * SUBS, SUBS), span)],
            send_sem=hand_sem.at[q % OUTS],
            recv_sem=passed,
            device_id=device,
            device_id_type=MESH,
        )
        return copy, there

    def write(q, action):
        if hosting is None:
            getattr(keep(q), action)()
            return

        @pl.when(jnp.logical_not(hosting.is_host))
        def _():
            getattr(keep(q), action)()

        copy, there = hand_over(q)

        @pl.when(hosting.is_host & there)
        def _():
            if action == "start":
                copy.start()
            else:
                copy.wait_send()

    def collect(q, stage):
        axis = order[stage]
        count = grid.sizes[axis] - 1
        for k in range(count):
            receive(q, stage, k).wait_recv()
        kept = block(q, stage, mine[axis])
        total = kept[...].astype(jnp.float32)
        for k in range(count):
            total = total + landing[stage][q % SLOTS, k].astype(jnp.float32)
        if stage < 2:
            kept[...] = total.astype(jnp.bfloat16)
        else:
            @pl.when(q >= OUTS)
            def _():
                write(q - OUTS, "wait")

            outs[q % OUTS] = total.astype(jnp.bfloat16)
            write(q, "start")
        for k in range(count):
            send(q, stage, k).wait_send()

        @pl.when(q + SLOTS < steps)
        def _():
            for k in range(count):
                pl.semaphore_signal(
                    credits[stage].at[mine[axis]], inc=1, device_id=grid.device(axis, grid.other(axis, k)),
                    device_id_type=MESH,
                )

    def launch(q, stage):
        axis = order[stage]
        count = grid.sizes[axis] - 1

        @pl.when(q >= SLOTS)
        def _():
            for k in range(count):
                pl.semaphore_wait(credits[stage].at[grid.other(axis, k)], 1)

        for k in range(count):
            send(q, stage, k).start()

    def begin(q):
        @pl.when(q >= SLOTS)
        def _():
            pl.semaphore_wait(c_credit, 1)

        for u in range(side):
            for v in range(side):
                give(q, u, v).start()
                load(q, u, v).start()

    def stage_c(q):
        for u in range(side):
            for v in range(side):
                load(q, u, v).wait()
                give(q, u, v).wait_recv()
                own[q % held, u, v] = (
                    own[q % held, u, v].astype(jnp.float32) + rc[q % SLOTS, u, v].astype(jnp.float32)
                ).astype(jnp.bfloat16)
        for u in range(side):
            for v in range(side):
                give(q, u, v).wait_send()

        @pl.when(q + SLOTS < steps)
        def _():
            pl.semaphore_signal(c_credit, inc=1, device_id=grid.sibling, device_id_type=MESH)

        launch(q, 0)

    def stage_one(q):
        collect(q, 0)
        launch(q, 1)

    def stage_two(q):
        collect(q, 1)
        launch(q, 2)

    def stage_three(q):
        collect(q, 2)

    return (begin, stage_c, stage_one, stage_two, stage_three), write


REDUCE_REFS = 21


MOD_BLOCKS = 6 * D // LANES
IMAGE_ROWS = SEGS * MOD_BLOCKS
SENT_ROWS = -(-IMAGE_ROWS // SUBS) * SUBS
COND_CHUNK = 128
MOD_REFS = 14
MOD_STEPS = 11 + D // COND_CHUNK


def modulation_stages(grid, part_ref, weight_ref, all_ref, cond_ref, refs):
    (arrived, dense, held, send_z, recv_z, send_v, recv_v, send_u, recv_u, send_c, recv_c, loads,
     done_sem, summed) = refs
    mine = grid.mine
    side = grid.side
    depth = grid.sizes["z"]
    here = grid.dp_of(mine["u"], mine["v"], grid.core)
    chunks = D // COND_CHUNK

    def to_z(k, seat):
        return pltpu.make_async_remote_copy(
            src_ref=part_ref, dst_ref=arrived.at[seat], send_sem=send_z.at[k], recv_sem=recv_z.at[seat],
            device_id=grid.device("z", grid.other("z", k)), device_id_type=MESH,
        )

    def rows_of(dp):
        return summed.at[dp]

    def one(dp, send, recv, device):
        return pltpu.make_async_remote_copy(
            src_ref=rows_of(dp), dst_ref=rows_of(dp), send_sem=send, recv_sem=recv, device_id=device,
            device_id_type=MESH,
        )

    def load(i):
        return pltpu.make_async_copy(
            weight_ref.at[pl.ds(pl.multiple_of(i * COND_CHUNK, COND_CHUNK), COND_CHUNK)],
            held.at[i % 2], loads.at[i % 2],
        )

    def v_copies():
        return [
            one(here, send_v.at[k], recv_v.at[grid.seat("v", grid.other("v", k))], grid.device("v", grid.other("v", k)))
            for k in range(side - 1)
        ]

    def u_copies():
        return [
            one(grid.dp_of(mine["u"], v, grid.core), send_u.at[k, v],
                recv_u.at[grid.seat("u", grid.other("u", k)), v], grid.device("u", grid.other("u", k)))
            for k in range(side - 1)
            for v in range(side)
        ]

    def c_copies():
        return [
            one(grid.dp_of(u, v, grid.core), send_c.at[u, v], recv_c.at[u, v], grid.sibling)
            for u in range(side)
            for v in range(side)
        ]

    def run(s):
        @pl.when(s == 0)
        def _():
            for k in range(depth - 1):
                to_z(k, grid.seat("z", grid.other("z", k))).start()

        @pl.when(s == 2)
        def _():
            for k in range(depth - 1):
                to_z(k, k).wait_recv()
            total = part_ref[...].astype(jnp.float32)
            for k in range(depth - 1):
                total = total + arrived[k].astype(jnp.float32)
            total = total.astype(jnp.bfloat16).astype(jnp.float32)
            summed[here] = total[:IMAGE_ROWS]
            for k in range(depth - 1):
                to_z(k, 0).wait_send()
            for copy in v_copies():
                copy.start()
            load(0).start()
            load(1).start()
            dense[...] = jnp.zeros_like(dense)
            for block in range(MOD_BLOCKS):
                dense[0:SEGS, block * LANES : (block + 1) * LANES] = summed[
                    here, pl.ds(block, SEGS, stride=MOD_BLOCKS), :
                ]

        @pl.when(s == 4)
        def _():
            for k in range(side - 1):
                one(here, send_v.at[k], recv_v.at[k], grid.sibling).wait_recv()
            for copy in v_copies():
                copy.wait_send()
            for copy in u_copies():
                copy.start()

        @pl.when(s == 6)
        def _():
            for k in range(side - 1):
                for v in range(side):
                    one(here, send_u.at[k, v], recv_u.at[k, v], grid.sibling).wait_recv()
            for copy in u_copies():
                copy.wait_send()
            for copy in c_copies():
                copy.start()

        @pl.when(s == 9)
        def _():
            for copy in c_copies():
                copy.wait_recv()
            for copy in c_copies():
                copy.wait_send()
            pltpu.make_async_copy(summed, all_ref, done_sem).start()

        i = s - 10

        @pl.when((i >= 0) & (i < chunks))
        def _():
            load(i).wait()
            cond_ref[:, pl.ds(pl.multiple_of(i * COND_CHUNK, COND_CHUNK), COND_CHUNK)] = lax.dot_general(
                dense[...].astype(jnp.bfloat16), held[i % 2], (((1,), (1,)), ((), ())),
                preferred_element_type=jnp.float32,
            )

            @pl.when(i + 2 < chunks)
            def _():
                load(i + 2).start()

        @pl.when(s == 10 + chunks)
        def _():
            pltpu.make_async_copy(summed, all_ref, done_sem).wait()

    return run


def reduce_body(side, depth, plan, slots, parts_ref, part_ref, weight_ref, out_ref, all_ref, cond_ref, *refs):
    hosts, share, kept, steps, parts = plan
    grid = Grid(side, depth)
    hosting = Hosting(grid, 2 * side * side * depth, hosts, share, kept, slots - kept) if hosts else None
    grid.greet(hosting)
    passed = refs[-1]
    modulation_step = modulation_stages(grid, part_ref, weight_ref, all_ref, cond_ref, refs[:MOD_REFS])
    refs = refs[MOD_REFS:]
    streams = []
    writes = []
    first = 0
    for number, (order, part) in enumerate(zip(ORDERS, parts)):
        span = part * SUBS
        stages, write = reduce_stream(
            grid, order, first, span, steps, parts_ref, out_ref,
            refs[REDUCE_REFS * number : REDUCE_REFS * (number + 1)], hosting, passed,
        )
        streams.append(stages)
        writes.append(write)
        first = first + steps * span

    def round_trip(s, carry):
        for late in range(4, -1, -1):
            q = s - LAG * late

            @pl.when((q >= 0) & (q < steps))
            def _(late=late, q=q):
                for stream in streams:
                    stream[late](q)

        modulation_step(s)
        return carry

    lax.fori_loop(0, max(steps + 4 * LAG, MOD_STEPS), round_trip, 0)
    for write in writes:
        for q in range(max(steps - OUTS, 0), steps):
            write(q, "wait")
    if hosting is not None:
        @pl.when(jnp.logical_not(hosting.is_host))
        def _():
            at = out_ref.at[pl.ds(kept * SUBS, (slots - kept) * SUBS)]
            pltpu.make_async_remote_copy(
                src_ref=at, dst_ref=at, send_sem=passed, recv_sem=passed, device_id=grid.sibling,
                device_id_type=MESH,
            ).wait_recv()


def reduce_slots(grads, mod_part, mod_weight, slots, data_count, seq_count):
    side = math.isqrt(data_count // 2)
    plan = host_plan(slots, data_count * seq_count, seq_count)
    kept, parts = plan[2], plan[4]
    held = HELD
    dma = pltpu.SemaphoreType.DMA
    regular = pltpu.SemaphoreType.REGULAR
    bf16 = jnp.bfloat16
    f32 = jnp.float32
    scratch = [
        pltpu.VMEM((seq_count - 1, SENT_ROWS, LANES), bf16),
        pltpu.VMEM((8, 6 * D), f32),
        pltpu.VMEM((2, COND_CHUNK, 6 * D), bf16),
        dma((seq_count - 1,)),
        dma((seq_count - 1,)),
        dma((side - 1,)),
        dma((side - 1,)),
        dma((side - 1, side)),
        dma((side - 1, side)),
        dma((side, side)),
        dma((side, side)),
        dma((2,)),
        dma,
        pltpu.VMEM((data_count, IMAGE_ROWS, LANES), f32),
    ]
    for order, part in zip(ORDERS, parts):
        span = part * SUBS
        sizes = {"u": side, "v": side, "z": seq_count}
        left = dict(sizes)
        scratch.append(pltpu.VMEM((held, side, side, seq_count, span, LANES), bf16))
        scratch.append(pltpu.VMEM((SLOTS, side, side, seq_count, span, LANES), bf16))
        for axis in order:
            del left[axis]
            rest = tuple(left[name] for name in ("u", "v", "z") if name in left)
            scratch.append(pltpu.VMEM((SLOTS, sizes[axis] - 1) + rest + (span, LANES), bf16))
        scratch.append(pltpu.VMEM((OUTS, span, LANES), bf16))
        scratch.append(dma((held, side, side)))
        scratch.append(dma((OUTS,)))
        scratch.append(dma((OUTS,)))
        scratch.append(dma((SLOTS, side, side)))
        scratch.append(dma((SLOTS, side, side)))
        for axis in order:
            scratch.append(dma((SLOTS, sizes[axis] - 1)))
            scratch.append(dma((SLOTS, sizes[axis] - 1)))
        scratch.append(regular)
        for axis in order:
            scratch.append(regular((sizes[axis],)))
    scratch.append(dma)
    return pl.pallas_call(
        partial(reduce_body, side, seq_count, plan, slots),
        out_shape=(
            jax.ShapeDtypeStruct((slots * SUBS, LANES), bf16),
            jax.ShapeDtypeStruct((data_count, IMAGE_ROWS, LANES), f32),
            jax.ShapeDtypeStruct((8, D), f32),
        ),
        in_specs=[
            pl.BlockSpec(memory_space=pl.ANY),
            pl.BlockSpec(memory_space=pltpu.VMEM),
            pl.BlockSpec(memory_space=pl.ANY),
        ],
        out_specs=(
            pl.BlockSpec(memory_space=pl.ANY),
            pl.BlockSpec(memory_space=pl.ANY),
            pl.BlockSpec(memory_space=pltpu.VMEM),
        ),
        scratch_shapes=scratch,
        compiler_params=pltpu.CompilerParams(
            collective_id=1, has_side_effects=True, vmem_limit_bytes=VMEM_LIMIT
        ),
        name="reduce_slots",
    )(grads.reshape(data_count, seq_count, kept * SUBS, LANES), mod_part, mod_weight)


UPDATE_TILES = 72


def update_body(mod_depth, own_ref, reduced, cond_ref, mod_ref, master, first, second,
                new_master, new_first, new_second, mod_rows, wide):
    step = pl.program_id(0)
    mod_blocks = 6 * D // LANES
    start_row = own_ref[0] * SUBS
    shift = lax.rem(start_row, mod_blocks)
    tiles = UPDATE_TILES
    piece = 9

    @pl.when((step == 0) & (start_row < MOD_ROWS))
    def _():
        images = cond_ref.shape[1]
        for begin in range(0, mod_blocks, piece):
            grads = [
                mod_ref[pl.ds(begin + block, images, stride=mod_blocks), :].astype(jnp.bfloat16)
                for block in range(piece)
            ]
            part = jnp.dot(
                cond_ref[...], jnp.concatenate(grads, axis=1), preferred_element_type=jnp.float32
            )
            for block in range(piece):
                mod_rows[pl.ds(begin + block, mod_depth, stride=mod_blocks), :] = part[
                    :, block * LANES : (block + 1) * LANES
                ]

    wide[...] = reduced[...].astype(jnp.float32)
    corr_one = 1.0 - beta_one**STEP
    corr_two = 1.0 - beta_two**STEP
    local = step * tiles + lax.broadcasted_iota(jnp.int32, (tiles, LANES), 0)
    used = local < own_ref[1]
    for sub in range(SUBS):
        columns = pl.ds(sub * LANES, LANES)
        from_mod = mod_rows[pl.ds(shift + step * tiles * SUBS + sub, tiles, stride=SUBS), :]
        is_mod = start_row + local * SUBS + sub < MOD_ROWS
        grad = jnp.where(is_mod, from_mod, wide[pl.ds(sub, tiles, stride=SUBS), :])
        grad = jnp.where(used, grad, 0.0)
        one = beta_one * first[:, columns] + (1.0 - beta_one) * grad
        two = beta_two * second[:, columns] + (1.0 - beta_two) * grad * grad
        held = master[:, columns]
        new_first[:, columns] = one
        new_second[:, columns] = two
        new_master[:, columns] = held - learn_rate * (
            one / corr_one / (jnp.sqrt(two / corr_two) + adam_eps) + weight_decay * held
        )


def own_conditions(cond_all, own_first, slots):
    images = cond_all.shape[0]
    steps = -(-slots // UPDATE_TILES)
    depth = -(-(steps * UPDATE_TILES * SUBS + MOD_BLOCKS) // MOD_BLOCKS)
    depth = -(-depth // 8) * 8
    extended = jnp.concatenate(
        [cond_all.T, jnp.ones((1, images), jnp.bfloat16), jnp.zeros((depth, images), jnp.bfloat16)],
        axis=0,
    )
    return lax.dynamic_slice_in_dim(
        extended, jnp.minimum(own_first[0] * SUBS // MOD_BLOCKS, D + 1), depth, 0
    )


def update(reduced, cond_own, mod_all, own_first, master, first, second):
    slots, tile_len = master.shape
    mod_depth, images = cond_own.shape
    tiles = UPDATE_TILES
    steps = -(-slots // tiles)
    wide_block = pl.BlockSpec((tiles, tile_len), lambda i, *_: (i, 0))
    return pl.pallas_call(
        partial(update_body, mod_depth),
        out_shape=(jax.ShapeDtypeStruct(master.shape, jnp.float32),) * 3,
        grid_spec=pltpu.PrefetchScalarGridSpec(
            num_scalar_prefetch=1,
            grid=(steps,),
            in_specs=[
                pl.BlockSpec((tiles * SUBS, LANES), lambda i, *_: (i, 0)),
                pl.BlockSpec((mod_depth, images), lambda i, *_: (0, 0)),
                pl.BlockSpec(mod_all.shape, lambda i, *_: (0, 0)),
                wide_block,
                wide_block,
                wide_block,
            ],
            out_specs=(wide_block,) * 3,
            scratch_shapes=[
                pltpu.VMEM((mod_depth * MOD_BLOCKS, LANES), jnp.float32),
                pltpu.VMEM((tiles * SUBS, LANES), jnp.float32),
            ],
        ),
        compiler_params=pltpu.CompilerParams(vmem_limit_bytes=VMEM_LIMIT),
        name="update",
    )(own_first, reduced, cond_own, mod_all, master, first, second)


def normalize(values):
    centred = values - jnp.mean(values, axis=-1, keepdims=True)
    spread = jnp.mean(centred * centred, axis=-1, keepdims=True)
    return centred * lax.rsqrt(spread + ln_eps)


def cosine_of(target, projected):
    inner_mean = jnp.mean(projected * target, axis=-1)
    return (
        inner_mean
        * lax.rsqrt(jnp.mean(projected * projected, axis=-1) + cos_eps)
        * lax.rsqrt(jnp.mean(target * target, axis=-1) + cos_eps)
    )


def gelu_tanh(values):
    return jax.nn.gelu(values, approximate=True)


def lane_pad(width):
    return -(-width // LANES) * LANES


def regroup_body(moves, fill, x_ref, out_ref):
    if fill is not None:
        start, width = fill
        for group in range(out_ref.shape[0]):
            out_ref[group, :, start : start + width] = jnp.zeros((out_ref.shape[1], width), out_ref.dtype)
    for from_group, start, to_group, target, width in moves:
        if from_group is None:
            values = x_ref[:, start : start + width]
        else:
            values = x_ref[from_group, :, start : start + width]
        if to_group is None:
            out_ref[:, target : target + width] = values
        else:
            out_ref[to_group, :, target : target + width] = values


def split_groups(x, parts, groups):
    tokens, total = x.shape
    width = total // parts // groups
    padded = lane_pad(parts * width) if parts > 1 else width
    moves = [
        (None, (part * groups + group) * width, group, part * width, width)
        for group in range(groups)
        for part in range(parts)
    ]
    fill = (parts * width, padded - parts * width) if padded > parts * width and parts > 1 else None
    return pl.pallas_call(
        partial(regroup_body, moves, fill),
        out_shape=jax.ShapeDtypeStruct((groups, tokens, padded), x.dtype),
        compiler_params=pltpu.CompilerParams(vmem_limit_bytes=VMEM_LIMIT),
        name="split_groups_%d" % parts,
    )(x)


def join_groups(x, parts, width):
    groups, tokens, _ = x.shape
    moves = [
        (group, part * width, None, (part * groups + group) * width, width)
        for group in range(groups)
        for part in range(parts)
    ]
    return pl.pallas_call(
        partial(regroup_body, moves, None),
        out_shape=jax.ShapeDtypeStruct((tokens, parts * groups * width), x.dtype),
        compiler_params=pltpu.CompilerParams(vmem_limit_bytes=VMEM_LIMIT),
        name="join_groups_%d" % parts,
    )(x)


QUERY_BLOCK = 256


def key_bias(seg_col, pad_col, seg_row, first):
    keys = seg_col.shape[0]
    queries = seg_row.shape[1]
    key_at = lax.broadcasted_iota(jnp.int32, (keys, queries), 0)
    query_at = first + lax.broadcasted_iota(jnp.int32, (keys, queries), 1)
    allowed = (seg_col == seg_row) & ((pad_col == 1) | (key_at == query_at))
    return jnp.where(allowed, 0.0, -1e30)


def spread_heads(rows_ref, held, heads):
    held[...] = jnp.zeros_like(held)
    for part in range(held.shape[0]):
        for head in range(heads):
            start = (part * heads + head) * HEAD_DIM
            held[part, head, :, 0:HEAD_DIM] = rows_ref[:, start : start + HEAD_DIM]


def probabilities(held, head, block, bias):
    scores = lax.dot_general(
        held[1, head], held[0, head, block, :], (((1,), (1,)), ((), ())), preferred_element_type=jnp.float32
    )
    scores = scores * (HEAD_DIM ** (-0.5)) + bias
    shifted = jnp.exp(scores - jnp.max(scores, axis=0, keepdims=True))
    return shifted * (1.0 / jnp.sum(shifted, axis=0, keepdims=True))


def attention_body(heads, rows_ref, seg_col, pad_col, seg_row, out_ref, held):
    step = pl.program_id(0)

    @pl.when(step == 0)
    def _():
        spread_heads(rows_ref, held, heads)

    first = pl.multiple_of(step * QUERY_BLOCK, QUERY_BLOCK)
    block = pl.ds(first, QUERY_BLOCK)
    bias = key_bias(seg_col[...], pad_col[...], seg_row[...], first)
    for head in range(heads):
        probs = probabilities(held, head, block, bias).astype(jnp.bfloat16)
        result = lax.dot_general(
            held[2, head], probs, (((0,), (0,)), ((), ())), preferred_element_type=jnp.float32
        )
        out_ref[:, head * HEAD_DIM : (head + 1) * HEAD_DIM] = result.T[:, :HEAD_DIM].astype(jnp.bfloat16)


def attention(rows, segments, padding, heads):
    length = rows.shape[0]
    whole = pl.BlockSpec((length, 1), lambda i: (0, 0))
    return pl.pallas_call(
        partial(attention_body, heads),
        out_shape=jax.ShapeDtypeStruct((length, heads * HEAD_DIM), jnp.bfloat16),
        grid=(length // QUERY_BLOCK,),
        in_specs=[
            pl.BlockSpec(rows.shape, lambda i: (0, 0)),
            whole,
            whole,
            pl.BlockSpec((1, QUERY_BLOCK), lambda i: (0, i)),
        ],
        out_specs=pl.BlockSpec((QUERY_BLOCK, heads * HEAD_DIM), lambda i: (i, 0)),
        scratch_shapes=[pltpu.VMEM((3, heads, length, LANES), jnp.bfloat16)],
        compiler_params=pltpu.CompilerParams(vmem_limit_bytes=VMEM_LIMIT),
        name="attention",
    )(rows, segments.reshape(length, 1), padding.reshape(length, 1), segments.reshape(1, length))


def attention_grad_body(heads, rows_ref, grad_ref, seg_col, pad_col, seg_row, out_ref, held, given, grad_k, grad_v):
    step = pl.program_id(0)
    scaling = HEAD_DIM ** (-0.5)

    @pl.when(step == 0)
    def _():
        spread_heads(rows_ref, held, heads)
        given[...] = jnp.zeros_like(given)
        grad_k[...] = jnp.zeros_like(grad_k)
        grad_v[...] = jnp.zeros_like(grad_v)
        out_ref[...] = jnp.zeros_like(out_ref)

    first = pl.multiple_of(step * QUERY_BLOCK, QUERY_BLOCK)
    block = pl.ds(first, QUERY_BLOCK)
    bias = key_bias(seg_col[...], pad_col[...], seg_row[...], first)
    for head in range(heads):
        given[:, 0:HEAD_DIM] = grad_ref[:, head * HEAD_DIM : (head + 1) * HEAD_DIM]
        upstream = given[...]
        probs = probabilities(held, head, block, bias)
        grad_v[head] += jnp.dot(probs.astype(jnp.bfloat16), upstream, preferred_element_type=jnp.float32)
        grad_probs = lax.dot_general(
            held[2, head], upstream, (((1,), (1,)), ((), ())), preferred_element_type=jnp.float32
        )
        inner = jnp.sum(probs * grad_probs, axis=0, keepdims=True)
        grad_scores = (probs * (grad_probs - inner)).astype(jnp.bfloat16)
        grad_k[head] += jnp.dot(grad_scores, held[0, head, block, :], preferred_element_type=jnp.float32)
        grad_q = lax.dot_general(
            held[1, head], grad_scores, (((0,), (0,)), ((), ())), preferred_element_type=jnp.float32
        )
        out_ref[block, head * HEAD_DIM : (head + 1) * HEAD_DIM] = (
            grad_q.T[:, :HEAD_DIM] * scaling
        ).astype(jnp.bfloat16)

    @pl.when(step == pl.num_programs(0) - 1)
    def _():
        for head in range(heads):
            start = (heads + head) * HEAD_DIM
            out_ref[:, start : start + HEAD_DIM] = (grad_k[head][:, :HEAD_DIM] * scaling).astype(jnp.bfloat16)
            start = (2 * heads + head) * HEAD_DIM
            out_ref[:, start : start + HEAD_DIM] = grad_v[head][:, :HEAD_DIM].astype(jnp.bfloat16)


def attention_grad(rows, grad, segments, padding, heads):
    length = rows.shape[0]
    whole = pl.BlockSpec((length, 1), lambda i: (0, 0))
    return pl.pallas_call(
        partial(attention_grad_body, heads),
        out_shape=jax.ShapeDtypeStruct(rows.shape, jnp.bfloat16),
        grid=(length // QUERY_BLOCK,),
        in_specs=[
            pl.BlockSpec(rows.shape, lambda i: (0, 0)),
            pl.BlockSpec((QUERY_BLOCK, grad.shape[1]), lambda i: (i, 0)),
            whole,
            whole,
            pl.BlockSpec((1, QUERY_BLOCK), lambda i: (0, i)),
        ],
        out_specs=pl.BlockSpec(rows.shape, lambda i: (0, 0)),
        scratch_shapes=[
            pltpu.VMEM((3, heads, length, LANES), jnp.bfloat16),
            pltpu.VMEM((QUERY_BLOCK, LANES), jnp.bfloat16),
            pltpu.VMEM((heads, length, LANES), jnp.float32),
            pltpu.VMEM((heads, length, LANES), jnp.float32),
        ],
        compiler_params=pltpu.CompilerParams(vmem_limit_bytes=VMEM_LIMIT),
        name="attention_grad",
    )(rows, grad, segments.reshape(length, 1), padding.reshape(length, 1), segments.reshape(1, length))


def shards(
    tokens,
    conditions,
    segment_ids,
    padding,
    targets,
    cotangent,
    tile_counts,
    master,
    first_moment,
    second_moment,
):
    seq_count = lax.axis_size("seq")
    data_count = lax.axis_size("dp")
    seq_place = lax.axis_index("seq")
    data_place = lax.axis_index("dp")
    owners = data_count * seq_count
    slot_count, tile_len = master.shape
    own_rows = slot_count * SUBS
    tile_ends = jnp.cumsum(tile_counts)
    starts = jnp.concatenate([jnp.zeros((1,), jnp.int32), tile_ends.astype(jnp.int32)])
    spans = jnp.asarray(chunk_spans()[0], jnp.int32)
    firsts = jnp.sum((tile_ends[None, :] <= spans[:, :1]).astype(jnp.int32), axis=1)
    lasts = jnp.sum((tile_ends[None, :] <= spans[:, 1:]).astype(jnp.int32), axis=1)
    plan = host_plan(slot_count, owners, seq_count)
    guests = jnp.asarray(
        guest_places((*plan[:3], slot_count - plan[2]), owners, seq_count), jnp.int32
    )
    edge_ids = jnp.asarray(EDGE_TILES, jnp.int32)
    edge_owner = jnp.sum((tile_ends[None, :] <= edge_ids[:, None]).astype(jnp.int32), axis=1)
    edge_slots = edge_owner * slot_count + edge_ids - jnp.take(starts, edge_owner)
    own_place = data_place * seq_count + seq_place
    own_start = lax.dynamic_index_in_dim(starts, own_place, 0, False)
    own_count = lax.dynamic_index_in_dim(tile_counts, own_place, 0, False)
    own_low = master.astype(jnp.bfloat16).reshape(own_rows, LANES)
    packed = gather_slots(own_low, slot_count, data_count, seq_count)

    own_first = jnp.stack([own_start, own_count])
    cond_f = conditions.astype(jnp.float32)
    cond_act, silu_cond_back = jax.vjp(jax.nn.silu, cond_f)
    cond_low = cond_act.astype(jnp.bfloat16)
    weights = {
        index: unpack_weight(index, packed, slot_count, firsts, lasts, starts)
        for index in (0, 2, 5, 7, 9, 15)
    }
    mod_weight, attend_weight, output_weight, hidden_weight, return_weight, proj_three = (
        weights[index] for index in (0, 2, 5, 7, 9, 15)
    )
    edges = edge_read(packed, edge_slots)
    edge_flat = edges.reshape(-1)

    def bias(index):
        row = param_rows()[index]
        at = EDGE_TILES.index(row // SUBS) * SUBS + row % SUBS
        return edge_flat[at * LANES : at * LANES + param_shapes()[index][0]]

    mod_bias = bias(1)
    modulation = (
        jnp.einsum("rsd,dc->rsc", cond_low, mod_weight, preferred_element_type=jnp.float32) + mod_bias
    )
    query_bias, value_bias, output_bias, hidden_bias, return_bias = (bias(i) for i in (3, 4, 6, 8, 10))
    proj_bias_one, proj_bias_two, proj_bias_three = (bias(i) for i in (12, 14, 16))
    rows_dev, local_len, model_width = tokens.shape
    full_len = segment_ids.shape[1]
    heads_local = HEADS // seq_count
    group_width = model_width // seq_count
    token_start = seq_place * local_len
    local_seg = lax.dynamic_slice_in_dim(segment_ids, token_start, local_len, 1)
    local_pad = lax.dynamic_slice_in_dim(padding, token_start, local_len, 1).astype(jnp.float32)
    onehot = (local_seg[:, :, None] == jnp.arange(SEGS, dtype=jnp.int32)).astype(jnp.float32)
    per_token = jnp.einsum("rts,rsc->rtc", onehot, modulation, precision=highest)
    shift_one, scale_one, gate_one, shift_two, scale_two, gate_two = jnp.split(
        per_token, 6, axis=-1
    )
    token_f = tokens.astype(jnp.float32)
    normed_one, norm_back_one = jax.vjp(normalize, token_f)
    attend_in = (normed_one * (1.0 + scale_one) + shift_one).astype(jnp.bfloat16)
    triple_bias = jnp.concatenate([query_bias, jnp.zeros_like(query_bias), value_bias])
    triple = (
        jnp.einsum("rtd,dc->rtc", attend_in, attend_weight, preferred_element_type=jnp.float32)
        + triple_bias
    )
    triple_low = split_groups(triple[0].astype(jnp.bfloat16), 3, seq_count)
    head_rows = lax.all_to_all(triple_low, "seq", split_axis=0, concat_axis=0, tiled=True)
    (head_rows, output_weight, hidden_weight, return_weight, proj_three) = lax.optimization_barrier(
        (head_rows, output_weight, hidden_weight, return_weight, proj_three)
    )
    head_rows = head_rows.reshape(full_len, head_rows.shape[-1])
    head_attended = attention(head_rows, segment_ids[0], padding[0], heads_local)
    head_attended = head_attended.reshape(seq_count, local_len, group_width)
    head_attended, packed = lax.optimization_barrier((head_attended, packed))
    proj_one, proj_two = (unpack_weight(index, packed, slot_count, firsts, lasts, starts) for index in (11, 13))
    attended = lax.all_to_all(head_attended, "seq", split_axis=0, concat_axis=0, tiled=True)
    attended, proj_one, proj_two = lax.optimization_barrier((attended, proj_one, proj_two))
    attended = join_groups(attended, 1, group_width)[None]
    branch_one = (
        jnp.einsum("rtd,dc->rtc", attended, output_weight, preferred_element_type=jnp.float32)
        + output_bias
    )
    middle = token_f + gate_one * branch_one
    normed_two, norm_back_two = jax.vjp(normalize, middle)
    mlp_in = (normed_two * (1.0 + scale_two) + shift_two).astype(jnp.bfloat16)
    hidden = (
        jnp.einsum("rtd,df->rtf", mlp_in, hidden_weight, preferred_element_type=jnp.float32)
        + hidden_bias
    )
    activated_f, gelu_back = jax.vjp(gelu_tanh, hidden)
    activated = activated_f.astype(jnp.bfloat16)
    branch_two = (
        jnp.einsum("rtf,fd->rtd", activated, return_weight, preferred_element_type=jnp.float32)
        + return_bias
    )
    result = middle + gate_two * branch_two
    feature = result.astype(jnp.bfloat16)
    first_pre = (
        jnp.einsum("rtd,dp->rtp", feature, proj_one, preferred_element_type=jnp.float32)
        + proj_bias_one
    )
    first_act, first_back = jax.vjp(jax.nn.silu, first_pre)
    first_low = first_act.astype(jnp.bfloat16)
    second_pre = (
        jnp.einsum("rtp,pc->rtc", first_low, proj_two, preferred_element_type=jnp.float32)
        + proj_bias_two
    )
    second_act, second_back = jax.vjp(jax.nn.silu, second_pre)
    second_low = second_act.astype(jnp.bfloat16)
    projected = (
        jnp.einsum("rtc,co->rto", second_low, proj_three, preferred_element_type=jnp.float32)
        + proj_bias_three
    )
    target_f = targets.astype(jnp.float32)
    cosine, cosine_back = jax.vjp(partial(cosine_of, target_f), projected)
    ends = {}

    def put(buffer, index, left, right):
        buffer, ends[index] = weight_grad(
            index,
            left.reshape(-1, left.shape[-1]),
            right.reshape(-1, right.shape[-1]),
            buffer,
            owners,
            slot_count,
            firsts,
            lasts,
            starts,
            guests,
            (plan[0], plan[2]),
        )
        return buffer

    def summed(grad):
        return jnp.sum(grad.astype(jnp.float32), axis=(0, 1))

    (grad_projected,) = cosine_back(local_pad * -repa_weight)
    grad_projected = grad_projected.astype(jnp.bfloat16)
    sum_sixteen = summed(grad_projected)
    (grad_second,) = second_back(
        jnp.einsum("rto,co->rtc", grad_projected, proj_three, preferred_element_type=jnp.float32)
    )
    grad_second = grad_second.astype(jnp.bfloat16)
    sum_fourteen = summed(grad_second)
    (grad_first,) = first_back(
        jnp.einsum("rtc,pc->rtp", grad_second, proj_two, preferred_element_type=jnp.float32)
    )
    grad_first = grad_first.astype(jnp.bfloat16)
    sum_twelve = summed(grad_first)
    grad_result = cotangent + jnp.einsum(
        "rtp,dp->rtd", grad_first, proj_one, preferred_element_type=jnp.float32
    )
    grad_gate_two = grad_result * branch_two
    grad_branch_two = (grad_result * gate_two).astype(jnp.bfloat16)
    sum_ten = summed(grad_branch_two)
    (grad_hidden,) = gelu_back(
        jnp.einsum(
            "rtd,fd->rtf", grad_branch_two, return_weight, preferred_element_type=jnp.float32
        )
    )
    grad_hidden = grad_hidden.astype(jnp.bfloat16)
    sum_eight = summed(grad_hidden)
    grad_mlp_in = jnp.einsum(
        "rtf,df->rtd", grad_hidden, hidden_weight, preferred_element_type=jnp.float32
    )
    grad_scale_two = grad_mlp_in * normed_two
    (grad_through_two,) = norm_back_two(grad_mlp_in * (1.0 + scale_two))
    grad_middle = grad_result + grad_through_two
    grad_gate_one = grad_middle * branch_one
    grad_branch_one = (grad_middle * gate_one).astype(jnp.bfloat16)
    sum_six = summed(grad_branch_one)
    grad_attended = jnp.einsum(
        "rtc,dc->rtd", grad_branch_one, output_weight, preferred_element_type=jnp.float32
    ).astype(jnp.bfloat16)
    grad_attended = split_groups(grad_attended[0], 1, seq_count)
    grad_attended, second_low = lax.optimization_barrier((grad_attended, second_low))
    head_grad = lax.all_to_all(grad_attended, "seq", split_axis=0, concat_axis=0, tiled=True)
    grad_buffer = put(None, 15, second_low, grad_projected)
    grad_buffer = put(grad_buffer, 11, feature, grad_first)
    head_grad, grad_buffer = lax.optimization_barrier((head_grad, grad_buffer))
    grad_triple_heads = attention_grad(
        head_rows, head_grad.reshape(full_len, group_width), segment_ids[0], padding[0], heads_local
    ).reshape(seq_count, local_len, head_rows.shape[-1])
    grad_triple_heads, grad_buffer, cond_low = lax.optimization_barrier(
        (grad_triple_heads, grad_buffer, cond_low)
    )
    grad_triple = lax.all_to_all(grad_triple_heads, "seq", split_axis=0, concat_axis=0, tiled=True)
    grad_buffer = put(grad_buffer, 13, first_low, grad_second)
    grad_buffer = put(grad_buffer, 9, activated, grad_branch_two)
    grad_buffer = put(grad_buffer, 7, mlp_in, grad_hidden)
    grad_buffer = put(grad_buffer, 5, attended, grad_branch_one)
    cond_all = lax.all_gather(cond_low, "dp", axis=0, tiled=True)
    image_rows = cond_all.shape[0]
    cond_own = own_conditions(cond_all.reshape(image_rows * SEGS, D), own_first, slot_count)
    grad_triple, grad_buffer, cond_own = lax.optimization_barrier((grad_triple, grad_buffer, cond_own))
    grad_triple = join_groups(grad_triple, 3, group_width)[None]
    grad_buffer = put(grad_buffer, 2, attend_in, grad_triple)
    triple_sums = summed(grad_triple)
    grad_attend_in = jnp.einsum(
        "rtc,dc->rtd", grad_triple, attend_weight, preferred_element_type=jnp.float32
    )
    grad_scale_one = grad_attend_in * normed_one
    (grad_through_one,) = norm_back_one(grad_attend_in * (1.0 + scale_one))
    grad_tokens = grad_middle + grad_through_one
    token_mod_grad = jnp.concatenate(
        [grad_attend_in, grad_scale_one, grad_gate_one, grad_mlp_in, grad_scale_two, grad_gate_two],
        axis=-1,
    )
    mod_part = jnp.einsum("rts,rtc->rsc", onehot, token_mod_grad, precision=highest)
    mod_sent = jnp.pad(
        mod_part.astype(jnp.bfloat16).reshape(IMAGE_ROWS, LANES), ((0, SENT_ROWS - IMAGE_ROWS), (0, 0))
    )
    rows_at = param_rows()

    def rows(vector):
        return vector.reshape(-1, LANES)


    def head(index):
        return (0, ends[index], rows_at[index] % SUBS, SUBS)

    def tail(index):
        return (0, ends[index], SUBS, SUBS + rows_at[index] % SUBS)

    def whole(vector):
        return (0, rows(vector), 0, vector.shape[0] // LANES)

    pieces = [
        (6,) + head(2)[1:],
        tail(2),
        whole(triple_sums[:model_width]),
        whole(triple_sums[2 * model_width :]),
        head(5),
        tail(5),
        whole(sum_six),
        head(7),
        tail(7),
        whole(sum_eight),
        head(9),
        tail(9),
        whole(sum_ten),
        head(11),
        tail(11),
        whole(sum_twelve),
        head(13),
        tail(13),
        whole(sum_fourteen),
        head(15),
        tail(15),
        whole(sum_sixteen),
    ]
    hosts, _, kept = plan[:3]
    edge_within = edge_ids - jnp.take(starts, edge_owner)
    edge_places = edge_owner * kept + edge_within
    if hosts:
        edge_places = jnp.where(
            edge_within < kept, edge_places, jnp.take(guests, edge_owner) + edge_within - kept
        )
    grad_buffer = edge_write(pieces, grad_buffer, edge_places[EDGE_TILES.index(3891) :])
    reduced, mod_all, cond_grad = reduce_slots(
        grad_buffer, mod_sent, mod_weight, slot_count, data_count, seq_count
    )
    (grad_conditions,) = silu_cond_back(cond_grad[None, :SEGS])
    mod_all = mod_all.reshape(image_rows * IMAGE_ROWS, LANES)
    new_master, new_first, new_second = update(
        reduced, cond_own, mod_all, own_first, master, first_moment, second_moment
    )
    return (
        result.astype(jnp.bfloat16),
        grad_tokens,
        grad_conditions,
        new_master,
        new_first,
        new_second,
    )


def solution(mesh):
    return jax.shard_map(
        shards,
        mesh=mesh,
        in_specs=(
            P("dp", "seq", None),
            P("dp", None, None),
            P("dp", None),
            P("dp", None),
            P("dp", "seq", None),
            P("dp", "seq", None),
            P(),
            P(("dp", "seq"), None),
            P(("dp", "seq"), None),
            P(("dp", "seq"), None),
        ),
        out_specs=(
            P("dp", "seq", None),
            P("dp", "seq", None),
            P("dp", None, None),
            P(("dp", "seq"), None),
            P(("dp", "seq"), None),
            P(("dp", "seq"), None),
        ),
        check_vma=False,
    )
```

```python
from functools import partial
import math

import jax
import jax.numpy as jnp
from jax import lax
from jax.experimental import pallas as pl
from jax.experimental.pallas import tpu as pltpu
from jax.sharding import PartitionSpec as P

HEADS = 16
HEAD_DIM = 72
D = 1152
FF = 4608
PROJ = 2048
TARGET = 768
SEGS = 4
STEP = 10
TILES = 15643


ln_eps = 1e-06
cos_eps = 1e-06
repa_weight = 0.5
beta_one = 0.5
beta_two = 0.5
learn_rate = 0.02
weight_decay = 0.01
adam_eps = 1e-08
highest = lax.Precision.HIGHEST


LANES = 128
SUBS = 16
MOD_ROWS = (D + 1) * 6 * D // LANES
VMEM_LIMIT = 56 * 1024 * 1024
MESH = pl.DeviceIdType.MESH


def param_shapes():
    return [
        (D, 6 * D),
        (6 * D,),
        (D, 3 * D),
        (D,),
        (D,),
        (D, D),
        (D,),
        (D, FF),
        (FF,),
        (FF, D),
        (D,),
        (D, PROJ),
        (PROJ,),
        (PROJ, PROJ),
        (PROJ,),
        (PROJ, TARGET),
        (TARGET,),
    ]


def param_rows():
    starts = []
    row = 0
    for dims in param_shapes():
        starts.append(row)
        row = row + math.prod(dims) // LANES
    return starts


CHUNK = {2: 128, 5: 384, 7: 128, 9: 512, 11: 384, 13: 256, 15: 1024}
EDGE_TILES = [3891, 5835, 5836, 6484, 6485, 9077, 9078, 9079, 11671, 12823, 12824, 14872, 14873, 15641, 15642]


def chunk_spans():
    spans = []
    base = {}
    rows = param_rows()
    for index, chunk in CHUNK.items():
        depth, width = param_shapes()[index]
        per_chunk = chunk * width // LANES // SUBS
        extra = 1 if rows[index] % SUBS else 0
        base[index] = len(spans)
        for step in range(depth // chunk):
            first = rows[index] // SUBS + step * per_chunk
            spans.append((first, first + per_chunk + extra - 1))
    return spans, base


def unpack_body(base, first_tile, per_chunk, tiles, shift, chunk, col_blocks, hosts, kept,
                first_ref, last_ref, starts_ref, guests_ref, packed, out_ref, landed, wide, sems):
    step = pl.program_id(0)

    def fetch(which, slot):
        low_tile = first_tile + which * per_chunk

        def run(begin, end, place):
            size = pl.multiple_of(jnp.maximum(end - begin, 0) * SUBS, SUBS)
            origin = pl.multiple_of(place * SUBS, SUBS)
            target = pl.multiple_of((begin - low_tile) * SUBS, SUBS)

            @pl.when(end > begin)
            def _():
                pltpu.make_async_copy(
                    packed.at[pl.ds(origin, size)], landed.at[slot, pl.ds(target, size)], sems.at[slot]
                ).start()

        def one(owner, carry):
            begin = jnp.maximum(starts_ref[owner], low_tile)
            end = jnp.minimum(starts_ref[owner + 1], low_tile + tiles)
            turn = starts_ref[owner] + kept
            run(begin, jnp.minimum(end, turn), owner * kept + begin - starts_ref[owner])
            if hosts:
                begin = jnp.maximum(begin, turn)
                run(begin, end, guests_ref[owner] + begin - turn)
            return carry

        lax.fori_loop(first_ref[base + which], last_ref[base + which] + 1, one, 0)

    @pl.when(step == 0)
    def _():
        fetch(0, 0)

    slot = step % 2

    @pl.when(step + 1 < pl.num_programs(0))
    def _():
        fetch(step + 1, (step + 1) % 2)

    pltpu.make_async_copy(packed.at[pl.ds(0, tiles * SUBS)], landed.at[slot], sems.at[slot]).wait()
    wide[...] = landed[slot].astype(jnp.float32)
    for block in range(col_blocks):
        out_ref[:, block * LANES : (block + 1) * LANES] = wide[
            pl.ds(shift + block, chunk, stride=col_blocks), :
        ].astype(jnp.bfloat16)


def unpack_weight(index, packed, plan, firsts, lasts, starts, guests):
    depth, width = param_shapes()[index]
    chunk = CHUNK[index]
    col_blocks = width // LANES
    row = param_rows()[index]
    shift = row % SUBS
    per_chunk = chunk * col_blocks // SUBS
    tiles = per_chunk + (1 if shift else 0)
    base = chunk_spans()[1][index]
    return pl.pallas_call(
        partial(unpack_body, base, row // SUBS, per_chunk, tiles, shift, chunk, col_blocks, plan[0], plan[2]),
        out_shape=jax.ShapeDtypeStruct((depth, width), jnp.bfloat16),
        grid_spec=pltpu.PrefetchScalarGridSpec(
            num_scalar_prefetch=4,
            grid=(depth // chunk,),
            in_specs=[pl.BlockSpec(memory_space=pl.ANY)],
            out_specs=pl.BlockSpec((chunk, width), lambda i, *_: (i, 0)),
            scratch_shapes=[
                pltpu.VMEM((2, tiles * SUBS, LANES), jnp.bfloat16),
                pltpu.VMEM((tiles * SUBS, LANES), jnp.float32),
                pltpu.SemaphoreType.DMA((2,)),
            ],
        ),
        compiler_params=pltpu.CompilerParams(vmem_limit_bytes=VMEM_LIMIT),
        cost_estimate=pl.CostEstimate(flops=0, bytes_accessed=depth * width * 4, transcendentals=0),
        name="unpack_%d" % index,
    )(firsts, lasts, starts, guests, packed)


def edge_read_body(table_ref, packed, out_ref, sem):
    count = out_ref.shape[0] // SUBS

    def one(i, carry):
        origin = pl.multiple_of(table_ref[i] * SUBS, SUBS)
        target = pl.multiple_of(i * SUBS, SUBS)
        pltpu.make_async_copy(packed.at[pl.ds(origin, SUBS)], out_ref.at[pl.ds(target, SUBS)], sem).start()
        return carry

    lax.fori_loop(0, count, one, 0)
    pltpu.make_async_copy(packed.at[pl.ds(0, count * SUBS)], out_ref, sem).wait()


def edge_read(packed, table):
    return pl.pallas_call(
        edge_read_body,
        out_shape=jax.ShapeDtypeStruct((len(EDGE_TILES) * SUBS, LANES), jnp.bfloat16),
        grid_spec=pltpu.PrefetchScalarGridSpec(
            num_scalar_prefetch=1,
            grid=(1,),
            in_specs=[pl.BlockSpec(memory_space=pl.ANY)],
            out_specs=pl.BlockSpec(memory_space=pltpu.VMEM),
            scratch_shapes=[pltpu.SemaphoreType.DMA],
        ),
        name="edge_read",
    )(table, packed)


def edge_write_body(layout, table_ref, *refs):
    pieces = refs[: len(layout)]
    out, wide, narrow, sem = refs[len(layout) + 1 :]
    wide[...] = jnp.zeros_like(wide)
    at = 0
    for piece, (skip, low, high) in zip(pieces, layout):
        at = at + skip
        wide[at : at + high - low, :] = piece[low:high, :]
        at = at + high - low
    narrow[...] = wide[...].astype(jnp.bfloat16)
    count = narrow.shape[0] // SUBS

    def one(i, carry):
        origin = pl.multiple_of(i * SUBS, SUBS)
        target = pl.multiple_of(table_ref[i] * SUBS, SUBS)
        pltpu.make_async_copy(narrow.at[pl.ds(origin, SUBS)], out.at[pl.ds(target, SUBS)], sem).start()
        return carry

    lax.fori_loop(0, count, one, 0)
    pltpu.make_async_copy(narrow, out.at[pl.ds(0, count * SUBS)], sem).wait()


def edge_write(pieces, buffer, table):
    count = table.shape[0]
    layout = [(skip, low, high) for skip, _, low, high in pieces]
    arrays = [array for _, array, _, _ in pieces]
    return pl.pallas_call(
        partial(edge_write_body, layout),
        out_shape=jax.ShapeDtypeStruct(buffer.shape, buffer.dtype),
        grid_spec=pltpu.PrefetchScalarGridSpec(
            num_scalar_prefetch=1,
            grid=(1,),
            in_specs=[pl.BlockSpec(memory_space=pltpu.VMEM)] * len(arrays)
            + [pl.BlockSpec(memory_space=pl.ANY)],
            out_specs=pl.BlockSpec(memory_space=pl.ANY),
            scratch_shapes=[
                pltpu.VMEM((count * SUBS, LANES), jnp.float32),
                pltpu.VMEM((count * SUBS, LANES), jnp.bfloat16),
                pltpu.SemaphoreType.DMA,
            ],
        ),
        input_output_aliases={1 + len(arrays): 0},
        name="edge_write",
    )(table, *arrays, buffer)


def weight_grad_body(base, first_tile, per_chunk, shift, chunk, col_blocks, slots, plan, piece, chained,
                     first_ref, last_ref, starts_ref, guests_ref, x_ref, dy_ref, *rest):
    if chained:
        rest = rest[1:]
    out, ends_ref, wide, narrow, sems = rest
    hosts, kept = plan
    step = pl.program_id(0)
    steps = pl.num_programs(0)
    slot = step % 2
    rows = chunk * col_blocks

    def drain(which):
        pltpu.make_async_copy(narrow.at[which], out.at[pl.ds(0, rows)], sems.at[which]).wait()

    @pl.when(step == 0)
    def _():
        wide[...] = jnp.zeros_like(wide)

    if shift:
        @pl.when(step > 0)
        def _():
            wide[0:SUBS, :] = wide[rows : rows + SUBS, :]

    left = x_ref[...].T
    for start in range(0, col_blocks, piece):
        part = jnp.dot(
            left, dy_ref[:, start * LANES : (start + piece) * LANES], preferred_element_type=jnp.float32
        )
        for block in range(piece):
            wide[pl.ds(shift + start + block, chunk, stride=col_blocks), :] = part[
                :, block * LANES : (block + 1) * LANES
            ]

    @pl.when(step >= 2)
    def _():
        drain(slot)

    narrow[slot] = wide[0:rows, :].astype(jnp.bfloat16)

    @pl.when(step == 0)
    def _():
        ends_ref[0:SUBS, :] = wide[0:SUBS, :]

    if shift:
        @pl.when(step == steps - 1)
        def _():
            ends_ref[SUBS : 2 * SUBS, :] = wide[rows : rows + SUBS, :]
    else:
        ends_ref[SUBS : 2 * SUBS, :] = jnp.zeros((SUBS, LANES), jnp.float32)

    low_tile = first_tile + step * per_chunk

    def run(begin, end, place):
        size = pl.multiple_of(jnp.maximum(end - begin, 0) * SUBS, SUBS)
        target = pl.multiple_of(place * SUBS, SUBS)
        origin = pl.multiple_of((begin - low_tile) * SUBS, SUBS)

        @pl.when(end > begin)
        def _():
            pltpu.make_async_copy(
                narrow.at[slot, pl.ds(origin, size)], out.at[pl.ds(target, size)], sems.at[slot]
            ).start()

    def one(owner, carry):
        begin = jnp.maximum(starts_ref[owner], low_tile)
        end = jnp.minimum(starts_ref[owner + 1], low_tile + per_chunk)
        turn = starts_ref[owner] + kept
        run(begin, jnp.minimum(end, turn), owner * kept + begin - starts_ref[owner])
        if hosts:
            begin = jnp.maximum(begin, turn)
            run(begin, end, guests_ref[owner] + begin - turn)
        return carry

    lax.fori_loop(first_ref[base + step], last_ref[base + step] + 1, one, 0)

    @pl.when(step == steps - 1)
    def _():
        drain(slot)

        @pl.when(steps > 1)
        def _():
            drain(1 - slot)


def weight_grad(index, left, right, buffer, owners, slots, firsts, lasts, starts, guests, plan):
    depth, width = param_shapes()[index]
    tokens = left.shape[0]
    chunk = CHUNK[index]
    col_blocks = width // LANES
    piece = next(p for p in (9, 8, 6) if col_blocks % p == 0)
    row = param_rows()[index]
    shift = row % SUBS
    per_chunk = chunk * col_blocks // SUBS
    base = chunk_spans()[1][index]
    shape = (owners * plan[1] * SUBS, LANES)
    in_specs = [
        pl.BlockSpec((tokens, chunk), lambda i, *_: (0, i)),
        pl.BlockSpec((tokens, width), lambda i, *_: (0, 0)),
    ]
    operands = [firsts, lasts, starts, guests, left, right]
    aliases = {}
    if buffer is not None:
        in_specs.append(pl.BlockSpec(memory_space=pl.ANY))
        operands.append(buffer)
        aliases = {6: 0}
    return pl.pallas_call(
        partial(weight_grad_body, base, row // SUBS, per_chunk, shift, chunk, col_blocks, slots, plan, piece,
                buffer is not None),
        out_shape=(
            jax.ShapeDtypeStruct(shape, jnp.bfloat16),
            jax.ShapeDtypeStruct((2 * SUBS, LANES), jnp.float32),
        ),
        grid_spec=pltpu.PrefetchScalarGridSpec(
            num_scalar_prefetch=4,
            grid=(depth // chunk,),
            in_specs=in_specs,
            out_specs=(
                pl.BlockSpec(memory_space=pl.ANY),
                pl.BlockSpec((2 * SUBS, LANES), lambda i, *_: (0, 0)),
            ),
            scratch_shapes=[
                pltpu.VMEM((chunk * col_blocks + SUBS, LANES), jnp.float32),
                pltpu.VMEM((2, chunk * col_blocks, LANES), jnp.bfloat16),
                pltpu.SemaphoreType.DMA((2,)),
            ],
        ),
        input_output_aliases=aliases,
        compiler_params=pltpu.CompilerParams(vmem_limit_bytes=VMEM_LIMIT),
        cost_estimate=pl.CostEstimate(
            flops=2 * tokens * depth * width, bytes_accessed=depth * width * 2, transcendentals=0
        ),
        name="weight_grad_%d" % index,
    )(*operands)


class Grid:
    def __init__(self, side, depth):
        self.side = side
        self.sizes = {"u": side, "v": side, "z": depth}
        self.place = lax.axis_index("dp")
        self.core = self.place % 2
        outer = self.place // 2 // side
        inner = self.place // 2 % side
        self.mine = {
            "u": jnp.where(self.core == 0, outer, inner),
            "v": jnp.where(self.core == 0, inner, outer),
            "z": lax.axis_index("seq"),
        }
        self.sibling = (
            self.place + 1 - 2 * self.core,
            self.mine["z"],
        )

    def dp_of(self, first, second, core):
        outer = jnp.where(core == 0, first, second)
        inner = jnp.where(core == 0, second, first)
        return (outer * self.side + inner) * 2 + core

    def device(self, axis, other):
        at = dict(self.mine)
        at[axis] = other
        return (self.dp_of(at["u"], at["v"], self.core), at["z"])

    def other(self, axis, k):
        return k + (k >= self.mine[axis]).astype(jnp.int32)

    def seat(self, axis, other):
        mine = self.mine[axis]
        return mine - (mine > other).astype(jnp.int32)

    def partners(self):
        found = [self.sibling]
        for axis in ("u", "v", "z"):
            for k in range(self.sizes[axis] - 1):
                found.append(self.device(axis, self.other(axis, k)))
        return found

    def greet(self, hosting=None, to_host=False):
        barrier = pltpu.get_barrier_semaphore()
        partners = self.partners()
        for partner in partners:
            pl.semaphore_signal(barrier, inc=1, device_id=partner, device_id_type=MESH)
        expected = len(partners)
        if hosting is not None and to_host:
            for piece in range(hosting.share):
                device, there = hosting.guest_at(piece)

                @pl.when(hosting.is_host & there)
                def _(device=device):
                    pl.semaphore_signal(barrier, inc=1, device_id=device, device_id_type=MESH)

            expected = expected + 1 - hosting.is_host.astype(jnp.int32)
        elif hosting is not None:
            @pl.when(jnp.logical_not(hosting.is_host))
            def _():
                pl.semaphore_signal(barrier, inc=1, device_id=hosting.host, device_id_type=MESH)

            expected = expected + hosting.guests
        pl.semaphore_wait(barrier, expected)


class Hosting:
    def __init__(self, grid, owners, hosts, share, kept, left):
        depth = grid.sizes["z"]
        z = grid.mine["z"]
        self.grid, self.depth, self.hosts, self.share, self.kept, self.left = grid, depth, hosts, share, kept, left
        self.places = owners // depth
        self.is_host = grid.place * depth + z < hosts
        here, _, room = level_counts(hosts, share, self.places, depth, z)
        index = grid.place - here
        back_here, _, back_room = level_counts(hosts, share, self.places, depth, z - depth // 2)
        own = index < room
        spot = jnp.maximum(jnp.where(own, index, back_room - 1 - (index - room)), 0)
        self.piece = lax.rem(spot, share)
        self.host = (spot // share, jnp.where(own | self.is_host, z, z - depth // 2))
        count = jnp.int32(0)
        for piece in range(share):
            count = count + self.guest_at(piece)[1].astype(jnp.int32)
        self.guests = jnp.where(self.is_host, count, 0)

    def guest_at(self, piece):
        there, near, over = guest_of(
            self.hosts, self.share, self.places, self.depth, self.grid.place, self.grid.mine["z"], piece
        )
        device = (jnp.where(near[0], near[1], over[1]), jnp.where(near[0], near[2], over[2]))
        return device, there & (piece < self.share)

    def guest(self, tile):
        piece = tile // self.left
        device, there = self.guest_at(piece)
        return device, there, self.kept + tile - piece * self.left


def split_slots(slots, shards):
    room = 32 * 1024 * 1024 // ((HELD + 2 * SLOTS) * shards * SUBS * LANES * 2)
    part = max(p for p in range(2, 13) if slots % p == 0 and p <= max(room, 2))
    late = max(1, round(part * 0.34))
    return slots // part, (part - late, late)


def level_counts(hosts, share, places, depth, z):
    here = (hosts - z + depth - 1) // depth
    return here, places - here, share * here


def guest_of(hosts, share, places, depth, place, z, piece):
    here, guests, room = level_counts(hosts, share, places, depth, z)
    index = place * share + piece
    far = z + depth // 2
    far_here, far_guests, far_room = level_counts(hosts, share, places, depth, far)
    back = room - 1 - index
    near = index < guests
    over = (far < depth) & (far_room + back < far_guests)
    return near | over, (near, here + index, z), (over, far_here + far_room + back, far)


def guest_places(plan, owners, depth):
    hosts, share, kept, left = plan
    places = [0] * owners
    for host in range(hosts):
        for piece in range(share):
            there, near, over = guest_of(hosts, share, owners // depth, depth, host // depth, host % depth, piece)
            if there:
                _, place, z = near if near[0] else over
                places[place * depth + z] = host * kept + piece * left
    return places


def host_plan(slots, owners, depth):
    hosts = MOD_ROWS // (slots * SUBS)
    shards = owners // 2
    room = 32 * 1024 * 1024 // ((HELD + 2 * SLOTS) * shards * SUBS * LANES * 2)
    share = -(-(owners - hosts) // hosts) if hosts else 0
    levels = [level_counts(hosts, share, owners // depth, depth, z) for z in range(depth)]
    for z, (_, guests, room_here) in enumerate(levels):
        if guests > room_here and (
            z < depth // 2
            or guests - room_here > levels[z - depth // 2][2] - levels[z - depth // 2][1]
        ):
            hosts = 0
    for kept in range(1, slots) if hosts else ():
        left = slots - kept
        if share * left > kept:
            continue
        for step in range(min(12, max(room, 2)), 5, -1):
            for late in (round(step * 0.34), step // 3, -(-step // 3)):
                early = step - late
                if kept % step or left % early:
                    continue
                middle = kept // step * early
                if all((i * left - middle) % late == 0 for i in range(share + 1) if i * left > middle):
                    return hosts, share, kept, kept // step, (early, late)
    steps, parts = split_slots(slots, shards)
    return 0, 0, slots, steps, parts


ORDERS = (("u", "v", "z"), ("u", "z", "v"))
LAG = 2
SLOTS = 4
OUTS = 8
LEAD = 4
HELD = 4 * LAG + 1


def gather_stream(grid, order, first_row, span, steps, own_ref, out_ref, sems, hosting):
    (send_a, recv_a, send_b, recv_b, send_c, recv_c, send_d, recv_d, kept_sem, arrive) = sems
    mine = grid.mine
    side = grid.side
    near, mid, far = order[2], order[1], order[0]

    def rows(q):
        return pl.ds(pl.multiple_of(first_row + q * span, SUBS), span)

    def copy(source, target, send, recv, device):
        return pltpu.make_async_remote_copy(
            src_ref=source, dst_ref=target, send_sem=send, recv_sem=recv, device_id=device,
            device_id_type=MESH,
        )

    def one_a(q, axis, k):
        other = grid.other(axis, k)
        mine_dp = grid.dp_of(mine["u"], mine["v"], grid.core)
        return copy(
            own_ref.at[rows(q)], out_ref.at[mine_dp, mine["z"], rows(q)],
            send_a.at[q % 4, k], recv_a.at[q, grid.seat(axis, other)],
            grid.device(axis, other),
        )

    def wait_a(q, axis, k):
        dp = grid.dp_of(mine["u"], mine["v"], grid.core)
        copy(
            own_ref.at[rows(q)], out_ref.at[dp, mine["z"], rows(q)],
            send_a.at[q % 4, k], recv_a.at[q, k], grid.device(axis, grid.other(axis, k)),
        ).wait_recv()

    def many_b(q, axis, k):
        other = grid.other(axis, k)
        seat = grid.seat(axis, other)
        if axis == "v":
            at = out_ref.at[grid.dp_of(mine["u"], mine["v"], grid.core), :, rows(q)]
            return [copy(at, at, send_b.at[q % 4, k], recv_b.at[q, seat], grid.device(axis, other))]
        found = []
        for v in range(side):
            at = out_ref.at[grid.dp_of(mine["u"], v, grid.core), mine["z"], rows(q)]
            found.append(copy(at, at, send_b.at[q % 4, k], recv_b.at[q, seat], grid.device(axis, other)))
        return found

    def many_c(q, k):
        other = grid.other("u", k)
        seat = grid.seat("u", other)
        found = []
        for v in range(side):
            at = out_ref.at[grid.dp_of(mine["u"], v, grid.core), :, rows(q)]
            found.append(copy(at, at, send_c.at[q % 4, k], recv_c.at[q, seat], grid.device("u", other)))
        return found

    def many_d(q):
        found = []
        for u in range(side):
            for v in range(side):
                at = out_ref.at[grid.dp_of(u, v, grid.core), :, rows(q)]
                found.append(copy(at, at, send_d.at[q % 4], recv_d.at[q], grid.sibling))
        return found

    def bulk(q, count, send, recv, device):
        at = out_ref.at[pl.ds(0, count), :, rows(q)]
        return copy(at, at, send, recv, device)

    def bulk_b(q, axis, send, recv):
        if axis == "v":
            at = out_ref.at[0, :, rows(q)]
        else:
            at = out_ref.at[pl.ds(0, side), 0, rows(q)]
        return copy(at, at, send, recv, grid.sibling)

    far_count = grid.sizes[near] - 1
    mid_count = grid.sizes[mid] - 1

    def stage_d(q):
        bulk(q, side, send_c.at[q % 4, 0], recv_c.at[q, 0], grid.sibling).wait_recv()
        for k in range(1, side - 1):
            bulk(q, side, send_c.at[q % 4, k], recv_c.at[q, k], grid.sibling).wait_recv()
        for k in range(side - 1):
            bulk(q, side, send_c.at[q % 4, k], recv_c.at[q, k], grid.sibling).wait_send()
        for one in many_d(q):
            one.start()

    def stage_c(q):
        for k in range(mid_count):
            bulk_b(q, mid, send_b.at[q % 4, k], recv_b.at[q, k]).wait_recv()
        for k in range(mid_count):
            bulk_b(q, mid, send_b.at[q % 4, k], recv_b.at[q, k]).wait_send()
        for k in range(side - 1):
            for one in many_c(q, k):
                one.start()

    def keep(q):
        dp = grid.dp_of(mine["u"], mine["v"], grid.core)
        return pltpu.make_async_copy(own_ref.at[rows(q)], out_ref.at[dp, mine["z"], rows(q)], kept_sem.at[q % 4])

    def stage_b(q):
        keep(q).wait()
        for k in range(far_count):
            wait_a(q, near, k)
        for k in range(far_count):
            one_a(q, near, k).wait_send()
        for k in range(mid_count):
            for one in many_b(q, mid, k):
                one.start()

    def stage_a(q):
        if hosting is not None:
            _, there, _ = hosting.guest((first_row + q * span) // SUBS)

            @pl.when(hosting.is_host & there)
            def _():
                copy(own_ref.at[rows(q)], own_ref.at[rows(q)], arrive.at[q], arrive.at[q], grid.sibling).wait_recv()

        keep(q).start()
        for k in range(far_count):
            one_a(q, near, k).start()

    def finish(q):
        whole = bulk(q, side * side, send_d.at[q % 4], recv_d.at[q], grid.sibling)
        whole.wait_recv()
        whole.wait_send()

    return (stage_a, stage_b, stage_c, stage_d, finish)


GATHER_REFS = 10


def gather_body(side, depth, plan, slots, images, own_ref, cond_ref, info_ref, out_ref, mod_ref, held_ref,
                mine_ref, own_sem, guest_sem, *refs):
    hosts, share, kept, steps, parts = plan
    grid = Grid(side, depth)
    hosting = Hosting(grid, 2 * side * side * depth, hosts, share, kept, slots - kept) if hosts else None
    fill = pltpu.make_async_copy(own_ref.at[pl.ds(0, kept * SUBS)], mine_ref, own_sem)

    def when_guest(action):
        if hosting is None:
            action()
        else:
            pl.when(jnp.logical_not(hosting.is_host))(action)

    when_guest(fill.start)
    grid.greet(hosting, to_host=True)
    streams = []
    arrivals = []
    first = 0
    for number, (order, part) in enumerate(zip(ORDERS, parts)):
        span = part * SUBS
        sems = refs[GATHER_REFS * number : GATHER_REFS * (number + 1)]
        streams.append(gather_stream(grid, order, first, span, steps, mine_ref, out_ref, sems, hosting))
        arrivals.append((first // SUBS, part, sems[-1]))
        first = first + steps * span
    if hosting is not None:
        left = slots - kept

        def send_chunks(q, carry):
            for low, part, arrive in arrivals:
                tile = low + q * part
                within = tile - hosting.piece * left

                @pl.when(jnp.logical_not(hosting.is_host) & (within >= 0) & (within < left))
                def _(tile=tile, within=within, part=part, arrive=arrive):
                    slot = jnp.clip(kept + within, kept, slots - part)
                    pltpu.make_async_remote_copy(
                        src_ref=own_ref.at[pl.ds(pl.multiple_of(slot * SUBS, SUBS), part * SUBS)],
                        dst_ref=mine_ref.at[pl.ds(pl.multiple_of(tile * SUBS, SUBS), part * SUBS)],
                        send_sem=guest_sem,
                        recv_sem=arrive.at[q],
                        device_id=hosting.host,
                        device_id_type=MESH,
                    ).start()

            return carry

        lax.fori_loop(0, min(LEAD, steps), send_chunks, 0)
    when_guest(fill.wait)
    modulation_step = modulation_stages(
        grid, images, slots, own_ref, info_ref, cond_ref, mod_ref, held_ref, refs[2 * GATHER_REFS :]
    )

    def round_trip(s, carry):
        for late in range(4, -1, -1):
            q = s - LAG * late

            @pl.when((q >= 0) & (q < steps))
            def _(late=late, q=q):
                for stream in streams:
                    stream[late](q)

        if hosting is not None:
            @pl.when(s + LEAD < steps)
            def _():
                send_chunks(s + LEAD, 0)

        modulation_step(s)
        return carry

    lax.fori_loop(0, max(steps + 4 * LAG, MOD_STEPS), round_trip, 0)
    if hosting is not None:
        @pl.when(jnp.logical_not(hosting.is_host))
        def _():
            at = own_ref.at[pl.ds(kept * SUBS, (slots - kept) * SUBS)]
            pltpu.make_async_remote_copy(
                src_ref=at, dst_ref=at, send_sem=guest_sem, recv_sem=guest_sem, device_id=grid.sibling,
                device_id_type=MESH,
            ).wait_send()


def gather_slots(own, cond_rows, info, slots, data_count, seq_count):
    side = math.isqrt(data_count // 2)
    images = data_count * SEGS
    plan = host_plan(slots, data_count * seq_count, seq_count)
    kept, steps = plan[2], plan[3]
    dma = pltpu.SemaphoreType.DMA
    sems = []
    for order in ORDERS:
        sizes = {"u": side - 1, "v": side - 1, "z": seq_count - 1}
        for axis in (order[2], order[1], order[0]):
            sems.append(dma((4, sizes[axis])))
            sems.append(dma((steps, sizes[axis])))
        sems.append(dma((4,)))
        sems.append(dma((steps,)))
        sems.append(dma((4,)))
        sems.append(dma((steps,)))
    vmem = pl.BlockSpec(memory_space=pltpu.VMEM)
    packed, modulation, held = pl.pallas_call(
        partial(gather_body, side, seq_count, plan, slots, images),
        out_shape=(
            jax.ShapeDtypeStruct((data_count, seq_count, kept * SUBS, LANES), jnp.bfloat16),
            jax.ShapeDtypeStruct((IMAGE_ROWS, LANES), jnp.float32),
            jax.ShapeDtypeStruct((condition_rows(slots), LANES), jnp.float32),
        ),
        in_specs=[vmem, vmem, pl.BlockSpec(memory_space=pltpu.SMEM)],
        out_specs=(pl.BlockSpec(memory_space=pl.ANY), vmem, vmem),
        scratch_shapes=[pltpu.VMEM((kept * SUBS, LANES), jnp.bfloat16), dma, dma]
        + sems
        + modulation_refs(side, seq_count, images, slots),
        compiler_params=pltpu.CompilerParams(
            collective_id=2, has_side_effects=True, vmem_limit_bytes=VMEM_LIMIT
        ),
        name="gather_slots",
    )(own, cond_rows, info)
    return packed.reshape(data_count * seq_count * kept * SUBS, LANES), modulation, held


def reduce_stream(grid, order, first_row, span, steps, parts_ref, out_ref, refs, hosting, passed):
    (own, rc, r1, r2, r3, outs, own_sem, out_sem, hand_sem, c_send, c_recv, s1, v1, s2, v2, s3, v3,
     c_credit, k1, k2, k3) = refs
    mine = grid.mine
    side = grid.side
    held = own.shape[0]
    mu, mv, mz = mine["u"], mine["v"], mine["z"]

    def rows(q):
        return pl.ds(pl.multiple_of(first_row + q * span, SUBS), span)

    def load(q, u, v):
        return pltpu.make_async_copy(
            parts_ref.at[grid.dp_of(u, v, grid.core), :, rows(q)], own.at[q % held, u, v], own_sem.at[q % held, u, v]
        )

    def give(q, u, v):
        return pltpu.make_async_remote_copy(
            src_ref=parts_ref.at[grid.dp_of(u, v, 1 - grid.core), :, rows(q)],
            dst_ref=rc.at[q % SLOTS, u, v],
            send_sem=c_send.at[q % SLOTS, u, v],
            recv_sem=c_recv.at[q % SLOTS, u, v],
            device_id=grid.sibling,
            device_id_type=MESH,
        )

    def block(q, stage, other):
        if stage == 0:
            return own.at[q % held, other]
        if order[1] == "v":
            return own.at[q % held, mu, other] if stage == 1 else own.at[q % held, mu, mv, other]
        return own.at[q % held, mu, :, other] if stage == 1 else own.at[q % held, mu, other, mz]

    landing = (r1, r2, r3)
    sends = (s1, s2, s3)
    arrivals = (v1, v2, v3)
    credits = (k1, k2, k3)

    def send(q, stage, k):
        axis = order[stage]
        other = grid.other(axis, k)
        seat = grid.seat(axis, other)
        return pltpu.make_async_remote_copy(
            src_ref=block(q, stage, other),
            dst_ref=landing[stage].at[q % SLOTS, seat],
            send_sem=sends[stage].at[q % SLOTS, k],
            recv_sem=arrivals[stage].at[q % SLOTS, seat],
            device_id=grid.device(axis, other),
            device_id_type=MESH,
        )

    def receive(q, stage, k):
        axis = order[stage]
        return pltpu.make_async_remote_copy(
            src_ref=block(q, stage, 0),
            dst_ref=landing[stage].at[q % SLOTS, k],
            send_sem=sends[stage].at[q % SLOTS, k],
            recv_sem=arrivals[stage].at[q % SLOTS, k],
            device_id=grid.device(axis, grid.other(axis, k)),
            device_id_type=MESH,
        )

    def keep(q):
        return pltpu.make_async_copy(outs.at[q % OUTS], out_ref.at[rows(q)], out_sem.at[q % OUTS])

    def hand_over(q):
        device, there, slot = hosting.guest((first_row + q * span) // SUBS)
        copy = pltpu.make_async_remote_copy(
            src_ref=outs.at[q % OUTS],
            dst_ref=out_ref.at[pl.ds(pl.multiple_of(slot * SUBS, SUBS), span)],
            send_sem=hand_sem.at[q % OUTS],
            recv_sem=passed,
            device_id=device,
            device_id_type=MESH,
        )
        return copy, there

    def write(q, action):
        if hosting is None:
            getattr(keep(q), action)()
            return

        @pl.when(jnp.logical_not(hosting.is_host))
        def _():
            getattr(keep(q), action)()

        copy, there = hand_over(q)

        @pl.when(hosting.is_host & there)
        def _():
            if action == "start":
                copy.start()
            else:
                copy.wait_send()

    def collect(q, stage):
        axis = order[stage]
        count = grid.sizes[axis] - 1
        for k in range(count):
            receive(q, stage, k).wait_recv()
        kept = block(q, stage, mine[axis])
        total = kept[...].astype(jnp.float32)
        for k in range(count):
            total = total + landing[stage][q % SLOTS, k].astype(jnp.float32)
        if stage < 2:
            kept[...] = total.astype(jnp.bfloat16)
        else:
            @pl.when(q >= OUTS)
            def _():
                write(q - OUTS, "wait")

            outs[q % OUTS] = total.astype(jnp.bfloat16)
            write(q, "start")
        for k in range(count):
            send(q, stage, k).wait_send()

        @pl.when(q + SLOTS < steps)
        def _():
            for k in range(count):
                pl.semaphore_signal(
                    credits[stage].at[mine[axis]], inc=1, device_id=grid.device(axis, grid.other(axis, k)),
                    device_id_type=MESH,
                )

    def launch(q, stage):
        axis = order[stage]
        count = grid.sizes[axis] - 1

        @pl.when(q >= SLOTS)
        def _():
            for k in range(count):
                pl.semaphore_wait(credits[stage].at[grid.other(axis, k)], 1)

        for k in range(count):
            send(q, stage, k).start()

    def begin(q):
        @pl.when(q >= SLOTS)
        def _():
            pl.semaphore_wait(c_credit, 1)

        for u in range(side):
            for v in range(side):
                give(q, u, v).start()
                load(q, u, v).start()

    def stage_c(q):
        for u in range(side):
            for v in range(side):
                load(q, u, v).wait()
                give(q, u, v).wait_recv()
                own[q % held, u, v] = (
                    own[q % held, u, v].astype(jnp.float32) + rc[q % SLOTS, u, v].astype(jnp.float32)
                ).astype(jnp.bfloat16)
        for u in range(side):
            for v in range(side):
                give(q, u, v).wait_send()

        @pl.when(q + SLOTS < steps)
        def _():
            pl.semaphore_signal(c_credit, inc=1, device_id=grid.sibling, device_id_type=MESH)

        launch(q, 0)

    def stage_one(q):
        collect(q, 0)
        launch(q, 1)

    def stage_two(q):
        collect(q, 1)
        launch(q, 2)

    def stage_three(q):
        collect(q, 2)

    return (begin, stage_c, stage_one, stage_two, stage_three), write


REDUCE_REFS = 21


MOD_BLOCKS = 6 * D // LANES
IMAGE_ROWS = SEGS * MOD_BLOCKS
SENT_ROWS = -(-IMAGE_ROWS // SUBS) * SUBS
COND_STRIDE = D // LANES + 1
COND_ROWS = SEGS * COND_STRIDE
FRONT = 56
MOD_STEPS = 31
FILL_STEPS = 8
PRODUCT_STEPS = 9


def held_depth(slots):
    depth = -(-(slots * SUBS + MOD_BLOCKS - 1) // MOD_BLOCKS)
    return -(-depth // 8) * 8


def condition_rows(slots):
    return -(-(D + 8 + max(held_depth(slots) + 32, 2 * LANES)) // LANES) * LANES


def spread_modulation(s, own_ref, info_ref, wide):
    rows = own_ref.shape[0]
    count = -(-rows // FILL_STEPS // SUBS) * SUBS

    @pl.when(s == 0)
    def _():
        wide[0:FRONT, :] = jnp.zeros((FRONT, LANES), jnp.float32)
        rest = wide.shape[0] - FRONT - rows
        wide[FRONT + rows :, :] = jnp.zeros((rest, LANES), jnp.float32)

    @pl.when(s < FILL_STEPS)
    def _():
        first = pl.multiple_of(jnp.minimum(s * count, rows - count), SUBS)
        at = first + lax.broadcasted_iota(jnp.int32, (count, LANES), 0)
        values = own_ref[pl.ds(first, count), :].astype(jnp.float32)
        wide[pl.ds(pl.multiple_of(FRONT + first, 8), count), :] = jnp.where(at < info_ref[2], values, 0.0)


def wide_rows(slots):
    return FRONT + MOD_BLOCKS * (held_depth(slots) + 1) + 8


def held_columns(wide, info_ref, depth, block):
    return wide[pl.ds(FRONT + block - info_ref[1], depth, stride=MOD_BLOCKS), :].astype(jnp.bfloat16)


def gather_blocks(grid, buffer, rows, sems):
    send_v, recv_v, send_u, recv_u, send_c, recv_c = sems
    mine = grid.mine
    side = grid.side

    def one(u, v, send, recv, device):
        at = buffer.at[pl.ds(pl.multiple_of(grid.dp_of(u, v, grid.core) * rows, 8), rows)]
        return pltpu.make_async_remote_copy(
            src_ref=at, dst_ref=at, send_sem=send, recv_sem=recv, device_id=device, device_id_type=MESH
        )

    def along(axis, k):
        return grid.device(axis, grid.other(axis, k)), grid.seat(axis, grid.other(axis, k))

    def v_copies():
        found = []
        for k in range(side - 1):
            device, seat = along("v", k)
            found.append(one(mine["u"], mine["v"], send_v.at[k], recv_v.at[seat], device))
        return found

    def u_copies():
        found = []
        for k in range(side - 1):
            device, seat = along("u", k)
            for v in range(side):
                found.append(one(mine["u"], v, send_u.at[k, v], recv_u.at[seat, v], device))
        return found

    def c_copies():
        return [
            one(u, v, send_c.at[u, v], recv_c.at[u, v], grid.sibling) for u in range(side) for v in range(side)
        ]

    def start():
        for copy in v_copies():
            copy.start()

    def second():
        for k in range(side - 1):
            one(mine["u"], mine["v"], send_v.at[k], recv_v.at[k], grid.sibling).wait_recv()
        for copy in v_copies():
            copy.wait_send()
        for copy in u_copies():
            copy.start()

    def third():
        for k in range(side - 1):
            for v in range(side):
                one(mine["u"], v, send_u.at[k, v], recv_u.at[k, v], grid.sibling).wait_recv()
        for copy in u_copies():
            copy.wait_send()
        for copy in c_copies():
            copy.start()

    def finish():
        for copy in c_copies():
            copy.wait_recv()
        for copy in c_copies():
            copy.wait_send()

    return start, second, third, finish


def gather_sems(side):
    dma = pltpu.SemaphoreType.DMA
    return [dma((side - 1,))] * 2 + [dma((side - 1, side))] * 2 + [dma((side, side))] * 2


def reduce_blocks(grid, buffer, rows, refs):
    from_c, from_u, from_v, from_z, send_c, recv_c, send_u, recv_u, send_v, recv_v, send_z, recv_z = refs
    mine = grid.mine
    side = grid.side
    depth = grid.sizes["z"]

    def block(u, v, core):
        return buffer.at[pl.ds(pl.multiple_of(grid.dp_of(u, v, core) * rows, 8), rows)]

    def copy(source, target, send, recv, device):
        return pltpu.make_async_remote_copy(
            src_ref=source, dst_ref=target, send_sem=send, recv_sem=recv, device_id=device, device_id_type=MESH
        )

    def along(axis, k):
        other = grid.other(axis, k)
        return other, grid.device(axis, other), grid.seat(axis, other)

    def c_copies():
        return [
            copy(block(u, v, 1 - grid.core), from_c.at[u, v], send_c.at[u, v], recv_c.at[u, v], grid.sibling)
            for u in range(side)
            for v in range(side)
        ]

    def u_copies():
        found = []
        for k in range(side - 1):
            other, device, seat = along("u", k)
            for v in range(side):
                found.append(
                    copy(block(other, v, grid.core), from_u.at[seat, v], send_u.at[k, v], recv_u.at[seat, v], device)
                )
        return found

    def v_copies():
        found = []
        for k in range(side - 1):
            other, device, seat = along("v", k)
            found.append(
                copy(block(mine["u"], other, grid.core), from_v.at[seat], send_v.at[k], recv_v.at[seat], device)
            )
        return found

    def z_copies():
        found = []
        for k in range(depth - 1):
            _, device, _ = along("z", k)
            found.append(
                copy(block(mine["u"], mine["v"], grid.core), from_z.at[mine["z"]], send_z.at[k],
                     recv_z.at[mine["z"]], device)
            )
        return found

    def start():
        for one in c_copies():
            one.start()

    def second():
        for one in c_copies():
            one.wait_recv()
        for one in c_copies():
            one.wait_send()
        for u in range(side):
            for v in range(side):
                at = block(u, v, grid.core)
                at[...] = at[...] + from_c[u, v]
        for one in u_copies():
            one.start()

    def third():
        for k in range(side - 1):
            for v in range(side):
                copy(from_u.at[k, v], from_u.at[k, v], send_u.at[k, v], recv_u.at[k, v], grid.sibling).wait_recv()
        for one in u_copies():
            one.wait_send()
        for v in range(side):
            at = block(mine["u"], v, grid.core)
            total = at[...]
            for k in range(side - 1):
                total = total + from_u[k, v]
            at[...] = total
        for one in v_copies():
            one.start()

    def fourth():
        for k in range(side - 1):
            copy(from_v.at[k], from_v.at[k], send_v.at[k], recv_v.at[k], grid.sibling).wait_recv()
        for one in v_copies():
            one.wait_send()
        at = block(mine["u"], mine["v"], grid.core)
        total = at[...]
        for k in range(side - 1):
            total = total + from_v[k]
        at[...] = total
        from_z[mine["z"]] = total
        for one in z_copies():
            one.start()

    def finish():
        for k in range(depth - 1):
            other = grid.other("z", k)
            copy(from_z.at[other], from_z.at[other], send_z.at[k], recv_z.at[other], grid.sibling).wait_recv()
        for one in z_copies():
            one.wait_send()
        total = from_z[0]
        for z in range(1, depth):
            total = total + from_z[z]
        return total

    return start, second, third, fourth, finish


def reduce_refs(side, depth, rows):
    dma = pltpu.SemaphoreType.DMA
    f32 = jnp.float32
    return [
        pltpu.VMEM((side, side, rows, LANES), f32),
        pltpu.VMEM((side - 1, side, rows, LANES), f32),
        pltpu.VMEM((side - 1, rows, LANES), f32),
        pltpu.VMEM((depth, rows, LANES), f32),
        dma((side, side)),
        dma((side, side)),
        dma((side - 1, side)),
        dma((side - 1, side)),
        dma((side - 1,)),
        dma((side - 1,)),
        dma((depth - 1,)),
        dma((depth,)),
    ]


def modulation_stages(grid, images, slots, own_ref, info_ref, cond_ref, mod_ref, held_ref, refs):
    everyone, wide, columns, parts, square = refs[:5]
    gather = gather_blocks(grid, everyone, COND_ROWS, refs[5:11])
    reduce = reduce_blocks(grid, parts, IMAGE_ROWS, refs[11:23])
    here = grid.place
    depth = held_depth(slots)

    def run(s):
        spread_modulation(s, own_ref, info_ref, wide)

        @pl.when(s == 0)
        def _():
            everyone[pl.ds(pl.multiple_of(here * COND_ROWS, 8), COND_ROWS), :] = cond_ref[...]
            gather[0]()
            square[...] = jnp.zeros_like(square)
            held_ref[...] = jnp.zeros_like(held_ref)

        @pl.when(s == 2)
        def _():
            gather[1]()

        @pl.when(s == 4)
        def _():
            gather[2]()

        @pl.when(s == 7)
        def _():
            gather[3]()

        @pl.when(s == 8)
        def _():
            for block in range(D // LANES):
                square[0:images, :] = everyone[pl.ds(block, images, stride=COND_STRIDE), :]
                held_ref[block * LANES : (block + 1) * LANES, :] = square[...].T
            held_ref[D : D + 8, :] = (lax.broadcasted_iota(jnp.int32, (8, LANES), 0) == 0).astype(jnp.float32)
            for part in range(columns.shape[1] // LANES):
                columns[:, part * LANES : (part + 1) * LANES] = (
                    held_ref[pl.ds(info_ref[0] + part * LANES, LANES), :].T.astype(jnp.bfloat16)
                )

        at_product = s - 9

        @pl.when((at_product >= 0) & (at_product < PRODUCT_STEPS))
        def _():
            left = columns[0:images, 0:depth]
            each = MOD_BLOCKS // 2 // PRODUCT_STEPS
            for pair in range(each):
                block = (at_product * each + pair) * 2
                right = jnp.concatenate(
                    [held_columns(wide, info_ref, depth, block), held_columns(wide, info_ref, depth, block + 1)],
                    axis=1,
                )
                found = jnp.dot(left, right, preferred_element_type=jnp.float32)
                parts[pl.ds(block, images, stride=MOD_BLOCKS), :] = found[:, :LANES]
                parts[pl.ds(block + 1, images, stride=MOD_BLOCKS), :] = found[:, LANES:]

        @pl.when(s == 18)
        def _():
            reduce[0]()

        for at, stage in ((20, 1), (23, 2), (26, 3)):
            @pl.when(s == at)
            def _(stage=stage):
                reduce[stage]()

        @pl.when(s == 29)
        def _():
            mod_ref[...] = reduce[4]()

    return run


def modulation_refs(side, depth, images, slots):
    data_count = side * side * 2
    lanes = -(-held_depth(slots) // LANES) * LANES
    f32 = jnp.float32
    return (
        [
            pltpu.VMEM((data_count * COND_ROWS, LANES), f32),
            pltpu.VMEM((wide_rows(slots), LANES), f32),
            pltpu.VMEM((LANES, lanes), jnp.bfloat16),
            pltpu.VMEM((data_count * IMAGE_ROWS, LANES), f32),
            pltpu.VMEM((LANES, LANES), f32),
        ]
        + gather_sems(side)
        + reduce_refs(side, depth, IMAGE_ROWS)
    )


def modulation_grad_stages(grid, images, slots, own_ref, info_ref, part_ref, all_ref, cond_ref, refs):
    arrived, summed, wide, around, parts, send_z, recv_z, done_sem = refs[:8]
    gather = gather_blocks(grid, summed, IMAGE_ROWS, refs[8:14])
    reduce = reduce_blocks(grid, parts, COND_ROWS, refs[14:26])
    mine = grid.mine
    sizes = grid.sizes["z"]
    here = pl.ds(pl.multiple_of(grid.place * IMAGE_ROWS, 8), IMAGE_ROWS)
    depth = held_depth(slots)

    def to_z(k):
        return pltpu.make_async_remote_copy(
            src_ref=part_ref, dst_ref=arrived.at[mine["z"]], send_sem=send_z.at[k], recv_sem=recv_z.at[mine["z"]],
            device_id=grid.device("z", grid.other("z", k)), device_id_type=MESH,
        )

    def run(s):
        spread_modulation(s, own_ref, info_ref, wide)

        @pl.when(s == 0)
        def _():
            for k in range(sizes - 1):
                to_z(k).start()
            arrived[mine["z"]] = part_ref[...]
            around[...] = jnp.zeros_like(around)
            parts[...] = jnp.zeros_like(parts)

        @pl.when(s == 2)
        def _():
            for k in range(sizes - 1):
                other = grid.other("z", k)
                pltpu.make_async_remote_copy(
                    src_ref=part_ref, dst_ref=arrived.at[other], send_sem=send_z.at[k], recv_sem=recv_z.at[other],
                    device_id=grid.sibling, device_id_type=MESH,
                ).wait_recv()
            for k in range(sizes - 1):
                to_z(k).wait_send()
            total = arrived[0].astype(jnp.float32)
            for z in range(1, sizes):
                total = total + arrived[z].astype(jnp.float32)
            summed[here, :] = total.astype(jnp.bfloat16).astype(jnp.float32)[:IMAGE_ROWS]
            gather[0]()

        @pl.when(s == 4)
        def _():
            gather[1]()

        @pl.when(s == 6)
        def _():
            gather[2]()

        @pl.when(s == 9)
        def _():
            gather[3]()
            pltpu.make_async_copy(summed, all_ref, done_sem).start()

        at_product = s - 10

        @pl.when((at_product >= 0) & (at_product < PRODUCT_STEPS))
        def _():
            total = around[D + 8 : D + 8 + depth, 0:images]
            each = MOD_BLOCKS // 2 // PRODUCT_STEPS
            for pair in range(each):
                block = (at_product * each + pair) * 2
                left = jnp.concatenate(
                    [held_columns(wide, info_ref, depth, block), held_columns(wide, info_ref, depth, block + 1)],
                    axis=1,
                )
                right = jnp.concatenate(
                    [
                        summed[pl.ds(block + more, images, stride=MOD_BLOCKS), :].astype(jnp.bfloat16)
                        for more in (0, 1)
                    ],
                    axis=1,
                )
                total = total + lax.dot_general(
                    left, right, (((1,), (1,)), ((), ())), preferred_element_type=jnp.float32
                )
            around[D + 8 : D + 8 + depth, 0:images] = total

        @pl.when(s == 19)
        def _():
            for block in range(D // LANES):
                piece = around[pl.ds(D + 8 - info_ref[0] + block * LANES, LANES), :].T
                parts[pl.ds(block, images, stride=COND_STRIDE), :] = piece[0:images, :]
            reduce[0]()

        for at, stage in ((21, 1), (24, 2), (27, 3)):
            @pl.when(s == at)
            def _(stage=stage):
                reduce[stage]()

        @pl.when(s == 30)
        def _():
            cond_ref[...] = reduce[4]()
            pltpu.make_async_copy(summed, all_ref, done_sem).wait()

    return run


MOD_GRAD_REFS = 26


def modulation_grad_refs(side, depth, images, slots):
    data_count = side * side * 2
    dma = pltpu.SemaphoreType.DMA
    f32 = jnp.float32
    return (
        [
            pltpu.VMEM((depth, SENT_ROWS, LANES), jnp.bfloat16),
            pltpu.VMEM((data_count * IMAGE_ROWS, LANES), f32),
            pltpu.VMEM((wide_rows(slots), LANES), f32),
            pltpu.VMEM((2 * (D + 8) + held_depth(slots), LANES), f32),
            pltpu.VMEM((data_count * COND_ROWS, LANES), f32),
            dma((depth - 1,)),
            dma((depth,)),
            dma,
        ]
        + gather_sems(side)
        + reduce_refs(side, depth, COND_ROWS)
    )


def reduce_body(side, depth, plan, slots, parts_ref, part_ref, own_ref, info_ref, out_ref, all_ref, cond_ref,
                *refs):
    hosts, share, kept, steps, parts = plan
    grid = Grid(side, depth)
    hosting = Hosting(grid, 2 * side * side * depth, hosts, share, kept, slots - kept) if hosts else None
    grid.greet(hosting)
    passed = refs[-1]
    modulation_step = modulation_grad_stages(
        grid, 2 * side * side * SEGS, slots, own_ref, info_ref, part_ref, all_ref, cond_ref, refs[:MOD_GRAD_REFS]
    )
    refs = refs[MOD_GRAD_REFS:]
    streams = []
    writes = []
    first = 0
    for number, (order, part) in enumerate(zip(ORDERS, parts)):
        span = part * SUBS
        stages, write = reduce_stream(
            grid, order, first, span, steps, parts_ref, out_ref,
            refs[REDUCE_REFS * number : REDUCE_REFS * (number + 1)], hosting, passed,
        )
        streams.append(stages)
        writes.append(write)
        first = first + steps * span

    def round_trip(s, carry):
        for late in range(4, -1, -1):
            q = s - LAG * late

            @pl.when((q >= 0) & (q < steps))
            def _(late=late, q=q):
                for stream in streams:
                    stream[late](q)

        modulation_step(s)
        return carry

    lax.fori_loop(0, max(steps + 4 * LAG, MOD_STEPS), round_trip, 0)
    for write in writes:
        for q in range(max(steps - OUTS, 0), steps):
            write(q, "wait")
    if hosting is not None:
        @pl.when(jnp.logical_not(hosting.is_host))
        def _():
            at = out_ref.at[pl.ds(kept * SUBS, (slots - kept) * SUBS)]
            pltpu.make_async_remote_copy(
                src_ref=at, dst_ref=at, send_sem=passed, recv_sem=passed, device_id=grid.sibling,
                device_id_type=MESH,
            ).wait_recv()


def reduce_slots(grads, mod_part, own, info, slots, data_count, seq_count):
    side = math.isqrt(data_count // 2)
    plan = host_plan(slots, data_count * seq_count, seq_count)
    kept, parts = plan[2], plan[4]
    held = HELD
    dma = pltpu.SemaphoreType.DMA
    regular = pltpu.SemaphoreType.REGULAR
    bf16 = jnp.bfloat16
    f32 = jnp.float32
    scratch = modulation_grad_refs(side, seq_count, data_count * SEGS, slots)
    for order, part in zip(ORDERS, parts):
        span = part * SUBS
        sizes = {"u": side, "v": side, "z": seq_count}
        left = dict(sizes)
        scratch.append(pltpu.VMEM((held, side, side, seq_count, span, LANES), bf16))
        scratch.append(pltpu.VMEM((SLOTS, side, side, seq_count, span, LANES), bf16))
        for axis in order:
            del left[axis]
            rest = tuple(left[name] for name in ("u", "v", "z") if name in left)
            scratch.append(pltpu.VMEM((SLOTS, sizes[axis] - 1) + rest + (span, LANES), bf16))
        scratch.append(pltpu.VMEM((OUTS, span, LANES), bf16))
        scratch.append(dma((held, side, side)))
        scratch.append(dma((OUTS,)))
        scratch.append(dma((OUTS,)))
        scratch.append(dma((SLOTS, side, side)))
        scratch.append(dma((SLOTS, side, side)))
        for axis in order:
            scratch.append(dma((SLOTS, sizes[axis] - 1)))
            scratch.append(dma((SLOTS, sizes[axis] - 1)))
        scratch.append(regular)
        for axis in order:
            scratch.append(regular((sizes[axis],)))
    scratch.append(dma)
    return pl.pallas_call(
        partial(reduce_body, side, seq_count, plan, slots),
        out_shape=(
            jax.ShapeDtypeStruct((slots * SUBS, LANES), bf16),
            jax.ShapeDtypeStruct((data_count * IMAGE_ROWS, LANES), f32),
            jax.ShapeDtypeStruct((COND_ROWS, LANES), f32),
        ),
        in_specs=[
            pl.BlockSpec(memory_space=pl.ANY),
            pl.BlockSpec(memory_space=pltpu.VMEM),
            pl.BlockSpec(memory_space=pltpu.VMEM),
            pl.BlockSpec(memory_space=pltpu.SMEM),
        ],
        out_specs=(
            pl.BlockSpec(memory_space=pl.ANY),
            pl.BlockSpec(memory_space=pl.ANY),
            pl.BlockSpec(memory_space=pltpu.VMEM),
        ),
        scratch_shapes=scratch,
        compiler_params=pltpu.CompilerParams(
            collective_id=1, has_side_effects=True, vmem_limit_bytes=VMEM_LIMIT
        ),
        name="reduce_slots",
    )(grads.reshape(data_count, seq_count, kept * SUBS, LANES), mod_part, own, info)


UPDATE_TILES = 72


def update_body(mod_depth, own_ref, reduced, cond_ref, mod_ref, master, first, second,
                new_master, new_first, new_second, mod_rows, wide):
    step = pl.program_id(0)
    mod_blocks = 6 * D // LANES
    start_row = own_ref[0] * SUBS
    shift = lax.rem(start_row, mod_blocks)
    tiles = UPDATE_TILES
    piece = 9

    @pl.when((step == 0) & (start_row < MOD_ROWS))
    def _():
        images = cond_ref.shape[1]
        for begin in range(0, mod_blocks, piece):
            grads = [
                mod_ref[pl.ds(begin + block, images, stride=mod_blocks), :].astype(jnp.bfloat16)
                for block in range(piece)
            ]
            part = jnp.dot(
                cond_ref[...], jnp.concatenate(grads, axis=1), preferred_element_type=jnp.float32
            )
            for block in range(piece):
                mod_rows[pl.ds(begin + block, mod_depth, stride=mod_blocks), :] = part[
                    :, block * LANES : (block + 1) * LANES
                ]

    wide[...] = reduced[...].astype(jnp.float32)
    corr_one = 1.0 - beta_one**STEP
    corr_two = 1.0 - beta_two**STEP
    local = step * tiles + lax.broadcasted_iota(jnp.int32, (tiles, LANES), 0)
    used = local < own_ref[1]
    for sub in range(SUBS):
        columns = pl.ds(sub * LANES, LANES)
        from_mod = mod_rows[pl.ds(shift + step * tiles * SUBS + sub, tiles, stride=SUBS), :]
        is_mod = start_row + local * SUBS + sub < MOD_ROWS
        grad = jnp.where(is_mod, from_mod, wide[pl.ds(sub, tiles, stride=SUBS), :])
        grad = jnp.where(used, grad, 0.0)
        one = beta_one * first[:, columns] + (1.0 - beta_one) * grad
        two = beta_two * second[:, columns] + (1.0 - beta_two) * grad * grad
        held = master[:, columns]
        new_first[:, columns] = one
        new_second[:, columns] = two
        new_master[:, columns] = held - learn_rate * (
            one / corr_one / (jnp.sqrt(two / corr_two) + adam_eps) + weight_decay * held
        )


def own_conditions(held, info, images, slots):
    steps = -(-slots // UPDATE_TILES)
    depth = -(-(steps * UPDATE_TILES * SUBS + MOD_BLOCKS) // MOD_BLOCKS)
    depth = -(-depth // 8) * 8
    return lax.dynamic_slice(held, (info[0], jnp.int32(0)), (depth, images)).astype(jnp.bfloat16)


def update(reduced, cond_own, mod_all, own_first, master, first, second):
    slots, tile_len = master.shape
    mod_depth, images = cond_own.shape
    tiles = UPDATE_TILES
    steps = -(-slots // tiles)
    wide_block = pl.BlockSpec((tiles, tile_len), lambda i, *_: (i, 0))
    return pl.pallas_call(
        partial(update_body, mod_depth),
        out_shape=(jax.ShapeDtypeStruct(master.shape, jnp.float32),) * 3,
        grid_spec=pltpu.PrefetchScalarGridSpec(
            num_scalar_prefetch=1,
            grid=(steps,),
            in_specs=[
                pl.BlockSpec((tiles * SUBS, LANES), lambda i, *_: (i, 0)),
                pl.BlockSpec((mod_depth, images), lambda i, *_: (0, 0)),
                pl.BlockSpec(mod_all.shape, lambda i, *_: (0, 0)),
                wide_block,
                wide_block,
                wide_block,
            ],
            out_specs=(wide_block,) * 3,
            scratch_shapes=[
                pltpu.VMEM((mod_depth * MOD_BLOCKS, LANES), jnp.float32),
                pltpu.VMEM((tiles * SUBS, LANES), jnp.float32),
            ],
        ),
        compiler_params=pltpu.CompilerParams(vmem_limit_bytes=VMEM_LIMIT),
        name="update",
    )(own_first, reduced, cond_own, mod_all, master, first, second)


def normalize(values):
    centred = values - jnp.mean(values, axis=-1, keepdims=True)
    spread = jnp.mean(centred * centred, axis=-1, keepdims=True)
    return centred * lax.rsqrt(spread + ln_eps)


def cosine_of(target, projected):
    inner_mean = jnp.mean(projected * target, axis=-1)
    return (
        inner_mean
        * lax.rsqrt(jnp.mean(projected * projected, axis=-1) + cos_eps)
        * lax.rsqrt(jnp.mean(target * target, axis=-1) + cos_eps)
    )


def gelu_tanh(values):
    return jax.nn.gelu(values, approximate=True)


def lane_pad(width):
    return -(-width // LANES) * LANES


def regroup_body(moves, fill, x_ref, out_ref):
    if fill is not None:
        start, width = fill
        for group in range(out_ref.shape[0]):
            out_ref[group, :, start : start + width] = jnp.zeros((out_ref.shape[1], width), out_ref.dtype)
    for from_group, start, to_group, target, width in moves:
        if from_group is None:
            values = x_ref[:, start : start + width]
        else:
            values = x_ref[from_group, :, start : start + width]
        if to_group is None:
            out_ref[:, target : target + width] = values
        else:
            out_ref[to_group, :, target : target + width] = values


def split_groups(x, parts, groups):
    tokens, total = x.shape
    width = total // parts // groups
    padded = lane_pad(parts * width) if parts > 1 else width
    moves = [
        (None, (part * groups + group) * width, group, part * width, width)
        for group in range(groups)
        for part in range(parts)
    ]
    fill = (parts * width, padded - parts * width) if padded > parts * width and parts > 1 else None
    return pl.pallas_call(
        partial(regroup_body, moves, fill),
        out_shape=jax.ShapeDtypeStruct((groups, tokens, padded), x.dtype),
        compiler_params=pltpu.CompilerParams(vmem_limit_bytes=VMEM_LIMIT),
        name="split_groups_%d" % parts,
    )(x)


def join_groups(x, parts, width):
    groups, tokens, _ = x.shape
    moves = [
        (group, part * width, None, (part * groups + group) * width, width)
        for group in range(groups)
        for part in range(parts)
    ]
    return pl.pallas_call(
        partial(regroup_body, moves, None),
        out_shape=jax.ShapeDtypeStruct((tokens, parts * groups * width), x.dtype),
        compiler_params=pltpu.CompilerParams(vmem_limit_bytes=VMEM_LIMIT),
        name="join_groups_%d" % parts,
    )(x)


QUERY_BLOCK = 256


def key_bias(seg_col, pad_col, seg_row, first):
    keys = seg_col.shape[0]
    queries = seg_row.shape[1]
    key_at = lax.broadcasted_iota(jnp.int32, (keys, queries), 0)
    query_at = first + lax.broadcasted_iota(jnp.int32, (keys, queries), 1)
    allowed = (seg_col == seg_row) & ((pad_col == 1) | (key_at == query_at))
    return jnp.where(allowed, 0.0, -1e30)


def spread_heads(rows_ref, held, heads):
    held[...] = jnp.zeros_like(held)
    for part in range(held.shape[0]):
        for head in range(heads):
            start = (part * heads + head) * HEAD_DIM
            held[part, head, :, 0:HEAD_DIM] = rows_ref[:, start : start + HEAD_DIM]


def probabilities(held, head, block, bias):
    scores = lax.dot_general(
        held[1, head], held[0, head, block, :], (((1,), (1,)), ((), ())), preferred_element_type=jnp.float32
    )
    scores = scores * (HEAD_DIM ** (-0.5)) + bias
    shifted = jnp.exp(scores - jnp.max(scores, axis=0, keepdims=True))
    return shifted * (1.0 / jnp.sum(shifted, axis=0, keepdims=True))


def attention_body(heads, rows_ref, seg_col, pad_col, seg_row, out_ref, held):
    step = pl.program_id(0)

    @pl.when(step == 0)
    def _():
        spread_heads(rows_ref, held, heads)

    first = pl.multiple_of(step * QUERY_BLOCK, QUERY_BLOCK)
    block = pl.ds(first, QUERY_BLOCK)
    bias = key_bias(seg_col[...], pad_col[...], seg_row[...], first)
    for head in range(heads):
        probs = probabilities(held, head, block, bias).astype(jnp.bfloat16)
        result = lax.dot_general(
            held[2, head], probs, (((0,), (0,)), ((), ())), preferred_element_type=jnp.float32
        )
        out_ref[:, head * HEAD_DIM : (head + 1) * HEAD_DIM] = result.T[:, :HEAD_DIM].astype(jnp.bfloat16)


def attention(rows, segments, padding, heads):
    length = rows.shape[0]
    whole = pl.BlockSpec((length, 1), lambda i: (0, 0))
    return pl.pallas_call(
        partial(attention_body, heads),
        out_shape=jax.ShapeDtypeStruct((length, heads * HEAD_DIM), jnp.bfloat16),
        grid=(length // QUERY_BLOCK,),
        in_specs=[
            pl.BlockSpec(rows.shape, lambda i: (0, 0)),
            whole,
            whole,
            pl.BlockSpec((1, QUERY_BLOCK), lambda i: (0, i)),
        ],
        out_specs=pl.BlockSpec((QUERY_BLOCK, heads * HEAD_DIM), lambda i: (i, 0)),
        scratch_shapes=[pltpu.VMEM((3, heads, length, LANES), jnp.bfloat16)],
        compiler_params=pltpu.CompilerParams(vmem_limit_bytes=VMEM_LIMIT),
        name="attention",
    )(rows, segments.reshape(length, 1), padding.reshape(length, 1), segments.reshape(1, length))


def attention_grad_body(heads, rows_ref, grad_ref, seg_col, pad_col, seg_row, out_ref, held, given, grad_k, grad_v):
    step = pl.program_id(0)
    scaling = HEAD_DIM ** (-0.5)

    @pl.when(step == 0)
    def _():
        spread_heads(rows_ref, held, heads)
        given[...] = jnp.zeros_like(given)
        grad_k[...] = jnp.zeros_like(grad_k)
        grad_v[...] = jnp.zeros_like(grad_v)
        out_ref[...] = jnp.zeros_like(out_ref)

    first = pl.multiple_of(step * QUERY_BLOCK, QUERY_BLOCK)
    block = pl.ds(first, QUERY_BLOCK)
    bias = key_bias(seg_col[...], pad_col[...], seg_row[...], first)
    for head in range(heads):
        given[:, 0:HEAD_DIM] = grad_ref[:, head * HEAD_DIM : (head + 1) * HEAD_DIM]
        upstream = given[...]
        probs = probabilities(held, head, block, bias)
        grad_v[head] += jnp.dot(probs.astype(jnp.bfloat16), upstream, preferred_element_type=jnp.float32)
        grad_probs = lax.dot_general(
            held[2, head], upstream, (((1,), (1,)), ((), ())), preferred_element_type=jnp.float32
        )
        inner = jnp.sum(probs * grad_probs, axis=0, keepdims=True)
        grad_scores = (probs * (grad_probs - inner)).astype(jnp.bfloat16)
        grad_k[head] += jnp.dot(grad_scores, held[0, head, block, :], preferred_element_type=jnp.float32)
        grad_q = lax.dot_general(
            held[1, head], grad_scores, (((0,), (0,)), ((), ())), preferred_element_type=jnp.float32
        )
        out_ref[block, head * HEAD_DIM : (head + 1) * HEAD_DIM] = (
            grad_q.T[:, :HEAD_DIM] * scaling
        ).astype(jnp.bfloat16)

    @pl.when(step == pl.num_programs(0) - 1)
    def _():
        for head in range(heads):
            start = (heads + head) * HEAD_DIM
            out_ref[:, start : start + HEAD_DIM] = (grad_k[head][:, :HEAD_DIM] * scaling).astype(jnp.bfloat16)
            start = (2 * heads + head) * HEAD_DIM
            out_ref[:, start : start + HEAD_DIM] = grad_v[head][:, :HEAD_DIM].astype(jnp.bfloat16)


def attention_grad(rows, grad, segments, padding, heads):
    length = rows.shape[0]
    whole = pl.BlockSpec((length, 1), lambda i: (0, 0))
    return pl.pallas_call(
        partial(attention_grad_body, heads),
        out_shape=jax.ShapeDtypeStruct(rows.shape, jnp.bfloat16),
        grid=(length // QUERY_BLOCK,),
        in_specs=[
            pl.BlockSpec(rows.shape, lambda i: (0, 0)),
            pl.BlockSpec((QUERY_BLOCK, grad.shape[1]), lambda i: (i, 0)),
            whole,
            whole,
            pl.BlockSpec((1, QUERY_BLOCK), lambda i: (0, i)),
        ],
        out_specs=pl.BlockSpec(rows.shape, lambda i: (0, 0)),
        scratch_shapes=[
            pltpu.VMEM((3, heads, length, LANES), jnp.bfloat16),
            pltpu.VMEM((QUERY_BLOCK, LANES), jnp.bfloat16),
            pltpu.VMEM((heads, length, LANES), jnp.float32),
            pltpu.VMEM((heads, length, LANES), jnp.float32),
        ],
        compiler_params=pltpu.CompilerParams(vmem_limit_bytes=VMEM_LIMIT),
        name="attention_grad",
    )(rows, grad, segments.reshape(length, 1), padding.reshape(length, 1), segments.reshape(1, length))


def shards(
    tokens,
    conditions,
    segment_ids,
    padding,
    targets,
    cotangent,
    tile_counts,
    master,
    first_moment,
    second_moment,
):
    seq_count = lax.axis_size("seq")
    data_count = lax.axis_size("dp")
    seq_place = lax.axis_index("seq")
    data_place = lax.axis_index("dp")
    owners = data_count * seq_count
    slot_count, tile_len = master.shape
    own_rows = slot_count * SUBS
    tile_ends = jnp.cumsum(tile_counts)
    starts = jnp.concatenate([jnp.zeros((1,), jnp.int32), tile_ends.astype(jnp.int32)])
    spans = jnp.asarray(chunk_spans()[0], jnp.int32)
    firsts = jnp.sum((tile_ends[None, :] <= spans[:, :1]).astype(jnp.int32), axis=1)
    lasts = jnp.sum((tile_ends[None, :] <= spans[:, 1:]).astype(jnp.int32), axis=1)
    plan = host_plan(slot_count, owners, seq_count)
    guests = jnp.asarray(
        guest_places((*plan[:3], slot_count - plan[2]), owners, seq_count), jnp.int32
    )
    edge_ids = jnp.asarray(EDGE_TILES, jnp.int32)
    edge_owner = jnp.sum((tile_ends[None, :] <= edge_ids[:, None]).astype(jnp.int32), axis=1)
    edge_within = edge_ids - jnp.take(starts, edge_owner)
    edge_places = edge_owner * plan[2] + edge_within
    if plan[0]:
        edge_places = jnp.where(
            edge_within < plan[2], edge_places, jnp.take(guests, edge_owner) + edge_within - plan[2]
        )
    own_place = data_place * seq_count + seq_place
    own_start = lax.dynamic_index_in_dim(starts, own_place, 0, False)
    own_count = lax.dynamic_index_in_dim(tile_counts, own_place, 0, False)
    own_low = master.astype(jnp.bfloat16).reshape(own_rows, LANES)
    info = jnp.stack(
        [
            jnp.minimum(own_start * SUBS // MOD_BLOCKS, D + 1),
            own_start * SUBS % MOD_BLOCKS,
            jnp.clip(jnp.minimum(own_count * SUBS, MOD_ROWS - own_start * SUBS), 0, own_rows),
        ]
    ).astype(jnp.int32)
    images = data_count * SEGS

    own_first = jnp.stack([own_start, own_count])
    cond_f = conditions.astype(jnp.float32)
    cond_act, silu_cond_back = jax.vjp(jax.nn.silu, cond_f)
    cond_low = cond_act.astype(jnp.bfloat16)
    cond_rows = jnp.pad(cond_low[0].astype(jnp.float32), ((0, 0), (0, LANES))).reshape(COND_ROWS, LANES)
    packed, modulation, cond_held = gather_slots(own_low, cond_rows, info, slot_count, data_count, seq_count)
    modulation = modulation.reshape(1, SEGS, 6 * D)
    weights = {
        index: unpack_weight(index, packed, plan, firsts, lasts, starts, guests)
        for index in (2, 5, 7, 9, 15)
    }
    attend_weight, output_weight, hidden_weight, return_weight, proj_three = (
        weights[index] for index in (2, 5, 7, 9, 15)
    )
    edges = edge_read(packed, edge_places)
    edge_flat = edges.reshape(-1)

    def bias(index):
        row = param_rows()[index]
        at = EDGE_TILES.index(row // SUBS) * SUBS + row % SUBS
        return edge_flat[at * LANES : at * LANES + param_shapes()[index][0]]

    query_bias, value_bias, output_bias, hidden_bias, return_bias = (bias(i) for i in (3, 4, 6, 8, 10))
    proj_bias_one, proj_bias_two, proj_bias_three = (bias(i) for i in (12, 14, 16))
    rows_dev, local_len, model_width = tokens.shape
    full_len = segment_ids.shape[1]
    heads_local = HEADS // seq_count
    group_width = model_width // seq_count
    token_start = seq_place * local_len
    local_seg = lax.dynamic_slice_in_dim(segment_ids, token_start, local_len, 1)
    local_pad = lax.dynamic_slice_in_dim(padding, token_start, local_len, 1).astype(jnp.float32)
    onehot = (local_seg[:, :, None] == jnp.arange(SEGS, dtype=jnp.int32)).astype(jnp.float32)
    per_token = jnp.einsum("rts,rsc->rtc", onehot, modulation, precision=highest)
    shift_one, scale_one, gate_one, shift_two, scale_two, gate_two = jnp.split(
        per_token, 6, axis=-1
    )
    token_f = tokens.astype(jnp.float32)
    normed_one, norm_back_one = jax.vjp(normalize, token_f)
    attend_in = (normed_one * (1.0 + scale_one) + shift_one).astype(jnp.bfloat16)
    triple_bias = jnp.concatenate([query_bias, jnp.zeros_like(query_bias), value_bias])
    triple = (
        jnp.einsum("rtd,dc->rtc", attend_in, attend_weight, preferred_element_type=jnp.float32)
        + triple_bias
    )
    triple_low = split_groups(triple[0].astype(jnp.bfloat16), 3, seq_count)
    head_rows = lax.all_to_all(triple_low, "seq", split_axis=0, concat_axis=0, tiled=True)
    (head_rows, output_weight, hidden_weight, return_weight, proj_three) = lax.optimization_barrier(
        (head_rows, output_weight, hidden_weight, return_weight, proj_three)
    )
    head_rows = head_rows.reshape(full_len, head_rows.shape[-1])
    head_attended = attention(head_rows, segment_ids[0], padding[0], heads_local)
    head_attended = head_attended.reshape(seq_count, local_len, group_width)
    head_attended, packed = lax.optimization_barrier((head_attended, packed))
    proj_one, proj_two = (unpack_weight(index, packed, plan, firsts, lasts, starts, guests) for index in (11, 13))
    attended = lax.all_to_all(head_attended, "seq", split_axis=0, concat_axis=0, tiled=True)
    attended, proj_one, proj_two = lax.optimization_barrier((attended, proj_one, proj_two))
    attended = join_groups(attended, 1, group_width)[None]
    branch_one = (
        jnp.einsum("rtd,dc->rtc", attended, output_weight, preferred_element_type=jnp.float32)
        + output_bias
    )
    middle = token_f + gate_one * branch_one
    normed_two, norm_back_two = jax.vjp(normalize, middle)
    mlp_in = (normed_two * (1.0 + scale_two) + shift_two).astype(jnp.bfloat16)
    hidden = (
        jnp.einsum("rtd,df->rtf", mlp_in, hidden_weight, preferred_element_type=jnp.float32)
        + hidden_bias
    )
    activated_f, gelu_back = jax.vjp(gelu_tanh, hidden)
    activated = activated_f.astype(jnp.bfloat16)
    branch_two = (
        jnp.einsum("rtf,fd->rtd", activated, return_weight, preferred_element_type=jnp.float32)
        + return_bias
    )
    result = middle + gate_two * branch_two
    feature = result.astype(jnp.bfloat16)
    first_pre = (
        jnp.einsum("rtd,dp->rtp", feature, proj_one, preferred_element_type=jnp.float32)
        + proj_bias_one
    )
    first_act, first_back = jax.vjp(jax.nn.silu, first_pre)
    first_low = first_act.astype(jnp.bfloat16)
    second_pre = (
        jnp.einsum("rtp,pc->rtc", first_low, proj_two, preferred_element_type=jnp.float32)
        + proj_bias_two
    )
    second_act, second_back = jax.vjp(jax.nn.silu, second_pre)
    second_low = second_act.astype(jnp.bfloat16)
    projected = (
        jnp.einsum("rtc,co->rto", second_low, proj_three, preferred_element_type=jnp.float32)
        + proj_bias_three
    )
    target_f = targets.astype(jnp.float32)
    cosine, cosine_back = jax.vjp(partial(cosine_of, target_f), projected)
    ends = {}

    def put(buffer, index, left, right):
        buffer, ends[index] = weight_grad(
            index,
            left.reshape(-1, left.shape[-1]),
            right.reshape(-1, right.shape[-1]),
            buffer,
            owners,
            slot_count,
            firsts,
            lasts,
            starts,
            guests,
            (plan[0], plan[2]),
        )
        return buffer

    def summed(grad):
        return jnp.sum(grad.astype(jnp.float32), axis=(0, 1))

    (grad_projected,) = cosine_back(local_pad * -repa_weight)
    grad_projected = grad_projected.astype(jnp.bfloat16)
    sum_sixteen = summed(grad_projected)
    (grad_second,) = second_back(
        jnp.einsum("rto,co->rtc", grad_projected, proj_three, preferred_element_type=jnp.float32)
    )
    grad_second = grad_second.astype(jnp.bfloat16)
    sum_fourteen = summed(grad_second)
    (grad_first,) = first_back(
        jnp.einsum("rtc,pc->rtp", grad_second, proj_two, preferred_element_type=jnp.float32)
    )
    grad_first = grad_first.astype(jnp.bfloat16)
    sum_twelve = summed(grad_first)
    grad_result = cotangent + jnp.einsum(
        "rtp,dp->rtd", grad_first, proj_one, preferred_element_type=jnp.float32
    )
    grad_gate_two = grad_result * branch_two
    grad_branch_two = (grad_result * gate_two).astype(jnp.bfloat16)
    sum_ten = summed(grad_branch_two)
    (grad_hidden,) = gelu_back(
        jnp.einsum(
            "rtd,fd->rtf", grad_branch_two, return_weight, preferred_element_type=jnp.float32
        )
    )
    grad_hidden = grad_hidden.astype(jnp.bfloat16)
    sum_eight = summed(grad_hidden)
    grad_mlp_in = jnp.einsum(
        "rtf,df->rtd", grad_hidden, hidden_weight, preferred_element_type=jnp.float32
    )
    grad_scale_two = grad_mlp_in * normed_two
    (grad_through_two,) = norm_back_two(grad_mlp_in * (1.0 + scale_two))
    grad_middle = grad_result + grad_through_two
    grad_gate_one = grad_middle * branch_one
    grad_branch_one = (grad_middle * gate_one).astype(jnp.bfloat16)
    sum_six = summed(grad_branch_one)
    grad_attended = jnp.einsum(
        "rtc,dc->rtd", grad_branch_one, output_weight, preferred_element_type=jnp.float32
    ).astype(jnp.bfloat16)
    grad_attended = split_groups(grad_attended[0], 1, seq_count)
    grad_attended, second_low = lax.optimization_barrier((grad_attended, second_low))
    head_grad = lax.all_to_all(grad_attended, "seq", split_axis=0, concat_axis=0, tiled=True)
    grad_buffer = put(None, 15, second_low, grad_projected)
    grad_buffer = put(grad_buffer, 11, feature, grad_first)
    head_grad, grad_buffer = lax.optimization_barrier((head_grad, grad_buffer))
    grad_triple_heads = attention_grad(
        head_rows, head_grad.reshape(full_len, group_width), segment_ids[0], padding[0], heads_local
    ).reshape(seq_count, local_len, head_rows.shape[-1])
    grad_triple_heads, grad_buffer, cond_held = lax.optimization_barrier(
        (grad_triple_heads, grad_buffer, cond_held)
    )
    grad_triple = lax.all_to_all(grad_triple_heads, "seq", split_axis=0, concat_axis=0, tiled=True)
    grad_buffer = put(grad_buffer, 13, first_low, grad_second)
    grad_buffer = put(grad_buffer, 9, activated, grad_branch_two)
    grad_buffer = put(grad_buffer, 7, mlp_in, grad_hidden)
    grad_buffer = put(grad_buffer, 5, attended, grad_branch_one)
    cond_own = own_conditions(cond_held, info, images, slot_count)
    grad_triple, grad_buffer, cond_own = lax.optimization_barrier((grad_triple, grad_buffer, cond_own))
    grad_triple = join_groups(grad_triple, 3, group_width)[None]
    grad_buffer = put(grad_buffer, 2, attend_in, grad_triple)
    triple_sums = summed(grad_triple)
    grad_attend_in = jnp.einsum(
        "rtc,dc->rtd", grad_triple, attend_weight, preferred_element_type=jnp.float32
    )
    grad_scale_one = grad_attend_in * normed_one
    (grad_through_one,) = norm_back_one(grad_attend_in * (1.0 + scale_one))
    grad_tokens = grad_middle + grad_through_one
    token_mod_grad = jnp.concatenate(
        [grad_attend_in, grad_scale_one, grad_gate_one, grad_mlp_in, grad_scale_two, grad_gate_two],
        axis=-1,
    )
    mod_part = jnp.einsum("rts,rtc->rsc", onehot, token_mod_grad, precision=highest)
    mod_sent = jnp.pad(
        mod_part.astype(jnp.bfloat16).reshape(IMAGE_ROWS, LANES), ((0, SENT_ROWS - IMAGE_ROWS), (0, 0))
    )
    rows_at = param_rows()

    def rows(vector):
        return vector.reshape(-1, LANES)


    def head(index):
        return (0, ends[index], rows_at[index] % SUBS, SUBS)

    def tail(index):
        return (0, ends[index], SUBS, SUBS + rows_at[index] % SUBS)

    def whole(vector):
        return (0, rows(vector), 0, vector.shape[0] // LANES)

    pieces = [
        (6,) + head(2)[1:],
        tail(2),
        whole(triple_sums[:model_width]),
        whole(triple_sums[2 * model_width :]),
        head(5),
        tail(5),
        whole(sum_six),
        head(7),
        tail(7),
        whole(sum_eight),
        head(9),
        tail(9),
        whole(sum_ten),
        head(11),
        tail(11),
        whole(sum_twelve),
        head(13),
        tail(13),
        whole(sum_fourteen),
        head(15),
        tail(15),
        whole(sum_sixteen),
    ]
    grad_buffer = edge_write(pieces, grad_buffer, edge_places[EDGE_TILES.index(3891) :])
    reduced, mod_all, cond_grad = reduce_slots(
        grad_buffer, mod_sent, own_low, info, slot_count, data_count, seq_count
    )
    (grad_conditions,) = silu_cond_back(cond_grad.reshape(1, SEGS, COND_STRIDE * LANES)[:, :, :D])
    new_master, new_first, new_second = update(
        reduced, cond_own, mod_all, own_first, master, first_moment, second_moment
    )
    return (
        result.astype(jnp.bfloat16),
        grad_tokens,
        grad_conditions,
        new_master,
        new_first,
        new_second,
    )


def solution(mesh):
    return jax.shard_map(
        shards,
        mesh=mesh,
        in_specs=(
            P("dp", "seq", None),
            P("dp", None, None),
            P("dp", None),
            P("dp", None),
            P("dp", "seq", None),
            P("dp", "seq", None),
            P(),
            P(("dp", "seq"), None),
            P(("dp", "seq"), None),
            P(("dp", "seq"), None),
        ),
        out_specs=(
            P("dp", "seq", None),
            P("dp", "seq", None),
            P("dp", None, None),
            P(("dp", "seq"), None),
            P(("dp", "seq"), None),
            P(("dp", "seq"), None),
        ),
        check_vma=False,
    )
```

```python
from functools import partial
import math

import jax
import jax.numpy as jnp
from jax import lax
from jax.experimental import pallas as pl
from jax.experimental.pallas import tpu as pltpu
from jax.sharding import PartitionSpec as P

HEADS = 16
HEAD_DIM = 72
D = 1152
FF = 4608
PROJ = 2048
TARGET = 768
SEGS = 4
STEP = 10
TILES = 15643


ln_eps = 1e-06
cos_eps = 1e-06
repa_weight = 0.5
beta_one = 0.5
beta_two = 0.5
learn_rate = 0.02
weight_decay = 0.01
adam_eps = 1e-08


LANES = 128
SUBS = 16
MOD_ROWS = (D + 1) * 6 * D // LANES
VMEM_LIMIT = 56 * 1024 * 1024
MESH = pl.DeviceIdType.MESH


def param_shapes():
    return [
        (D, 6 * D),
        (6 * D,),
        (D, 3 * D),
        (D,),
        (D,),
        (D, D),
        (D,),
        (D, FF),
        (FF,),
        (FF, D),
        (D,),
        (D, PROJ),
        (PROJ,),
        (PROJ, PROJ),
        (PROJ,),
        (PROJ, TARGET),
        (TARGET,),
    ]


def param_rows():
    starts = []
    row = 0
    for dims in param_shapes():
        starts.append(row)
        row = row + math.prod(dims) // LANES
    return starts


CHUNK = {2: 384, 5: 384, 7: 384, 9: 1536, 11: 384, 13: 512, 15: 1024}
EDGE_TILES = [3891, 5835, 5836, 6484, 6485, 9077, 9078, 9079, 11671, 12823, 12824, 14872, 14873, 15641, 15642]


def chunk_spans():
    spans = []
    base = {}
    rows = param_rows()
    for index, chunk in CHUNK.items():
        depth, width = param_shapes()[index]
        per_chunk = chunk * width // LANES // SUBS
        extra = 1 if rows[index] % SUBS else 0
        base[index] = len(spans)
        for step in range(depth // chunk):
            first = rows[index] // SUBS + step * per_chunk
            spans.append((first, first + per_chunk + extra - 1))
    return spans, base


def unpack_body(base, first_tile, per_chunk, tiles, shift, chunk, col_blocks, hosts, kept,
                first_ref, last_ref, starts_ref, guests_ref, packed, out_ref, landed, wide, sems):
    step = pl.program_id(0)

    def fetch(which, slot):
        low_tile = first_tile + which * per_chunk

        def run(begin, end, place):
            size = pl.multiple_of(jnp.maximum(end - begin, 0) * SUBS, SUBS)
            origin = pl.multiple_of(place * SUBS, SUBS)
            target = pl.multiple_of((begin - low_tile) * SUBS, SUBS)

            @pl.when(end > begin)
            def _():
                pltpu.make_async_copy(
                    packed.at[pl.ds(origin, size)], landed.at[slot, pl.ds(target, size)], sems.at[slot]
                ).start()

        def one(owner, carry):
            begin = jnp.maximum(starts_ref[owner], low_tile)
            end = jnp.minimum(starts_ref[owner + 1], low_tile + tiles)
            turn = starts_ref[owner] + kept
            run(begin, jnp.minimum(end, turn), owner * kept + begin - starts_ref[owner])
            if hosts:
                begin = jnp.maximum(begin, turn)
                run(begin, end, guests_ref[owner] + begin - turn)
            return carry

        lax.fori_loop(first_ref[base + which], last_ref[base + which] + 1, one, 0)

    @pl.when(step == 0)
    def _():
        fetch(0, 0)

    slot = step % 2

    @pl.when(step + 1 < pl.num_programs(0))
    def _():
        fetch(step + 1, (step + 1) % 2)

    pltpu.make_async_copy(packed.at[pl.ds(0, tiles * SUBS)], landed.at[slot], sems.at[slot]).wait()
    wide[...] = landed[slot].astype(jnp.float32)
    for block in range(col_blocks):
        out_ref[:, block * LANES : (block + 1) * LANES] = wide[
            pl.ds(shift + block, chunk, stride=col_blocks), :
        ].astype(jnp.bfloat16)


def unpack_weight(index, packed, plan, firsts, lasts, starts, guests):
    depth, width = param_shapes()[index]
    chunk = CHUNK[index]
    col_blocks = width // LANES
    row = param_rows()[index]
    shift = row % SUBS
    per_chunk = chunk * col_blocks // SUBS
    tiles = per_chunk + (1 if shift else 0)
    base = chunk_spans()[1][index]
    return pl.pallas_call(
        partial(unpack_body, base, row // SUBS, per_chunk, tiles, shift, chunk, col_blocks, plan[0], plan[2]),
        out_shape=jax.ShapeDtypeStruct((depth, width), jnp.bfloat16),
        grid_spec=pltpu.PrefetchScalarGridSpec(
            num_scalar_prefetch=4,
            grid=(depth // chunk,),
            in_specs=[pl.BlockSpec(memory_space=pl.ANY)],
            out_specs=pl.BlockSpec((chunk, width), lambda i, *_: (i, 0)),
            scratch_shapes=[
                pltpu.VMEM((2, tiles * SUBS, LANES), jnp.bfloat16),
                pltpu.VMEM((tiles * SUBS, LANES), jnp.float32),
                pltpu.SemaphoreType.DMA((2,)),
            ],
        ),
        compiler_params=pltpu.CompilerParams(vmem_limit_bytes=VMEM_LIMIT),
        cost_estimate=pl.CostEstimate(flops=0, bytes_accessed=depth * width * 4, transcendentals=0),
        name="unpack_%d" % index,
    )(firsts, lasts, starts, guests, packed)


def edge_read_body(table_ref, packed, out_ref, sem):
    count = out_ref.shape[0] // SUBS

    def one(i, carry):
        origin = pl.multiple_of(table_ref[i] * SUBS, SUBS)
        target = pl.multiple_of(i * SUBS, SUBS)
        pltpu.make_async_copy(packed.at[pl.ds(origin, SUBS)], out_ref.at[pl.ds(target, SUBS)], sem).start()
        return carry

    lax.fori_loop(0, count, one, 0)
    pltpu.make_async_copy(packed.at[pl.ds(0, count * SUBS)], out_ref, sem).wait()


def edge_read(packed, table):
    return pl.pallas_call(
        edge_read_body,
        out_shape=jax.ShapeDtypeStruct((len(EDGE_TILES) * SUBS, LANES), jnp.bfloat16),
        grid_spec=pltpu.PrefetchScalarGridSpec(
            num_scalar_prefetch=1,
            grid=(1,),
            in_specs=[pl.BlockSpec(memory_space=pl.ANY)],
            out_specs=pl.BlockSpec(memory_space=pltpu.VMEM),
            scratch_shapes=[pltpu.SemaphoreType.DMA],
        ),
        name="edge_read",
    )(table, packed)


def edge_write_body(layout, table_ref, *refs):
    pieces = refs[: len(layout)]
    out, wide, narrow, sem = refs[len(layout) + 1 :]
    wide[...] = jnp.zeros_like(wide)
    at = 0
    for piece, (skip, low, high) in zip(pieces, layout):
        at = at + skip
        wide[at : at + high - low, :] = piece[low:high, :]
        at = at + high - low
    narrow[...] = wide[...].astype(jnp.bfloat16)
    count = narrow.shape[0] // SUBS

    def one(i, carry):
        origin = pl.multiple_of(i * SUBS, SUBS)
        target = pl.multiple_of(table_ref[i] * SUBS, SUBS)
        pltpu.make_async_copy(narrow.at[pl.ds(origin, SUBS)], out.at[pl.ds(target, SUBS)], sem).start()
        return carry

    lax.fori_loop(0, count, one, 0)
    pltpu.make_async_copy(narrow, out.at[pl.ds(0, count * SUBS)], sem).wait()


def edge_write(pieces, buffer, table):
    count = table.shape[0]
    layout = [(skip, low, high) for skip, _, low, high in pieces]
    arrays = [array for _, array, _, _ in pieces]
    return pl.pallas_call(
        partial(edge_write_body, layout),
        out_shape=jax.ShapeDtypeStruct(buffer.shape, buffer.dtype),
        grid_spec=pltpu.PrefetchScalarGridSpec(
            num_scalar_prefetch=1,
            grid=(1,),
            in_specs=[pl.BlockSpec(memory_space=pltpu.VMEM)] * len(arrays)
            + [pl.BlockSpec(memory_space=pl.ANY)],
            out_specs=pl.BlockSpec(memory_space=pl.ANY),
            scratch_shapes=[
                pltpu.VMEM((count * SUBS, LANES), jnp.float32),
                pltpu.VMEM((count * SUBS, LANES), jnp.bfloat16),
                pltpu.SemaphoreType.DMA,
            ],
        ),
        input_output_aliases={1 + len(arrays): 0},
        name="edge_write",
    )(table, *arrays, buffer)


def weight_grad_body(base, first_tile, per_chunk, shift, chunk, col_blocks, slots, plan, piece, chained,
                     first_ref, last_ref, starts_ref, guests_ref, x_ref, dy_ref, *rest):
    if chained:
        rest = rest[1:]
    out, ends_ref, wide, narrow, sems = rest
    hosts, kept = plan
    step = pl.program_id(0)
    steps = pl.num_programs(0)
    slot = step % 2
    rows = chunk * col_blocks

    def drain(which):
        pltpu.make_async_copy(narrow.at[which], out.at[pl.ds(0, rows)], sems.at[which]).wait()

    @pl.when(step == 0)
    def _():
        wide[...] = jnp.zeros_like(wide)

    if shift:
        @pl.when(step > 0)
        def _():
            wide[0:SUBS, :] = wide[rows : rows + SUBS, :]

    left = x_ref[...].T
    for start in range(0, col_blocks, piece):
        part = jnp.dot(
            left, dy_ref[:, start * LANES : (start + piece) * LANES], preferred_element_type=jnp.float32
        )
        for block in range(piece):
            wide[pl.ds(shift + start + block, chunk, stride=col_blocks), :] = part[
                :, block * LANES : (block + 1) * LANES
            ]

    @pl.when(step >= 2)
    def _():
        drain(slot)

    narrow[slot] = wide[0:rows, :].astype(jnp.bfloat16)

    @pl.when(step == 0)
    def _():
        ends_ref[0:SUBS, :] = wide[0:SUBS, :]

    if shift:
        @pl.when(step == steps - 1)
        def _():
            ends_ref[SUBS : 2 * SUBS, :] = wide[rows : rows + SUBS, :]
    else:
        ends_ref[SUBS : 2 * SUBS, :] = jnp.zeros((SUBS, LANES), jnp.float32)

    low_tile = first_tile + step * per_chunk

    def run(begin, end, place):
        size = pl.multiple_of(jnp.maximum(end - begin, 0) * SUBS, SUBS)
        target = pl.multiple_of(place * SUBS, SUBS)
        origin = pl.multiple_of((begin - low_tile) * SUBS, SUBS)

        @pl.when(end > begin)
        def _():
            pltpu.make_async_copy(
                narrow.at[slot, pl.ds(origin, size)], out.at[pl.ds(target, size)], sems.at[slot]
            ).start()

    def one(owner, carry):
        begin = jnp.maximum(starts_ref[owner], low_tile)
        end = jnp.minimum(starts_ref[owner + 1], low_tile + per_chunk)
        turn = starts_ref[owner] + kept
        run(begin, jnp.minimum(end, turn), owner * kept + begin - starts_ref[owner])
        if hosts:
            begin = jnp.maximum(begin, turn)
            run(begin, end, guests_ref[owner] + begin - turn)
        return carry

    lax.fori_loop(first_ref[base + step], last_ref[base + step] + 1, one, 0)

    @pl.when(step == steps - 1)
    def _():
        drain(slot)

        @pl.when(steps > 1)
        def _():
            drain(1 - slot)


def weight_grad(index, left, right, buffer, owners, slots, firsts, lasts, starts, guests, plan):
    depth, width = param_shapes()[index]
    tokens = left.shape[0]
    chunk = CHUNK[index]
    col_blocks = width // LANES
    piece = next(p for p in (9, 8, 6) if col_blocks % p == 0)
    row = param_rows()[index]
    shift = row % SUBS
    per_chunk = chunk * col_blocks // SUBS
    base = chunk_spans()[1][index]
    shape = (owners * plan[1] * SUBS, LANES)
    in_specs = [
        pl.BlockSpec((tokens, chunk), lambda i, *_: (0, i)),
        pl.BlockSpec((tokens, width), lambda i, *_: (0, 0)),
    ]
    operands = [firsts, lasts, starts, guests, left, right]
    aliases = {}
    if buffer is not None:
        in_specs.append(pl.BlockSpec(memory_space=pl.ANY))
        operands.append(buffer)
        aliases = {6: 0}
    return pl.pallas_call(
        partial(weight_grad_body, base, row // SUBS, per_chunk, shift, chunk, col_blocks, slots, plan, piece,
                buffer is not None),
        out_shape=(
            jax.ShapeDtypeStruct(shape, jnp.bfloat16),
            jax.ShapeDtypeStruct((2 * SUBS, LANES), jnp.float32),
        ),
        grid_spec=pltpu.PrefetchScalarGridSpec(
            num_scalar_prefetch=4,
            grid=(depth // chunk,),
            in_specs=in_specs,
            out_specs=(
                pl.BlockSpec(memory_space=pl.ANY),
                pl.BlockSpec((2 * SUBS, LANES), lambda i, *_: (0, 0)),
            ),
            scratch_shapes=[
                pltpu.VMEM((chunk * col_blocks + SUBS, LANES), jnp.float32),
                pltpu.VMEM((2, chunk * col_blocks, LANES), jnp.bfloat16),
                pltpu.SemaphoreType.DMA((2,)),
            ],
        ),
        input_output_aliases=aliases,
        compiler_params=pltpu.CompilerParams(vmem_limit_bytes=VMEM_LIMIT),
        cost_estimate=pl.CostEstimate(
            flops=2 * tokens * depth * width, bytes_accessed=depth * width * 2, transcendentals=0
        ),
        name="weight_grad_%d" % index,
    )(*operands)


class Grid:
    def __init__(self, side, depth):
        self.side = side
        self.sizes = {"u": side, "v": side, "z": depth}
        self.place = lax.axis_index("dp")
        self.core = self.place % 2
        outer = self.place // 2 // side
        inner = self.place // 2 % side
        self.mine = {
            "u": jnp.where(self.core == 0, outer, inner),
            "v": jnp.where(self.core == 0, inner, outer),
            "z": lax.axis_index("seq"),
        }
        self.sibling = (
            self.place + 1 - 2 * self.core,
            self.mine["z"],
        )

    def dp_of(self, first, second, core):
        outer = jnp.where(core == 0, first, second)
        inner = jnp.where(core == 0, second, first)
        return (outer * self.side + inner) * 2 + core

    def device(self, axis, other):
        at = dict(self.mine)
        at[axis] = other
        return (self.dp_of(at["u"], at["v"], self.core), at["z"])

    def other(self, axis, k):
        return k + (k >= self.mine[axis]).astype(jnp.int32)

    def seat(self, axis, other):
        mine = self.mine[axis]
        return mine - (mine > other).astype(jnp.int32)

    def partners(self):
        found = [self.sibling]
        for axis in ("u", "v", "z"):
            for k in range(self.sizes[axis] - 1):
                found.append(self.device(axis, self.other(axis, k)))
        return found

    def greet(self, hosting=None, to_host=False):
        barrier = pltpu.get_barrier_semaphore()
        partners = self.partners()
        for partner in partners:
            pl.semaphore_signal(barrier, inc=1, device_id=partner, device_id_type=MESH)
        expected = len(partners)
        if hosting is not None and to_host:
            for piece in range(hosting.share):
                device, there = hosting.guest_at(piece)

                @pl.when(hosting.is_host & there)
                def _(device=device):
                    pl.semaphore_signal(barrier, inc=1, device_id=device, device_id_type=MESH)

            expected = expected + 1 - hosting.is_host.astype(jnp.int32)
        elif hosting is not None:
            @pl.when(jnp.logical_not(hosting.is_host))
            def _():
                pl.semaphore_signal(barrier, inc=1, device_id=hosting.host, device_id_type=MESH)

            expected = expected + hosting.guests
        pl.semaphore_wait(barrier, expected)


class Hosting:
    def __init__(self, grid, owners, hosts, share, kept, left):
        depth = grid.sizes["z"]
        z = grid.mine["z"]
        self.grid, self.depth, self.hosts, self.share, self.kept, self.left = grid, depth, hosts, share, kept, left
        self.places = owners // depth
        self.is_host = grid.place * depth + z < hosts
        here, _, room = level_counts(hosts, share, self.places, depth, z)
        index = grid.place - here
        back_here, _, back_room = level_counts(hosts, share, self.places, depth, z - depth // 2)
        own = index < room
        spot = jnp.maximum(jnp.where(own, index, back_room - 1 - (index - room)), 0)
        self.piece = lax.rem(spot, share)
        self.host = (spot // share, jnp.where(own | self.is_host, z, z - depth // 2))
        count = jnp.int32(0)
        for piece in range(share):
            count = count + self.guest_at(piece)[1].astype(jnp.int32)
        self.guests = jnp.where(self.is_host, count, 0)

    def guest_at(self, piece):
        there, near, over = guest_of(
            self.hosts, self.share, self.places, self.depth, self.grid.place, self.grid.mine["z"], piece
        )
        device = (jnp.where(near[0], near[1], over[1]), jnp.where(near[0], near[2], over[2]))
        return device, there & (piece < self.share)

    def guest(self, tile):
        piece = tile // self.left
        device, there = self.guest_at(piece)
        return device, there, self.kept + tile - piece * self.left


def split_slots(slots, shards):
    room = 32 * 1024 * 1024 // ((HELD + 2 * SLOTS) * shards * SUBS * LANES * 2)
    part = max(p for p in range(2, 13) if slots % p == 0 and p <= max(room, 2))
    late = max(1, round(part * 0.34))
    return slots // part, (part - late, late)


def level_counts(hosts, share, places, depth, z):
    here = (hosts - z + depth - 1) // depth
    return here, places - here, share * here


def guest_of(hosts, share, places, depth, place, z, piece):
    here, guests, room = level_counts(hosts, share, places, depth, z)
    index = place * share + piece
    far = z + depth // 2
    far_here, far_guests, far_room = level_counts(hosts, share, places, depth, far)
    back = room - 1 - index
    near = index < guests
    over = (far < depth) & (far_room + back < far_guests)
    return near | over, (near, here + index, z), (over, far_here + far_room + back, far)


def guest_places(plan, owners, depth):
    hosts, share, kept, left = plan
    places = [0] * owners
    for host in range(hosts):
        for piece in range(share):
            there, near, over = guest_of(hosts, share, owners // depth, depth, host // depth, host % depth, piece)
            if there:
                _, place, z = near if near[0] else over
                places[place * depth + z] = host * kept + piece * left
    return places


def host_plan(slots, owners, depth):
    hosts = MOD_ROWS // (slots * SUBS)
    shards = owners // 2
    room = 32 * 1024 * 1024 // ((HELD + 2 * SLOTS) * shards * SUBS * LANES * 2)
    share = -(-(owners - hosts) // hosts) if hosts else 0
    levels = [level_counts(hosts, share, owners // depth, depth, z) for z in range(depth)]
    for z, (_, guests, room_here) in enumerate(levels):
        if guests > room_here and (
            z < depth // 2
            or guests - room_here > levels[z - depth // 2][2] - levels[z - depth // 2][1]
        ):
            hosts = 0
    for kept in range(1, slots) if hosts else ():
        left = slots - kept
        if share * left > kept:
            continue
        for step in range(min(12, max(room, 2)), 5, -1):
            for late in (round(step * 0.34), step // 3, -(-step // 3)):
                early = step - late
                if kept % step or left % early:
                    continue
                middle = kept // step * early
                if all((i * left - middle) % late == 0 for i in range(share + 1) if i * left > middle):
                    return hosts, share, kept, kept // step, (early, late)
    steps, parts = split_slots(slots, shards)
    return 0, 0, slots, steps, parts


ORDERS = (("u", "v", "z"), ("u", "z", "v"))
LAG = 2
SLOTS = 4
OUTS = 8
LEAD = 4
HELD = 4 * LAG + 1


def gather_stream(grid, order, first_row, span, steps, own_ref, out_ref, sems, hosting):
    (send_a, recv_a, send_b, recv_b, send_c, recv_c, send_d, recv_d, kept_sem, arrive) = sems
    mine = grid.mine
    side = grid.side
    near, mid, far = order[2], order[1], order[0]

    def rows(q):
        return pl.ds(pl.multiple_of(first_row + q * span, SUBS), span)

    def copy(source, target, send, recv, device):
        return pltpu.make_async_remote_copy(
            src_ref=source, dst_ref=target, send_sem=send, recv_sem=recv, device_id=device,
            device_id_type=MESH,
        )

    def one_a(q, axis, k):
        other = grid.other(axis, k)
        mine_dp = grid.dp_of(mine["u"], mine["v"], grid.core)
        return copy(
            own_ref.at[rows(q)], out_ref.at[mine_dp, mine["z"], rows(q)],
            send_a.at[q % 4, k], recv_a.at[q, grid.seat(axis, other)],
            grid.device(axis, other),
        )

    def wait_a(q, axis, k):
        dp = grid.dp_of(mine["u"], mine["v"], grid.core)
        copy(
            own_ref.at[rows(q)], out_ref.at[dp, mine["z"], rows(q)],
            send_a.at[q % 4, k], recv_a.at[q, k], grid.device(axis, grid.other(axis, k)),
        ).wait_recv()

    def many_b(q, axis, k):
        other = grid.other(axis, k)
        seat = grid.seat(axis, other)
        if axis == "v":
            at = out_ref.at[grid.dp_of(mine["u"], mine["v"], grid.core), :, rows(q)]
            return [copy(at, at, send_b.at[q % 4, k], recv_b.at[q, seat], grid.device(axis, other))]
        found = []
        for v in range(side):
            at = out_ref.at[grid.dp_of(mine["u"], v, grid.core), mine["z"], rows(q)]
            found.append(copy(at, at, send_b.at[q % 4, k], recv_b.at[q, seat], grid.device(axis, other)))
        return found

    def many_c(q, k):
        other = grid.other("u", k)
        seat = grid.seat("u", other)
        found = []
        for v in range(side):
            at = out_ref.at[grid.dp_of(mine["u"], v, grid.core), :, rows(q)]
            found.append(copy(at, at, send_c.at[q % 4, k], recv_c.at[q, seat], grid.device("u", other)))
        return found

    def many_d(q):
        found = []
        for u in range(side):
            for v in range(side):
                at = out_ref.at[grid.dp_of(u, v, grid.core), :, rows(q)]
                found.append(copy(at, at, send_d.at[q % 4], recv_d.at[q], grid.sibling))
        return found

    def bulk(q, count, send, recv, device):
        at = out_ref.at[pl.ds(0, count), :, rows(q)]
        return copy(at, at, send, recv, device)

    def bulk_b(q, axis, send, recv):
        if axis == "v":
            at = out_ref.at[0, :, rows(q)]
        else:
            at = out_ref.at[pl.ds(0, side), 0, rows(q)]
        return copy(at, at, send, recv, grid.sibling)

    far_count = grid.sizes[near] - 1
    mid_count = grid.sizes[mid] - 1

    def stage_d(q):
        bulk(q, side, send_c.at[q % 4, 0], recv_c.at[q, 0], grid.sibling).wait_recv()
        for k in range(1, side - 1):
            bulk(q, side, send_c.at[q % 4, k], recv_c.at[q, k], grid.sibling).wait_recv()
        for k in range(side - 1):
            bulk(q, side, send_c.at[q % 4, k], recv_c.at[q, k], grid.sibling).wait_send()
        for one in many_d(q):
            one.start()

    def stage_c(q):
        for k in range(mid_count):
            bulk_b(q, mid, send_b.at[q % 4, k], recv_b.at[q, k]).wait_recv()
        for k in range(mid_count):
            bulk_b(q, mid, send_b.at[q % 4, k], recv_b.at[q, k]).wait_send()
        for k in range(side - 1):
            for one in many_c(q, k):
                one.start()

    def keep(q):
        dp = grid.dp_of(mine["u"], mine["v"], grid.core)
        return pltpu.make_async_copy(own_ref.at[rows(q)], out_ref.at[dp, mine["z"], rows(q)], kept_sem.at[q % 4])

    def stage_b(q):
        keep(q).wait()
        for k in range(far_count):
            wait_a(q, near, k)
        for k in range(far_count):
            one_a(q, near, k).wait_send()
        for k in range(mid_count):
            for one in many_b(q, mid, k):
                one.start()

    def stage_a(q):
        if hosting is not None:
            _, there, _ = hosting.guest((first_row + q * span) // SUBS)

            @pl.when(hosting.is_host & there)
            def _():
                copy(own_ref.at[rows(q)], own_ref.at[rows(q)], arrive.at[q], arrive.at[q], grid.sibling).wait_recv()

        keep(q).start()
        for k in range(far_count):
            one_a(q, near, k).start()

    def finish(q):
        whole = bulk(q, side * side, send_d.at[q % 4], recv_d.at[q], grid.sibling)
        whole.wait_recv()
        whole.wait_send()

    return (stage_a, stage_b, stage_c, stage_d, finish)


GATHER_REFS = 10


def gather_body(side, depth, plan, slots, images, own_ref, cond_ref, info_ref, out_ref, mod_ref, held_ref,
                mine_ref, own_sem, guest_sem, *refs):
    hosts, share, kept, steps, parts = plan
    grid = Grid(side, depth)
    hosting = Hosting(grid, 2 * side * side * depth, hosts, share, kept, slots - kept) if hosts else None
    fill = pltpu.make_async_copy(own_ref.at[pl.ds(0, kept * SUBS)], mine_ref, own_sem)

    def when_guest(action):
        if hosting is None:
            action()
        else:
            pl.when(jnp.logical_not(hosting.is_host))(action)

    when_guest(fill.start)
    grid.greet(hosting, to_host=True)
    streams = []
    arrivals = []
    first = 0
    for number, (order, part) in enumerate(zip(ORDERS, parts)):
        span = part * SUBS
        sems = refs[GATHER_REFS * number : GATHER_REFS * (number + 1)]
        streams.append(gather_stream(grid, order, first, span, steps, mine_ref, out_ref, sems, hosting))
        arrivals.append((first // SUBS, part, sems[-1]))
        first = first + steps * span
    if hosting is not None:
        left = slots - kept

        def send_chunks(q, carry):
            for low, part, arrive in arrivals:
                tile = low + q * part
                within = tile - hosting.piece * left

                @pl.when(jnp.logical_not(hosting.is_host) & (within >= 0) & (within < left))
                def _(tile=tile, within=within, part=part, arrive=arrive):
                    slot = jnp.clip(kept + within, kept, slots - part)
                    pltpu.make_async_remote_copy(
                        src_ref=own_ref.at[pl.ds(pl.multiple_of(slot * SUBS, SUBS), part * SUBS)],
                        dst_ref=mine_ref.at[pl.ds(pl.multiple_of(tile * SUBS, SUBS), part * SUBS)],
                        send_sem=guest_sem,
                        recv_sem=arrive.at[q],
                        device_id=hosting.host,
                        device_id_type=MESH,
                    ).start()

            return carry

        lax.fori_loop(0, min(LEAD, steps), send_chunks, 0)
    when_guest(fill.wait)
    modulation_step = modulation_stages(
        grid, images, slots, own_ref, info_ref, cond_ref, mod_ref, held_ref, refs[2 * GATHER_REFS :]
    )

    def round_trip(s, carry):
        for late in range(4, -1, -1):
            q = s - LAG * late

            @pl.when((q >= 0) & (q < steps))
            def _(late=late, q=q):
                for stream in streams:
                    stream[late](q)

        if hosting is not None:
            @pl.when(s + LEAD < steps)
            def _():
                send_chunks(s + LEAD, 0)

        modulation_step(s)
        return carry

    lax.fori_loop(0, max(steps + 4 * LAG, MOD_STEPS), round_trip, 0)
    if hosting is not None:
        @pl.when(jnp.logical_not(hosting.is_host))
        def _():
            at = own_ref.at[pl.ds(kept * SUBS, (slots - kept) * SUBS)]
            pltpu.make_async_remote_copy(
                src_ref=at, dst_ref=at, send_sem=guest_sem, recv_sem=guest_sem, device_id=grid.sibling,
                device_id_type=MESH,
            ).wait_send()


def gather_slots(own, cond_rows, info, slots, data_count, seq_count):
    side = math.isqrt(data_count // 2)
    images = data_count * SEGS
    plan = host_plan(slots, data_count * seq_count, seq_count)
    kept, steps = plan[2], plan[3]
    dma = pltpu.SemaphoreType.DMA
    sems = []
    for order in ORDERS:
        sizes = {"u": side - 1, "v": side - 1, "z": seq_count - 1}
        for axis in (order[2], order[1], order[0]):
            sems.append(dma((4, sizes[axis])))
            sems.append(dma((steps, sizes[axis])))
        sems.append(dma((4,)))
        sems.append(dma((steps,)))
        sems.append(dma((4,)))
        sems.append(dma((steps,)))
    vmem = pl.BlockSpec(memory_space=pltpu.VMEM)
    packed, modulation, held = pl.pallas_call(
        partial(gather_body, side, seq_count, plan, slots, images),
        out_shape=(
            jax.ShapeDtypeStruct((data_count, seq_count, kept * SUBS, LANES), jnp.bfloat16),
            jax.ShapeDtypeStruct((IMAGE_ROWS, LANES), jnp.float32),
            jax.ShapeDtypeStruct((condition_rows(slots), LANES), jnp.float32),
        ),
        in_specs=[vmem, vmem, pl.BlockSpec(memory_space=pltpu.SMEM)],
        out_specs=(pl.BlockSpec(memory_space=pl.ANY), vmem, vmem),
        scratch_shapes=[pltpu.VMEM((kept * SUBS, LANES), jnp.bfloat16), dma, dma]
        + sems
        + modulation_refs(side, seq_count, images, slots),
        compiler_params=pltpu.CompilerParams(
            collective_id=2, has_side_effects=True, vmem_limit_bytes=VMEM_LIMIT
        ),
        name="gather_slots",
    )(own, cond_rows, info)
    return packed.reshape(data_count * seq_count * kept * SUBS, LANES), modulation, held


def reduce_stream(grid, order, first_row, span, steps, parts_ref, out_ref, refs, hosting, passed):
    (own, rc, r1, r2, r3, outs, own_sem, out_sem, hand_sem, c_send, c_recv, s1, v1, s2, v2, s3, v3,
     c_credit, k1, k2, k3) = refs
    mine = grid.mine
    side = grid.side
    held = own.shape[0]
    mu, mv, mz = mine["u"], mine["v"], mine["z"]

    def rows(q):
        return pl.ds(pl.multiple_of(first_row + q * span, SUBS), span)

    def load(q, u, v):
        return pltpu.make_async_copy(
            parts_ref.at[grid.dp_of(u, v, grid.core), :, rows(q)], own.at[q % held, u, v], own_sem.at[q % held, u, v]
        )

    def give(q, u, v):
        return pltpu.make_async_remote_copy(
            src_ref=parts_ref.at[grid.dp_of(u, v, 1 - grid.core), :, rows(q)],
            dst_ref=rc.at[q % SLOTS, u, v],
            send_sem=c_send.at[q % SLOTS, u, v],
            recv_sem=c_recv.at[q % SLOTS, u, v],
            device_id=grid.sibling,
            device_id_type=MESH,
        )

    def block(q, stage, other):
        if stage == 0:
            return own.at[q % held, other]
        if order[1] == "v":
            return own.at[q % held, mu, other] if stage == 1 else own.at[q % held, mu, mv, other]
        return own.at[q % held, mu, :, other] if stage == 1 else own.at[q % held, mu, other, mz]

    landing = (r1, r2, r3)
    sends = (s1, s2, s3)
    arrivals = (v1, v2, v3)
    credits = (k1, k2, k3)

    def send(q, stage, k):
        axis = order[stage]
        other = grid.other(axis, k)
        seat = grid.seat(axis, other)
        return pltpu.make_async_remote_copy(
            src_ref=block(q, stage, other),
            dst_ref=landing[stage].at[q % SLOTS, seat],
            send_sem=sends[stage].at[q % SLOTS, k],
            recv_sem=arrivals[stage].at[q % SLOTS, seat],
            device_id=grid.device(axis, other),
            device_id_type=MESH,
        )

    def receive(q, stage, k):
        axis = order[stage]
        return pltpu.make_async_remote_copy(
            src_ref=block(q, stage, 0),
            dst_ref=landing[stage].at[q % SLOTS, k],
            send_sem=sends[stage].at[q % SLOTS, k],
            recv_sem=arrivals[stage].at[q % SLOTS, k],
            device_id=grid.device(axis, grid.other(axis, k)),
            device_id_type=MESH,
        )

    def keep(q):
        return pltpu.make_async_copy(outs.at[q % OUTS], out_ref.at[rows(q)], out_sem.at[q % OUTS])

    def hand_over(q):
        device, there, slot = hosting.guest((first_row + q * span) // SUBS)
        copy = pltpu.make_async_remote_copy(
            src_ref=outs.at[q % OUTS],
            dst_ref=out_ref.at[pl.ds(pl.multiple_of(slot * SUBS, SUBS), span)],
            send_sem=hand_sem.at[q % OUTS],
            recv_sem=passed,
            device_id=device,
            device_id_type=MESH,
        )
        return copy, there

    def write(q, action):
        if hosting is None:
            getattr(keep(q), action)()
            return

        @pl.when(jnp.logical_not(hosting.is_host))
        def _():
            getattr(keep(q), action)()

        copy, there = hand_over(q)

        @pl.when(hosting.is_host & there)
        def _():
            if action == "start":
                copy.start()
            else:
                copy.wait_send()

    def collect(q, stage):
        axis = order[stage]
        count = grid.sizes[axis] - 1
        for k in range(count):
            receive(q, stage, k).wait_recv()
        kept = block(q, stage, mine[axis])
        total = kept[...].astype(jnp.float32)
        for k in range(count):
            total = total + landing[stage][q % SLOTS, k].astype(jnp.float32)
        if stage < 2:
            kept[...] = total.astype(jnp.bfloat16)
        else:
            @pl.when(q >= OUTS)
            def _():
                write(q - OUTS, "wait")

            outs[q % OUTS] = total.astype(jnp.bfloat16)
            write(q, "start")
        for k in range(count):
            send(q, stage, k).wait_send()

        @pl.when(q + SLOTS < steps)
        def _():
            for k in range(count):
                pl.semaphore_signal(
                    credits[stage].at[mine[axis]], inc=1, device_id=grid.device(axis, grid.other(axis, k)),
                    device_id_type=MESH,
                )

    def launch(q, stage):
        axis = order[stage]
        count = grid.sizes[axis] - 1

        @pl.when(q >= SLOTS)
        def _():
            for k in range(count):
                pl.semaphore_wait(credits[stage].at[grid.other(axis, k)], 1)

        for k in range(count):
            send(q, stage, k).start()

    def begin(q):
        @pl.when(q >= SLOTS)
        def _():
            pl.semaphore_wait(c_credit, 1)

        for u in range(side):
            for v in range(side):
                give(q, u, v).start()
                load(q, u, v).start()

    def stage_c(q):
        for u in range(side):
            for v in range(side):
                load(q, u, v).wait()
                give(q, u, v).wait_recv()
                own[q % held, u, v] = (
                    own[q % held, u, v].astype(jnp.float32) + rc[q % SLOTS, u, v].astype(jnp.float32)
                ).astype(jnp.bfloat16)
        for u in range(side):
            for v in range(side):
                give(q, u, v).wait_send()

        @pl.when(q + SLOTS < steps)
        def _():
            pl.semaphore_signal(c_credit, inc=1, device_id=grid.sibling, device_id_type=MESH)

        launch(q, 0)

    def stage_one(q):
        collect(q, 0)
        launch(q, 1)

    def stage_two(q):
        collect(q, 1)
        launch(q, 2)

    def stage_three(q):
        collect(q, 2)

    return (begin, stage_c, stage_one, stage_two, stage_three), write


REDUCE_REFS = 21


MOD_BLOCKS = 6 * D // LANES
IMAGE_ROWS = SEGS * MOD_BLOCKS
SENT_ROWS = -(-IMAGE_ROWS // SUBS) * SUBS
COND_STRIDE = D // LANES + 1
COND_ROWS = SEGS * COND_STRIDE
FRONT = 56
MOD_STEPS = 31
FILL_STEPS = 8
PRODUCT_STEPS = 9


def held_depth(slots):
    depth = -(-(slots * SUBS + MOD_BLOCKS - 1) // MOD_BLOCKS)
    return -(-depth // 8) * 8


def condition_rows(slots):
    return -(-(D + 8 + max(held_depth(slots) + 32, 2 * LANES)) // LANES) * LANES


def spread_modulation(s, own_ref, info_ref, wide):
    rows = own_ref.shape[0]
    count = -(-rows // FILL_STEPS // SUBS) * SUBS

    @pl.when(s == 0)
    def _():
        wide[0:FRONT, :] = jnp.zeros((FRONT, LANES), jnp.float32)
        rest = wide.shape[0] - FRONT - rows
        wide[FRONT + rows :, :] = jnp.zeros((rest, LANES), jnp.float32)

    @pl.when(s < FILL_STEPS)
    def _():
        first = pl.multiple_of(jnp.minimum(s * count, rows - count), SUBS)
        at = first + lax.broadcasted_iota(jnp.int32, (count, LANES), 0)
        values = own_ref[pl.ds(first, count), :].astype(jnp.float32)
        wide[pl.ds(pl.multiple_of(FRONT + first, 8), count), :] = jnp.where(at < info_ref[2], values, 0.0)


def wide_rows(slots):
    return FRONT + MOD_BLOCKS * (held_depth(slots) + 1) + 8


def held_columns(wide, info_ref, depth, block):
    return wide[pl.ds(FRONT + block - info_ref[1], depth, stride=MOD_BLOCKS), :].astype(jnp.bfloat16)


def gather_blocks(grid, buffer, rows, sems):
    send_v, recv_v, send_u, recv_u, send_c, recv_c = sems
    mine = grid.mine
    side = grid.side

    def one(u, v, send, recv, device):
        at = buffer.at[pl.ds(pl.multiple_of(grid.dp_of(u, v, grid.core) * rows, 8), rows)]
        return pltpu.make_async_remote_copy(
            src_ref=at, dst_ref=at, send_sem=send, recv_sem=recv, device_id=device, device_id_type=MESH
        )

    def along(axis, k):
        return grid.device(axis, grid.other(axis, k)), grid.seat(axis, grid.other(axis, k))

    def v_copies():
        found = []
        for k in range(side - 1):
            device, seat = along("v", k)
            found.append(one(mine["u"], mine["v"], send_v.at[k], recv_v.at[seat], device))
        return found

    def u_copies():
        found = []
        for k in range(side - 1):
            device, seat = along("u", k)
            for v in range(side):
                found.append(one(mine["u"], v, send_u.at[k, v], recv_u.at[seat, v], device))
        return found

    def c_copies():
        return [
            one(u, v, send_c.at[u, v], recv_c.at[u, v], grid.sibling) for u in range(side) for v in range(side)
        ]

    def start():
        for copy in v_copies():
            copy.start()

    def second():
        for k in range(side - 1):
            one(mine["u"], mine["v"], send_v.at[k], recv_v.at[k], grid.sibling).wait_recv()
        for copy in v_copies():
            copy.wait_send()
        for copy in u_copies():
            copy.start()

    def third():
        for k in range(side - 1):
            for v in range(side):
                one(mine["u"], v, send_u.at[k, v], recv_u.at[k, v], grid.sibling).wait_recv()
        for copy in u_copies():
            copy.wait_send()
        for copy in c_copies():
            copy.start()

    def finish():
        for copy in c_copies():
            copy.wait_recv()
        for copy in c_copies():
            copy.wait_send()

    return start, second, third, finish


def gather_sems(side):
    dma = pltpu.SemaphoreType.DMA
    return [dma((side - 1,))] * 2 + [dma((side - 1, side))] * 2 + [dma((side, side))] * 2


def reduce_blocks(grid, buffer, rows, refs):
    from_c, from_u, from_v, from_z, send_c, recv_c, send_u, recv_u, send_v, recv_v, send_z, recv_z = refs
    mine = grid.mine
    side = grid.side
    depth = grid.sizes["z"]

    def block(u, v, core):
        return buffer.at[pl.ds(pl.multiple_of(grid.dp_of(u, v, core) * rows, 8), rows)]

    def copy(source, target, send, recv, device):
        return pltpu.make_async_remote_copy(
            src_ref=source, dst_ref=target, send_sem=send, recv_sem=recv, device_id=device, device_id_type=MESH
        )

    def along(axis, k):
        other = grid.other(axis, k)
        return other, grid.device(axis, other), grid.seat(axis, other)

    def c_copies():
        return [
            copy(block(u, v, 1 - grid.core), from_c.at[u, v], send_c.at[u, v], recv_c.at[u, v], grid.sibling)
            for u in range(side)
            for v in range(side)
        ]

    def u_copies():
        found = []
        for k in range(side - 1):
            other, device, seat = along("u", k)
            for v in range(side):
                found.append(
                    copy(block(other, v, grid.core), from_u.at[seat, v], send_u.at[k, v], recv_u.at[seat, v], device)
                )
        return found

    def v_copies():
        found = []
        for k in range(side - 1):
            other, device, seat = along("v", k)
            found.append(
                copy(block(mine["u"], other, grid.core), from_v.at[seat], send_v.at[k], recv_v.at[seat], device)
            )
        return found

    def z_copies():
        found = []
        for k in range(depth - 1):
            _, device, _ = along("z", k)
            found.append(
                copy(block(mine["u"], mine["v"], grid.core), from_z.at[mine["z"]], send_z.at[k],
                     recv_z.at[mine["z"]], device)
            )
        return found

    def start():
        for one in c_copies():
            one.start()

    def second():
        for one in c_copies():
            one.wait_recv()
        for one in c_copies():
            one.wait_send()
        for u in range(side):
            for v in range(side):
                at = block(u, v, grid.core)
                at[...] = at[...] + from_c[u, v]
        for one in u_copies():
            one.start()

    def third():
        for k in range(side - 1):
            for v in range(side):
                copy(from_u.at[k, v], from_u.at[k, v], send_u.at[k, v], recv_u.at[k, v], grid.sibling).wait_recv()
        for one in u_copies():
            one.wait_send()
        for v in range(side):
            at = block(mine["u"], v, grid.core)
            total = at[...]
            for k in range(side - 1):
                total = total + from_u[k, v]
            at[...] = total
        for one in v_copies():
            one.start()

    def fourth():
        for k in range(side - 1):
            copy(from_v.at[k], from_v.at[k], send_v.at[k], recv_v.at[k], grid.sibling).wait_recv()
        for one in v_copies():
            one.wait_send()
        at = block(mine["u"], mine["v"], grid.core)
        total = at[...]
        for k in range(side - 1):
            total = total + from_v[k]
        at[...] = total
        from_z[mine["z"]] = total
        for one in z_copies():
            one.start()

    def finish():
        for k in range(depth - 1):
            other = grid.other("z", k)
            copy(from_z.at[other], from_z.at[other], send_z.at[k], recv_z.at[other], grid.sibling).wait_recv()
        for one in z_copies():
            one.wait_send()
        total = from_z[0]
        for z in range(1, depth):
            total = total + from_z[z]
        return total

    return start, second, third, fourth, finish


def reduce_refs(side, depth, rows):
    dma = pltpu.SemaphoreType.DMA
    f32 = jnp.float32
    return [
        pltpu.VMEM((side, side, rows, LANES), f32),
        pltpu.VMEM((side - 1, side, rows, LANES), f32),
        pltpu.VMEM((side - 1, rows, LANES), f32),
        pltpu.VMEM((depth, rows, LANES), f32),
        dma((side, side)),
        dma((side, side)),
        dma((side - 1, side)),
        dma((side - 1, side)),
        dma((side - 1,)),
        dma((side - 1,)),
        dma((depth - 1,)),
        dma((depth,)),
    ]


def modulation_stages(grid, images, slots, own_ref, info_ref, cond_ref, mod_ref, held_ref, refs):
    everyone, wide, columns, parts, square = refs[:5]
    gather = gather_blocks(grid, everyone, COND_ROWS, refs[5:11])
    reduce = reduce_blocks(grid, parts, IMAGE_ROWS, refs[11:23])
    here = grid.place
    depth = held_depth(slots)

    def run(s):
        spread_modulation(s, own_ref, info_ref, wide)

        @pl.when(s == 0)
        def _():
            everyone[pl.ds(pl.multiple_of(here * COND_ROWS, 8), COND_ROWS), :] = cond_ref[...]
            gather[0]()
            square[...] = jnp.zeros_like(square)
            held_ref[...] = jnp.zeros_like(held_ref)

        @pl.when(s == 2)
        def _():
            gather[1]()

        @pl.when(s == 4)
        def _():
            gather[2]()

        @pl.when(s == 7)
        def _():
            gather[3]()

        @pl.when(s == 8)
        def _():
            for block in range(D // LANES):
                square[0:images, :] = everyone[pl.ds(block, images, stride=COND_STRIDE), :]
                held_ref[block * LANES : (block + 1) * LANES, :] = square[...].T
            held_ref[D : D + 8, :] = (lax.broadcasted_iota(jnp.int32, (8, LANES), 0) == 0).astype(jnp.float32)
            for part in range(columns.shape[1] // LANES):
                columns[:, part * LANES : (part + 1) * LANES] = (
                    held_ref[pl.ds(info_ref[0] + part * LANES, LANES), :].T.astype(jnp.bfloat16)
                )

        at_product = s - 9

        @pl.when((at_product >= 0) & (at_product < PRODUCT_STEPS))
        def _():
            left = columns[0:images, 0:depth]
            each = MOD_BLOCKS // 2 // PRODUCT_STEPS
            for pair in range(each):
                block = (at_product * each + pair) * 2
                right = jnp.concatenate(
                    [held_columns(wide, info_ref, depth, block), held_columns(wide, info_ref, depth, block + 1)],
                    axis=1,
                )
                found = jnp.dot(left, right, preferred_element_type=jnp.float32)
                parts[pl.ds(block, images, stride=MOD_BLOCKS), :] = found[:, :LANES]
                parts[pl.ds(block + 1, images, stride=MOD_BLOCKS), :] = found[:, LANES:]

        @pl.when(s == 18)
        def _():
            reduce[0]()

        for at, stage in ((20, 1), (23, 2), (26, 3)):
            @pl.when(s == at)
            def _(stage=stage):
                reduce[stage]()

        @pl.when(s == 29)
        def _():
            mod_ref[...] = reduce[4]()

    return run


def modulation_refs(side, depth, images, slots):
    data_count = side * side * 2
    lanes = -(-held_depth(slots) // LANES) * LANES
    f32 = jnp.float32
    return (
        [
            pltpu.VMEM((data_count * COND_ROWS, LANES), f32),
            pltpu.VMEM((wide_rows(slots), LANES), f32),
            pltpu.VMEM((LANES, lanes), jnp.bfloat16),
            pltpu.VMEM((data_count * IMAGE_ROWS, LANES), f32),
            pltpu.VMEM((LANES, LANES), f32),
        ]
        + gather_sems(side)
        + reduce_refs(side, depth, IMAGE_ROWS)
    )


def modulation_grad_stages(grid, images, slots, own_ref, info_ref, part_ref, all_ref, cond_ref, refs):
    arrived, summed, wide, around, parts, send_z, recv_z, done_sem = refs[:8]
    gather = gather_blocks(grid, summed, IMAGE_ROWS, refs[8:14])
    reduce = reduce_blocks(grid, parts, COND_ROWS, refs[14:26])
    mine = grid.mine
    sizes = grid.sizes["z"]
    here = pl.ds(pl.multiple_of(grid.place * IMAGE_ROWS, 8), IMAGE_ROWS)
    depth = held_depth(slots)

    def to_z(k):
        return pltpu.make_async_remote_copy(
            src_ref=part_ref, dst_ref=arrived.at[mine["z"]], send_sem=send_z.at[k], recv_sem=recv_z.at[mine["z"]],
            device_id=grid.device("z", grid.other("z", k)), device_id_type=MESH,
        )

    def run(s):
        spread_modulation(s, own_ref, info_ref, wide)

        @pl.when(s == 0)
        def _():
            for k in range(sizes - 1):
                to_z(k).start()
            arrived[mine["z"]] = part_ref[...]
            around[...] = jnp.zeros_like(around)
            parts[...] = jnp.zeros_like(parts)

        @pl.when(s == 2)
        def _():
            for k in range(sizes - 1):
                other = grid.other("z", k)
                pltpu.make_async_remote_copy(
                    src_ref=part_ref, dst_ref=arrived.at[other], send_sem=send_z.at[k], recv_sem=recv_z.at[other],
                    device_id=grid.sibling, device_id_type=MESH,
                ).wait_recv()
            for k in range(sizes - 1):
                to_z(k).wait_send()
            total = arrived[0].astype(jnp.float32)
            for z in range(1, sizes):
                total = total + arrived[z].astype(jnp.float32)
            summed[here, :] = total.astype(jnp.bfloat16).astype(jnp.float32)[:IMAGE_ROWS]
            gather[0]()

        @pl.when(s == 4)
        def _():
            gather[1]()

        @pl.when(s == 6)
        def _():
            gather[2]()

        @pl.when(s == 9)
        def _():
            gather[3]()
            pltpu.make_async_copy(summed, all_ref, done_sem).start()

        at_product = s - 10

        @pl.when((at_product >= 0) & (at_product < PRODUCT_STEPS))
        def _():
            total = around[D + 8 : D + 8 + depth, 0:images]
            each = MOD_BLOCKS // 2 // PRODUCT_STEPS
            for pair in range(each):
                block = (at_product * each + pair) * 2
                left = jnp.concatenate(
                    [held_columns(wide, info_ref, depth, block), held_columns(wide, info_ref, depth, block + 1)],
                    axis=1,
                )
                right = jnp.concatenate(
                    [
                        summed[pl.ds(block + more, images, stride=MOD_BLOCKS), :].astype(jnp.bfloat16)
                        for more in (0, 1)
                    ],
                    axis=1,
                )
                total = total + lax.dot_general(
                    left, right, (((1,), (1,)), ((), ())), preferred_element_type=jnp.float32
                )
            around[D + 8 : D + 8 + depth, 0:images] = total

        @pl.when(s == 19)
        def _():
            for block in range(D // LANES):
                piece = around[pl.ds(D + 8 - info_ref[0] + block * LANES, LANES), :].T
                parts[pl.ds(block, images, stride=COND_STRIDE), :] = piece[0:images, :]
            reduce[0]()

        for at, stage in ((21, 1), (24, 2), (27, 3)):
            @pl.when(s == at)
            def _(stage=stage):
                reduce[stage]()

        @pl.when(s == 30)
        def _():
            cond_ref[...] = reduce[4]()
            pltpu.make_async_copy(summed, all_ref, done_sem).wait()

    return run


MOD_GRAD_REFS = 26


def modulation_grad_refs(side, depth, images, slots):
    data_count = side * side * 2
    dma = pltpu.SemaphoreType.DMA
    f32 = jnp.float32
    return (
        [
            pltpu.VMEM((depth, SENT_ROWS, LANES), jnp.bfloat16),
            pltpu.VMEM((data_count * IMAGE_ROWS, LANES), f32),
            pltpu.VMEM((wide_rows(slots), LANES), f32),
            pltpu.VMEM((2 * (D + 8) + held_depth(slots), LANES), f32),
            pltpu.VMEM((data_count * COND_ROWS, LANES), f32),
            dma((depth - 1,)),
            dma((depth,)),
            dma,
        ]
        + gather_sems(side)
        + reduce_refs(side, depth, COND_ROWS)
    )


def reduce_body(side, depth, plan, slots, parts_ref, part_ref, own_ref, info_ref, out_ref, all_ref, cond_ref,
                *refs):
    hosts, share, kept, steps, parts = plan
    grid = Grid(side, depth)
    hosting = Hosting(grid, 2 * side * side * depth, hosts, share, kept, slots - kept) if hosts else None
    grid.greet(hosting)
    passed = refs[-1]
    modulation_step = modulation_grad_stages(
        grid, 2 * side * side * SEGS, slots, own_ref, info_ref, part_ref, all_ref, cond_ref, refs[:MOD_GRAD_REFS]
    )
    refs = refs[MOD_GRAD_REFS:]
    streams = []
    writes = []
    first = 0
    for number, (order, part) in enumerate(zip(ORDERS, parts)):
        span = part * SUBS
        stages, write = reduce_stream(
            grid, order, first, span, steps, parts_ref, out_ref,
            refs[REDUCE_REFS * number : REDUCE_REFS * (number + 1)], hosting, passed,
        )
        streams.append(stages)
        writes.append(write)
        first = first + steps * span

    def round_trip(s, carry):
        for late in range(4, -1, -1):
            q = s - LAG * late

            @pl.when((q >= 0) & (q < steps))
            def _(late=late, q=q):
                for stream in streams:
                    stream[late](q)

        modulation_step(s)
        return carry

    lax.fori_loop(0, max(steps + 4 * LAG, MOD_STEPS), round_trip, 0)
    for write in writes:
        for q in range(max(steps - OUTS, 0), steps):
            write(q, "wait")
    if hosting is not None:
        @pl.when(jnp.logical_not(hosting.is_host))
        def _():
            at = out_ref.at[pl.ds(kept * SUBS, (slots - kept) * SUBS)]
            pltpu.make_async_remote_copy(
                src_ref=at, dst_ref=at, send_sem=passed, recv_sem=passed, device_id=grid.sibling,
                device_id_type=MESH,
            ).wait_recv()


def reduce_slots(grads, mod_part, own, info, slots, data_count, seq_count):
    side = math.isqrt(data_count // 2)
    plan = host_plan(slots, data_count * seq_count, seq_count)
    kept, parts = plan[2], plan[4]
    held = HELD
    dma = pltpu.SemaphoreType.DMA
    regular = pltpu.SemaphoreType.REGULAR
    bf16 = jnp.bfloat16
    f32 = jnp.float32
    scratch = modulation_grad_refs(side, seq_count, data_count * SEGS, slots)
    for order, part in zip(ORDERS, parts):
        span = part * SUBS
        sizes = {"u": side, "v": side, "z": seq_count}
        left = dict(sizes)
        scratch.append(pltpu.VMEM((held, side, side, seq_count, span, LANES), bf16))
        scratch.append(pltpu.VMEM((SLOTS, side, side, seq_count, span, LANES), bf16))
        for axis in order:
            del left[axis]
            rest = tuple(left[name] for name in ("u", "v", "z") if name in left)
            scratch.append(pltpu.VMEM((SLOTS, sizes[axis] - 1) + rest + (span, LANES), bf16))
        scratch.append(pltpu.VMEM((OUTS, span, LANES), bf16))
        scratch.append(dma((held, side, side)))
        scratch.append(dma((OUTS,)))
        scratch.append(dma((OUTS,)))
        scratch.append(dma((SLOTS, side, side)))
        scratch.append(dma((SLOTS, side, side)))
        for axis in order:
            scratch.append(dma((SLOTS, sizes[axis] - 1)))
            scratch.append(dma((SLOTS, sizes[axis] - 1)))
        scratch.append(regular)
        for axis in order:
            scratch.append(regular((sizes[axis],)))
    scratch.append(dma)
    return pl.pallas_call(
        partial(reduce_body, side, seq_count, plan, slots),
        out_shape=(
            jax.ShapeDtypeStruct((slots * SUBS, LANES), bf16),
            jax.ShapeDtypeStruct((data_count * IMAGE_ROWS, LANES), f32),
            jax.ShapeDtypeStruct((COND_ROWS, LANES), f32),
        ),
        in_specs=[
            pl.BlockSpec(memory_space=pl.ANY),
            pl.BlockSpec(memory_space=pltpu.VMEM),
            pl.BlockSpec(memory_space=pltpu.VMEM),
            pl.BlockSpec(memory_space=pltpu.SMEM),
        ],
        out_specs=(
            pl.BlockSpec(memory_space=pl.ANY),
            pl.BlockSpec(memory_space=pl.ANY),
            pl.BlockSpec(memory_space=pltpu.VMEM),
        ),
        scratch_shapes=scratch,
        compiler_params=pltpu.CompilerParams(
            collective_id=1, has_side_effects=True, vmem_limit_bytes=VMEM_LIMIT
        ),
        name="reduce_slots",
    )(grads.reshape(data_count, seq_count, kept * SUBS, LANES), mod_part, own, info)


UPDATE_TILES = 72


def update_body(mod_depth, own_ref, reduced, cond_ref, mod_ref, master, first, second,
                new_master, new_first, new_second, mod_rows, wide):
    step = pl.program_id(0)
    mod_blocks = 6 * D // LANES
    start_row = own_ref[0] * SUBS
    shift = lax.rem(start_row, mod_blocks)
    tiles = UPDATE_TILES
    piece = 9

    @pl.when((step == 0) & (start_row < MOD_ROWS))
    def _():
        images = cond_ref.shape[1]
        for begin in range(0, mod_blocks, piece):
            grads = [
                mod_ref[pl.ds(begin + block, images, stride=mod_blocks), :].astype(jnp.bfloat16)
                for block in range(piece)
            ]
            part = jnp.dot(
                cond_ref[...], jnp.concatenate(grads, axis=1), preferred_element_type=jnp.float32
            )
            for block in range(piece):
                mod_rows[pl.ds(begin + block, mod_depth, stride=mod_blocks), :] = part[
                    :, block * LANES : (block + 1) * LANES
                ]

    wide[...] = reduced[...].astype(jnp.float32)
    corr_one = 1.0 - beta_one**STEP
    corr_two = 1.0 - beta_two**STEP
    local = step * tiles + lax.broadcasted_iota(jnp.int32, (tiles, LANES), 0)
    used = local < own_ref[1]
    for sub in range(SUBS):
        columns = pl.ds(sub * LANES, LANES)
        from_mod = mod_rows[pl.ds(shift + step * tiles * SUBS + sub, tiles, stride=SUBS), :]
        is_mod = start_row + local * SUBS + sub < MOD_ROWS
        grad = jnp.where(is_mod, from_mod, wide[pl.ds(sub, tiles, stride=SUBS), :])
        grad = jnp.where(used, grad, 0.0)
        one = beta_one * first[:, columns] + (1.0 - beta_one) * grad
        two = beta_two * second[:, columns] + (1.0 - beta_two) * grad * grad
        held = master[:, columns]
        new_first[:, columns] = one
        new_second[:, columns] = two
        new_master[:, columns] = held - learn_rate * (
            one / corr_one / (jnp.sqrt(two / corr_two) + adam_eps) + weight_decay * held
        )


def own_conditions(held, info, images, slots):
    steps = -(-slots // UPDATE_TILES)
    depth = -(-(steps * UPDATE_TILES * SUBS + MOD_BLOCKS) // MOD_BLOCKS)
    depth = -(-depth // 8) * 8
    return lax.dynamic_slice(held, (info[0], jnp.int32(0)), (depth, images)).astype(jnp.bfloat16)


def update(reduced, cond_own, mod_all, own_first, master, first, second):
    slots, tile_len = master.shape
    mod_depth, images = cond_own.shape
    tiles = UPDATE_TILES
    steps = -(-slots // tiles)
    wide_block = pl.BlockSpec((tiles, tile_len), lambda i, *_: (i, 0))
    return pl.pallas_call(
        partial(update_body, mod_depth),
        out_shape=(jax.ShapeDtypeStruct(master.shape, jnp.float32),) * 3,
        grid_spec=pltpu.PrefetchScalarGridSpec(
            num_scalar_prefetch=1,
            grid=(steps,),
            in_specs=[
                pl.BlockSpec((tiles * SUBS, LANES), lambda i, *_: (i, 0)),
                pl.BlockSpec((mod_depth, images), lambda i, *_: (0, 0)),
                pl.BlockSpec(mod_all.shape, lambda i, *_: (0, 0)),
                wide_block,
                wide_block,
                wide_block,
            ],
            out_specs=(wide_block,) * 3,
            scratch_shapes=[
                pltpu.VMEM((mod_depth * MOD_BLOCKS, LANES), jnp.float32),
                pltpu.VMEM((tiles * SUBS, LANES), jnp.float32),
            ],
        ),
        compiler_params=pltpu.CompilerParams(vmem_limit_bytes=VMEM_LIMIT),
        name="update",
    )(own_first, reduced, cond_own, mod_all, master, first, second)


def normalize(values):
    centred = values - jnp.mean(values, axis=-1, keepdims=True)
    spread = jnp.mean(centred * centred, axis=-1, keepdims=True)
    return centred * lax.rsqrt(spread + ln_eps)


def cosine_of(target, projected):
    inner_mean = jnp.mean(projected * target, axis=-1)
    return (
        inner_mean
        * lax.rsqrt(jnp.mean(projected * projected, axis=-1) + cos_eps)
        * lax.rsqrt(jnp.mean(target * target, axis=-1) + cos_eps)
    )


def gelu_tanh(values):
    return jax.nn.gelu(values, approximate=True)


def lane_pad(width):
    return -(-width // LANES) * LANES


def regroup_body(moves, fill, x_ref, out_ref):
    if fill is not None:
        start, width = fill
        for group in range(out_ref.shape[0]):
            out_ref[group, :, start : start + width] = jnp.zeros((out_ref.shape[1], width), out_ref.dtype)
    for from_group, start, to_group, target, width in moves:
        if from_group is None:
            values = x_ref[:, start : start + width]
        else:
            values = x_ref[from_group, :, start : start + width]
        if to_group is None:
            out_ref[:, target : target + width] = values
        else:
            out_ref[to_group, :, target : target + width] = values


def split_groups(x, parts, groups):
    tokens, total = x.shape
    width = total // parts // groups
    padded = lane_pad(parts * width)
    moves = [
        (None, (part * groups + group) * width, group, part * width, width)
        for group in range(groups)
        for part in range(parts)
    ]
    fill = (parts * width, padded - parts * width) if padded > parts * width else None
    return pl.pallas_call(
        partial(regroup_body, moves, fill),
        out_shape=jax.ShapeDtypeStruct((groups, tokens, padded), x.dtype),
        compiler_params=pltpu.CompilerParams(vmem_limit_bytes=VMEM_LIMIT),
        name="split_groups_%d" % parts,
    )(x)


def join_groups(x, parts, width):
    groups, tokens, _ = x.shape
    moves = [
        (group, part * width, None, (part * groups + group) * width, width)
        for group in range(groups)
        for part in range(parts)
    ]
    return pl.pallas_call(
        partial(regroup_body, moves, None),
        out_shape=jax.ShapeDtypeStruct((tokens, parts * groups * width), x.dtype),
        compiler_params=pltpu.CompilerParams(vmem_limit_bytes=VMEM_LIMIT),
        name="join_groups_%d" % parts,
    )(x)


QUERY_BLOCK = 256


def key_bias(seg_col, pad_col, seg_row, first):
    keys = seg_col.shape[0]
    queries = seg_row.shape[1]
    key_at = lax.broadcasted_iota(jnp.int32, (keys, queries), 0)
    query_at = first + lax.broadcasted_iota(jnp.int32, (keys, queries), 1)
    allowed = (seg_col == seg_row) & ((pad_col == 1) | (key_at == query_at))
    return jnp.where(allowed, 0.0, -1e30)


def spread_heads(rows_ref, held, heads):
    held[...] = jnp.zeros_like(held)
    for part in range(held.shape[0]):
        for head in range(heads):
            start = (part * heads + head) * HEAD_DIM
            held[part, head, :, 0:HEAD_DIM] = rows_ref[:, start : start + HEAD_DIM]


def probabilities(held, head, block, bias):
    scores = lax.dot_general(
        held[1, head], held[0, head, block, :], (((1,), (1,)), ((), ())), preferred_element_type=jnp.float32
    )
    scores = scores + bias
    shifted = jnp.exp2((scores - jnp.max(scores, axis=0, keepdims=True)) * (HEAD_DIM ** (-0.5) * math.log2(math.e)))
    return shifted * (1.0 / jnp.sum(shifted, axis=0, keepdims=True))


def attention_body(heads, rows_ref, seg_col, pad_col, seg_row, out_ref, held):
    step = pl.program_id(0)

    @pl.when(step == 0)
    def _():
        spread_heads(rows_ref, held, heads)

    first = pl.multiple_of(step * QUERY_BLOCK, QUERY_BLOCK)
    block = pl.ds(first, QUERY_BLOCK)
    bias = key_bias(seg_col[...], pad_col[...], seg_row[...], first)
    rest = out_ref.shape[1] - heads * HEAD_DIM
    if rest:
        out_ref[:, heads * HEAD_DIM :] = jnp.zeros((QUERY_BLOCK, rest), jnp.bfloat16)
    for head in range(heads):
        probs = probabilities(held, head, block, bias).astype(jnp.bfloat16)
        result = lax.dot_general(
            held[2, head], probs, (((0,), (0,)), ((), ())), preferred_element_type=jnp.float32
        )
        out_ref[:, head * HEAD_DIM : (head + 1) * HEAD_DIM] = result.T[:, :HEAD_DIM].astype(jnp.bfloat16)


def attention(rows, segments, padding, heads):
    length = rows.shape[0]
    whole = pl.BlockSpec((length, 1), lambda i: (0, 0))
    return pl.pallas_call(
        partial(attention_body, heads),
        out_shape=jax.ShapeDtypeStruct((length, lane_pad(heads * HEAD_DIM)), jnp.bfloat16),
        grid=(length // QUERY_BLOCK,),
        in_specs=[
            pl.BlockSpec(rows.shape, lambda i: (0, 0)),
            whole,
            whole,
            pl.BlockSpec((1, QUERY_BLOCK), lambda i: (0, i)),
        ],
        out_specs=pl.BlockSpec((QUERY_BLOCK, lane_pad(heads * HEAD_DIM)), lambda i: (i, 0)),
        scratch_shapes=[pltpu.VMEM((3, heads, length, LANES), jnp.bfloat16)],
        compiler_params=pltpu.CompilerParams(vmem_limit_bytes=VMEM_LIMIT),
        name="attention",
    )(rows, segments.reshape(length, 1), padding.reshape(length, 1), segments.reshape(1, length))


def attention_grad_body(heads, rows_ref, grad_ref, seg_col, pad_col, seg_row, out_ref, held, given, grad_k, grad_v):
    step = pl.program_id(0)
    scaling = HEAD_DIM ** (-0.5)

    @pl.when(step == 0)
    def _():
        spread_heads(rows_ref, held, heads)
        given[...] = jnp.zeros_like(given)
        grad_k[...] = jnp.zeros_like(grad_k)
        grad_v[...] = jnp.zeros_like(grad_v)
        out_ref[...] = jnp.zeros_like(out_ref)

    first = pl.multiple_of(step * QUERY_BLOCK, QUERY_BLOCK)
    block = pl.ds(first, QUERY_BLOCK)
    bias = key_bias(seg_col[...], pad_col[...], seg_row[...], first)
    for head in range(heads):
        given[:, 0:HEAD_DIM] = grad_ref[:, head * HEAD_DIM : (head + 1) * HEAD_DIM]
        upstream = given[...]
        probs = probabilities(held, head, block, bias)
        grad_v[head] += jnp.dot(probs.astype(jnp.bfloat16), upstream, preferred_element_type=jnp.float32)
        grad_probs = lax.dot_general(
            held[2, head], upstream, (((1,), (1,)), ((), ())), preferred_element_type=jnp.float32
        )
        inner = jnp.sum(probs * grad_probs, axis=0, keepdims=True)
        grad_scores = (probs * (grad_probs - inner)).astype(jnp.bfloat16)
        grad_k[head] += jnp.dot(grad_scores, held[0, head, block, :], preferred_element_type=jnp.float32)
        grad_q = lax.dot_general(
            held[1, head], grad_scores, (((0,), (0,)), ((), ())), preferred_element_type=jnp.float32
        )
        out_ref[block, head * HEAD_DIM : (head + 1) * HEAD_DIM] = (
            grad_q.T[:, :HEAD_DIM] * scaling
        ).astype(jnp.bfloat16)

    @pl.when(step == pl.num_programs(0) - 1)
    def _():
        for head in range(heads):
            start = (heads + head) * HEAD_DIM
            out_ref[:, start : start + HEAD_DIM] = (grad_k[head][:, :HEAD_DIM] * scaling).astype(jnp.bfloat16)
            start = (2 * heads + head) * HEAD_DIM
            out_ref[:, start : start + HEAD_DIM] = grad_v[head][:, :HEAD_DIM].astype(jnp.bfloat16)


def attention_grad(rows, grad, segments, padding, heads):
    length = rows.shape[0]
    whole = pl.BlockSpec((length, 1), lambda i: (0, 0))
    return pl.pallas_call(
        partial(attention_grad_body, heads),
        out_shape=jax.ShapeDtypeStruct(rows.shape, jnp.bfloat16),
        grid=(length // QUERY_BLOCK,),
        in_specs=[
            pl.BlockSpec(rows.shape, lambda i: (0, 0)),
            pl.BlockSpec((QUERY_BLOCK, grad.shape[1]), lambda i: (i, 0)),
            whole,
            whole,
            pl.BlockSpec((1, QUERY_BLOCK), lambda i: (0, i)),
        ],
        out_specs=pl.BlockSpec(rows.shape, lambda i: (0, 0)),
        scratch_shapes=[
            pltpu.VMEM((3, heads, length, LANES), jnp.bfloat16),
            pltpu.VMEM((QUERY_BLOCK, LANES), jnp.bfloat16),
            pltpu.VMEM((heads, length, LANES), jnp.float32),
            pltpu.VMEM((heads, length, LANES), jnp.float32),
        ],
        compiler_params=pltpu.CompilerParams(vmem_limit_bytes=VMEM_LIMIT),
        name="attention_grad",
    )(rows, grad, segments.reshape(length, 1), padding.reshape(length, 1), segments.reshape(1, length))


def shards(
    tokens,
    conditions,
    segment_ids,
    padding,
    targets,
    cotangent,
    tile_counts,
    master,
    first_moment,
    second_moment,
):
    seq_count = lax.axis_size("seq")
    data_count = lax.axis_size("dp")
    seq_place = lax.axis_index("seq")
    data_place = lax.axis_index("dp")
    owners = data_count * seq_count
    slot_count, tile_len = master.shape
    own_rows = slot_count * SUBS
    tile_ends = jnp.cumsum(tile_counts)
    starts = jnp.concatenate([jnp.zeros((1,), jnp.int32), tile_ends.astype(jnp.int32)])
    spans = jnp.asarray(chunk_spans()[0], jnp.int32)
    firsts = jnp.sum((tile_ends[None, :] <= spans[:, :1]).astype(jnp.int32), axis=1)
    lasts = jnp.sum((tile_ends[None, :] <= spans[:, 1:]).astype(jnp.int32), axis=1)
    plan = host_plan(slot_count, owners, seq_count)
    guests = jnp.asarray(
        guest_places((*plan[:3], slot_count - plan[2]), owners, seq_count), jnp.int32
    )
    edge_ids = jnp.asarray(EDGE_TILES, jnp.int32)
    edge_owner = jnp.sum((tile_ends[None, :] <= edge_ids[:, None]).astype(jnp.int32), axis=1)
    edge_within = edge_ids - jnp.take(starts, edge_owner)
    edge_places = edge_owner * plan[2] + edge_within
    if plan[0]:
        edge_places = jnp.where(
            edge_within < plan[2], edge_places, jnp.take(guests, edge_owner) + edge_within - plan[2]
        )
    own_place = data_place * seq_count + seq_place
    own_start = lax.dynamic_index_in_dim(starts, own_place, 0, False)
    own_count = lax.dynamic_index_in_dim(tile_counts, own_place, 0, False)
    own_low = master.astype(jnp.bfloat16).reshape(own_rows, LANES)
    info = jnp.stack(
        [
            jnp.minimum(own_start * SUBS // MOD_BLOCKS, D + 1),
            own_start * SUBS % MOD_BLOCKS,
            jnp.clip(jnp.minimum(own_count * SUBS, MOD_ROWS - own_start * SUBS), 0, own_rows),
        ]
    ).astype(jnp.int32)
    images = data_count * SEGS

    own_first = jnp.stack([own_start, own_count])
    cond_f = conditions.astype(jnp.float32)
    cond_act, silu_cond_back = jax.vjp(jax.nn.silu, cond_f)
    cond_low = cond_act.astype(jnp.bfloat16)
    cond_rows = jnp.pad(cond_low[0].astype(jnp.float32), ((0, 0), (0, LANES))).reshape(COND_ROWS, LANES)
    packed, modulation, cond_held = gather_slots(own_low, cond_rows, info, slot_count, data_count, seq_count)
    modulation = modulation.reshape(1, SEGS, 6 * D)
    weights = {
        index: unpack_weight(index, packed, plan, firsts, lasts, starts, guests)
        for index in (2, 5, 7, 9, 11)
    }
    attend_weight, output_weight, hidden_weight, return_weight, proj_one = (
        weights[index] for index in (2, 5, 7, 9, 11)
    )
    edges = edge_read(packed, edge_places)
    edge_flat = edges.reshape(-1)

    def bias(index):
        row = param_rows()[index]
        at = EDGE_TILES.index(row // SUBS) * SUBS + row % SUBS
        return edge_flat[at * LANES : at * LANES + param_shapes()[index][0]]

    query_bias, value_bias, output_bias, hidden_bias, return_bias = (bias(i) for i in (3, 4, 6, 8, 10))
    proj_bias_one, proj_bias_two, proj_bias_three = (bias(i) for i in (12, 14, 16))
    rows_dev, local_len, model_width = tokens.shape
    full_len = segment_ids.shape[1]
    heads_local = HEADS // seq_count
    group_width = model_width // seq_count
    token_start = seq_place * local_len
    local_seg = lax.dynamic_slice_in_dim(segment_ids, token_start, local_len, 1)
    local_pad = lax.dynamic_slice_in_dim(padding, token_start, local_len, 1).astype(jnp.float32)
    onehot = (local_seg[:, :, None] == jnp.arange(SEGS, dtype=jnp.int32)).astype(jnp.float32)
    per_token = jnp.einsum("rts,rsc->rtc", onehot, modulation, precision=lax.Precision.HIGH)
    shift_one, scale_one, gate_one, shift_two, scale_two, gate_two = jnp.split(
        per_token, 6, axis=-1
    )
    token_f = tokens.astype(jnp.float32)
    normed_one, norm_back_one = jax.vjp(normalize, token_f)
    attend_in = (normed_one * (1.0 + scale_one) + shift_one).astype(jnp.bfloat16)
    triple_bias = jnp.concatenate([query_bias, jnp.zeros_like(query_bias), value_bias])
    triple = (
        jnp.einsum("rtd,dc->rtc", attend_in, attend_weight, preferred_element_type=jnp.float32)
        + triple_bias
    )
    triple_low = split_groups(triple[0].astype(jnp.bfloat16), 3, seq_count)
    head_rows = lax.all_to_all(triple_low, "seq", split_axis=0, concat_axis=0, tiled=True)
    (head_rows, output_weight, hidden_weight, return_weight, proj_one) = lax.optimization_barrier(
        (head_rows, output_weight, hidden_weight, return_weight, proj_one)
    )
    head_rows = head_rows.reshape(full_len, head_rows.shape[-1])
    head_attended = attention(head_rows, segment_ids[0], padding[0], heads_local)
    head_attended = head_attended.reshape(seq_count, local_len, head_attended.shape[-1])
    head_attended, packed = lax.optimization_barrier((head_attended, packed))
    proj_two, proj_three = (unpack_weight(index, packed, plan, firsts, lasts, starts, guests) for index in (13, 15))
    attended = lax.all_to_all(head_attended, "seq", split_axis=0, concat_axis=0, tiled=True)
    attended, proj_two, proj_three = lax.optimization_barrier((attended, proj_two, proj_three))
    attended = join_groups(attended, 1, group_width)[None]
    branch_one = (
        jnp.einsum("rtd,dc->rtc", attended, output_weight, preferred_element_type=jnp.float32)
        + output_bias
    )
    middle = token_f + gate_one * branch_one
    normed_two, norm_back_two = jax.vjp(normalize, middle)
    mlp_in = (normed_two * (1.0 + scale_two) + shift_two).astype(jnp.bfloat16)
    hidden = (
        jnp.einsum("rtd,df->rtf", mlp_in, hidden_weight, preferred_element_type=jnp.float32)
        + hidden_bias
    )
    activated_f, gelu_back = jax.vjp(gelu_tanh, hidden)
    activated = activated_f.astype(jnp.bfloat16)
    branch_two = (
        jnp.einsum("rtf,fd->rtd", activated, return_weight, preferred_element_type=jnp.float32)
        + return_bias
    )
    result = middle + gate_two * branch_two
    feature = result.astype(jnp.bfloat16)
    first_pre = (
        jnp.einsum("rtd,dp->rtp", feature, proj_one, preferred_element_type=jnp.float32)
        + proj_bias_one
    )
    first_act, first_back = jax.vjp(jax.nn.silu, first_pre)
    first_low = first_act.astype(jnp.bfloat16)
    second_pre = (
        jnp.einsum("rtp,pc->rtc", first_low, proj_two, preferred_element_type=jnp.float32)
        + proj_bias_two
    )
    second_act, second_back = jax.vjp(jax.nn.silu, second_pre)
    second_low = second_act.astype(jnp.bfloat16)
    projected = (
        jnp.einsum("rtc,co->rto", second_low, proj_three, preferred_element_type=jnp.float32)
        + proj_bias_three
    )
    target_f = targets.astype(jnp.float32)
    cosine, cosine_back = jax.vjp(partial(cosine_of, target_f), projected)
    ends = {}

    def put(buffer, index, left, right):
        buffer, ends[index] = weight_grad(
            index,
            left.reshape(-1, left.shape[-1]),
            right.reshape(-1, right.shape[-1]),
            buffer,
            owners,
            slot_count,
            firsts,
            lasts,
            starts,
            guests,
            (plan[0], plan[2]),
        )
        return buffer

    def summed(grad):
        return jnp.sum(grad.astype(jnp.float32), axis=(0, 1))

    (grad_projected,) = cosine_back(local_pad * -repa_weight)
    grad_projected = grad_projected.astype(jnp.bfloat16)
    sum_sixteen = summed(grad_projected)
    (grad_second,) = second_back(
        jnp.einsum("rto,co->rtc", grad_projected, proj_three, preferred_element_type=jnp.float32)
    )
    grad_second = grad_second.astype(jnp.bfloat16)
    sum_fourteen = summed(grad_second)
    (grad_first,) = first_back(
        jnp.einsum("rtc,pc->rtp", grad_second, proj_two, preferred_element_type=jnp.float32)
    )
    grad_first = grad_first.astype(jnp.bfloat16)
    sum_twelve = summed(grad_first)
    grad_result = cotangent + jnp.einsum(
        "rtp,dp->rtd", grad_first, proj_one, preferred_element_type=jnp.float32
    )
    grad_gate_two = grad_result * branch_two
    grad_branch_two = (grad_result * gate_two).astype(jnp.bfloat16)
    sum_ten = summed(grad_branch_two)
    (grad_hidden,) = gelu_back(
        jnp.einsum(
            "rtd,fd->rtf", grad_branch_two, return_weight, preferred_element_type=jnp.float32
        )
    )
    grad_hidden = grad_hidden.astype(jnp.bfloat16)
    sum_eight = summed(grad_hidden)
    grad_mlp_in = jnp.einsum(
        "rtf,df->rtd", grad_hidden, hidden_weight, preferred_element_type=jnp.float32
    )
    grad_scale_two = grad_mlp_in * normed_two
    (grad_through_two,) = norm_back_two(grad_mlp_in * (1.0 + scale_two))
    grad_middle = grad_result + grad_through_two
    grad_gate_one = grad_middle * branch_one
    grad_branch_one = (grad_middle * gate_one).astype(jnp.bfloat16)
    sum_six = summed(grad_branch_one)
    grad_attended = jnp.einsum(
        "rtc,dc->rtd", grad_branch_one, output_weight, preferred_element_type=jnp.float32
    ).astype(jnp.bfloat16)
    grad_attended = split_groups(grad_attended[0], 1, seq_count)
    grad_attended, second_low = lax.optimization_barrier((grad_attended, second_low))
    head_grad = lax.all_to_all(grad_attended, "seq", split_axis=0, concat_axis=0, tiled=True)
    grad_buffer = put(None, 15, second_low, grad_projected)
    grad_buffer = put(grad_buffer, 13, first_low, grad_second)
    head_grad, grad_buffer = lax.optimization_barrier((head_grad, grad_buffer))
    grad_triple_heads = attention_grad(
        head_rows, head_grad.reshape(full_len, head_grad.shape[-1]), segment_ids[0], padding[0], heads_local
    ).reshape(seq_count, local_len, head_rows.shape[-1])
    grad_triple_heads, grad_buffer, cond_held = lax.optimization_barrier(
        (grad_triple_heads, grad_buffer, cond_held)
    )
    grad_triple = lax.all_to_all(grad_triple_heads, "seq", split_axis=0, concat_axis=0, tiled=True)
    grad_buffer = put(grad_buffer, 11, feature, grad_first)
    grad_buffer = put(grad_buffer, 9, activated, grad_branch_two)
    grad_buffer = put(grad_buffer, 7, mlp_in, grad_hidden)
    grad_buffer = put(grad_buffer, 5, attended, grad_branch_one)
    cond_own = own_conditions(cond_held, info, images, slot_count)
    grad_triple, grad_buffer, cond_own = lax.optimization_barrier((grad_triple, grad_buffer, cond_own))
    grad_triple = join_groups(grad_triple, 3, group_width)[None]
    grad_buffer = put(grad_buffer, 2, attend_in, grad_triple)
    triple_sums = summed(grad_triple)
    grad_attend_in = jnp.einsum(
        "rtc,dc->rtd", grad_triple, attend_weight, preferred_element_type=jnp.float32
    )
    grad_scale_one = grad_attend_in * normed_one
    (grad_through_one,) = norm_back_one(grad_attend_in * (1.0 + scale_one))
    grad_tokens = grad_middle + grad_through_one
    token_mod_grad = jnp.concatenate(
        [grad_attend_in, grad_scale_one, grad_gate_one, grad_mlp_in, grad_scale_two, grad_gate_two],
        axis=-1,
    )
    mod_part = jnp.einsum("rts,rtc->rsc", onehot, token_mod_grad, precision=lax.Precision.HIGH)
    mod_sent = jnp.pad(
        mod_part.astype(jnp.bfloat16).reshape(IMAGE_ROWS, LANES), ((0, SENT_ROWS - IMAGE_ROWS), (0, 0))
    )
    rows_at = param_rows()

    def rows(vector):
        return vector.reshape(-1, LANES)


    def head(index):
        return (0, ends[index], rows_at[index] % SUBS, SUBS)

    def tail(index):
        return (0, ends[index], SUBS, SUBS + rows_at[index] % SUBS)

    def whole(vector):
        return (0, rows(vector), 0, vector.shape[0] // LANES)

    pieces = [
        (6,) + head(2)[1:],
        tail(2),
        whole(triple_sums[:model_width]),
        whole(triple_sums[2 * model_width :]),
        head(5),
        tail(5),
        whole(sum_six),
        head(7),
        tail(7),
        whole(sum_eight),
        head(9),
        tail(9),
        whole(sum_ten),
        head(11),
        tail(11),
        whole(sum_twelve),
        head(13),
        tail(13),
        whole(sum_fourteen),
        head(15),
        tail(15),
        whole(sum_sixteen),
    ]
    grad_buffer = edge_write(pieces, grad_buffer, edge_places[EDGE_TILES.index(3891) :])
    reduced, mod_all, cond_grad = reduce_slots(
        grad_buffer, mod_sent, own_low, info, slot_count, data_count, seq_count
    )
    (grad_conditions,) = silu_cond_back(cond_grad.reshape(1, SEGS, COND_STRIDE * LANES)[:, :, :D])
    new_master, new_first, new_second = update(
        reduced, cond_own, mod_all, own_first, master, first_moment, second_moment
    )
    return (
        result.astype(jnp.bfloat16),
        grad_tokens,
        grad_conditions,
        new_master,
        new_first,
        new_second,
    )


def solution(mesh):
    return jax.shard_map(
        shards,
        mesh=mesh,
        in_specs=(
            P("dp", "seq", None),
            P("dp", None, None),
            P("dp", None),
            P("dp", None),
            P("dp", "seq", None),
            P("dp", "seq", None),
            P(),
            P(("dp", "seq"), None),
            P(("dp", "seq"), None),
            P(("dp", "seq"), None),
        ),
        out_specs=(
            P("dp", "seq", None),
            P("dp", "seq", None),
            P("dp", None, None),
            P(("dp", "seq"), None),
            P(("dp", "seq"), None),
            P(("dp", "seq"), None),
        ),
        check_vma=False,
    )
```

```python
from functools import partial
import math

import jax
import jax.numpy as jnp
from jax import lax
from jax.experimental import pallas as pl
from jax.experimental.pallas import tpu as pltpu
from jax.sharding import PartitionSpec as P

HEADS = 16
HEAD_DIM = 72
D = 1152
FF = 4608
PROJ = 2048
TARGET = 768
SEGS = 4
STEP = 10
TILES = 15643


ln_eps = 1e-06
cos_eps = 1e-06
repa_weight = 0.5
beta_one = 0.5
beta_two = 0.5
learn_rate = 0.02
weight_decay = 0.01
adam_eps = 1e-08


LANES = 128
SUBS = 16
MOD_ROWS = (D + 1) * 6 * D // LANES
VMEM_LIMIT = 56 * 1024 * 1024
MESH = pl.DeviceIdType.MESH


def param_shapes():
    return [
        (D, 6 * D),
        (6 * D,),
        (D, 3 * D),
        (D,),
        (D,),
        (D, D),
        (D,),
        (D, FF),
        (FF,),
        (FF, D),
        (D,),
        (D, PROJ),
        (PROJ,),
        (PROJ, PROJ),
        (PROJ,),
        (PROJ, TARGET),
        (TARGET,),
    ]


def param_rows():
    starts = []
    row = 0
    for dims in param_shapes():
        starts.append(row)
        row = row + math.prod(dims) // LANES
    return starts


CHUNK = {2: 384, 5: 384, 7: 384, 9: 1536, 11: 384, 13: 512, 15: 1024}
EDGE_TILES = [3891, 5835, 5836, 6484, 6485, 9077, 9078, 9079, 11671, 12823, 12824, 14872, 14873, 15641, 15642]


def chunk_spans():
    spans = []
    base = {}
    rows = param_rows()
    for index, chunk in CHUNK.items():
        depth, width = param_shapes()[index]
        per_chunk = chunk * width // LANES // SUBS
        extra = 1 if rows[index] % SUBS else 0
        base[index] = len(spans)
        for step in range(depth // chunk):
            first = rows[index] // SUBS + step * per_chunk
            spans.append((first, first + per_chunk + extra - 1))
    return spans, base


def unpack_body(base, first_tile, per_chunk, tiles, shift, chunk, col_blocks, hosts, kept,
                first_ref, last_ref, starts_ref, guests_ref, packed, out_ref, landed, wide, sems):
    step = pl.program_id(0)

    def fetch(which, slot):
        low_tile = first_tile + which * per_chunk

        def run(begin, end, place):
            size = pl.multiple_of(jnp.maximum(end - begin, 0) * SUBS, SUBS)
            origin = pl.multiple_of(place * SUBS, SUBS)
            target = pl.multiple_of((begin - low_tile) * SUBS, SUBS)

            @pl.when(end > begin)
            def _():
                pltpu.make_async_copy(
                    packed.at[pl.ds(origin, size)], landed.at[slot, pl.ds(target, size)], sems.at[slot]
                ).start()

        def one(owner, carry):
            begin = jnp.maximum(starts_ref[owner], low_tile)
            end = jnp.minimum(starts_ref[owner + 1], low_tile + tiles)
            turn = starts_ref[owner] + kept
            run(begin, jnp.minimum(end, turn), owner * kept + begin - starts_ref[owner])
            if hosts:
                begin = jnp.maximum(begin, turn)
                run(begin, end, guests_ref[owner] + begin - turn)
            return carry

        lax.fori_loop(first_ref[base + which], last_ref[base + which] + 1, one, 0)

    @pl.when(step == 0)
    def _():
        fetch(0, 0)

    slot = step % 2

    @pl.when(step + 1 < pl.num_programs(0))
    def _():
        fetch(step + 1, (step + 1) % 2)

    pltpu.make_async_copy(packed.at[pl.ds(0, tiles * SUBS)], landed.at[slot], sems.at[slot]).wait()
    wide[...] = landed[slot].astype(jnp.float32)
    for block in range(col_blocks):
        out_ref[:, block * LANES : (block + 1) * LANES] = wide[
            pl.ds(shift + block, chunk, stride=col_blocks), :
        ].astype(jnp.bfloat16)


def unpack_weight(index, packed, plan, firsts, lasts, starts, guests):
    depth, width = param_shapes()[index]
    chunk = CHUNK[index]
    col_blocks = width // LANES
    row = param_rows()[index]
    shift = row % SUBS
    per_chunk = chunk * col_blocks // SUBS
    tiles = per_chunk + (1 if shift else 0)
    base = chunk_spans()[1][index]
    return pl.pallas_call(
        partial(unpack_body, base, row // SUBS, per_chunk, tiles, shift, chunk, col_blocks, plan[0], plan[2]),
        out_shape=jax.ShapeDtypeStruct((depth, width), jnp.bfloat16),
        grid_spec=pltpu.PrefetchScalarGridSpec(
            num_scalar_prefetch=4,
            grid=(depth // chunk,),
            in_specs=[pl.BlockSpec(memory_space=pl.ANY)],
            out_specs=pl.BlockSpec((chunk, width), lambda i, *_: (i, 0)),
            scratch_shapes=[
                pltpu.VMEM((2, tiles * SUBS, LANES), jnp.bfloat16),
                pltpu.VMEM((tiles * SUBS, LANES), jnp.float32),
                pltpu.SemaphoreType.DMA((2,)),
            ],
        ),
        compiler_params=pltpu.CompilerParams(vmem_limit_bytes=VMEM_LIMIT),
        cost_estimate=pl.CostEstimate(flops=0, bytes_accessed=depth * width * 4, transcendentals=0),
        name="unpack_%d" % index,
    )(firsts, lasts, starts, guests, packed)


def edge_read_body(table_ref, packed, out_ref, sem):
    count = out_ref.shape[0] // SUBS

    def one(i, carry):
        origin = pl.multiple_of(table_ref[i] * SUBS, SUBS)
        target = pl.multiple_of(i * SUBS, SUBS)
        pltpu.make_async_copy(packed.at[pl.ds(origin, SUBS)], out_ref.at[pl.ds(target, SUBS)], sem).start()
        return carry

    lax.fori_loop(0, count, one, 0)
    pltpu.make_async_copy(packed.at[pl.ds(0, count * SUBS)], out_ref, sem).wait()


def edge_read(packed, table):
    return pl.pallas_call(
        edge_read_body,
        out_shape=jax.ShapeDtypeStruct((len(EDGE_TILES) * SUBS, LANES), jnp.bfloat16),
        grid_spec=pltpu.PrefetchScalarGridSpec(
            num_scalar_prefetch=1,
            grid=(1,),
            in_specs=[pl.BlockSpec(memory_space=pl.ANY)],
            out_specs=pl.BlockSpec(memory_space=pltpu.VMEM),
            scratch_shapes=[pltpu.SemaphoreType.DMA],
        ),
        name="edge_read",
    )(table, packed)


def edge_write_body(layout, table_ref, *refs):
    pieces = refs[: len(layout)]
    out, wide, narrow, sem = refs[len(layout) + 1 :]
    wide[...] = jnp.zeros_like(wide)
    at = 0
    for piece, (skip, low, high) in zip(pieces, layout):
        at = at + skip
        wide[at : at + high - low, :] = piece[low:high, :]
        at = at + high - low
    narrow[...] = wide[...].astype(jnp.bfloat16)
    count = narrow.shape[0] // SUBS

    def one(i, carry):
        origin = pl.multiple_of(i * SUBS, SUBS)
        target = pl.multiple_of(table_ref[i] * SUBS, SUBS)
        pltpu.make_async_copy(narrow.at[pl.ds(origin, SUBS)], out.at[pl.ds(target, SUBS)], sem).start()
        return carry

    lax.fori_loop(0, count, one, 0)
    pltpu.make_async_copy(narrow, out.at[pl.ds(0, count * SUBS)], sem).wait()


def edge_write(pieces, buffer, table):
    count = table.shape[0]
    layout = [(skip, low, high) for skip, _, low, high in pieces]
    arrays = [array for _, array, _, _ in pieces]
    return pl.pallas_call(
        partial(edge_write_body, layout),
        out_shape=jax.ShapeDtypeStruct(buffer.shape, buffer.dtype),
        grid_spec=pltpu.PrefetchScalarGridSpec(
            num_scalar_prefetch=1,
            grid=(1,),
            in_specs=[pl.BlockSpec(memory_space=pltpu.VMEM)] * len(arrays)
            + [pl.BlockSpec(memory_space=pl.ANY)],
            out_specs=pl.BlockSpec(memory_space=pl.ANY),
            scratch_shapes=[
                pltpu.VMEM((count * SUBS, LANES), jnp.float32),
                pltpu.VMEM((count * SUBS, LANES), jnp.bfloat16),
                pltpu.SemaphoreType.DMA,
            ],
        ),
        input_output_aliases={1 + len(arrays): 0},
        name="edge_write",
    )(table, *arrays, buffer)


def weight_grad_body(base, first_tile, per_chunk, shift, chunk, col_blocks, slots, plan, piece, chained,
                     first_ref, last_ref, starts_ref, guests_ref, x_ref, dy_ref, *rest):
    if chained:
        rest = rest[1:]
    out, ends_ref, wide, narrow, sems = rest
    hosts, kept = plan
    step = pl.program_id(0)
    steps = pl.num_programs(0)
    slot = step % 2
    rows = chunk * col_blocks

    def drain(which):
        pltpu.make_async_copy(narrow.at[which], out.at[pl.ds(0, rows)], sems.at[which]).wait()

    @pl.when(step == 0)
    def _():
        wide[...] = jnp.zeros_like(wide)

    if shift:
        @pl.when(step > 0)
        def _():
            wide[0:SUBS, :] = wide[rows : rows + SUBS, :]

    left = x_ref[...].T
    for start in range(0, col_blocks, piece):
        part = jnp.dot(
            left, dy_ref[:, start * LANES : (start + piece) * LANES], preferred_element_type=jnp.float32
        )
        for block in range(piece):
            wide[pl.ds(shift + start + block, chunk, stride=col_blocks), :] = part[
                :, block * LANES : (block + 1) * LANES
            ]

    @pl.when(step >= 2)
    def _():
        drain(slot)

    narrow[slot] = wide[0:rows, :].astype(jnp.bfloat16)

    @pl.when(step == 0)
    def _():
        ends_ref[0:SUBS, :] = wide[0:SUBS, :]

    if shift:
        @pl.when(step == steps - 1)
        def _():
            ends_ref[SUBS : 2 * SUBS, :] = wide[rows : rows + SUBS, :]
    else:
        ends_ref[SUBS : 2 * SUBS, :] = jnp.zeros((SUBS, LANES), jnp.float32)

    low_tile = first_tile + step * per_chunk

    def run(begin, end, place):
        size = pl.multiple_of(jnp.maximum(end - begin, 0) * SUBS, SUBS)
        target = pl.multiple_of(place * SUBS, SUBS)
        origin = pl.multiple_of((begin - low_tile) * SUBS, SUBS)

        @pl.when(end > begin)
        def _():
            pltpu.make_async_copy(
                narrow.at[slot, pl.ds(origin, size)], out.at[pl.ds(target, size)], sems.at[slot]
            ).start()

    def one(owner, carry):
        begin = jnp.maximum(starts_ref[owner], low_tile)
        end = jnp.minimum(starts_ref[owner + 1], low_tile + per_chunk)
        turn = starts_ref[owner] + kept
        run(begin, jnp.minimum(end, turn), owner * kept + begin - starts_ref[owner])
        if hosts:
            begin = jnp.maximum(begin, turn)
            run(begin, end, guests_ref[owner] + begin - turn)
        return carry

    lax.fori_loop(first_ref[base + step], last_ref[base + step] + 1, one, 0)

    @pl.when(step == steps - 1)
    def _():
        drain(slot)

        @pl.when(steps > 1)
        def _():
            drain(1 - slot)


def weight_grad(index, left, right, buffer, owners, slots, firsts, lasts, starts, guests, plan):
    depth, width = param_shapes()[index]
    tokens = left.shape[0]
    chunk = CHUNK[index]
    col_blocks = width // LANES
    piece = next(p for p in (9, 8, 6) if col_blocks % p == 0)
    row = param_rows()[index]
    shift = row % SUBS
    per_chunk = chunk * col_blocks // SUBS
    base = chunk_spans()[1][index]
    shape = (owners * plan[1] * SUBS, LANES)
    in_specs = [
        pl.BlockSpec((tokens, chunk), lambda i, *_: (0, i)),
        pl.BlockSpec((tokens, width), lambda i, *_: (0, 0)),
    ]
    operands = [firsts, lasts, starts, guests, left, right]
    aliases = {}
    if buffer is not None:
        in_specs.append(pl.BlockSpec(memory_space=pl.ANY))
        operands.append(buffer)
        aliases = {6: 0}
    return pl.pallas_call(
        partial(weight_grad_body, base, row // SUBS, per_chunk, shift, chunk, col_blocks, slots, plan, piece,
                buffer is not None),
        out_shape=(
            jax.ShapeDtypeStruct(shape, jnp.bfloat16),
            jax.ShapeDtypeStruct((2 * SUBS, LANES), jnp.float32),
        ),
        grid_spec=pltpu.PrefetchScalarGridSpec(
            num_scalar_prefetch=4,
            grid=(depth // chunk,),
            in_specs=in_specs,
            out_specs=(
                pl.BlockSpec(memory_space=pl.ANY),
                pl.BlockSpec((2 * SUBS, LANES), lambda i, *_: (0, 0)),
            ),
            scratch_shapes=[
                pltpu.VMEM((chunk * col_blocks + SUBS, LANES), jnp.float32),
                pltpu.VMEM((2, chunk * col_blocks, LANES), jnp.bfloat16),
                pltpu.SemaphoreType.DMA((2,)),
            ],
        ),
        input_output_aliases=aliases,
        compiler_params=pltpu.CompilerParams(vmem_limit_bytes=VMEM_LIMIT),
        cost_estimate=pl.CostEstimate(
            flops=2 * tokens * depth * width, bytes_accessed=depth * width * 2, transcendentals=0
        ),
        name="weight_grad_%d" % index,
    )(*operands)


class Grid:
    def __init__(self, side, depth):
        self.side = side
        self.sizes = {"u": side, "v": side, "z": depth}
        self.place = lax.axis_index("dp")
        self.core = self.place % 2
        outer = self.place // 2 // side
        inner = self.place // 2 % side
        self.mine = {
            "u": jnp.where(self.core == 0, outer, inner),
            "v": jnp.where(self.core == 0, inner, outer),
            "z": lax.axis_index("seq"),
        }
        self.sibling = (
            self.place + 1 - 2 * self.core,
            self.mine["z"],
        )

    def dp_of(self, first, second, core):
        outer = jnp.where(core == 0, first, second)
        inner = jnp.where(core == 0, second, first)
        return (outer * self.side + inner) * 2 + core

    def device(self, axis, other):
        at = dict(self.mine)
        at[axis] = other
        return (self.dp_of(at["u"], at["v"], self.core), at["z"])

    def other(self, axis, k):
        return k + (k >= self.mine[axis]).astype(jnp.int32)

    def seat(self, axis, other):
        mine = self.mine[axis]
        return mine - (mine > other).astype(jnp.int32)

    def partners(self):
        found = [self.sibling]
        for axis in ("u", "v", "z"):
            for k in range(self.sizes[axis] - 1):
                found.append(self.device(axis, self.other(axis, k)))
        return found

    def greet(self, hosting=None, to_host=False):
        barrier = pltpu.get_barrier_semaphore()
        partners = self.partners()
        for partner in partners:
            pl.semaphore_signal(barrier, inc=1, device_id=partner, device_id_type=MESH)
        expected = len(partners)
        if hosting is not None and to_host:
            for piece in range(hosting.share):
                device, there = hosting.guest_at(piece)

                @pl.when(hosting.is_host & there)
                def _(device=device):
                    pl.semaphore_signal(barrier, inc=1, device_id=device, device_id_type=MESH)

            expected = expected + 1 - hosting.is_host.astype(jnp.int32)
        elif hosting is not None:
            @pl.when(jnp.logical_not(hosting.is_host))
            def _():
                pl.semaphore_signal(barrier, inc=1, device_id=hosting.host, device_id_type=MESH)

            expected = expected + hosting.guests
        pl.semaphore_wait(barrier, expected)


class Hosting:
    def __init__(self, grid, owners, hosts, share, kept, left):
        depth = grid.sizes["z"]
        z = grid.mine["z"]
        self.grid, self.depth, self.hosts, self.share, self.kept, self.left = grid, depth, hosts, share, kept, left
        self.places = owners // depth
        self.is_host = grid.place * depth + z < hosts
        here, _, room = level_counts(hosts, share, self.places, depth, z)
        index = grid.place - here
        back_here, _, back_room = level_counts(hosts, share, self.places, depth, z - depth // 2)
        own = index < room
        spot = jnp.maximum(jnp.where(own, index, back_room - 1 - (index - room)), 0)
        self.piece = lax.rem(spot, share)
        self.host = (spot // share, jnp.where(own | self.is_host, z, z - depth // 2))
        count = jnp.int32(0)
        for piece in range(share):
            count = count + self.guest_at(piece)[1].astype(jnp.int32)
        self.guests = jnp.where(self.is_host, count, 0)

    def guest_at(self, piece):
        there, near, over = guest_of(
            self.hosts, self.share, self.places, self.depth, self.grid.place, self.grid.mine["z"], piece
        )
        device = (jnp.where(near[0], near[1], over[1]), jnp.where(near[0], near[2], over[2]))
        return device, there & (piece < self.share)

    def guest(self, tile):
        piece = tile // self.left
        device, there = self.guest_at(piece)
        return device, there, self.kept + tile - piece * self.left


def split_slots(slots, shards):
    room = 32 * 1024 * 1024 // ((HELD + 2 * SLOTS) * shards * SUBS * LANES * 2)
    part = max(p for p in range(2, 13) if slots % p == 0 and p <= max(room, 2))
    late = max(1, round(part * 0.34))
    return slots // part, (part - late, late)


def level_counts(hosts, share, places, depth, z):
    here = (hosts - z + depth - 1) // depth
    return here, places - here, share * here


def guest_of(hosts, share, places, depth, place, z, piece):
    here, guests, room = level_counts(hosts, share, places, depth, z)
    index = place * share + piece
    far = z + depth // 2
    far_here, far_guests, far_room = level_counts(hosts, share, places, depth, far)
    back = room - 1 - index
    near = index < guests
    over = (far < depth) & (far_room + back < far_guests)
    return near | over, (near, here + index, z), (over, far_here + far_room + back, far)


def guest_places(plan, owners, depth):
    hosts, share, kept, left = plan
    places = [0] * owners
    for host in range(hosts):
        for piece in range(share):
            there, near, over = guest_of(hosts, share, owners // depth, depth, host // depth, host % depth, piece)
            if there:
                _, place, z = near if near[0] else over
                places[place * depth + z] = host * kept + piece * left
    return places


def host_plan(slots, owners, depth):
    hosts = MOD_ROWS // (slots * SUBS)
    shards = owners // 2
    room = 32 * 1024 * 1024 // ((HELD + 2 * SLOTS) * shards * SUBS * LANES * 2)
    share = -(-(owners - hosts) // hosts) if hosts else 0
    levels = [level_counts(hosts, share, owners // depth, depth, z) for z in range(depth)]
    for z, (_, guests, room_here) in enumerate(levels):
        if guests > room_here and (
            z < depth // 2
            or guests - room_here > levels[z - depth // 2][2] - levels[z - depth // 2][1]
        ):
            hosts = 0
    for kept in range(1, slots) if hosts else ():
        left = slots - kept
        if share * left > kept:
            continue
        for step in range(min(12, max(room, 2)), 5, -1):
            for late in (round(step * 0.34), step // 3, -(-step // 3)):
                early = step - late
                if kept % step or left % early:
                    continue
                middle = kept // step * early
                if all((i * left - middle) % late == 0 for i in range(share + 1) if i * left > middle):
                    return hosts, share, kept, kept // step, (early, late)
    steps, parts = split_slots(slots, shards)
    return 0, 0, slots, steps, parts


ORDERS = (("u", "v", "z"), ("u", "z", "v"))
LAG = 2
SLOTS = 4
OUTS = 8
LEAD = 4
HELD = 4 * LAG + 1


def gather_stream(grid, order, first_row, span, steps, own_ref, out_ref, sems, hosting):
    (send_a, recv_a, send_b, recv_b, send_c, recv_c, send_d, recv_d, kept_sem, arrive) = sems
    mine = grid.mine
    side = grid.side
    near, mid, far = order[2], order[1], order[0]

    def rows(q):
        return pl.ds(pl.multiple_of(first_row + q * span, SUBS), span)

    def copy(source, target, send, recv, device):
        return pltpu.make_async_remote_copy(
            src_ref=source, dst_ref=target, send_sem=send, recv_sem=recv, device_id=device,
            device_id_type=MESH,
        )

    def one_a(q, axis, k):
        other = grid.other(axis, k)
        mine_dp = grid.dp_of(mine["u"], mine["v"], grid.core)
        return copy(
            own_ref.at[rows(q)], out_ref.at[mine_dp, mine["z"], rows(q)],
            send_a.at[q % 4, k], recv_a.at[q, grid.seat(axis, other)],
            grid.device(axis, other),
        )

    def wait_a(q, axis, k):
        dp = grid.dp_of(mine["u"], mine["v"], grid.core)
        copy(
            own_ref.at[rows(q)], out_ref.at[dp, mine["z"], rows(q)],
            send_a.at[q % 4, k], recv_a.at[q, k], grid.device(axis, grid.other(axis, k)),
        ).wait_recv()

    def many_b(q, axis, k):
        other = grid.other(axis, k)
        seat = grid.seat(axis, other)
        if axis == "v":
            at = out_ref.at[grid.dp_of(mine["u"], mine["v"], grid.core), :, rows(q)]
            return [copy(at, at, send_b.at[q % 4, k], recv_b.at[q, seat], grid.device(axis, other))]
        found = []
        for v in range(side):
            at = out_ref.at[grid.dp_of(mine["u"], v, grid.core), mine["z"], rows(q)]
            found.append(copy(at, at, send_b.at[q % 4, k], recv_b.at[q, seat], grid.device(axis, other)))
        return found

    def many_c(q, k):
        other = grid.other("u", k)
        seat = grid.seat("u", other)
        found = []
        for v in range(side):
            at = out_ref.at[grid.dp_of(mine["u"], v, grid.core), :, rows(q)]
            found.append(copy(at, at, send_c.at[q % 4, k], recv_c.at[q, seat], grid.device("u", other)))
        return found

    def many_d(q):
        found = []
        for u in range(side):
            for v in range(side):
                at = out_ref.at[grid.dp_of(u, v, grid.core), :, rows(q)]
                found.append(copy(at, at, send_d.at[q % 4], recv_d.at[q], grid.sibling))
        return found

    def bulk(q, count, send, recv, device):
        at = out_ref.at[pl.ds(0, count), :, rows(q)]
        return copy(at, at, send, recv, device)

    def bulk_b(q, axis, send, recv):
        if axis == "v":
            at = out_ref.at[0, :, rows(q)]
        else:
            at = out_ref.at[pl.ds(0, side), 0, rows(q)]
        return copy(at, at, send, recv, grid.sibling)

    far_count = grid.sizes[near] - 1
    mid_count = grid.sizes[mid] - 1

    def stage_d(q):
        bulk(q, side, send_c.at[q % 4, 0], recv_c.at[q, 0], grid.sibling).wait_recv()
        for k in range(1, side - 1):
            bulk(q, side, send_c.at[q % 4, k], recv_c.at[q, k], grid.sibling).wait_recv()
        for k in range(side - 1):
            bulk(q, side, send_c.at[q % 4, k], recv_c.at[q, k], grid.sibling).wait_send()
        for one in many_d(q):
            one.start()

    def stage_c(q):
        for k in range(mid_count):
            bulk_b(q, mid, send_b.at[q % 4, k], recv_b.at[q, k]).wait_recv()
        for k in range(mid_count):
            bulk_b(q, mid, send_b.at[q % 4, k], recv_b.at[q, k]).wait_send()
        for k in range(side - 1):
            for one in many_c(q, k):
                one.start()

    def keep(q):
        dp = grid.dp_of(mine["u"], mine["v"], grid.core)
        return pltpu.make_async_copy(own_ref.at[rows(q)], out_ref.at[dp, mine["z"], rows(q)], kept_sem.at[q % 4])

    def stage_b(q):
        keep(q).wait()
        for k in range(far_count):
            wait_a(q, near, k)
        for k in range(far_count):
            one_a(q, near, k).wait_send()
        for k in range(mid_count):
            for one in many_b(q, mid, k):
                one.start()

    def stage_a(q):
        if hosting is not None:
            _, there, _ = hosting.guest((first_row + q * span) // SUBS)

            @pl.when(hosting.is_host & there)
            def _():
                copy(own_ref.at[rows(q)], own_ref.at[rows(q)], arrive.at[q], arrive.at[q], grid.sibling).wait_recv()

        keep(q).start()
        for k in range(far_count):
            one_a(q, near, k).start()

    def finish(q):
        whole = bulk(q, side * side, send_d.at[q % 4], recv_d.at[q], grid.sibling)
        whole.wait_recv()
        whole.wait_send()

    return (stage_a, stage_b, stage_c, stage_d, finish)


GATHER_REFS = 10


def gather_body(side, depth, plan, slots, images, own_ref, cond_ref, info_ref, out_ref, mod_ref, held_ref,
                mine_ref, own_sem, guest_sem, *refs):
    hosts, share, kept, steps, parts = plan
    grid = Grid(side, depth)
    hosting = Hosting(grid, 2 * side * side * depth, hosts, share, kept, slots - kept) if hosts else None
    fill = pltpu.make_async_copy(own_ref.at[pl.ds(0, kept * SUBS)], mine_ref, own_sem)

    def when_guest(action):
        if hosting is None:
            action()
        else:
            pl.when(jnp.logical_not(hosting.is_host))(action)

    when_guest(fill.start)
    grid.greet(hosting, to_host=True)
    streams = []
    arrivals = []
    first = 0
    for number, (order, part) in enumerate(zip(ORDERS, parts)):
        span = part * SUBS
        sems = refs[GATHER_REFS * number : GATHER_REFS * (number + 1)]
        streams.append(gather_stream(grid, order, first, span, steps, mine_ref, out_ref, sems, hosting))
        arrivals.append((first // SUBS, part, sems[-1]))
        first = first + steps * span
    if hosting is not None:
        left = slots - kept

        def send_chunks(q, carry):
            for low, part, arrive in arrivals:
                tile = low + q * part
                within = tile - hosting.piece * left

                @pl.when(jnp.logical_not(hosting.is_host) & (within >= 0) & (within < left))
                def _(tile=tile, within=within, part=part, arrive=arrive):
                    slot = jnp.clip(kept + within, kept, slots - part)
                    pltpu.make_async_remote_copy(
                        src_ref=own_ref.at[pl.ds(pl.multiple_of(slot * SUBS, SUBS), part * SUBS)],
                        dst_ref=mine_ref.at[pl.ds(pl.multiple_of(tile * SUBS, SUBS), part * SUBS)],
                        send_sem=guest_sem,
                        recv_sem=arrive.at[q],
                        device_id=hosting.host,
                        device_id_type=MESH,
                    ).start()

            return carry

        lax.fori_loop(0, min(LEAD, steps), send_chunks, 0)
    when_guest(fill.wait)
    modulation_step = modulation_stages(
        grid, images, slots, own_ref, info_ref, cond_ref, mod_ref, held_ref, refs[2 * GATHER_REFS :]
    )

    def round_trip(s, carry):
        for late in range(4, -1, -1):
            q = s - LAG * late

            @pl.when((q >= 0) & (q < steps))
            def _(late=late, q=q):
                for stream in streams:
                    stream[late](q)

        if hosting is not None:
            @pl.when(s + LEAD < steps)
            def _():
                send_chunks(s + LEAD, 0)

        modulation_step(s)
        return carry

    lax.fori_loop(0, max(steps + 4 * LAG, MOD_STEPS), round_trip, 0)
    if hosting is not None:
        @pl.when(jnp.logical_not(hosting.is_host))
        def _():
            at = own_ref.at[pl.ds(kept * SUBS, (slots - kept) * SUBS)]
            pltpu.make_async_remote_copy(
                src_ref=at, dst_ref=at, send_sem=guest_sem, recv_sem=guest_sem, device_id=grid.sibling,
                device_id_type=MESH,
            ).wait_send()


def gather_slots(own, cond_rows, info, slots, data_count, seq_count):
    side = math.isqrt(data_count // 2)
    images = data_count * SEGS
    plan = host_plan(slots, data_count * seq_count, seq_count)
    kept, steps = plan[2], plan[3]
    dma = pltpu.SemaphoreType.DMA
    sems = []
    for order in ORDERS:
        sizes = {"u": side - 1, "v": side - 1, "z": seq_count - 1}
        for axis in (order[2], order[1], order[0]):
            sems.append(dma((4, sizes[axis])))
            sems.append(dma((steps, sizes[axis])))
        sems.append(dma((4,)))
        sems.append(dma((steps,)))
        sems.append(dma((4,)))
        sems.append(dma((steps,)))
    vmem = pl.BlockSpec(memory_space=pltpu.VMEM)
    packed, modulation, held = pl.pallas_call(
        partial(gather_body, side, seq_count, plan, slots, images),
        out_shape=(
            jax.ShapeDtypeStruct((data_count, seq_count, kept * SUBS, LANES), jnp.bfloat16),
            jax.ShapeDtypeStruct((IMAGE_ROWS, LANES), jnp.float32),
            jax.ShapeDtypeStruct((condition_rows(slots), LANES), jnp.float32),
        ),
        in_specs=[vmem, vmem, pl.BlockSpec(memory_space=pltpu.SMEM)],
        out_specs=(pl.BlockSpec(memory_space=pl.ANY), vmem, vmem),
        scratch_shapes=[pltpu.VMEM((kept * SUBS, LANES), jnp.bfloat16), dma, dma]
        + sems
        + modulation_refs(side, seq_count, images, slots),
        compiler_params=pltpu.CompilerParams(
            collective_id=2, has_side_effects=True, vmem_limit_bytes=VMEM_LIMIT
        ),
        name="gather_slots",
    )(own, cond_rows, info)
    return packed.reshape(data_count * seq_count * kept * SUBS, LANES), modulation, held


def reduce_stream(grid, order, first_row, span, steps, parts_ref, out_ref, refs, hosting, passed):
    (own, rc, r1, r2, r3, outs, own_sem, out_sem, hand_sem, c_send, c_recv, s1, v1, s2, v2, s3, v3,
     c_credit, k1, k2, k3) = refs
    mine = grid.mine
    side = grid.side
    held = own.shape[0]
    mu, mv, mz = mine["u"], mine["v"], mine["z"]

    def rows(q):
        return pl.ds(pl.multiple_of(first_row + q * span, SUBS), span)

    def load(q, u, v):
        return pltpu.make_async_copy(
            parts_ref.at[grid.dp_of(u, v, grid.core), :, rows(q)], own.at[q % held, u, v], own_sem.at[q % held, u, v]
        )

    def give(q, u, v):
        return pltpu.make_async_remote_copy(
            src_ref=parts_ref.at[grid.dp_of(u, v, 1 - grid.core), :, rows(q)],
            dst_ref=rc.at[q % SLOTS, u, v],
            send_sem=c_send.at[q % SLOTS, u, v],
            recv_sem=c_recv.at[q % SLOTS, u, v],
            device_id=grid.sibling,
            device_id_type=MESH,
        )

    def block(q, stage, other):
        if stage == 0:
            return own.at[q % held, other]
        if order[1] == "v":
            return own.at[q % held, mu, other] if stage == 1 else own.at[q % held, mu, mv, other]
        return own.at[q % held, mu, :, other] if stage == 1 else own.at[q % held, mu, other, mz]

    landing = (r1, r2, r3)
    sends = (s1, s2, s3)
    arrivals = (v1, v2, v3)
    credits = (k1, k2, k3)

    def send(q, stage, k):
        axis = order[stage]
        other = grid.other(axis, k)
        seat = grid.seat(axis, other)
        return pltpu.make_async_remote_copy(
            src_ref=block(q, stage, other),
            dst_ref=landing[stage].at[q % SLOTS, seat],
            send_sem=sends[stage].at[q % SLOTS, k],
            recv_sem=arrivals[stage].at[q % SLOTS, seat],
            device_id=grid.device(axis, other),
            device_id_type=MESH,
        )

    def receive(q, stage, k):
        axis = order[stage]
        return pltpu.make_async_remote_copy(
            src_ref=block(q, stage, 0),
            dst_ref=landing[stage].at[q % SLOTS, k],
            send_sem=sends[stage].at[q % SLOTS, k],
            recv_sem=arrivals[stage].at[q % SLOTS, k],
            device_id=grid.device(axis, grid.other(axis, k)),
            device_id_type=MESH,
        )

    def keep(q):
        return pltpu.make_async_copy(outs.at[q % OUTS], out_ref.at[rows(q)], out_sem.at[q % OUTS])

    def hand_over(q):
        device, there, slot = hosting.guest((first_row + q * span) // SUBS)
        copy = pltpu.make_async_remote_copy(
            src_ref=outs.at[q % OUTS],
            dst_ref=out_ref.at[pl.ds(pl.multiple_of(slot * SUBS, SUBS), span)],
            send_sem=hand_sem.at[q % OUTS],
            recv_sem=passed,
            device_id=device,
            device_id_type=MESH,
        )
        return copy, there

    def write(q, action):
        if hosting is None:
            getattr(keep(q), action)()
            return

        @pl.when(jnp.logical_not(hosting.is_host))
        def _():
            getattr(keep(q), action)()

        copy, there = hand_over(q)

        @pl.when(hosting.is_host & there)
        def _():
            if action == "start":
                copy.start()
            else:
                copy.wait_send()

    def collect(q, stage):
        axis = order[stage]
        count = grid.sizes[axis] - 1
        for k in range(count):
            receive(q, stage, k).wait_recv()
        kept = block(q, stage, mine[axis])
        total = kept[...].astype(jnp.float32)
        for k in range(count):
            total = total + landing[stage][q % SLOTS, k].astype(jnp.float32)
        if stage < 2:
            kept[...] = total.astype(jnp.bfloat16)
        else:
            @pl.when(q >= OUTS)
            def _():
                write(q - OUTS, "wait")

            outs[q % OUTS] = total.astype(jnp.bfloat16)
            write(q, "start")
        for k in range(count):
            send(q, stage, k).wait_send()

        @pl.when(q + SLOTS < steps)
        def _():
            for k in range(count):
                pl.semaphore_signal(
                    credits[stage].at[mine[axis]], inc=1, device_id=grid.device(axis, grid.other(axis, k)),
                    device_id_type=MESH,
                )

    def launch(q, stage):
        axis = order[stage]
        count = grid.sizes[axis] - 1

        @pl.when(q >= SLOTS)
        def _():
            for k in range(count):
                pl.semaphore_wait(credits[stage].at[grid.other(axis, k)], 1)

        for k in range(count):
            send(q, stage, k).start()

    def begin(q):
        @pl.when(q >= SLOTS)
        def _():
            pl.semaphore_wait(c_credit, 1)

        for u in range(side):
            for v in range(side):
                give(q, u, v).start()
                load(q, u, v).start()

    def stage_c(q):
        for u in range(side):
            for v in range(side):
                load(q, u, v).wait()
                give(q, u, v).wait_recv()
                own[q % held, u, v] = (
                    own[q % held, u, v].astype(jnp.float32) + rc[q % SLOTS, u, v].astype(jnp.float32)
                ).astype(jnp.bfloat16)
        for u in range(side):
            for v in range(side):
                give(q, u, v).wait_send()

        @pl.when(q + SLOTS < steps)
        def _():
            pl.semaphore_signal(c_credit, inc=1, device_id=grid.sibling, device_id_type=MESH)

        launch(q, 0)

    def stage_one(q):
        collect(q, 0)
        launch(q, 1)

    def stage_two(q):
        collect(q, 1)
        launch(q, 2)

    def stage_three(q):
        collect(q, 2)

    return (begin, stage_c, stage_one, stage_two, stage_three), write


REDUCE_REFS = 21


MOD_BLOCKS = 6 * D // LANES
IMAGE_ROWS = SEGS * MOD_BLOCKS
SENT_ROWS = -(-IMAGE_ROWS // SUBS) * SUBS
COND_STRIDE = D // LANES + 1
COND_ROWS = SEGS * COND_STRIDE
FRONT = 56
SPARE = 64
MOD_STEPS = 31
FILL_STEPS = 8
PRODUCT_STEPS = 9


def held_depth(slots):
    depth = -(-(slots * SUBS + MOD_BLOCKS - 1) // MOD_BLOCKS)
    return -(-depth // 8) * 8


def condition_rows(slots):
    return -(-(D + 8 + max(held_depth(slots) + 32, 2 * LANES)) // LANES) * LANES


def spread_modulation(s, own_ref, info_ref, wide):
    rows = own_ref.shape[0]
    count = -(-rows // FILL_STEPS // SUBS) * SUBS

    @pl.when(s == 0)
    def _():
        wide[0:FRONT, :] = jnp.zeros((FRONT, LANES), jnp.float32)
        rest = wide.shape[0] - FRONT - rows
        wide[FRONT + rows :, :] = jnp.zeros((rest, LANES), jnp.float32)

    @pl.when(s < FILL_STEPS)
    def _():
        first = pl.multiple_of(jnp.minimum(s * count, rows - count), SUBS)
        at = first + lax.broadcasted_iota(jnp.int32, (count, LANES), 0)
        values = own_ref[pl.ds(first, count), :].astype(jnp.float32)
        wide[pl.ds(pl.multiple_of(FRONT + first, 8), count), :] = jnp.where(at < info_ref[2], values, 0.0)


def wide_rows(slots):
    return FRONT + MOD_BLOCKS * (held_depth(slots) + 1) + 8


def held_columns(wide, info_ref, depth, block):
    return wide[pl.ds(FRONT + block - info_ref[1], depth, stride=MOD_BLOCKS), :].astype(jnp.bfloat16)


def gather_blocks(grid, buffer, rows, sems):
    send_v, recv_v, send_u, recv_u, send_c, recv_c = sems
    mine = grid.mine
    side = grid.side

    def one(u, v, send, recv, device):
        at = buffer.at[pl.ds(pl.multiple_of(grid.dp_of(u, v, grid.core) * rows, 8), rows)]
        return pltpu.make_async_remote_copy(
            src_ref=at, dst_ref=at, send_sem=send, recv_sem=recv, device_id=device, device_id_type=MESH
        )

    def along(axis, k):
        return grid.device(axis, grid.other(axis, k)), grid.seat(axis, grid.other(axis, k))

    def v_copies():
        found = []
        for k in range(side - 1):
            device, seat = along("v", k)
            found.append(one(mine["u"], mine["v"], send_v.at[k], recv_v.at[seat], device))
        return found

    def u_copies():
        found = []
        for k in range(side - 1):
            device, seat = along("u", k)
            for v in range(side):
                found.append(one(mine["u"], v, send_u.at[k, v], recv_u.at[seat, v], device))
        return found

    def c_copies():
        return [
            one(u, v, send_c.at[u, v], recv_c.at[u, v], grid.sibling) for u in range(side) for v in range(side)
        ]

    def start():
        for copy in v_copies():
            copy.start()

    def second():
        for k in range(side - 1):
            one(mine["u"], mine["v"], send_v.at[k], recv_v.at[k], grid.sibling).wait_recv()
        for copy in v_copies():
            copy.wait_send()
        for copy in u_copies():
            copy.start()

    def third():
        for k in range(side - 1):
            for v in range(side):
                one(mine["u"], v, send_u.at[k, v], recv_u.at[k, v], grid.sibling).wait_recv()
        for copy in u_copies():
            copy.wait_send()
        for copy in c_copies():
            copy.start()

    def finish():
        for copy in c_copies():
            copy.wait_recv()
        for copy in c_copies():
            copy.wait_send()

    return start, second, third, finish


def gather_sems(side):
    dma = pltpu.SemaphoreType.DMA
    return [dma((side - 1,))] * 2 + [dma((side - 1, side))] * 2 + [dma((side, side))] * 2


def reduce_blocks(grid, buffer, rows, refs):
    from_c, from_u, from_v, from_z, send_c, recv_c, send_u, recv_u, send_v, recv_v, send_z, recv_z = refs
    mine = grid.mine
    side = grid.side
    depth = grid.sizes["z"]

    def block(u, v, core):
        return buffer.at[pl.ds(pl.multiple_of(grid.dp_of(u, v, core) * rows, 8), rows)]

    def copy(source, target, send, recv, device):
        return pltpu.make_async_remote_copy(
            src_ref=source, dst_ref=target, send_sem=send, recv_sem=recv, device_id=device, device_id_type=MESH
        )

    def along(axis, k):
        other = grid.other(axis, k)
        return other, grid.device(axis, other), grid.seat(axis, other)

    def c_copies():
        return [
            copy(block(u, v, 1 - grid.core), from_c.at[u, v], send_c.at[u, v], recv_c.at[u, v], grid.sibling)
            for u in range(side)
            for v in range(side)
        ]

    def u_copies():
        found = []
        for k in range(side - 1):
            other, device, seat = along("u", k)
            for v in range(side):
                found.append(
                    copy(block(other, v, grid.core), from_u.at[seat, v], send_u.at[k, v], recv_u.at[seat, v], device)
                )
        return found

    def v_copies():
        found = []
        for k in range(side - 1):
            other, device, seat = along("v", k)
            found.append(
                copy(block(mine["u"], other, grid.core), from_v.at[seat], send_v.at[k], recv_v.at[seat], device)
            )
        return found

    def z_copies():
        found = []
        for k in range(depth - 1):
            _, device, _ = along("z", k)
            found.append(
                copy(block(mine["u"], mine["v"], grid.core), from_z.at[mine["z"]], send_z.at[k],
                     recv_z.at[mine["z"]], device)
            )
        return found

    def start():
        for one in c_copies():
            one.start()

    def second():
        for one in c_copies():
            one.wait_recv()
        for one in c_copies():
            one.wait_send()
        for u in range(side):
            for v in range(side):
                at = block(u, v, grid.core)
                at[...] = at[...] + from_c[u, v]
        for one in u_copies():
            one.start()

    def third():
        for k in range(side - 1):
            for v in range(side):
                copy(from_u.at[k, v], from_u.at[k, v], send_u.at[k, v], recv_u.at[k, v], grid.sibling).wait_recv()
        for one in u_copies():
            one.wait_send()
        for v in range(side):
            at = block(mine["u"], v, grid.core)
            total = at[...]
            for k in range(side - 1):
                total = total + from_u[k, v]
            at[...] = total
        for one in v_copies():
            one.start()

    def fourth():
        for k in range(side - 1):
            copy(from_v.at[k], from_v.at[k], send_v.at[k], recv_v.at[k], grid.sibling).wait_recv()
        for one in v_copies():
            one.wait_send()
        at = block(mine["u"], mine["v"], grid.core)
        total = at[...]
        for k in range(side - 1):
            total = total + from_v[k]
        at[...] = total
        from_z[mine["z"]] = total
        for one in z_copies():
            one.start()

    def finish():
        for k in range(depth - 1):
            other = grid.other("z", k)
            copy(from_z.at[other], from_z.at[other], send_z.at[k], recv_z.at[other], grid.sibling).wait_recv()
        for one in z_copies():
            one.wait_send()
        total = from_z[0]
        for z in range(1, depth):
            total = total + from_z[z]
        return total

    return start, second, third, fourth, finish


def reduce_refs(side, depth, rows):
    dma = pltpu.SemaphoreType.DMA
    f32 = jnp.float32
    return [
        pltpu.VMEM((side, side, rows, LANES), f32),
        pltpu.VMEM((side - 1, side, rows, LANES), f32),
        pltpu.VMEM((side - 1, rows, LANES), f32),
        pltpu.VMEM((depth, rows, LANES), f32),
        dma((side, side)),
        dma((side, side)),
        dma((side - 1, side)),
        dma((side - 1, side)),
        dma((side - 1,)),
        dma((side - 1,)),
        dma((depth - 1,)),
        dma((depth,)),
    ]


def modulation_stages(grid, images, slots, own_ref, info_ref, cond_ref, mod_ref, held_ref, refs):
    everyone, wide, columns, parts, square = refs[:5]
    gather = gather_blocks(grid, everyone, COND_ROWS, refs[5:11])
    reduce = reduce_blocks(grid, parts, IMAGE_ROWS, refs[11:23])
    here = grid.place
    depth = held_depth(slots)

    def run(s):
        spread_modulation(s, own_ref, info_ref, wide)

        @pl.when(s == 0)
        def _():
            everyone[pl.ds(pl.multiple_of(here * COND_ROWS, 8), COND_ROWS), :] = cond_ref[...]
            gather[0]()
            square[...] = jnp.zeros_like(square)
            held_ref[...] = jnp.zeros_like(held_ref)

        @pl.when(s == 2)
        def _():
            gather[1]()

        @pl.when(s == 4)
        def _():
            gather[2]()

        @pl.when(s == 7)
        def _():
            gather[3]()

        @pl.when(s == 8)
        def _():
            for block in range(D // LANES):
                square[0:images, :] = everyone[pl.ds(block, images, stride=COND_STRIDE), :]
                held_ref[block * LANES : (block + 1) * LANES, :] = square[...].T
            held_ref[D : D + 8, :] = (lax.broadcasted_iota(jnp.int32, (8, LANES), 0) == 0).astype(jnp.float32)
            for part in range(columns.shape[1] // LANES):
                columns[:, part * LANES : (part + 1) * LANES] = (
                    held_ref[pl.ds(info_ref[0] + part * LANES, LANES), :].T.astype(jnp.bfloat16)
                )

        at_product = s - 9

        @pl.when((at_product >= 0) & (at_product < PRODUCT_STEPS))
        def _():
            left = columns[0:images, 0:depth]
            each = MOD_BLOCKS // 2 // PRODUCT_STEPS
            for pair in range(each):
                block = (at_product * each + pair) * 2
                right = jnp.concatenate(
                    [held_columns(wide, info_ref, depth, block), held_columns(wide, info_ref, depth, block + 1)],
                    axis=1,
                )
                found = jnp.dot(left, right, preferred_element_type=jnp.float32)
                parts[pl.ds(block, images, stride=MOD_BLOCKS), :] = found[:, :LANES]
                parts[pl.ds(block + 1, images, stride=MOD_BLOCKS), :] = found[:, LANES:]

        @pl.when(s == 18)
        def _():
            reduce[0]()

        for at, stage in ((20, 1), (23, 2), (26, 3)):
            @pl.when(s == at)
            def _(stage=stage):
                reduce[stage]()

        @pl.when(s == 29)
        def _():
            mod_ref[...] = reduce[4]()

    return run


def modulation_refs(side, depth, images, slots):
    data_count = side * side * 2
    lanes = -(-held_depth(slots) // LANES) * LANES
    f32 = jnp.float32
    return (
        [
            pltpu.VMEM((data_count * COND_ROWS, LANES), f32),
            pltpu.VMEM((wide_rows(slots), LANES), f32),
            pltpu.VMEM((LANES, lanes), jnp.bfloat16),
            pltpu.VMEM((data_count * IMAGE_ROWS + SPARE, LANES), f32),
            pltpu.VMEM((LANES, LANES), f32),
        ]
        + gather_sems(side)
        + reduce_refs(side, depth, IMAGE_ROWS)
    )


def modulation_grad_stages(grid, images, slots, own_ref, info_ref, part_ref, all_ref, cond_ref, refs):
    arrived, summed, wide, around, parts, send_z, recv_z, done_sem = refs[:8]
    gather = gather_blocks(grid, summed, IMAGE_ROWS, refs[8:14])
    reduce = reduce_blocks(grid, parts, COND_ROWS, refs[14:26])
    mine = grid.mine
    sizes = grid.sizes["z"]
    here = pl.ds(pl.multiple_of(grid.place * IMAGE_ROWS, 8), IMAGE_ROWS)
    depth = held_depth(slots)

    def to_z(k):
        return pltpu.make_async_remote_copy(
            src_ref=part_ref, dst_ref=arrived.at[mine["z"]], send_sem=send_z.at[k], recv_sem=recv_z.at[mine["z"]],
            device_id=grid.device("z", grid.other("z", k)), device_id_type=MESH,
        )

    def done():
        return pltpu.make_async_copy(summed.at[pl.ds(0, all_ref.shape[0])], all_ref, done_sem)

    def run(s):
        spread_modulation(s, own_ref, info_ref, wide)

        @pl.when(s == 0)
        def _():
            for k in range(sizes - 1):
                to_z(k).start()
            arrived[mine["z"]] = part_ref[...]
            around[...] = jnp.zeros_like(around)
            parts[...] = jnp.zeros_like(parts)

        @pl.when(s == 2)
        def _():
            for k in range(sizes - 1):
                other = grid.other("z", k)
                pltpu.make_async_remote_copy(
                    src_ref=part_ref, dst_ref=arrived.at[other], send_sem=send_z.at[k], recv_sem=recv_z.at[other],
                    device_id=grid.sibling, device_id_type=MESH,
                ).wait_recv()
            for k in range(sizes - 1):
                to_z(k).wait_send()
            total = arrived[0].astype(jnp.float32)
            for z in range(1, sizes):
                total = total + arrived[z].astype(jnp.float32)
            summed[here, :] = total.astype(jnp.bfloat16).astype(jnp.float32)[:IMAGE_ROWS]
            gather[0]()

        @pl.when(s == 4)
        def _():
            gather[1]()

        @pl.when(s == 6)
        def _():
            gather[2]()

        @pl.when(s == 9)
        def _():
            gather[3]()
            done().start()

        at_product = s - 10

        @pl.when((at_product >= 0) & (at_product < PRODUCT_STEPS))
        def _():
            total = around[D + 8 : D + 8 + depth, 0:images]
            each = MOD_BLOCKS // 2 // PRODUCT_STEPS
            for pair in range(each):
                block = (at_product * each + pair) * 2
                left = jnp.concatenate(
                    [held_columns(wide, info_ref, depth, block), held_columns(wide, info_ref, depth, block + 1)],
                    axis=1,
                )
                right = jnp.concatenate(
                    [
                        summed[pl.ds(block + more, images, stride=MOD_BLOCKS), :].astype(jnp.bfloat16)
                        for more in (0, 1)
                    ],
                    axis=1,
                )
                total = total + lax.dot_general(
                    left, right, (((1,), (1,)), ((), ())), preferred_element_type=jnp.float32
                )
            around[D + 8 : D + 8 + depth, 0:images] = total

        @pl.when(s == 19)
        def _():
            for block in range(D // LANES):
                piece = around[pl.ds(D + 8 - info_ref[0] + block * LANES, LANES), :].T
                parts[pl.ds(block, images, stride=COND_STRIDE), :] = piece[0:images, :]
            reduce[0]()

        for at, stage in ((21, 1), (24, 2), (27, 3)):
            @pl.when(s == at)
            def _(stage=stage):
                reduce[stage]()

        @pl.when(s == 30)
        def _():
            cond_ref[...] = reduce[4]()
            done().wait()

    return run


MOD_GRAD_REFS = 26


def modulation_grad_refs(side, depth, images, slots):
    data_count = side * side * 2
    dma = pltpu.SemaphoreType.DMA
    f32 = jnp.float32
    return (
        [
            pltpu.VMEM((depth, SENT_ROWS, LANES), jnp.bfloat16),
            pltpu.VMEM((data_count * IMAGE_ROWS + SPARE, LANES), f32),
            pltpu.VMEM((wide_rows(slots), LANES), f32),
            pltpu.VMEM((2 * (D + 8) + held_depth(slots), LANES), f32),
            pltpu.VMEM((data_count * COND_ROWS, LANES), f32),
            dma((depth - 1,)),
            dma((depth,)),
            dma,
        ]
        + gather_sems(side)
        + reduce_refs(side, depth, COND_ROWS)
    )


def reduce_body(side, depth, plan, slots, parts_ref, part_ref, own_ref, info_ref, out_ref, all_ref, cond_ref,
                *refs):
    hosts, share, kept, steps, parts = plan
    grid = Grid(side, depth)
    hosting = Hosting(grid, 2 * side * side * depth, hosts, share, kept, slots - kept) if hosts else None
    grid.greet(hosting)
    passed = refs[-1]
    modulation_step = modulation_grad_stages(
        grid, 2 * side * side * SEGS, slots, own_ref, info_ref, part_ref, all_ref, cond_ref, refs[:MOD_GRAD_REFS]
    )
    refs = refs[MOD_GRAD_REFS:]
    streams = []
    writes = []
    first = 0
    for number, (order, part) in enumerate(zip(ORDERS, parts)):
        span = part * SUBS
        stages, write = reduce_stream(
            grid, order, first, span, steps, parts_ref, out_ref,
            refs[REDUCE_REFS * number : REDUCE_REFS * (number + 1)], hosting, passed,
        )
        streams.append(stages)
        writes.append(write)
        first = first + steps * span

    def round_trip(s, carry):
        for late in range(4, -1, -1):
            q = s - LAG * late

            @pl.when((q >= 0) & (q < steps))
            def _(late=late, q=q):
                for stream in streams:
                    stream[late](q)

        modulation_step(s)
        return carry

    lax.fori_loop(0, max(steps + 4 * LAG, MOD_STEPS), round_trip, 0)
    for write in writes:
        for q in range(max(steps - OUTS, 0), steps):
            write(q, "wait")
    if hosting is not None:
        @pl.when(jnp.logical_not(hosting.is_host))
        def _():
            at = out_ref.at[pl.ds(kept * SUBS, (slots - kept) * SUBS)]
            pltpu.make_async_remote_copy(
                src_ref=at, dst_ref=at, send_sem=passed, recv_sem=passed, device_id=grid.sibling,
                device_id_type=MESH,
            ).wait_recv()


def reduce_slots(grads, mod_part, own, info, slots, data_count, seq_count):
    side = math.isqrt(data_count // 2)
    plan = host_plan(slots, data_count * seq_count, seq_count)
    kept, parts = plan[2], plan[4]
    held = HELD
    dma = pltpu.SemaphoreType.DMA
    regular = pltpu.SemaphoreType.REGULAR
    bf16 = jnp.bfloat16
    f32 = jnp.float32
    scratch = modulation_grad_refs(side, seq_count, data_count * SEGS, slots)
    for order, part in zip(ORDERS, parts):
        span = part * SUBS
        sizes = {"u": side, "v": side, "z": seq_count}
        left = dict(sizes)
        scratch.append(pltpu.VMEM((held, side, side, seq_count, span, LANES), bf16))
        scratch.append(pltpu.VMEM((SLOTS, side, side, seq_count, span, LANES), bf16))
        for axis in order:
            del left[axis]
            rest = tuple(left[name] for name in ("u", "v", "z") if name in left)
            scratch.append(pltpu.VMEM((SLOTS, sizes[axis] - 1) + rest + (span, LANES), bf16))
        scratch.append(pltpu.VMEM((OUTS, span, LANES), bf16))
        scratch.append(dma((held, side, side)))
        scratch.append(dma((OUTS,)))
        scratch.append(dma((OUTS,)))
        scratch.append(dma((SLOTS, side, side)))
        scratch.append(dma((SLOTS, side, side)))
        for axis in order:
            scratch.append(dma((SLOTS, sizes[axis] - 1)))
            scratch.append(dma((SLOTS, sizes[axis] - 1)))
        scratch.append(regular)
        for axis in order:
            scratch.append(regular((sizes[axis],)))
    scratch.append(dma)
    return pl.pallas_call(
        partial(reduce_body, side, seq_count, plan, slots),
        out_shape=(
            jax.ShapeDtypeStruct((slots * SUBS, LANES), bf16),
            jax.ShapeDtypeStruct((data_count * IMAGE_ROWS, LANES), f32),
            jax.ShapeDtypeStruct((COND_ROWS, LANES), f32),
        ),
        in_specs=[
            pl.BlockSpec(memory_space=pl.ANY),
            pl.BlockSpec(memory_space=pltpu.VMEM),
            pl.BlockSpec(memory_space=pltpu.VMEM),
            pl.BlockSpec(memory_space=pltpu.SMEM),
        ],
        out_specs=(
            pl.BlockSpec(memory_space=pl.ANY),
            pl.BlockSpec(memory_space=pl.ANY),
            pl.BlockSpec(memory_space=pltpu.VMEM),
        ),
        scratch_shapes=scratch,
        compiler_params=pltpu.CompilerParams(
            collective_id=1, has_side_effects=True, vmem_limit_bytes=VMEM_LIMIT
        ),
        name="reduce_slots",
    )(grads.reshape(data_count, seq_count, kept * SUBS, LANES), mod_part, own, info)


UPDATE_TILES = 72


def update_body(mod_depth, own_ref, reduced, cond_ref, mod_ref, master, first, second,
                new_master, new_first, new_second, mod_rows, wide):
    step = pl.program_id(0)
    mod_blocks = 6 * D // LANES
    start_row = own_ref[0] * SUBS
    shift = lax.rem(start_row, mod_blocks)
    tiles = UPDATE_TILES
    piece = 9

    @pl.when((step == 0) & (start_row < MOD_ROWS))
    def _():
        images = cond_ref.shape[1]
        for begin in range(0, mod_blocks, piece):
            grads = [
                mod_ref[pl.ds(begin + block, images, stride=mod_blocks), :].astype(jnp.bfloat16)
                for block in range(piece)
            ]
            part = jnp.dot(
                cond_ref[...], jnp.concatenate(grads, axis=1), preferred_element_type=jnp.float32
            )
            for block in range(piece):
                mod_rows[pl.ds(begin + block, mod_depth, stride=mod_blocks), :] = part[
                    :, block * LANES : (block + 1) * LANES
                ]

    wide[...] = reduced[...].astype(jnp.float32)
    corr_one = 1.0 - beta_one**STEP
    corr_two = 1.0 - beta_two**STEP
    local = step * tiles + lax.broadcasted_iota(jnp.int32, (tiles, LANES), 0)
    used = local < own_ref[1]
    for sub in range(SUBS):
        columns = pl.ds(sub * LANES, LANES)
        from_mod = mod_rows[pl.ds(shift + step * tiles * SUBS + sub, tiles, stride=SUBS), :]
        is_mod = start_row + local * SUBS + sub < MOD_ROWS
        grad = jnp.where(is_mod, from_mod, wide[pl.ds(sub, tiles, stride=SUBS), :])
        grad = jnp.where(used, grad, 0.0)
        one = beta_one * first[:, columns] + (1.0 - beta_one) * grad
        two = beta_two * second[:, columns] + (1.0 - beta_two) * grad * grad
        held = master[:, columns]
        new_first[:, columns] = one
        new_second[:, columns] = two
        new_master[:, columns] = held - learn_rate * (
            one / corr_one / (jnp.sqrt(two / corr_two) + adam_eps) + weight_decay * held
        )


def own_conditions(held, info, images, slots):
    steps = -(-slots // UPDATE_TILES)
    depth = -(-(steps * UPDATE_TILES * SUBS + MOD_BLOCKS) // MOD_BLOCKS)
    depth = -(-depth // 8) * 8
    return lax.dynamic_slice(held, (info[0], jnp.int32(0)), (depth, images)).astype(jnp.bfloat16)


def update(reduced, cond_own, mod_all, own_first, master, first, second):
    slots, tile_len = master.shape
    mod_depth, images = cond_own.shape
    tiles = UPDATE_TILES
    steps = -(-slots // tiles)
    wide_block = pl.BlockSpec((tiles, tile_len), lambda i, *_: (i, 0))
    return pl.pallas_call(
        partial(update_body, mod_depth),
        out_shape=(jax.ShapeDtypeStruct(master.shape, jnp.float32),) * 3,
        grid_spec=pltpu.PrefetchScalarGridSpec(
            num_scalar_prefetch=1,
            grid=(steps,),
            in_specs=[
                pl.BlockSpec((tiles * SUBS, LANES), lambda i, *_: (i, 0)),
                pl.BlockSpec((mod_depth, images), lambda i, *_: (0, 0)),
                pl.BlockSpec(mod_all.shape, lambda i, *_: (0, 0)),
                wide_block,
                wide_block,
                wide_block,
            ],
            out_specs=(wide_block,) * 3,
            scratch_shapes=[
                pltpu.VMEM(((mod_depth + 1) * MOD_BLOCKS, LANES), jnp.float32),
                pltpu.VMEM((tiles * SUBS, LANES), jnp.float32),
            ],
        ),
        compiler_params=pltpu.CompilerParams(vmem_limit_bytes=VMEM_LIMIT),
        name="update",
    )(own_first, reduced, cond_own, mod_all, master, first, second)


def normalize(values):
    centred = values - jnp.mean(values, axis=-1, keepdims=True)
    spread = jnp.mean(centred * centred, axis=-1, keepdims=True)
    return centred * lax.rsqrt(spread + ln_eps)


def cosine_of(target, projected):
    inner_mean = jnp.mean(projected * target, axis=-1)
    return (
        inner_mean
        * lax.rsqrt(jnp.mean(projected * projected, axis=-1) + cos_eps)
        * lax.rsqrt(jnp.mean(target * target, axis=-1) + cos_eps)
    )


def gelu_tanh(values):
    return jax.nn.gelu(values, approximate=True)


def lane_pad(width):
    return -(-width // LANES) * LANES


def regroup_body(moves, fill, x_ref, out_ref):
    if fill is not None:
        start, width = fill
        for group in range(out_ref.shape[0]):
            out_ref[group, :, start : start + width] = jnp.zeros((out_ref.shape[1], width), out_ref.dtype)
    for from_group, start, to_group, target, width in moves:
        if from_group is None:
            values = x_ref[:, start : start + width]
        else:
            values = x_ref[from_group, :, start : start + width]
        if to_group is None:
            out_ref[:, target : target + width] = values
        else:
            out_ref[to_group, :, target : target + width] = values


def split_groups(x, parts, groups):
    tokens, total = x.shape
    width = total // parts // groups
    padded = lane_pad(parts * width)
    moves = [
        (None, (part * groups + group) * width, group, part * width, width)
        for group in range(groups)
        for part in range(parts)
    ]
    fill = (parts * width, padded - parts * width) if padded > parts * width else None
    return pl.pallas_call(
        partial(regroup_body, moves, fill),
        out_shape=jax.ShapeDtypeStruct((groups, tokens, padded), x.dtype),
        compiler_params=pltpu.CompilerParams(vmem_limit_bytes=VMEM_LIMIT),
        name="split_groups_%d" % parts,
    )(x)


def join_groups(x, parts, width):
    groups, tokens, _ = x.shape
    moves = [
        (group, part * width, None, (part * groups + group) * width, width)
        for group in range(groups)
        for part in range(parts)
    ]
    return pl.pallas_call(
        partial(regroup_body, moves, None),
        out_shape=jax.ShapeDtypeStruct((tokens, parts * groups * width), x.dtype),
        compiler_params=pltpu.CompilerParams(vmem_limit_bytes=VMEM_LIMIT),
        name="join_groups_%d" % parts,
    )(x)


QUERY_BLOCK = 1024


def key_bias(seg_col, pad_col, seg_row, first):
    keys = seg_col.shape[0]
    queries = seg_row.shape[1]
    key_at = lax.broadcasted_iota(jnp.int32, (keys, queries), 0)
    query_at = first + lax.broadcasted_iota(jnp.int32, (keys, queries), 1)
    allowed = (seg_col == seg_row) & ((pad_col == 1) | (key_at == query_at))
    return jnp.where(allowed, 0.0, -1e30)


def spread_heads(rows_ref, held, heads):
    held[...] = jnp.zeros_like(held)
    for part in range(held.shape[0]):
        for head in range(heads):
            start = (part * heads + head) * HEAD_DIM
            held[part, head, :, 0:HEAD_DIM] = rows_ref[:, start : start + HEAD_DIM]


def probabilities(held, head, block, bias):
    scores = lax.dot_general(
        held[1, head], held[0, head, block, :], (((1,), (1,)), ((), ())), preferred_element_type=jnp.float32
    )
    scores = scores + bias
    shifted = jnp.exp2((scores - jnp.max(scores, axis=0, keepdims=True)) * (HEAD_DIM ** (-0.5) * math.log2(math.e)))
    return shifted * (1.0 / jnp.sum(shifted, axis=0, keepdims=True))


def attention_body(heads, rows_ref, seg_col, pad_col, seg_row, out_ref, held):
    step = pl.program_id(0)

    @pl.when(step == 0)
    def _():
        spread_heads(rows_ref, held, heads)

    first = pl.multiple_of(step * QUERY_BLOCK, QUERY_BLOCK)
    block = pl.ds(first, QUERY_BLOCK)
    bias = key_bias(seg_col[...], pad_col[...], seg_row[...], first)
    rest = out_ref.shape[1] - heads * HEAD_DIM
    if rest:
        out_ref[:, heads * HEAD_DIM :] = jnp.zeros((QUERY_BLOCK, rest), jnp.bfloat16)
    for head in range(heads):
        probs = probabilities(held, head, block, bias).astype(jnp.bfloat16)
        result = lax.dot_general(
            held[2, head], probs, (((0,), (0,)), ((), ())), preferred_element_type=jnp.float32
        )
        out_ref[:, head * HEAD_DIM : (head + 1) * HEAD_DIM] = result.T[:, :HEAD_DIM].astype(jnp.bfloat16)


def attention(rows, segments, padding, heads):
    length = rows.shape[0]
    whole = pl.BlockSpec((length, 1), lambda i: (0, 0))
    return pl.pallas_call(
        partial(attention_body, heads),
        out_shape=jax.ShapeDtypeStruct((length, lane_pad(heads * HEAD_DIM)), jnp.bfloat16),
        grid=(length // QUERY_BLOCK,),
        in_specs=[
            pl.BlockSpec(rows.shape, lambda i: (0, 0)),
            whole,
            whole,
            pl.BlockSpec((1, QUERY_BLOCK), lambda i: (0, i)),
        ],
        out_specs=pl.BlockSpec((QUERY_BLOCK, lane_pad(heads * HEAD_DIM)), lambda i: (i, 0)),
        scratch_shapes=[pltpu.VMEM((3, heads, length, LANES), jnp.bfloat16)],
        compiler_params=pltpu.CompilerParams(vmem_limit_bytes=VMEM_LIMIT),
        name="attention",
    )(rows, segments.reshape(length, 1), padding.reshape(length, 1), segments.reshape(1, length))


def attention_grad_body(heads, rows_ref, grad_ref, seg_col, pad_col, seg_row, out_ref, held, given, grad_k, grad_v):
    step = pl.program_id(0)
    scaling = HEAD_DIM ** (-0.5)

    @pl.when(step == 0)
    def _():
        spread_heads(rows_ref, held, heads)
        given[...] = jnp.zeros_like(given)
        grad_k[...] = jnp.zeros_like(grad_k)
        grad_v[...] = jnp.zeros_like(grad_v)
        out_ref[...] = jnp.zeros_like(out_ref)

    first = pl.multiple_of(step * QUERY_BLOCK, QUERY_BLOCK)
    block = pl.ds(first, QUERY_BLOCK)
    bias = key_bias(seg_col[...], pad_col[...], seg_row[...], first)
    for head in range(heads):
        given[:, 0:HEAD_DIM] = grad_ref[:, head * HEAD_DIM : (head + 1) * HEAD_DIM]
        upstream = given[...]
        probs = probabilities(held, head, block, bias)
        grad_v[head] += jnp.dot(probs.astype(jnp.bfloat16), upstream, preferred_element_type=jnp.float32)
        grad_probs = lax.dot_general(
            held[2, head], upstream, (((1,), (1,)), ((), ())), preferred_element_type=jnp.float32
        )
        inner = jnp.sum(probs * grad_probs, axis=0, keepdims=True)
        grad_scores = (probs * (grad_probs - inner)).astype(jnp.bfloat16)
        grad_k[head] += jnp.dot(grad_scores, held[0, head, block, :], preferred_element_type=jnp.float32)
        grad_q = lax.dot_general(
            held[1, head], grad_scores, (((0,), (0,)), ((), ())), preferred_element_type=jnp.float32
        )
        out_ref[block, head * HEAD_DIM : (head + 1) * HEAD_DIM] = (
            grad_q.T[:, :HEAD_DIM] * scaling
        ).astype(jnp.bfloat16)

    @pl.when(step == pl.num_programs(0) - 1)
    def _():
        for head in range(heads):
            start = (heads + head) * HEAD_DIM
            out_ref[:, start : start + HEAD_DIM] = (grad_k[head][:, :HEAD_DIM] * scaling).astype(jnp.bfloat16)
            start = (2 * heads + head) * HEAD_DIM
            out_ref[:, start : start + HEAD_DIM] = grad_v[head][:, :HEAD_DIM].astype(jnp.bfloat16)


def attention_grad(rows, grad, segments, padding, heads):
    length = rows.shape[0]
    whole = pl.BlockSpec((length, 1), lambda i: (0, 0))
    return pl.pallas_call(
        partial(attention_grad_body, heads),
        out_shape=jax.ShapeDtypeStruct(rows.shape, jnp.bfloat16),
        grid=(length // QUERY_BLOCK,),
        in_specs=[
            pl.BlockSpec(rows.shape, lambda i: (0, 0)),
            pl.BlockSpec((QUERY_BLOCK, grad.shape[1]), lambda i: (i, 0)),
            whole,
            whole,
            pl.BlockSpec((1, QUERY_BLOCK), lambda i: (0, i)),
        ],
        out_specs=pl.BlockSpec(rows.shape, lambda i: (0, 0)),
        scratch_shapes=[
            pltpu.VMEM((3, heads, length, LANES), jnp.bfloat16),
            pltpu.VMEM((QUERY_BLOCK, LANES), jnp.bfloat16),
            pltpu.VMEM((heads, length, LANES), jnp.float32),
            pltpu.VMEM((heads, length, LANES), jnp.float32),
        ],
        compiler_params=pltpu.CompilerParams(vmem_limit_bytes=VMEM_LIMIT),
        name="attention_grad",
    )(rows, grad, segments.reshape(length, 1), padding.reshape(length, 1), segments.reshape(1, length))


def shards(
    tokens,
    conditions,
    segment_ids,
    padding,
    targets,
    cotangent,
    tile_counts,
    master,
    first_moment,
    second_moment,
):
    seq_count = lax.axis_size("seq")
    data_count = lax.axis_size("dp")
    seq_place = lax.axis_index("seq")
    data_place = lax.axis_index("dp")
    owners = data_count * seq_count
    slot_count, tile_len = master.shape
    own_rows = slot_count * SUBS
    tile_ends = jnp.cumsum(tile_counts)
    starts = jnp.concatenate([jnp.zeros((1,), jnp.int32), tile_ends.astype(jnp.int32)])
    spans = jnp.asarray(chunk_spans()[0], jnp.int32)
    firsts = jnp.sum((tile_ends[None, :] <= spans[:, :1]).astype(jnp.int32), axis=1)
    lasts = jnp.sum((tile_ends[None, :] <= spans[:, 1:]).astype(jnp.int32), axis=1)
    plan = host_plan(slot_count, owners, seq_count)
    guests = jnp.asarray(
        guest_places((*plan[:3], slot_count - plan[2]), owners, seq_count), jnp.int32
    )
    edge_ids = jnp.asarray(EDGE_TILES, jnp.int32)
    edge_owner = jnp.sum((tile_ends[None, :] <= edge_ids[:, None]).astype(jnp.int32), axis=1)
    edge_within = edge_ids - jnp.take(starts, edge_owner)
    edge_places = edge_owner * plan[2] + edge_within
    if plan[0]:
        edge_places = jnp.where(
            edge_within < plan[2], edge_places, jnp.take(guests, edge_owner) + edge_within - plan[2]
        )
    own_place = data_place * seq_count + seq_place
    own_start = lax.dynamic_index_in_dim(starts, own_place, 0, False)
    own_count = lax.dynamic_index_in_dim(tile_counts, own_place, 0, False)
    own_low = master.astype(jnp.bfloat16).reshape(own_rows, LANES)
    info = jnp.stack(
        [
            jnp.minimum(own_start * SUBS // MOD_BLOCKS, D + 1),
            own_start * SUBS % MOD_BLOCKS,
            jnp.clip(jnp.minimum(own_count * SUBS, MOD_ROWS - own_start * SUBS), 0, own_rows),
        ]
    ).astype(jnp.int32)
    images = data_count * SEGS

    own_first = jnp.stack([own_start, own_count])
    cond_f = conditions.astype(jnp.float32)
    cond_act, silu_cond_back = jax.vjp(jax.nn.silu, cond_f)
    cond_low = cond_act.astype(jnp.bfloat16)
    cond_rows = jnp.pad(cond_low[0].astype(jnp.float32), ((0, 0), (0, LANES))).reshape(COND_ROWS, LANES)
    packed, modulation, cond_held = gather_slots(own_low, cond_rows, info, slot_count, data_count, seq_count)
    modulation = modulation.reshape(1, SEGS, 6 * D)
    weights = {
        index: unpack_weight(index, packed, plan, firsts, lasts, starts, guests)
        for index in (2, 5, 7, 9, 11)
    }
    attend_weight, output_weight, hidden_weight, return_weight, proj_one = (
        weights[index] for index in (2, 5, 7, 9, 11)
    )
    edges = edge_read(packed, edge_places)
    edge_flat = edges.reshape(-1)

    def bias(index):
        row = param_rows()[index]
        at = EDGE_TILES.index(row // SUBS) * SUBS + row % SUBS
        return edge_flat[at * LANES : at * LANES + param_shapes()[index][0]]

    query_bias, value_bias, output_bias, hidden_bias, return_bias = (bias(i) for i in (3, 4, 6, 8, 10))
    proj_bias_one, proj_bias_two, proj_bias_three = (bias(i) for i in (12, 14, 16))
    rows_dev, local_len, model_width = tokens.shape
    full_len = segment_ids.shape[1]
    heads_local = HEADS // seq_count
    group_width = model_width // seq_count
    token_start = seq_place * local_len
    local_seg = lax.dynamic_slice_in_dim(segment_ids, token_start, local_len, 1)
    local_pad = lax.dynamic_slice_in_dim(padding, token_start, local_len, 1).astype(jnp.float32)
    onehot = (local_seg[:, :, None] == jnp.arange(SEGS, dtype=jnp.int32)).astype(jnp.float32)
    per_token = jnp.einsum("rts,rsc->rtc", onehot, modulation, precision=lax.Precision.HIGH)
    shift_one, scale_one, gate_one, shift_two, scale_two, gate_two = jnp.split(
        per_token, 6, axis=-1
    )
    token_f = tokens.astype(jnp.float32)
    normed_one, norm_back_one = jax.vjp(normalize, token_f)
    attend_in = (normed_one * (1.0 + scale_one) + shift_one).astype(jnp.bfloat16)
    triple_bias = jnp.concatenate([query_bias, jnp.zeros_like(query_bias), value_bias])
    triple = (
        jnp.einsum("rtd,dc->rtc", attend_in, attend_weight, preferred_element_type=jnp.float32)
        + triple_bias
    )
    triple_low = split_groups(triple[0].astype(jnp.bfloat16), 3, seq_count)
    head_rows = lax.all_to_all(triple_low, "seq", split_axis=0, concat_axis=0, tiled=True)
    (head_rows, output_weight, hidden_weight, return_weight, proj_one) = lax.optimization_barrier(
        (head_rows, output_weight, hidden_weight, return_weight, proj_one)
    )
    head_rows = head_rows.reshape(full_len, head_rows.shape[-1])
    head_attended = attention(head_rows, segment_ids[0], padding[0], heads_local)
    head_attended = head_attended.reshape(seq_count, local_len, head_attended.shape[-1])
    head_attended, packed = lax.optimization_barrier((head_attended, packed))
    proj_two, proj_three = (unpack_weight(index, packed, plan, firsts, lasts, starts, guests) for index in (13, 15))
    attended = lax.all_to_all(head_attended, "seq", split_axis=0, concat_axis=0, tiled=True)
    attended, proj_two, proj_three = lax.optimization_barrier((attended, proj_two, proj_three))
    attended = join_groups(attended, 1, group_width)[None]
    branch_one = (
        jnp.einsum("rtd,dc->rtc", attended, output_weight, preferred_element_type=jnp.float32)
        + output_bias
    )
    middle = token_f + gate_one * branch_one
    normed_two, norm_back_two = jax.vjp(normalize, middle)
    mlp_in = (normed_two * (1.0 + scale_two) + shift_two).astype(jnp.bfloat16)
    hidden = (
        jnp.einsum("rtd,df->rtf", mlp_in, hidden_weight, preferred_element_type=jnp.float32)
        + hidden_bias
    )
    activated_f, gelu_back = jax.vjp(gelu_tanh, hidden)
    activated = activated_f.astype(jnp.bfloat16)
    branch_two = (
        jnp.einsum("rtf,fd->rtd", activated, return_weight, preferred_element_type=jnp.float32)
        + return_bias
    )
    result = middle + gate_two * branch_two
    feature = result.astype(jnp.bfloat16)
    first_pre = (
        jnp.einsum("rtd,dp->rtp", feature, proj_one, preferred_element_type=jnp.float32)
        + proj_bias_one
    )
    first_act, first_back = jax.vjp(jax.nn.silu, first_pre)
    first_low = first_act.astype(jnp.bfloat16)
    second_pre = (
        jnp.einsum("rtp,pc->rtc", first_low, proj_two, preferred_element_type=jnp.float32)
        + proj_bias_two
    )
    second_act, second_back = jax.vjp(jax.nn.silu, second_pre)
    second_low = second_act.astype(jnp.bfloat16)
    projected = (
        jnp.einsum("rtc,co->rto", second_low, proj_three, preferred_element_type=jnp.float32)
        + proj_bias_three
    )
    target_f = targets.astype(jnp.float32)
    cosine, cosine_back = jax.vjp(partial(cosine_of, target_f), projected)
    ends = {}

    def put(buffer, index, left, right):
        buffer, ends[index] = weight_grad(
            index,
            left.reshape(-1, left.shape[-1]),
            right.reshape(-1, right.shape[-1]),
            buffer,
            owners,
            slot_count,
            firsts,
            lasts,
            starts,
            guests,
            (plan[0], plan[2]),
        )
        return buffer

    def summed(grad):
        return jnp.sum(grad.astype(jnp.float32), axis=(0, 1))

    (grad_projected,) = cosine_back(local_pad * -repa_weight)
    grad_projected = grad_projected.astype(jnp.bfloat16)
    sum_sixteen = summed(grad_projected)
    (grad_second,) = second_back(
        jnp.einsum("rto,co->rtc", grad_projected, proj_three, preferred_element_type=jnp.float32)
    )
    grad_second = grad_second.astype(jnp.bfloat16)
    sum_fourteen = summed(grad_second)
    (grad_first,) = first_back(
        jnp.einsum("rtc,pc->rtp", grad_second, proj_two, preferred_element_type=jnp.float32)
    )
    grad_first = grad_first.astype(jnp.bfloat16)
    sum_twelve = summed(grad_first)
    grad_result = cotangent + jnp.einsum(
        "rtp,dp->rtd", grad_first, proj_one, preferred_element_type=jnp.float32
    )
    grad_gate_two = grad_result * branch_two
    grad_branch_two = (grad_result * gate_two).astype(jnp.bfloat16)
    sum_ten = summed(grad_branch_two)
    (grad_hidden,) = gelu_back(
        jnp.einsum(
            "rtd,fd->rtf", grad_branch_two, return_weight, preferred_element_type=jnp.float32
        )
    )
    grad_hidden = grad_hidden.astype(jnp.bfloat16)
    sum_eight = summed(grad_hidden)
    grad_mlp_in = jnp.einsum(
        "rtf,df->rtd", grad_hidden, hidden_weight, preferred_element_type=jnp.float32
    )
    grad_scale_two = grad_mlp_in * normed_two
    (grad_through_two,) = norm_back_two(grad_mlp_in * (1.0 + scale_two))
    grad_middle = grad_result + grad_through_two
    grad_gate_one = grad_middle * branch_one
    grad_branch_one = (grad_middle * gate_one).astype(jnp.bfloat16)
    sum_six = summed(grad_branch_one)
    grad_attended = jnp.einsum(
        "rtc,dc->rtd", grad_branch_one, output_weight, preferred_element_type=jnp.float32
    ).astype(jnp.bfloat16)
    grad_attended = split_groups(grad_attended[0], 1, seq_count)
    grad_attended, second_low = lax.optimization_barrier((grad_attended, second_low))
    head_grad = lax.all_to_all(grad_attended, "seq", split_axis=0, concat_axis=0, tiled=True)
    grad_buffer = put(None, 15, second_low, grad_projected)
    grad_buffer = put(grad_buffer, 13, first_low, grad_second)
    head_grad, grad_buffer = lax.optimization_barrier((head_grad, grad_buffer))
    grad_triple_heads = attention_grad(
        head_rows, head_grad.reshape(full_len, head_grad.shape[-1]), segment_ids[0], padding[0], heads_local
    ).reshape(seq_count, local_len, head_rows.shape[-1])
    grad_triple_heads, grad_buffer, cond_held = lax.optimization_barrier(
        (grad_triple_heads, grad_buffer, cond_held)
    )
    grad_triple = lax.all_to_all(grad_triple_heads, "seq", split_axis=0, concat_axis=0, tiled=True)
    grad_buffer = put(grad_buffer, 11, feature, grad_first)
    grad_buffer = put(grad_buffer, 9, activated, grad_branch_two)
    grad_buffer = put(grad_buffer, 7, mlp_in, grad_hidden)
    grad_buffer = put(grad_buffer, 5, attended, grad_branch_one)
    cond_own = own_conditions(cond_held, info, images, slot_count)
    grad_triple, grad_buffer, cond_own = lax.optimization_barrier((grad_triple, grad_buffer, cond_own))
    grad_triple = join_groups(grad_triple, 3, group_width)[None]
    grad_buffer = put(grad_buffer, 2, attend_in, grad_triple)
    triple_sums = summed(grad_triple)
    grad_attend_in = jnp.einsum(
        "rtc,dc->rtd", grad_triple, attend_weight, preferred_element_type=jnp.float32
    )
    grad_scale_one = grad_attend_in * normed_one
    (grad_through_one,) = norm_back_one(grad_attend_in * (1.0 + scale_one))
    grad_tokens = grad_middle + grad_through_one
    token_mod_grad = jnp.concatenate(
        [grad_attend_in, grad_scale_one, grad_gate_one, grad_mlp_in, grad_scale_two, grad_gate_two],
        axis=-1,
    )
    mod_part = jnp.einsum("rts,rtc->rsc", onehot, token_mod_grad, precision=lax.Precision.HIGH)
    mod_sent = jnp.pad(
        mod_part.astype(jnp.bfloat16).reshape(IMAGE_ROWS, LANES), ((0, SENT_ROWS - IMAGE_ROWS), (0, 0))
    )
    rows_at = param_rows()

    def rows(vector):
        return vector.reshape(-1, LANES)


    def head(index):
        return (0, ends[index], rows_at[index] % SUBS, SUBS)

    def tail(index):
        return (0, ends[index], SUBS, SUBS + rows_at[index] % SUBS)

    def whole(vector):
        return (0, rows(vector), 0, vector.shape[0] // LANES)

    pieces = [
        (6,) + head(2)[1:],
        tail(2),
        whole(triple_sums[:model_width]),
        whole(triple_sums[2 * model_width :]),
        head(5),
        tail(5),
        whole(sum_six),
        head(7),
        tail(7),
        whole(sum_eight),
        head(9),
        tail(9),
        whole(sum_ten),
        head(11),
        tail(11),
        whole(sum_twelve),
        head(13),
        tail(13),
        whole(sum_fourteen),
        head(15),
        tail(15),
        whole(sum_sixteen),
    ]
    grad_buffer = edge_write(pieces, grad_buffer, edge_places[EDGE_TILES.index(3891) :])
    reduced, mod_all, cond_grad = reduce_slots(
        grad_buffer, mod_sent, own_low, info, slot_count, data_count, seq_count
    )
    (grad_conditions,) = silu_cond_back(cond_grad.reshape(1, SEGS, COND_STRIDE * LANES)[:, :, :D])
    new_master, new_first, new_second = update(
        reduced, cond_own, mod_all, own_first, master, first_moment, second_moment
    )
    return (
        result.astype(jnp.bfloat16),
        grad_tokens,
        grad_conditions,
        new_master,
        new_first,
        new_second,
    )


def solution(mesh):
    return jax.shard_map(
        shards,
        mesh=mesh,
        in_specs=(
            P("dp", "seq", None),
            P("dp", None, None),
            P("dp", None),
            P("dp", None),
            P("dp", "seq", None),
            P("dp", "seq", None),
            P(),
            P(("dp", "seq"), None),
            P(("dp", "seq"), None),
            P(("dp", "seq"), None),
        ),
        out_specs=(
            P("dp", "seq", None),
            P("dp", "seq", None),
            P("dp", None, None),
            P(("dp", "seq"), None),
            P(("dp", "seq"), None),
            P(("dp", "seq"), None),
        ),
        check_vma=False,
    )
```

```python
from functools import partial
import math

import jax
import jax.numpy as jnp
from jax import lax
from jax.experimental import pallas as pl
from jax.experimental.pallas import tpu as pltpu
from jax.sharding import PartitionSpec as P

HEADS = 16
HEAD_DIM = 72
D = 1152
FF = 4608
PROJ = 2048
TARGET = 768
SEGS = 4
STEP = 10
TILES = 15643


ln_eps = 1e-06
cos_eps = 1e-06
repa_weight = 0.5
beta_one = 0.5
beta_two = 0.5
learn_rate = 0.02
weight_decay = 0.01
adam_eps = 1e-08


LANES = 128
SUBS = 16
MOD_ROWS = (D + 1) * 6 * D // LANES
VMEM_LIMIT = 56 * 1024 * 1024
MESH = pl.DeviceIdType.MESH


def param_shapes():
    return [
        (D, 6 * D),
        (6 * D,),
        (D, 3 * D),
        (D,),
        (D,),
        (D, D),
        (D,),
        (D, FF),
        (FF,),
        (FF, D),
        (D,),
        (D, PROJ),
        (PROJ,),
        (PROJ, PROJ),
        (PROJ,),
        (PROJ, TARGET),
        (TARGET,),
    ]


def param_rows():
    starts = []
    row = 0
    for dims in param_shapes():
        starts.append(row)
        row = row + math.prod(dims) // LANES
    return starts


CHUNK = {2: 384, 5: 384, 7: 384, 9: 1536, 11: 384, 13: 512, 15: 1024}
EDGE_TILES = [3891, 5835, 5836, 6484, 6485, 9077, 9078, 9079, 11671, 12823, 12824, 14872, 14873, 15641, 15642]


def chunk_spans():
    spans = []
    base = {}
    rows = param_rows()
    for index, chunk in CHUNK.items():
        depth, width = param_shapes()[index]
        per_chunk = chunk * width // LANES // SUBS
        extra = 1 if rows[index] % SUBS else 0
        base[index] = len(spans)
        for step in range(depth // chunk):
            first = rows[index] // SUBS + step * per_chunk
            spans.append((first, first + per_chunk + extra - 1))
    return spans, base


def unpack_body(base, first_tile, per_chunk, tiles, shift, chunk, col_blocks, hosts, kept,
                first_ref, last_ref, starts_ref, guests_ref, packed, out_ref, landed, wide, sems):
    step = pl.program_id(0)

    def fetch(which, slot):
        low_tile = first_tile + which * per_chunk

        def run(begin, end, place):
            size = pl.multiple_of(jnp.maximum(end - begin, 0) * SUBS, SUBS)
            origin = pl.multiple_of(place * SUBS, SUBS)
            target = pl.multiple_of((begin - low_tile) * SUBS, SUBS)

            @pl.when(end > begin)
            def _():
                pltpu.make_async_copy(
                    packed.at[pl.ds(origin, size)], landed.at[slot, pl.ds(target, size)], sems.at[slot]
                ).start()

        def one(owner, carry):
            begin = jnp.maximum(starts_ref[owner], low_tile)
            end = jnp.minimum(starts_ref[owner + 1], low_tile + tiles)
            turn = starts_ref[owner] + kept
            run(begin, jnp.minimum(end, turn), owner * kept + begin - starts_ref[owner])
            if hosts:
                begin = jnp.maximum(begin, turn)
                run(begin, end, guests_ref[owner] + begin - turn)
            return carry

        lax.fori_loop(first_ref[base + which], last_ref[base + which] + 1, one, 0)

    @pl.when(step == 0)
    def _():
        fetch(0, 0)

    slot = step % 2

    @pl.when(step + 1 < pl.num_programs(0))
    def _():
        fetch(step + 1, (step + 1) % 2)

    pltpu.make_async_copy(packed.at[pl.ds(0, tiles * SUBS)], landed.at[slot], sems.at[slot]).wait()
    wide[...] = landed[slot].astype(jnp.float32)
    for block in range(col_blocks):
        out_ref[:, block * LANES : (block + 1) * LANES] = wide[
            pl.ds(shift + block, chunk, stride=col_blocks), :
        ].astype(jnp.bfloat16)


def unpack_weight(index, packed, plan, firsts, lasts, starts, guests):
    depth, width = param_shapes()[index]
    chunk = CHUNK[index]
    col_blocks = width // LANES
    row = param_rows()[index]
    shift = row % SUBS
    per_chunk = chunk * col_blocks // SUBS
    tiles = per_chunk + (1 if shift else 0)
    base = chunk_spans()[1][index]
    return pl.pallas_call(
        partial(unpack_body, base, row // SUBS, per_chunk, tiles, shift, chunk, col_blocks, plan[0], plan[2]),
        out_shape=jax.ShapeDtypeStruct((depth, width), jnp.bfloat16),
        grid_spec=pltpu.PrefetchScalarGridSpec(
            num_scalar_prefetch=4,
            grid=(depth // chunk,),
            in_specs=[pl.BlockSpec(memory_space=pl.ANY)],
            out_specs=pl.BlockSpec((chunk, width), lambda i, *_: (i, 0)),
            scratch_shapes=[
                pltpu.VMEM((2, tiles * SUBS, LANES), jnp.bfloat16),
                pltpu.VMEM((tiles * SUBS, LANES), jnp.float32),
                pltpu.SemaphoreType.DMA((2,)),
            ],
        ),
        compiler_params=pltpu.CompilerParams(vmem_limit_bytes=VMEM_LIMIT),
        cost_estimate=pl.CostEstimate(flops=0, bytes_accessed=depth * width * 4, transcendentals=0),
        name="unpack_%d" % index,
    )(firsts, lasts, starts, guests, packed)


def edge_read_body(table_ref, packed, out_ref, sem):
    count = out_ref.shape[0] // SUBS

    def one(i, carry):
        origin = pl.multiple_of(table_ref[i] * SUBS, SUBS)
        target = pl.multiple_of(i * SUBS, SUBS)
        pltpu.make_async_copy(packed.at[pl.ds(origin, SUBS)], out_ref.at[pl.ds(target, SUBS)], sem).start()
        return carry

    lax.fori_loop(0, count, one, 0)
    pltpu.make_async_copy(packed.at[pl.ds(0, count * SUBS)], out_ref, sem).wait()


def edge_read(packed, table):
    return pl.pallas_call(
        edge_read_body,
        out_shape=jax.ShapeDtypeStruct((len(EDGE_TILES) * SUBS, LANES), jnp.bfloat16),
        grid_spec=pltpu.PrefetchScalarGridSpec(
            num_scalar_prefetch=1,
            grid=(1,),
            in_specs=[pl.BlockSpec(memory_space=pl.ANY)],
            out_specs=pl.BlockSpec(memory_space=pltpu.VMEM),
            scratch_shapes=[pltpu.SemaphoreType.DMA],
        ),
        name="edge_read",
    )(table, packed)


def edge_write_body(layout, table_ref, *refs):
    pieces = refs[: len(layout)]
    out, wide, narrow, sem = refs[len(layout) + 1 :]
    wide[...] = jnp.zeros_like(wide)
    at = 0
    for piece, (skip, low, high) in zip(pieces, layout):
        at = at + skip
        wide[at : at + high - low, :] = piece[low:high, :]
        at = at + high - low
    narrow[...] = wide[...].astype(jnp.bfloat16)
    count = narrow.shape[0] // SUBS

    def one(i, carry):
        origin = pl.multiple_of(i * SUBS, SUBS)
        target = pl.multiple_of(table_ref[i] * SUBS, SUBS)
        pltpu.make_async_copy(narrow.at[pl.ds(origin, SUBS)], out.at[pl.ds(target, SUBS)], sem).start()
        return carry

    lax.fori_loop(0, count, one, 0)
    pltpu.make_async_copy(narrow, out.at[pl.ds(0, count * SUBS)], sem).wait()


def edge_write(pieces, buffer, table):
    count = table.shape[0]
    layout = [(skip, low, high) for skip, _, low, high in pieces]
    arrays = [array for _, array, _, _ in pieces]
    return pl.pallas_call(
        partial(edge_write_body, layout),
        out_shape=jax.ShapeDtypeStruct(buffer.shape, buffer.dtype),
        grid_spec=pltpu.PrefetchScalarGridSpec(
            num_scalar_prefetch=1,
            grid=(1,),
            in_specs=[pl.BlockSpec(memory_space=pltpu.VMEM)] * len(arrays)
            + [pl.BlockSpec(memory_space=pl.ANY)],
            out_specs=pl.BlockSpec(memory_space=pl.ANY),
            scratch_shapes=[
                pltpu.VMEM((count * SUBS, LANES), jnp.float32),
                pltpu.VMEM((count * SUBS, LANES), jnp.bfloat16),
                pltpu.SemaphoreType.DMA,
            ],
        ),
        input_output_aliases={1 + len(arrays): 0},
        name="edge_write",
    )(table, *arrays, buffer)


def weight_grad_body(base, first_tile, per_chunk, shift, chunk, col_blocks, slots, plan, piece, chained,
                     first_ref, last_ref, starts_ref, guests_ref, x_ref, dy_ref, *rest):
    if chained:
        rest = rest[1:]
    out, ends_ref, wide, narrow, sems = rest
    hosts, kept = plan
    step = pl.program_id(0)
    steps = pl.num_programs(0)
    slot = step % 2
    rows = chunk * col_blocks

    def drain(which):
        pltpu.make_async_copy(narrow.at[which], out.at[pl.ds(0, rows)], sems.at[which]).wait()

    @pl.when(step == 0)
    def _():
        wide[...] = jnp.zeros_like(wide)

    if shift:
        @pl.when(step > 0)
        def _():
            wide[0:SUBS, :] = wide[rows : rows + SUBS, :]

    left = x_ref[...].T
    for start in range(0, col_blocks, piece):
        part = jnp.dot(
            left, dy_ref[:, start * LANES : (start + piece) * LANES], preferred_element_type=jnp.float32
        )
        for block in range(piece):
            wide[pl.ds(shift + start + block, chunk, stride=col_blocks), :] = part[
                :, block * LANES : (block + 1) * LANES
            ]

    @pl.when(step >= 2)
    def _():
        drain(slot)

    narrow[slot] = wide[0:rows, :].astype(jnp.bfloat16)

    @pl.when(step == 0)
    def _():
        ends_ref[0:SUBS, :] = wide[0:SUBS, :]

    if shift:
        @pl.when(step == steps - 1)
        def _():
            ends_ref[SUBS : 2 * SUBS, :] = wide[rows : rows + SUBS, :]
    else:
        ends_ref[SUBS : 2 * SUBS, :] = jnp.zeros((SUBS, LANES), jnp.float32)

    low_tile = first_tile + step * per_chunk

    def run(begin, end, place):
        size = pl.multiple_of(jnp.maximum(end - begin, 0) * SUBS, SUBS)
        target = pl.multiple_of(place * SUBS, SUBS)
        origin = pl.multiple_of((begin - low_tile) * SUBS, SUBS)

        @pl.when(end > begin)
        def _():
            pltpu.make_async_copy(
                narrow.at[slot, pl.ds(origin, size)], out.at[pl.ds(target, size)], sems.at[slot]
            ).start()

    def one(owner, carry):
        begin = jnp.maximum(starts_ref[owner], low_tile)
        end = jnp.minimum(starts_ref[owner + 1], low_tile + per_chunk)
        turn = starts_ref[owner] + kept
        run(begin, jnp.minimum(end, turn), owner * kept + begin - starts_ref[owner])
        if hosts:
            begin = jnp.maximum(begin, turn)
            run(begin, end, guests_ref[owner] + begin - turn)
        return carry

    lax.fori_loop(first_ref[base + step], last_ref[base + step] + 1, one, 0)

    @pl.when(step == steps - 1)
    def _():
        drain(slot)

        @pl.when(steps > 1)
        def _():
            drain(1 - slot)


def weight_grad(index, left, right, buffer, owners, slots, firsts, lasts, starts, guests, plan):
    depth, width = param_shapes()[index]
    tokens = left.shape[0]
    chunk = CHUNK[index]
    col_blocks = width // LANES
    piece = next(p for p in (9, 8, 6) if col_blocks % p == 0)
    row = param_rows()[index]
    shift = row % SUBS
    per_chunk = chunk * col_blocks // SUBS
    base = chunk_spans()[1][index]
    shape = (owners * plan[1] * SUBS, LANES)
    in_specs = [
        pl.BlockSpec((tokens, chunk), lambda i, *_: (0, i)),
        pl.BlockSpec((tokens, width), lambda i, *_: (0, 0)),
    ]
    operands = [firsts, lasts, starts, guests, left, right]
    aliases = {}
    if buffer is not None:
        in_specs.append(pl.BlockSpec(memory_space=pl.ANY))
        operands.append(buffer)
        aliases = {6: 0}
    return pl.pallas_call(
        partial(weight_grad_body, base, row // SUBS, per_chunk, shift, chunk, col_blocks, slots, plan, piece,
                buffer is not None),
        out_shape=(
            jax.ShapeDtypeStruct(shape, jnp.bfloat16),
            jax.ShapeDtypeStruct((2 * SUBS, LANES), jnp.float32),
        ),
        grid_spec=pltpu.PrefetchScalarGridSpec(
            num_scalar_prefetch=4,
            grid=(depth // chunk,),
            in_specs=in_specs,
            out_specs=(
                pl.BlockSpec(memory_space=pl.ANY),
                pl.BlockSpec((2 * SUBS, LANES), lambda i, *_: (0, 0)),
            ),
            scratch_shapes=[
                pltpu.VMEM((chunk * col_blocks + SUBS, LANES), jnp.float32),
                pltpu.VMEM((2, chunk * col_blocks, LANES), jnp.bfloat16),
                pltpu.SemaphoreType.DMA((2,)),
            ],
        ),
        input_output_aliases=aliases,
        compiler_params=pltpu.CompilerParams(vmem_limit_bytes=VMEM_LIMIT),
        cost_estimate=pl.CostEstimate(
            flops=2 * tokens * depth * width, bytes_accessed=depth * width * 2, transcendentals=0
        ),
        name="weight_grad_%d" % index,
    )(*operands)


class Grid:
    def __init__(self, side, depth):
        self.side = side
        self.sizes = {"u": side, "v": side, "z": depth}
        self.place = lax.axis_index("dp")
        self.core = self.place % 2
        outer = self.place // 2 // side
        inner = self.place // 2 % side
        self.mine = {
            "u": jnp.where(self.core == 0, outer, inner),
            "v": jnp.where(self.core == 0, inner, outer),
            "z": lax.axis_index("seq"),
        }
        self.sibling = (
            self.place + 1 - 2 * self.core,
            self.mine["z"],
        )

    def dp_of(self, first, second, core):
        outer = jnp.where(core == 0, first, second)
        inner = jnp.where(core == 0, second, first)
        return (outer * self.side + inner) * 2 + core

    def device(self, axis, other):
        at = dict(self.mine)
        at[axis] = other
        return (self.dp_of(at["u"], at["v"], self.core), at["z"])

    def other(self, axis, k):
        return k + (k >= self.mine[axis]).astype(jnp.int32)

    def seat(self, axis, other):
        mine = self.mine[axis]
        return mine - (mine > other).astype(jnp.int32)

    def partners(self):
        found = [self.sibling]
        for axis in ("u", "v", "z"):
            for k in range(self.sizes[axis] - 1):
                found.append(self.device(axis, self.other(axis, k)))
        return found

    def greet(self, hosting=None, to_host=False):
        barrier = pltpu.get_barrier_semaphore()
        partners = self.partners()
        for partner in partners:
            pl.semaphore_signal(barrier, inc=1, device_id=partner, device_id_type=MESH)
        expected = len(partners)
        if hosting is not None and to_host:
            for piece in range(hosting.share):
                device, there = hosting.guest_at(piece)

                @pl.when(hosting.is_host & there)
                def _(device=device):
                    pl.semaphore_signal(barrier, inc=1, device_id=device, device_id_type=MESH)

            expected = expected + 1 - hosting.is_host.astype(jnp.int32)
        elif hosting is not None:
            @pl.when(jnp.logical_not(hosting.is_host))
            def _():
                pl.semaphore_signal(barrier, inc=1, device_id=hosting.host, device_id_type=MESH)

            expected = expected + hosting.guests
        pl.semaphore_wait(barrier, expected)


class Hosting:
    def __init__(self, grid, owners, hosts, share, kept, left):
        depth = grid.sizes["z"]
        z = grid.mine["z"]
        self.grid, self.depth, self.hosts, self.share, self.kept, self.left = grid, depth, hosts, share, kept, left
        self.places = owners // depth
        self.is_host = grid.place * depth + z < hosts
        here, _, room = level_counts(hosts, share, self.places, depth, z)
        index = grid.place - here
        back_here, _, back_room = level_counts(hosts, share, self.places, depth, z - depth // 2)
        own = index < room
        spot = jnp.maximum(jnp.where(own, index, back_room - 1 - (index - room)), 0)
        self.piece = lax.rem(spot, share)
        self.host = (spot // share, jnp.where(own | self.is_host, z, z - depth // 2))
        count = jnp.int32(0)
        for piece in range(share):
            count = count + self.guest_at(piece)[1].astype(jnp.int32)
        self.guests = jnp.where(self.is_host, count, 0)

    def guest_at(self, piece):
        there, near, over = guest_of(
            self.hosts, self.share, self.places, self.depth, self.grid.place, self.grid.mine["z"], piece
        )
        device = (jnp.where(near[0], near[1], over[1]), jnp.where(near[0], near[2], over[2]))
        return device, there & (piece < self.share)

    def guest(self, tile):
        piece = tile // self.left
        device, there = self.guest_at(piece)
        return device, there, self.kept + tile - piece * self.left


def split_slots(slots, shards):
    room = 32 * 1024 * 1024 // ((HELD + 2 * SLOTS) * shards * SUBS * LANES * 2)
    part = max(p for p in range(2, 13) if slots % p == 0 and p <= max(room, 2))
    late = max(1, round(part * 0.34))
    return slots // part, (part - late, late)


def level_counts(hosts, share, places, depth, z):
    here = (hosts - z + depth - 1) // depth
    return here, places - here, share * here


def guest_of(hosts, share, places, depth, place, z, piece):
    here, guests, room = level_counts(hosts, share, places, depth, z)
    index = place * share + piece
    far = z + depth // 2
    far_here, far_guests, far_room = level_counts(hosts, share, places, depth, far)
    back = room - 1 - index
    near = index < guests
    over = (far < depth) & (far_room + back < far_guests)
    return near | over, (near, here + index, z), (over, far_here + far_room + back, far)


def guest_places(plan, owners, depth):
    hosts, share, kept, left = plan
    places = [0] * owners
    for host in range(hosts):
        for piece in range(share):
            there, near, over = guest_of(hosts, share, owners // depth, depth, host // depth, host % depth, piece)
            if there:
                _, place, z = near if near[0] else over
                places[place * depth + z] = host * kept + piece * left
    return places


def host_plan(slots, owners, depth):
    hosts = MOD_ROWS // (slots * SUBS)
    shards = owners // 2
    room = 32 * 1024 * 1024 // ((HELD + 2 * SLOTS) * shards * SUBS * LANES * 2)
    share = -(-(owners - hosts) // hosts) if hosts else 0
    levels = [level_counts(hosts, share, owners // depth, depth, z) for z in range(depth)]
    for z, (_, guests, room_here) in enumerate(levels):
        if guests > room_here and (
            z < depth // 2
            or guests - room_here > levels[z - depth // 2][2] - levels[z - depth // 2][1]
        ):
            hosts = 0
    for kept in range(1, slots) if hosts else ():
        left = slots - kept
        if share * left > kept:
            continue
        for step in range(min(12, max(room, 2)), 5, -1):
            for late in (round(step * 0.34), step // 3, -(-step // 3)):
                early = step - late
                if kept % step or left % early:
                    continue
                middle = kept // step * early
                if all((i * left - middle) % late == 0 for i in range(share + 1) if i * left > middle):
                    return hosts, share, kept, kept // step, (early, late)
    steps, parts = split_slots(slots, shards)
    return 0, 0, slots, steps, parts


ORDERS = (("u", "v", "z"), ("u", "z", "v"))
LAG = 2
SLOTS = 4
OUTS = 8
LEAD = 4
HELD = 4 * LAG + 1


def gather_stream(grid, order, first_row, span, steps, own_ref, out_ref, sems, hosting):
    (send_a, recv_a, send_b, recv_b, send_c, recv_c, send_d, recv_d, kept_sem, arrive) = sems
    mine = grid.mine
    side = grid.side
    near, mid, far = order[2], order[1], order[0]

    def rows(q):
        return pl.ds(pl.multiple_of(first_row + q * span, SUBS), span)

    def copy(source, target, send, recv, device):
        return pltpu.make_async_remote_copy(
            src_ref=source, dst_ref=target, send_sem=send, recv_sem=recv, device_id=device,
            device_id_type=MESH,
        )

    def one_a(q, axis, k):
        other = grid.other(axis, k)
        mine_dp = grid.dp_of(mine["u"], mine["v"], grid.core)
        return copy(
            own_ref.at[rows(q)], out_ref.at[mine_dp, mine["z"], rows(q)],
            send_a.at[q % 4, k], recv_a.at[q, grid.seat(axis, other)],
            grid.device(axis, other),
        )

    def wait_a(q, axis, k):
        dp = grid.dp_of(mine["u"], mine["v"], grid.core)
        copy(
            own_ref.at[rows(q)], out_ref.at[dp, mine["z"], rows(q)],
            send_a.at[q % 4, k], recv_a.at[q, k], grid.device(axis, grid.other(axis, k)),
        ).wait_recv()

    def many_b(q, axis, k):
        other = grid.other(axis, k)
        seat = grid.seat(axis, other)
        if axis == "v":
            at = out_ref.at[grid.dp_of(mine["u"], mine["v"], grid.core), :, rows(q)]
            return [copy(at, at, send_b.at[q % 4, k], recv_b.at[q, seat], grid.device(axis, other))]
        found = []
        for v in range(side):
            at = out_ref.at[grid.dp_of(mine["u"], v, grid.core), mine["z"], rows(q)]
            found.append(copy(at, at, send_b.at[q % 4, k], recv_b.at[q, seat], grid.device(axis, other)))
        return found

    def many_c(q, k):
        other = grid.other("u", k)
        seat = grid.seat("u", other)
        found = []
        for v in range(side):
            at = out_ref.at[grid.dp_of(mine["u"], v, grid.core), :, rows(q)]
            found.append(copy(at, at, send_c.at[q % 4, k], recv_c.at[q, seat], grid.device("u", other)))
        return found

    def many_d(q):
        found = []
        for u in range(side):
            for v in range(side):
                at = out_ref.at[grid.dp_of(u, v, grid.core), :, rows(q)]
                found.append(copy(at, at, send_d.at[q % 4], recv_d.at[q], grid.sibling))
        return found

    def bulk(q, count, send, recv, device):
        at = out_ref.at[pl.ds(0, count), :, rows(q)]
        return copy(at, at, send, recv, device)

    def bulk_b(q, axis, send, recv):
        if axis == "v":
            at = out_ref.at[0, :, rows(q)]
        else:
            at = out_ref.at[pl.ds(0, side), 0, rows(q)]
        return copy(at, at, send, recv, grid.sibling)

    far_count = grid.sizes[near] - 1
    mid_count = grid.sizes[mid] - 1

    def stage_d(q):
        bulk(q, side, send_c.at[q % 4, 0], recv_c.at[q, 0], grid.sibling).wait_recv()
        for k in range(1, side - 1):
            bulk(q, side, send_c.at[q % 4, k], recv_c.at[q, k], grid.sibling).wait_recv()
        for k in range(side - 1):
            bulk(q, side, send_c.at[q % 4, k], recv_c.at[q, k], grid.sibling).wait_send()
        for one in many_d(q):
            one.start()

    def stage_c(q):
        for k in range(mid_count):
            bulk_b(q, mid, send_b.at[q % 4, k], recv_b.at[q, k]).wait_recv()
        for k in range(mid_count):
            bulk_b(q, mid, send_b.at[q % 4, k], recv_b.at[q, k]).wait_send()
        for k in range(side - 1):
            for one in many_c(q, k):
                one.start()

    def keep(q):
        dp = grid.dp_of(mine["u"], mine["v"], grid.core)
        return pltpu.make_async_copy(own_ref.at[rows(q)], out_ref.at[dp, mine["z"], rows(q)], kept_sem.at[q % 4])

    def stage_b(q):
        keep(q).wait()
        for k in range(far_count):
            wait_a(q, near, k)
        for k in range(far_count):
            one_a(q, near, k).wait_send()
        for k in range(mid_count):
            for one in many_b(q, mid, k):
                one.start()

    def stage_a(q):
        if hosting is not None:
            _, there, _ = hosting.guest((first_row + q * span) // SUBS)

            @pl.when(hosting.is_host & there)
            def _():
                copy(own_ref.at[rows(q)], own_ref.at[rows(q)], arrive.at[q], arrive.at[q], grid.sibling).wait_recv()

        keep(q).start()
        for k in range(far_count):
            one_a(q, near, k).start()

    def finish(q):
        whole = bulk(q, side * side, send_d.at[q % 4], recv_d.at[q], grid.sibling)
        whole.wait_recv()
        whole.wait_send()

    return (stage_a, stage_b, stage_c, stage_d, finish)


GATHER_REFS = 10


def gather_body(side, depth, plan, slots, images, own_ref, cond_ref, info_ref, out_ref, mod_ref, held_ref,
                mine_ref, own_sem, guest_sem, *refs):
    hosts, share, kept, steps, parts = plan
    grid = Grid(side, depth)
    hosting = Hosting(grid, 2 * side * side * depth, hosts, share, kept, slots - kept) if hosts else None
    fill = pltpu.make_async_copy(own_ref.at[pl.ds(0, kept * SUBS)], mine_ref, own_sem)

    def when_guest(action):
        if hosting is None:
            action()
        else:
            pl.when(jnp.logical_not(hosting.is_host))(action)

    when_guest(fill.start)
    grid.greet(hosting, to_host=True)
    streams = []
    arrivals = []
    first = 0
    for number, (order, part) in enumerate(zip(ORDERS, parts)):
        span = part * SUBS
        sems = refs[GATHER_REFS * number : GATHER_REFS * (number + 1)]
        streams.append(gather_stream(grid, order, first, span, steps, mine_ref, out_ref, sems, hosting))
        arrivals.append((first // SUBS, part, sems[-1]))
        first = first + steps * span
    if hosting is not None:
        left = slots - kept

        def send_chunks(q, carry):
            for low, part, arrive in arrivals:
                tile = low + q * part
                within = tile - hosting.piece * left

                @pl.when(jnp.logical_not(hosting.is_host) & (within >= 0) & (within < left))
                def _(tile=tile, within=within, part=part, arrive=arrive):
                    slot = jnp.clip(kept + within, kept, slots - part)
                    pltpu.make_async_remote_copy(
                        src_ref=own_ref.at[pl.ds(pl.multiple_of(slot * SUBS, SUBS), part * SUBS)],
                        dst_ref=mine_ref.at[pl.ds(pl.multiple_of(tile * SUBS, SUBS), part * SUBS)],
                        send_sem=guest_sem,
                        recv_sem=arrive.at[q],
                        device_id=hosting.host,
                        device_id_type=MESH,
                    ).start()

            return carry

        lax.fori_loop(0, min(LEAD, steps), send_chunks, 0)
    when_guest(fill.wait)
    modulation_step = modulation_stages(
        grid, images, slots, own_ref, info_ref, cond_ref, mod_ref, held_ref, refs[2 * GATHER_REFS :]
    )

    def round_trip(s, carry):
        for late in range(4, -1, -1):
            q = s - LAG * late

            @pl.when((q >= 0) & (q < steps))
            def _(late=late, q=q):
                for stream in streams:
                    stream[late](q)

        if hosting is not None:
            @pl.when(s + LEAD < steps)
            def _():
                send_chunks(s + LEAD, 0)

        modulation_step(s)
        return carry

    lax.fori_loop(0, max(steps + 4 * LAG, MOD_STEPS), round_trip, 0)
    if hosting is not None:
        @pl.when(jnp.logical_not(hosting.is_host))
        def _():
            at = own_ref.at[pl.ds(kept * SUBS, (slots - kept) * SUBS)]
            pltpu.make_async_remote_copy(
                src_ref=at, dst_ref=at, send_sem=guest_sem, recv_sem=guest_sem, device_id=grid.sibling,
                device_id_type=MESH,
            ).wait_send()


def gather_slots(own, cond_rows, info, slots, data_count, seq_count):
    side = math.isqrt(data_count // 2)
    images = data_count * SEGS
    plan = host_plan(slots, data_count * seq_count, seq_count)
    kept, steps = plan[2], plan[3]
    dma = pltpu.SemaphoreType.DMA
    sems = []
    for order in ORDERS:
        sizes = {"u": side - 1, "v": side - 1, "z": seq_count - 1}
        for axis in (order[2], order[1], order[0]):
            sems.append(dma((4, sizes[axis])))
            sems.append(dma((steps, sizes[axis])))
        sems.append(dma((4,)))
        sems.append(dma((steps,)))
        sems.append(dma((4,)))
        sems.append(dma((steps,)))
    vmem = pl.BlockSpec(memory_space=pltpu.VMEM)
    packed, modulation, held = pl.pallas_call(
        partial(gather_body, side, seq_count, plan, slots, images),
        out_shape=(
            jax.ShapeDtypeStruct((data_count, seq_count, kept * SUBS, LANES), jnp.bfloat16),
            jax.ShapeDtypeStruct((IMAGE_ROWS, LANES), jnp.float32),
            jax.ShapeDtypeStruct((condition_rows(slots), LANES), jnp.float32),
        ),
        in_specs=[vmem, vmem, pl.BlockSpec(memory_space=pltpu.SMEM)],
        out_specs=(pl.BlockSpec(memory_space=pl.ANY), vmem, vmem),
        scratch_shapes=[pltpu.VMEM((kept * SUBS, LANES), jnp.bfloat16), dma, dma]
        + sems
        + modulation_refs(side, seq_count, images, slots),
        compiler_params=pltpu.CompilerParams(
            collective_id=2, has_side_effects=True, vmem_limit_bytes=VMEM_LIMIT
        ),
        name="gather_slots",
    )(own, cond_rows, info)
    return packed.reshape(data_count * seq_count * kept * SUBS, LANES), modulation, held


def reduce_stream(grid, order, first_row, span, steps, parts_ref, out_ref, refs, hosting, passed):
    (own, rc, r1, r2, r3, outs, own_sem, out_sem, hand_sem, c_send, c_recv, s1, v1, s2, v2, s3, v3,
     c_credit, k1, k2, k3) = refs
    mine = grid.mine
    side = grid.side
    held = own.shape[0]
    mu, mv, mz = mine["u"], mine["v"], mine["z"]

    def rows(q):
        return pl.ds(pl.multiple_of(first_row + q * span, SUBS), span)

    def load(q, u, v):
        return pltpu.make_async_copy(
            parts_ref.at[grid.dp_of(u, v, grid.core), :, rows(q)], own.at[q % held, u, v], own_sem.at[q % held, u, v]
        )

    def give(q, u, v):
        return pltpu.make_async_remote_copy(
            src_ref=parts_ref.at[grid.dp_of(u, v, 1 - grid.core), :, rows(q)],
            dst_ref=rc.at[q % SLOTS, u, v],
            send_sem=c_send.at[q % SLOTS, u, v],
            recv_sem=c_recv.at[q % SLOTS, u, v],
            device_id=grid.sibling,
            device_id_type=MESH,
        )

    def block(q, stage, other):
        if stage == 0:
            return own.at[q % held, other]
        if order[1] == "v":
            return own.at[q % held, mu, other] if stage == 1 else own.at[q % held, mu, mv, other]
        return own.at[q % held, mu, :, other] if stage == 1 else own.at[q % held, mu, other, mz]

    landing = (r1, r2, r3)
    sends = (s1, s2, s3)
    arrivals = (v1, v2, v3)
    credits = (k1, k2, k3)

    def send(q, stage, k):
        axis = order[stage]
        other = grid.other(axis, k)
        seat = grid.seat(axis, other)
        return pltpu.make_async_remote_copy(
            src_ref=block(q, stage, other),
            dst_ref=landing[stage].at[q % SLOTS, seat],
            send_sem=sends[stage].at[q % SLOTS, k],
            recv_sem=arrivals[stage].at[q % SLOTS, seat],
            device_id=grid.device(axis, other),
            device_id_type=MESH,
        )

    def receive(q, stage, k):
        axis = order[stage]
        return pltpu.make_async_remote_copy(
            src_ref=block(q, stage, 0),
            dst_ref=landing[stage].at[q % SLOTS, k],
            send_sem=sends[stage].at[q % SLOTS, k],
            recv_sem=arrivals[stage].at[q % SLOTS, k],
            device_id=grid.device(axis, grid.other(axis, k)),
            device_id_type=MESH,
        )

    def keep(q):
        return pltpu.make_async_copy(outs.at[q % OUTS], out_ref.at[rows(q)], out_sem.at[q % OUTS])

    def hand_over(q):
        device, there, slot = hosting.guest((first_row + q * span) // SUBS)
        copy = pltpu.make_async_remote_copy(
            src_ref=outs.at[q % OUTS],
            dst_ref=out_ref.at[pl.ds(pl.multiple_of(slot * SUBS, SUBS), span)],
            send_sem=hand_sem.at[q % OUTS],
            recv_sem=passed,
            device_id=device,
            device_id_type=MESH,
        )
        return copy, there

    def write(q, action):
        if hosting is None:
            getattr(keep(q), action)()
            return

        @pl.when(jnp.logical_not(hosting.is_host))
        def _():
            getattr(keep(q), action)()

        copy, there = hand_over(q)

        @pl.when(hosting.is_host & there)
        def _():
            if action == "start":
                copy.start()
            else:
                copy.wait_send()

    def collect(q, stage):
        axis = order[stage]
        count = grid.sizes[axis] - 1
        for k in range(count):
            receive(q, stage, k).wait_recv()
        kept = block(q, stage, mine[axis])
        total = kept[...].astype(jnp.float32)
        for k in range(count):
            total = total + landing[stage][q % SLOTS, k].astype(jnp.float32)
        if stage < 2:
            kept[...] = total.astype(jnp.bfloat16)
        else:
            @pl.when(q >= OUTS)
            def _():
                write(q - OUTS, "wait")

            outs[q % OUTS] = total.astype(jnp.bfloat16)
            write(q, "start")
        for k in range(count):
            send(q, stage, k).wait_send()

        @pl.when(q + SLOTS < steps)
        def _():
            for k in range(count):
                pl.semaphore_signal(
                    credits[stage].at[mine[axis]], inc=1, device_id=grid.device(axis, grid.other(axis, k)),
                    device_id_type=MESH,
                )

    def launch(q, stage):
        axis = order[stage]
        count = grid.sizes[axis] - 1

        @pl.when(q >= SLOTS)
        def _():
            for k in range(count):
                pl.semaphore_wait(credits[stage].at[grid.other(axis, k)], 1)

        for k in range(count):
            send(q, stage, k).start()

    def begin(q):
        @pl.when(q >= SLOTS)
        def _():
            pl.semaphore_wait(c_credit, 1)

        for u in range(side):
            for v in range(side):
                give(q, u, v).start()
                load(q, u, v).start()

    def stage_c(q):
        for u in range(side):
            for v in range(side):
                load(q, u, v).wait()
                give(q, u, v).wait_recv()
                own[q % held, u, v] = (
                    own[q % held, u, v].astype(jnp.float32) + rc[q % SLOTS, u, v].astype(jnp.float32)
                ).astype(jnp.bfloat16)
        for u in range(side):
            for v in range(side):
                give(q, u, v).wait_send()

        @pl.when(q + SLOTS < steps)
        def _():
            pl.semaphore_signal(c_credit, inc=1, device_id=grid.sibling, device_id_type=MESH)

        launch(q, 0)

    def stage_one(q):
        collect(q, 0)
        launch(q, 1)

    def stage_two(q):
        collect(q, 1)
        launch(q, 2)

    def stage_three(q):
        collect(q, 2)

    return (begin, stage_c, stage_one, stage_two, stage_three), write


REDUCE_REFS = 21


MOD_BLOCKS = 6 * D // LANES
IMAGE_ROWS = SEGS * MOD_BLOCKS
SENT_ROWS = -(-IMAGE_ROWS // SUBS) * SUBS
COND_STRIDE = D // LANES + 1
COND_ROWS = SEGS * COND_STRIDE
FRONT = 56
SPARE = 64
MOD_STEPS = 31
FILL_STEPS = 8
PRODUCT_STEPS = 9


def held_depth(slots):
    depth = -(-(slots * SUBS + MOD_BLOCKS - 1) // MOD_BLOCKS)
    return -(-depth // 8) * 8


def condition_rows(slots):
    return -(-(D + 8 + max(held_depth(slots) + 32, 2 * LANES)) // LANES) * LANES


def spread_modulation(s, own_ref, info_ref, wide):
    rows = own_ref.shape[0]
    count = -(-rows // FILL_STEPS // SUBS) * SUBS

    @pl.when(s == 0)
    def _():
        wide[0:FRONT, :] = jnp.zeros((FRONT, LANES), jnp.float32)
        rest = wide.shape[0] - FRONT - rows
        wide[FRONT + rows :, :] = jnp.zeros((rest, LANES), jnp.float32)

    @pl.when(s < FILL_STEPS)
    def _():
        first = pl.multiple_of(jnp.minimum(s * count, rows - count), SUBS)
        at = first + lax.broadcasted_iota(jnp.int32, (count, LANES), 0)
        values = own_ref[pl.ds(first, count), :].astype(jnp.float32)
        wide[pl.ds(pl.multiple_of(FRONT + first, 8), count), :] = jnp.where(at < info_ref[2], values, 0.0)


def wide_rows(slots):
    return FRONT + MOD_BLOCKS * (held_depth(slots) + 1) + 8


def held_columns(wide, info_ref, depth, block):
    return wide[pl.ds(FRONT + block - info_ref[1], depth, stride=MOD_BLOCKS), :].astype(jnp.bfloat16)


def gather_blocks(grid, buffer, rows, sems):
    send_v, recv_v, send_u, recv_u, send_c, recv_c = sems
    mine = grid.mine
    side = grid.side

    def one(u, v, send, recv, device):
        at = buffer.at[pl.ds(pl.multiple_of(grid.dp_of(u, v, grid.core) * rows, 8), rows)]
        return pltpu.make_async_remote_copy(
            src_ref=at, dst_ref=at, send_sem=send, recv_sem=recv, device_id=device, device_id_type=MESH
        )

    def along(axis, k):
        return grid.device(axis, grid.other(axis, k)), grid.seat(axis, grid.other(axis, k))

    def v_copies():
        found = []
        for k in range(side - 1):
            device, seat = along("v", k)
            found.append(one(mine["u"], mine["v"], send_v.at[k], recv_v.at[seat], device))
        return found

    def u_copies():
        found = []
        for k in range(side - 1):
            device, seat = along("u", k)
            for v in range(side):
                found.append(one(mine["u"], v, send_u.at[k, v], recv_u.at[seat, v], device))
        return found

    def c_copies():
        return [
            one(u, v, send_c.at[u, v], recv_c.at[u, v], grid.sibling) for u in range(side) for v in range(side)
        ]

    def start():
        for copy in v_copies():
            copy.start()

    def second():
        for k in range(side - 1):
            one(mine["u"], mine["v"], send_v.at[k], recv_v.at[k], grid.sibling).wait_recv()
        for copy in v_copies():
            copy.wait_send()
        for copy in u_copies():
            copy.start()

    def third():
        for k in range(side - 1):
            for v in range(side):
                one(mine["u"], v, send_u.at[k, v], recv_u.at[k, v], grid.sibling).wait_recv()
        for copy in u_copies():
            copy.wait_send()
        for copy in c_copies():
            copy.start()

    def finish():
        for copy in c_copies():
            copy.wait_recv()
        for copy in c_copies():
            copy.wait_send()

    return start, second, third, finish


def gather_sems(side):
    dma = pltpu.SemaphoreType.DMA
    return [dma((side - 1,))] * 2 + [dma((side - 1, side))] * 2 + [dma((side, side))] * 2


def reduce_blocks(grid, buffer, rows, refs):
    from_c, from_u, from_v, from_z, send_c, recv_c, send_u, recv_u, send_v, recv_v, send_z, recv_z = refs
    mine = grid.mine
    side = grid.side
    depth = grid.sizes["z"]

    def block(u, v, core):
        return buffer.at[pl.ds(pl.multiple_of(grid.dp_of(u, v, core) * rows, 8), rows)]

    def copy(source, target, send, recv, device):
        return pltpu.make_async_remote_copy(
            src_ref=source, dst_ref=target, send_sem=send, recv_sem=recv, device_id=device, device_id_type=MESH
        )

    def along(axis, k):
        other = grid.other(axis, k)
        return other, grid.device(axis, other), grid.seat(axis, other)

    def c_copies():
        return [
            copy(block(u, v, 1 - grid.core), from_c.at[u, v], send_c.at[u, v], recv_c.at[u, v], grid.sibling)
            for u in range(side)
            for v in range(side)
        ]

    def u_copies():
        found = []
        for k in range(side - 1):
            other, device, seat = along("u", k)
            for v in range(side):
                found.append(
                    copy(block(other, v, grid.core), from_u.at[seat, v], send_u.at[k, v], recv_u.at[seat, v], device)
                )
        return found

    def v_copies():
        found = []
        for k in range(side - 1):
            other, device, seat = along("v", k)
            found.append(
                copy(block(mine["u"], other, grid.core), from_v.at[seat], send_v.at[k], recv_v.at[seat], device)
            )
        return found

    def z_copies():
        found = []
        for k in range(depth - 1):
            _, device, _ = along("z", k)
            found.append(
                copy(block(mine["u"], mine["v"], grid.core), from_z.at[mine["z"]], send_z.at[k],
                     recv_z.at[mine["z"]], device)
            )
        return found

    def start():
        for one in c_copies():
            one.start()

    def second():
        for one in c_copies():
            one.wait_recv()
        for one in c_copies():
            one.wait_send()
        for u in range(side):
            for v in range(side):
                at = block(u, v, grid.core)
                at[...] = at[...] + from_c[u, v]
        for one in u_copies():
            one.start()

    def third():
        for k in range(side - 1):
            for v in range(side):
                copy(from_u.at[k, v], from_u.at[k, v], send_u.at[k, v], recv_u.at[k, v], grid.sibling).wait_recv()
        for one in u_copies():
            one.wait_send()
        for v in range(side):
            at = block(mine["u"], v, grid.core)
            total = at[...]
            for k in range(side - 1):
                total = total + from_u[k, v]
            at[...] = total
        for one in v_copies():
            one.start()

    def fourth():
        for k in range(side - 1):
            copy(from_v.at[k], from_v.at[k], send_v.at[k], recv_v.at[k], grid.sibling).wait_recv()
        for one in v_copies():
            one.wait_send()
        at = block(mine["u"], mine["v"], grid.core)
        total = at[...]
        for k in range(side - 1):
            total = total + from_v[k]
        at[...] = total
        from_z[mine["z"]] = total
        for one in z_copies():
            one.start()

    def finish():
        for k in range(depth - 1):
            other = grid.other("z", k)
            copy(from_z.at[other], from_z.at[other], send_z.at[k], recv_z.at[other], grid.sibling).wait_recv()
        for one in z_copies():
            one.wait_send()
        total = from_z[0]
        for z in range(1, depth):
            total = total + from_z[z]
        return total

    return start, second, third, fourth, finish


def reduce_refs(side, depth, rows):
    dma = pltpu.SemaphoreType.DMA
    f32 = jnp.float32
    return [
        pltpu.VMEM((side, side, rows, LANES), f32),
        pltpu.VMEM((side - 1, side, rows, LANES), f32),
        pltpu.VMEM((side - 1, rows, LANES), f32),
        pltpu.VMEM((depth, rows, LANES), f32),
        dma((side, side)),
        dma((side, side)),
        dma((side - 1, side)),
        dma((side - 1, side)),
        dma((side - 1,)),
        dma((side - 1,)),
        dma((depth - 1,)),
        dma((depth,)),
    ]


def modulation_stages(grid, images, slots, own_ref, info_ref, cond_ref, mod_ref, held_ref, refs):
    everyone, wide, columns, parts, square = refs[:5]
    gather = gather_blocks(grid, everyone, COND_ROWS, refs[5:11])
    reduce = reduce_blocks(grid, parts, IMAGE_ROWS, refs[11:23])
    here = grid.place
    depth = held_depth(slots)

    def run(s):
        spread_modulation(s, own_ref, info_ref, wide)

        @pl.when(s == 0)
        def _():
            everyone[pl.ds(pl.multiple_of(here * COND_ROWS, 8), COND_ROWS), :] = cond_ref[...]
            gather[0]()
            square[...] = jnp.zeros_like(square)
            held_ref[...] = jnp.zeros_like(held_ref)

        @pl.when(s == 2)
        def _():
            gather[1]()

        @pl.when(s == 4)
        def _():
            gather[2]()

        @pl.when(s == 7)
        def _():
            gather[3]()

        @pl.when(s == 8)
        def _():
            for block in range(D // LANES):
                square[0:images, :] = everyone[pl.ds(block, images, stride=COND_STRIDE), :]
                held_ref[block * LANES : (block + 1) * LANES, :] = square[...].T
            held_ref[D : D + 8, :] = (lax.broadcasted_iota(jnp.int32, (8, LANES), 0) == 0).astype(jnp.float32)
            for part in range(columns.shape[1] // LANES):
                columns[:, part * LANES : (part + 1) * LANES] = (
                    held_ref[pl.ds(info_ref[0] + part * LANES, LANES), :].T.astype(jnp.bfloat16)
                )

        at_product = s - 9

        @pl.when((at_product >= 0) & (at_product < PRODUCT_STEPS))
        def _():
            left = columns[0:images, 0:depth]
            each = MOD_BLOCKS // 2 // PRODUCT_STEPS
            for pair in range(each):
                block = (at_product * each + pair) * 2
                right = jnp.concatenate(
                    [held_columns(wide, info_ref, depth, block), held_columns(wide, info_ref, depth, block + 1)],
                    axis=1,
                )
                found = jnp.dot(left, right, preferred_element_type=jnp.float32)
                parts[pl.ds(block, images, stride=MOD_BLOCKS), :] = found[:, :LANES]
                parts[pl.ds(block + 1, images, stride=MOD_BLOCKS), :] = found[:, LANES:]

        @pl.when(s == 18)
        def _():
            reduce[0]()

        for at, stage in ((20, 1), (23, 2), (26, 3)):
            @pl.when(s == at)
            def _(stage=stage):
                reduce[stage]()

        @pl.when(s == 29)
        def _():
            mod_ref[...] = reduce[4]()

    return run


def modulation_refs(side, depth, images, slots):
    data_count = side * side * 2
    lanes = -(-held_depth(slots) // LANES) * LANES
    f32 = jnp.float32
    return (
        [
            pltpu.VMEM((data_count * COND_ROWS, LANES), f32),
            pltpu.VMEM((wide_rows(slots), LANES), f32),
            pltpu.VMEM((LANES, lanes), jnp.bfloat16),
            pltpu.VMEM((data_count * IMAGE_ROWS + SPARE, LANES), f32),
            pltpu.VMEM((LANES, LANES), f32),
        ]
        + gather_sems(side)
        + reduce_refs(side, depth, IMAGE_ROWS)
    )


def modulation_grad_stages(grid, images, slots, own_ref, info_ref, part_ref, all_ref, cond_ref, refs):
    arrived, summed, wide, around, parts, send_z, recv_z, done_sem = refs[:8]
    gather = gather_blocks(grid, summed, IMAGE_ROWS, refs[8:14])
    reduce = reduce_blocks(grid, parts, COND_ROWS, refs[14:26])
    mine = grid.mine
    sizes = grid.sizes["z"]
    here = pl.ds(pl.multiple_of(grid.place * IMAGE_ROWS, 8), IMAGE_ROWS)
    depth = held_depth(slots)

    def to_z(k):
        return pltpu.make_async_remote_copy(
            src_ref=part_ref, dst_ref=arrived.at[mine["z"]], send_sem=send_z.at[k], recv_sem=recv_z.at[mine["z"]],
            device_id=grid.device("z", grid.other("z", k)), device_id_type=MESH,
        )

    def done():
        return pltpu.make_async_copy(summed.at[pl.ds(0, all_ref.shape[0])], all_ref, done_sem)

    def run(s):
        spread_modulation(s, own_ref, info_ref, wide)

        @pl.when(s == 0)
        def _():
            for k in range(sizes - 1):
                to_z(k).start()
            arrived[mine["z"]] = part_ref[...]
            around[...] = jnp.zeros_like(around)
            parts[...] = jnp.zeros_like(parts)

        @pl.when(s == 2)
        def _():
            for k in range(sizes - 1):
                other = grid.other("z", k)
                pltpu.make_async_remote_copy(
                    src_ref=part_ref, dst_ref=arrived.at[other], send_sem=send_z.at[k], recv_sem=recv_z.at[other],
                    device_id=grid.sibling, device_id_type=MESH,
                ).wait_recv()
            for k in range(sizes - 1):
                to_z(k).wait_send()
            total = arrived[0].astype(jnp.float32)
            for z in range(1, sizes):
                total = total + arrived[z].astype(jnp.float32)
            summed[here, :] = total.astype(jnp.bfloat16).astype(jnp.float32)[:IMAGE_ROWS]
            gather[0]()

        @pl.when(s == 4)
        def _():
            gather[1]()

        @pl.when(s == 6)
        def _():
            gather[2]()

        @pl.when(s == 9)
        def _():
            gather[3]()
            done().start()

        at_product = s - 10

        @pl.when((at_product >= 0) & (at_product < PRODUCT_STEPS))
        def _():
            total = around[D + 8 : D + 8 + depth, 0:images]
            each = MOD_BLOCKS // 2 // PRODUCT_STEPS
            for pair in range(each):
                block = (at_product * each + pair) * 2
                left = jnp.concatenate(
                    [held_columns(wide, info_ref, depth, block), held_columns(wide, info_ref, depth, block + 1)],
                    axis=1,
                )
                right = jnp.concatenate(
                    [
                        summed[pl.ds(block + more, images, stride=MOD_BLOCKS), :].astype(jnp.bfloat16)
                        for more in (0, 1)
                    ],
                    axis=1,
                )
                total = total + lax.dot_general(
                    left, right, (((1,), (1,)), ((), ())), preferred_element_type=jnp.float32
                )
            around[D + 8 : D + 8 + depth, 0:images] = total

        @pl.when(s == 19)
        def _():
            for block in range(D // LANES):
                piece = around[pl.ds(D + 8 - info_ref[0] + block * LANES, LANES), :].T
                parts[pl.ds(block, images, stride=COND_STRIDE), :] = piece[0:images, :]
            reduce[0]()

        for at, stage in ((21, 1), (24, 2), (27, 3)):
            @pl.when(s == at)
            def _(stage=stage):
                reduce[stage]()

        @pl.when(s == 30)
        def _():
            cond_ref[...] = reduce[4]()
            done().wait()

    return run


MOD_GRAD_REFS = 26


def modulation_grad_refs(side, depth, images, slots):
    data_count = side * side * 2
    dma = pltpu.SemaphoreType.DMA
    f32 = jnp.float32
    return (
        [
            pltpu.VMEM((depth, SENT_ROWS, LANES), jnp.bfloat16),
            pltpu.VMEM((data_count * IMAGE_ROWS + SPARE, LANES), f32),
            pltpu.VMEM((wide_rows(slots), LANES), f32),
            pltpu.VMEM((2 * (D + 8) + held_depth(slots), LANES), f32),
            pltpu.VMEM((data_count * COND_ROWS, LANES), f32),
            dma((depth - 1,)),
            dma((depth,)),
            dma,
        ]
        + gather_sems(side)
        + reduce_refs(side, depth, COND_ROWS)
    )


def reduce_body(side, depth, plan, slots, parts_ref, part_ref, own_ref, info_ref, out_ref, all_ref, cond_ref,
                *refs):
    hosts, share, kept, steps, parts = plan
    grid = Grid(side, depth)
    hosting = Hosting(grid, 2 * side * side * depth, hosts, share, kept, slots - kept) if hosts else None
    grid.greet(hosting)
    passed = refs[-1]
    modulation_step = modulation_grad_stages(
        grid, 2 * side * side * SEGS, slots, own_ref, info_ref, part_ref, all_ref, cond_ref, refs[:MOD_GRAD_REFS]
    )
    refs = refs[MOD_GRAD_REFS:]
    streams = []
    writes = []
    first = 0
    for number, (order, part) in enumerate(zip(ORDERS, parts)):
        span = part * SUBS
        stages, write = reduce_stream(
            grid, order, first, span, steps, parts_ref, out_ref,
            refs[REDUCE_REFS * number : REDUCE_REFS * (number + 1)], hosting, passed,
        )
        streams.append(stages)
        writes.append(write)
        first = first + steps * span

    def round_trip(s, carry):
        for late in range(4, -1, -1):
            q = s - LAG * late

            @pl.when((q >= 0) & (q < steps))
            def _(late=late, q=q):
                for stream in streams:
                    stream[late](q)

        modulation_step(s)
        return carry

    lax.fori_loop(0, max(steps + 4 * LAG, MOD_STEPS), round_trip, 0)
    for write in writes:
        for q in range(max(steps - OUTS, 0), steps):
            write(q, "wait")
    if hosting is not None:
        @pl.when(jnp.logical_not(hosting.is_host))
        def _():
            at = out_ref.at[pl.ds(kept * SUBS, (slots - kept) * SUBS)]
            pltpu.make_async_remote_copy(
                src_ref=at, dst_ref=at, send_sem=passed, recv_sem=passed, device_id=grid.sibling,
                device_id_type=MESH,
            ).wait_recv()


def reduce_slots(grads, mod_part, own, info, slots, data_count, seq_count):
    side = math.isqrt(data_count // 2)
    plan = host_plan(slots, data_count * seq_count, seq_count)
    kept, parts = plan[2], plan[4]
    held = HELD
    dma = pltpu.SemaphoreType.DMA
    regular = pltpu.SemaphoreType.REGULAR
    bf16 = jnp.bfloat16
    f32 = jnp.float32
    scratch = modulation_grad_refs(side, seq_count, data_count * SEGS, slots)
    for order, part in zip(ORDERS, parts):
        span = part * SUBS
        sizes = {"u": side, "v": side, "z": seq_count}
        left = dict(sizes)
        scratch.append(pltpu.VMEM((held, side, side, seq_count, span, LANES), bf16))
        scratch.append(pltpu.VMEM((SLOTS, side, side, seq_count, span, LANES), bf16))
        for axis in order:
            del left[axis]
            rest = tuple(left[name] for name in ("u", "v", "z") if name in left)
            scratch.append(pltpu.VMEM((SLOTS, sizes[axis] - 1) + rest + (span, LANES), bf16))
        scratch.append(pltpu.VMEM((OUTS, span, LANES), bf16))
        scratch.append(dma((held, side, side)))
        scratch.append(dma((OUTS,)))
        scratch.append(dma((OUTS,)))
        scratch.append(dma((SLOTS, side, side)))
        scratch.append(dma((SLOTS, side, side)))
        for axis in order:
            scratch.append(dma((SLOTS, sizes[axis] - 1)))
            scratch.append(dma((SLOTS, sizes[axis] - 1)))
        scratch.append(regular)
        for axis in order:
            scratch.append(regular((sizes[axis],)))
    scratch.append(dma)
    return pl.pallas_call(
        partial(reduce_body, side, seq_count, plan, slots),
        out_shape=(
            jax.ShapeDtypeStruct((slots * SUBS, LANES), bf16),
            jax.ShapeDtypeStruct((data_count * IMAGE_ROWS, LANES), f32),
            jax.ShapeDtypeStruct((COND_ROWS, LANES), f32),
        ),
        in_specs=[
            pl.BlockSpec(memory_space=pl.ANY),
            pl.BlockSpec(memory_space=pltpu.VMEM),
            pl.BlockSpec(memory_space=pltpu.VMEM),
            pl.BlockSpec(memory_space=pltpu.SMEM),
        ],
        out_specs=(
            pl.BlockSpec(memory_space=pl.ANY),
            pl.BlockSpec(memory_space=pl.ANY),
            pl.BlockSpec(memory_space=pltpu.VMEM),
        ),
        scratch_shapes=scratch,
        compiler_params=pltpu.CompilerParams(
            collective_id=1, has_side_effects=True, vmem_limit_bytes=VMEM_LIMIT
        ),
        name="reduce_slots",
    )(grads.reshape(data_count, seq_count, kept * SUBS, LANES), mod_part, own, info)


UPDATE_TILES = 104


def update_body(mod_depth, own_ref, reduced, cond_ref, mod_ref, master, first, second,
                new_master, new_first, new_second, mod_rows, wide):
    step = pl.program_id(0)
    mod_blocks = 6 * D // LANES
    start_row = own_ref[0] * SUBS
    shift = lax.rem(start_row, mod_blocks)
    tiles = UPDATE_TILES
    piece = 9

    @pl.when((step == 0) & (start_row < MOD_ROWS))
    def _():
        images = cond_ref.shape[1]
        for begin in range(0, mod_blocks, piece):
            grads = [
                mod_ref[pl.ds(begin + block, images, stride=mod_blocks), :].astype(jnp.bfloat16)
                for block in range(piece)
            ]
            part = jnp.dot(
                cond_ref[...], jnp.concatenate(grads, axis=1), preferred_element_type=jnp.float32
            )
            for block in range(piece):
                mod_rows[pl.ds(begin + block, mod_depth, stride=mod_blocks), :] = part[
                    :, block * LANES : (block + 1) * LANES
                ]

    wide[...] = reduced[...].astype(jnp.float32)
    corr_one = 1.0 - beta_one**STEP
    corr_two = 1.0 - beta_two**STEP
    local = step * tiles + lax.broadcasted_iota(jnp.int32, (tiles, LANES), 0)
    used = local < own_ref[1]
    for sub in range(SUBS):
        columns = pl.ds(sub * LANES, LANES)
        from_mod = mod_rows[pl.ds(shift + step * tiles * SUBS + sub, tiles, stride=SUBS), :]
        is_mod = start_row + local * SUBS + sub < MOD_ROWS
        grad = jnp.where(is_mod, from_mod, wide[pl.ds(sub, tiles, stride=SUBS), :])
        grad = jnp.where(used, grad, 0.0)
        one = beta_one * first[:, columns] + (1.0 - beta_one) * grad
        two = beta_two * second[:, columns] + (1.0 - beta_two) * grad * grad
        held = master[:, columns]
        new_first[:, columns] = one
        new_second[:, columns] = two
        new_master[:, columns] = held - learn_rate * (
            one / corr_one / (jnp.sqrt(two / corr_two) + adam_eps) + weight_decay * held
        )


def own_conditions(held, info, images, slots):
    steps = -(-slots // UPDATE_TILES)
    depth = -(-(steps * UPDATE_TILES * SUBS + MOD_BLOCKS) // MOD_BLOCKS)
    depth = -(-depth // 8) * 8
    return lax.dynamic_slice(held, (info[0], jnp.int32(0)), (depth, images)).astype(jnp.bfloat16)


def update(reduced, cond_own, mod_all, own_first, master, first, second):
    slots, tile_len = master.shape
    mod_depth, images = cond_own.shape
    tiles = UPDATE_TILES
    steps = -(-slots // tiles)
    wide_block = pl.BlockSpec((tiles, tile_len), lambda i, *_: (i, 0))
    return pl.pallas_call(
        partial(update_body, mod_depth),
        out_shape=(jax.ShapeDtypeStruct(master.shape, jnp.float32),) * 3,
        grid_spec=pltpu.PrefetchScalarGridSpec(
            num_scalar_prefetch=1,
            grid=(steps,),
            in_specs=[
                pl.BlockSpec((tiles * SUBS, LANES), lambda i, *_: (i, 0)),
                pl.BlockSpec((mod_depth, images), lambda i, *_: (0, 0)),
                pl.BlockSpec(mod_all.shape, lambda i, *_: (0, 0)),
                wide_block,
                wide_block,
                wide_block,
            ],
            out_specs=(wide_block,) * 3,
            scratch_shapes=[
                pltpu.VMEM(((mod_depth + 1) * MOD_BLOCKS, LANES), jnp.float32),
                pltpu.VMEM((tiles * SUBS, LANES), jnp.float32),
            ],
        ),
        compiler_params=pltpu.CompilerParams(vmem_limit_bytes=VMEM_LIMIT),
        name="update",
    )(own_first, reduced, cond_own, mod_all, master, first, second)


def normalize(values):
    centred = values - jnp.mean(values, axis=-1, keepdims=True)
    spread = jnp.mean(centred * centred, axis=-1, keepdims=True)
    return centred * lax.rsqrt(spread + ln_eps)


def cosine_of(target, projected):
    inner_mean = jnp.mean(projected * target, axis=-1)
    return (
        inner_mean
        * lax.rsqrt(jnp.mean(projected * projected, axis=-1) + cos_eps)
        * lax.rsqrt(jnp.mean(target * target, axis=-1) + cos_eps)
    )


def gelu_tanh(values):
    return jax.nn.gelu(values, approximate=True)


def lane_pad(width):
    return -(-width // LANES) * LANES


def regroup_body(moves, fill, x_ref, out_ref):
    if fill is not None:
        start, width = fill
        for group in range(out_ref.shape[0]):
            out_ref[group, :, start : start + width] = jnp.zeros((out_ref.shape[1], width), out_ref.dtype)
    for from_group, start, to_group, target, width in moves:
        if from_group is None:
            values = x_ref[:, start : start + width]
        else:
            values = x_ref[from_group, :, start : start + width]
        if to_group is None:
            out_ref[:, target : target + width] = values
        else:
            out_ref[to_group, :, target : target + width] = values


def split_groups(x, parts, groups):
    tokens, total = x.shape
    width = total // parts // groups
    padded = lane_pad(parts * width)
    moves = [
        (None, (part * groups + group) * width, group, part * width, width)
        for group in range(groups)
        for part in range(parts)
    ]
    fill = (parts * width, padded - parts * width) if padded > parts * width else None
    return pl.pallas_call(
        partial(regroup_body, moves, fill),
        out_shape=jax.ShapeDtypeStruct((groups, tokens, padded), x.dtype),
        compiler_params=pltpu.CompilerParams(vmem_limit_bytes=VMEM_LIMIT),
        name="split_groups_%d" % parts,
    )(x)


def join_groups(x, parts, width):
    groups, tokens, _ = x.shape
    moves = [
        (group, part * width, None, (part * groups + group) * width, width)
        for group in range(groups)
        for part in range(parts)
    ]
    return pl.pallas_call(
        partial(regroup_body, moves, None),
        out_shape=jax.ShapeDtypeStruct((tokens, parts * groups * width), x.dtype),
        compiler_params=pltpu.CompilerParams(vmem_limit_bytes=VMEM_LIMIT),
        name="join_groups_%d" % parts,
    )(x)


QUERY_BLOCK = 1024


def key_bias(seg_col, pad_col, seg_row, first):
    keys = seg_col.shape[0]
    queries = seg_row.shape[1]
    key_at = lax.broadcasted_iota(jnp.int32, (keys, queries), 0)
    query_at = first + lax.broadcasted_iota(jnp.int32, (keys, queries), 1)
    allowed = (seg_col == seg_row) & ((pad_col == 1) | (key_at == query_at))
    return jnp.where(allowed, 0.0, -1e30)


def spread_heads(rows_ref, held, heads):
    held[...] = jnp.zeros_like(held)
    for part in range(held.shape[0]):
        for head in range(heads):
            start = (part * heads + head) * HEAD_DIM
            held[part, head, :, 0:HEAD_DIM] = rows_ref[:, start : start + HEAD_DIM]


def probabilities(held, head, block, bias):
    scores = lax.dot_general(
        held[1, head], held[0, head, block, :], (((1,), (1,)), ((), ())), preferred_element_type=jnp.float32
    )
    scores = scores + bias
    shifted = jnp.exp2((scores - jnp.max(scores, axis=0, keepdims=True)) * (HEAD_DIM ** (-0.5) * math.log2(math.e)))
    return shifted * (1.0 / jnp.sum(shifted, axis=0, keepdims=True))


def attention_body(heads, rows_ref, seg_col, pad_col, seg_row, out_ref, held):
    step = pl.program_id(0)

    @pl.when(step == 0)
    def _():
        spread_heads(rows_ref, held, heads)

    first = pl.multiple_of(step * QUERY_BLOCK, QUERY_BLOCK)
    block = pl.ds(first, QUERY_BLOCK)
    bias = key_bias(seg_col[...], pad_col[...], seg_row[...], first)
    rest = out_ref.shape[1] - heads * HEAD_DIM
    if rest:
        out_ref[:, heads * HEAD_DIM :] = jnp.zeros((QUERY_BLOCK, rest), jnp.bfloat16)
    for head in range(heads):
        probs = probabilities(held, head, block, bias).astype(jnp.bfloat16)
        result = lax.dot_general(
            held[2, head], probs, (((0,), (0,)), ((), ())), preferred_element_type=jnp.float32
        )
        out_ref[:, head * HEAD_DIM : (head + 1) * HEAD_DIM] = result.T[:, :HEAD_DIM].astype(jnp.bfloat16)


def attention(rows, segments, padding, heads):
    length = rows.shape[0]
    whole = pl.BlockSpec((length, 1), lambda i: (0, 0))
    return pl.pallas_call(
        partial(attention_body, heads),
        out_shape=jax.ShapeDtypeStruct((length, lane_pad(heads * HEAD_DIM)), jnp.bfloat16),
        grid=(length // QUERY_BLOCK,),
        in_specs=[
            pl.BlockSpec(rows.shape, lambda i: (0, 0)),
            whole,
            whole,
            pl.BlockSpec((1, QUERY_BLOCK), lambda i: (0, i)),
        ],
        out_specs=pl.BlockSpec((QUERY_BLOCK, lane_pad(heads * HEAD_DIM)), lambda i: (i, 0)),
        scratch_shapes=[pltpu.VMEM((3, heads, length, LANES), jnp.bfloat16)],
        compiler_params=pltpu.CompilerParams(vmem_limit_bytes=VMEM_LIMIT),
        name="attention",
    )(rows, segments.reshape(length, 1), padding.reshape(length, 1), segments.reshape(1, length))


def attention_grad_body(heads, rows_ref, grad_ref, seg_col, pad_col, seg_row, out_ref, held, given, grad_k, grad_v):
    step = pl.program_id(0)
    scaling = HEAD_DIM ** (-0.5)

    @pl.when(step == 0)
    def _():
        spread_heads(rows_ref, held, heads)
        given[...] = jnp.zeros_like(given)
        grad_k[...] = jnp.zeros_like(grad_k)
        grad_v[...] = jnp.zeros_like(grad_v)
        out_ref[...] = jnp.zeros_like(out_ref)

    first = pl.multiple_of(step * QUERY_BLOCK, QUERY_BLOCK)
    block = pl.ds(first, QUERY_BLOCK)
    bias = key_bias(seg_col[...], pad_col[...], seg_row[...], first)
    for head in range(heads):
        given[:, 0:HEAD_DIM] = grad_ref[:, head * HEAD_DIM : (head + 1) * HEAD_DIM]
        upstream = given[...]
        probs = probabilities(held, head, block, bias)
        grad_v[head] += jnp.dot(probs.astype(jnp.bfloat16), upstream, preferred_element_type=jnp.float32)
        grad_probs = lax.dot_general(
            held[2, head], upstream, (((1,), (1,)), ((), ())), preferred_element_type=jnp.float32
        )
        inner = jnp.sum(probs * grad_probs, axis=0, keepdims=True)
        grad_scores = (probs * (grad_probs - inner)).astype(jnp.bfloat16)
        grad_k[head] += jnp.dot(grad_scores, held[0, head, block, :], preferred_element_type=jnp.float32)
        grad_q = lax.dot_general(
            held[1, head], grad_scores, (((0,), (0,)), ((), ())), preferred_element_type=jnp.float32
        )
        out_ref[block, head * HEAD_DIM : (head + 1) * HEAD_DIM] = (
            grad_q.T[:, :HEAD_DIM] * scaling
        ).astype(jnp.bfloat16)

    @pl.when(step == pl.num_programs(0) - 1)
    def _():
        for head in range(heads):
            start = (heads + head) * HEAD_DIM
            out_ref[:, start : start + HEAD_DIM] = (grad_k[head][:, :HEAD_DIM] * scaling).astype(jnp.bfloat16)
            start = (2 * heads + head) * HEAD_DIM
            out_ref[:, start : start + HEAD_DIM] = grad_v[head][:, :HEAD_DIM].astype(jnp.bfloat16)


def attention_grad(rows, grad, segments, padding, heads):
    length = rows.shape[0]
    whole = pl.BlockSpec((length, 1), lambda i: (0, 0))
    return pl.pallas_call(
        partial(attention_grad_body, heads),
        out_shape=jax.ShapeDtypeStruct(rows.shape, jnp.bfloat16),
        grid=(length // QUERY_BLOCK,),
        in_specs=[
            pl.BlockSpec(rows.shape, lambda i: (0, 0)),
            pl.BlockSpec((QUERY_BLOCK, grad.shape[1]), lambda i: (i, 0)),
            whole,
            whole,
            pl.BlockSpec((1, QUERY_BLOCK), lambda i: (0, i)),
        ],
        out_specs=pl.BlockSpec(rows.shape, lambda i: (0, 0)),
        scratch_shapes=[
            pltpu.VMEM((3, heads, length, LANES), jnp.bfloat16),
            pltpu.VMEM((QUERY_BLOCK, LANES), jnp.bfloat16),
            pltpu.VMEM((heads, length, LANES), jnp.float32),
            pltpu.VMEM((heads, length, LANES), jnp.float32),
        ],
        compiler_params=pltpu.CompilerParams(vmem_limit_bytes=VMEM_LIMIT),
        name="attention_grad",
    )(rows, grad, segments.reshape(length, 1), padding.reshape(length, 1), segments.reshape(1, length))


def shards(
    tokens,
    conditions,
    segment_ids,
    padding,
    targets,
    cotangent,
    tile_counts,
    master,
    first_moment,
    second_moment,
):
    seq_count = lax.axis_size("seq")
    data_count = lax.axis_size("dp")
    seq_place = lax.axis_index("seq")
    data_place = lax.axis_index("dp")
    owners = data_count * seq_count
    slot_count, tile_len = master.shape
    own_rows = slot_count * SUBS
    tile_ends = jnp.cumsum(tile_counts)
    starts = jnp.concatenate([jnp.zeros((1,), jnp.int32), tile_ends.astype(jnp.int32)])
    spans = jnp.asarray(chunk_spans()[0], jnp.int32)
    firsts = jnp.sum((tile_ends[None, :] <= spans[:, :1]).astype(jnp.int32), axis=1)
    lasts = jnp.sum((tile_ends[None, :] <= spans[:, 1:]).astype(jnp.int32), axis=1)
    plan = host_plan(slot_count, owners, seq_count)
    guests = jnp.asarray(
        guest_places((*plan[:3], slot_count - plan[2]), owners, seq_count), jnp.int32
    )
    edge_ids = jnp.asarray(EDGE_TILES, jnp.int32)
    edge_owner = jnp.sum((tile_ends[None, :] <= edge_ids[:, None]).astype(jnp.int32), axis=1)
    edge_within = edge_ids - jnp.take(starts, edge_owner)
    edge_places = edge_owner * plan[2] + edge_within
    if plan[0]:
        edge_places = jnp.where(
            edge_within < plan[2], edge_places, jnp.take(guests, edge_owner) + edge_within - plan[2]
        )
    own_place = data_place * seq_count + seq_place
    own_start = lax.dynamic_index_in_dim(starts, own_place, 0, False)
    own_count = lax.dynamic_index_in_dim(tile_counts, own_place, 0, False)
    own_low = master.astype(jnp.bfloat16).reshape(own_rows, LANES)
    info = jnp.stack(
        [
            jnp.minimum(own_start * SUBS // MOD_BLOCKS, D + 1),
            own_start * SUBS % MOD_BLOCKS,
            jnp.clip(jnp.minimum(own_count * SUBS, MOD_ROWS - own_start * SUBS), 0, own_rows),
        ]
    ).astype(jnp.int32)
    images = data_count * SEGS

    own_first = jnp.stack([own_start, own_count])
    cond_f = conditions.astype(jnp.float32)
    cond_act, silu_cond_back = jax.vjp(jax.nn.silu, cond_f)
    cond_low = cond_act.astype(jnp.bfloat16)
    cond_rows = jnp.pad(cond_low[0].astype(jnp.float32), ((0, 0), (0, LANES))).reshape(COND_ROWS, LANES)
    packed, modulation, cond_held = gather_slots(own_low, cond_rows, info, slot_count, data_count, seq_count)
    modulation = modulation.reshape(1, SEGS, 6 * D)
    weights = {
        index: unpack_weight(index, packed, plan, firsts, lasts, starts, guests)
        for index in (2, 5, 7, 9, 11)
    }
    attend_weight, output_weight, hidden_weight, return_weight, proj_one = (
        weights[index] for index in (2, 5, 7, 9, 11)
    )
    edges = edge_read(packed, edge_places)
    edge_flat = edges.reshape(-1)

    def bias(index):
        row = param_rows()[index]
        at = EDGE_TILES.index(row // SUBS) * SUBS + row % SUBS
        return edge_flat[at * LANES : at * LANES + param_shapes()[index][0]]

    query_bias, value_bias, output_bias, hidden_bias, return_bias = (bias(i) for i in (3, 4, 6, 8, 10))
    proj_bias_one, proj_bias_two, proj_bias_three = (bias(i) for i in (12, 14, 16))
    rows_dev, local_len, model_width = tokens.shape
    full_len = segment_ids.shape[1]
    heads_local = HEADS // seq_count
    group_width = model_width // seq_count
    token_start = seq_place * local_len
    local_seg = lax.dynamic_slice_in_dim(segment_ids, token_start, local_len, 1)
    local_pad = lax.dynamic_slice_in_dim(padding, token_start, local_len, 1).astype(jnp.float32)
    onehot = (local_seg[:, :, None] == jnp.arange(SEGS, dtype=jnp.int32)).astype(jnp.float32)
    per_token = jnp.einsum("rts,rsc->rtc", onehot, modulation, precision=lax.Precision.HIGH)
    shift_one, scale_one, gate_one, shift_two, scale_two, gate_two = jnp.split(
        per_token, 6, axis=-1
    )
    token_f = tokens.astype(jnp.float32)
    normed_one, norm_back_one = jax.vjp(normalize, token_f)
    attend_in = (normed_one * (1.0 + scale_one) + shift_one).astype(jnp.bfloat16)
    triple_bias = jnp.concatenate([query_bias, jnp.zeros_like(query_bias), value_bias])
    triple = (
        jnp.einsum("rtd,dc->rtc", attend_in, attend_weight, preferred_element_type=jnp.float32)
        + triple_bias
    )
    triple_low = split_groups(triple[0].astype(jnp.bfloat16), 3, seq_count)
    head_rows = lax.all_to_all(triple_low, "seq", split_axis=0, concat_axis=0, tiled=True)
    (head_rows, output_weight, hidden_weight, return_weight, proj_one) = lax.optimization_barrier(
        (head_rows, output_weight, hidden_weight, return_weight, proj_one)
    )
    head_rows = head_rows.reshape(full_len, head_rows.shape[-1])
    head_attended = attention(head_rows, segment_ids[0], padding[0], heads_local)
    head_attended = head_attended.reshape(seq_count, local_len, head_attended.shape[-1])
    head_attended, packed = lax.optimization_barrier((head_attended, packed))
    proj_two, proj_three = (unpack_weight(index, packed, plan, firsts, lasts, starts, guests) for index in (13, 15))
    attended = lax.all_to_all(head_attended, "seq", split_axis=0, concat_axis=0, tiled=True)
    attended, proj_two, proj_three = lax.optimization_barrier((attended, proj_two, proj_three))
    attended = join_groups(attended, 1, group_width)[None]
    branch_one = (
        jnp.einsum("rtd,dc->rtc", attended, output_weight, preferred_element_type=jnp.float32)
        + output_bias
    )
    middle = token_f + gate_one * branch_one
    normed_two, norm_back_two = jax.vjp(normalize, middle)
    mlp_in = (normed_two * (1.0 + scale_two) + shift_two).astype(jnp.bfloat16)
    hidden = (
        jnp.einsum("rtd,df->rtf", mlp_in, hidden_weight, preferred_element_type=jnp.float32)
        + hidden_bias
    )
    activated_f, gelu_back = jax.vjp(gelu_tanh, hidden)
    activated = activated_f.astype(jnp.bfloat16)
    branch_two = (
        jnp.einsum("rtf,fd->rtd", activated, return_weight, preferred_element_type=jnp.float32)
        + return_bias
    )
    result = middle + gate_two * branch_two
    feature = result.astype(jnp.bfloat16)
    first_pre = (
        jnp.einsum("rtd,dp->rtp", feature, proj_one, preferred_element_type=jnp.float32)
        + proj_bias_one
    )
    first_act, first_back = jax.vjp(jax.nn.silu, first_pre)
    first_low = first_act.astype(jnp.bfloat16)
    second_pre = (
        jnp.einsum("rtp,pc->rtc", first_low, proj_two, preferred_element_type=jnp.float32)
        + proj_bias_two
    )
    second_act, second_back = jax.vjp(jax.nn.silu, second_pre)
    second_low = second_act.astype(jnp.bfloat16)
    projected = (
        jnp.einsum("rtc,co->rto", second_low, proj_three, preferred_element_type=jnp.float32)
        + proj_bias_three
    )
    target_f = targets.astype(jnp.float32)
    cosine, cosine_back = jax.vjp(partial(cosine_of, target_f), projected)
    ends = {}

    def put(buffer, index, left, right):
        buffer, ends[index] = weight_grad(
            index,
            left.reshape(-1, left.shape[-1]),
            right.reshape(-1, right.shape[-1]),
            buffer,
            owners,
            slot_count,
            firsts,
            lasts,
            starts,
            guests,
            (plan[0], plan[2]),
        )
        return buffer

    def summed(grad):
        return jnp.sum(grad.astype(jnp.float32), axis=(0, 1))

    (grad_projected,) = cosine_back(local_pad * -repa_weight)
    grad_projected = grad_projected.astype(jnp.bfloat16)
    sum_sixteen = summed(grad_projected)
    (grad_second,) = second_back(
        jnp.einsum("rto,co->rtc", grad_projected, proj_three, preferred_element_type=jnp.float32)
    )
    grad_second = grad_second.astype(jnp.bfloat16)
    sum_fourteen = summed(grad_second)
    (grad_first,) = first_back(
        jnp.einsum("rtc,pc->rtp", grad_second, proj_two, preferred_element_type=jnp.float32)
    )
    grad_first = grad_first.astype(jnp.bfloat16)
    sum_twelve = summed(grad_first)
    grad_result = cotangent + jnp.einsum(
        "rtp,dp->rtd", grad_first, proj_one, preferred_element_type=jnp.float32
    )
    grad_gate_two = grad_result * branch_two
    grad_branch_two = (grad_result * gate_two).astype(jnp.bfloat16)
    sum_ten = summed(grad_branch_two)
    (grad_hidden,) = gelu_back(
        jnp.einsum(
            "rtd,fd->rtf", grad_branch_two, return_weight, preferred_element_type=jnp.float32
        )
    )
    grad_hidden = grad_hidden.astype(jnp.bfloat16)
    sum_eight = summed(grad_hidden)
    grad_mlp_in = jnp.einsum(
        "rtf,df->rtd", grad_hidden, hidden_weight, preferred_element_type=jnp.float32
    )
    grad_scale_two = grad_mlp_in * normed_two
    (grad_through_two,) = norm_back_two(grad_mlp_in * (1.0 + scale_two))
    grad_middle = grad_result + grad_through_two
    grad_gate_one = grad_middle * branch_one
    grad_branch_one = (grad_middle * gate_one).astype(jnp.bfloat16)
    sum_six = summed(grad_branch_one)
    grad_attended = jnp.einsum(
        "rtc,dc->rtd", grad_branch_one, output_weight, preferred_element_type=jnp.float32
    ).astype(jnp.bfloat16)
    grad_attended = split_groups(grad_attended[0], 1, seq_count)
    grad_attended, second_low = lax.optimization_barrier((grad_attended, second_low))
    head_grad = lax.all_to_all(grad_attended, "seq", split_axis=0, concat_axis=0, tiled=True)
    grad_buffer = put(None, 15, second_low, grad_projected)
    grad_buffer = put(grad_buffer, 13, first_low, grad_second)
    head_grad, grad_buffer = lax.optimization_barrier((head_grad, grad_buffer))
    grad_triple_heads = attention_grad(
        head_rows, head_grad.reshape(full_len, head_grad.shape[-1]), segment_ids[0], padding[0], heads_local
    ).reshape(seq_count, local_len, head_rows.shape[-1])
    grad_triple_heads, grad_buffer, cond_held = lax.optimization_barrier(
        (grad_triple_heads, grad_buffer, cond_held)
    )
    grad_triple = lax.all_to_all(grad_triple_heads, "seq", split_axis=0, concat_axis=0, tiled=True)
    grad_buffer = put(grad_buffer, 11, feature, grad_first)
    grad_buffer = put(grad_buffer, 9, activated, grad_branch_two)
    grad_buffer = put(grad_buffer, 7, mlp_in, grad_hidden)
    grad_buffer = put(grad_buffer, 5, attended, grad_branch_one)
    cond_own = own_conditions(cond_held, info, images, slot_count)
    grad_triple, grad_buffer, cond_own = lax.optimization_barrier((grad_triple, grad_buffer, cond_own))
    grad_triple = join_groups(grad_triple, 3, group_width)[None]
    grad_buffer = put(grad_buffer, 2, attend_in, grad_triple)
    triple_sums = summed(grad_triple)
    grad_attend_in = jnp.einsum(
        "rtc,dc->rtd", grad_triple, attend_weight, preferred_element_type=jnp.float32
    )
    grad_scale_one = grad_attend_in * normed_one
    (grad_through_one,) = norm_back_one(grad_attend_in * (1.0 + scale_one))
    grad_tokens = grad_middle + grad_through_one
    token_mod_grad = jnp.concatenate(
        [grad_attend_in, grad_scale_one, grad_gate_one, grad_mlp_in, grad_scale_two, grad_gate_two],
        axis=-1,
    )
    mod_part = jnp.einsum("rts,rtc->rsc", onehot, token_mod_grad, precision=lax.Precision.HIGH)
    mod_sent = jnp.pad(
        mod_part.astype(jnp.bfloat16).reshape(IMAGE_ROWS, LANES), ((0, SENT_ROWS - IMAGE_ROWS), (0, 0))
    )
    rows_at = param_rows()

    def rows(vector):
        return vector.reshape(-1, LANES)


    def head(index):
        return (0, ends[index], rows_at[index] % SUBS, SUBS)

    def tail(index):
        return (0, ends[index], SUBS, SUBS + rows_at[index] % SUBS)

    def whole(vector):
        return (0, rows(vector), 0, vector.shape[0] // LANES)

    pieces = [
        (6,) + head(2)[1:],
        tail(2),
        whole(triple_sums[:model_width]),
        whole(triple_sums[2 * model_width :]),
        head(5),
        tail(5),
        whole(sum_six),
        head(7),
        tail(7),
        whole(sum_eight),
        head(9),
        tail(9),
        whole(sum_ten),
        head(11),
        tail(11),
        whole(sum_twelve),
        head(13),
        tail(13),
        whole(sum_fourteen),
        head(15),
        tail(15),
        whole(sum_sixteen),
    ]
    grad_buffer = edge_write(pieces, grad_buffer, edge_places[EDGE_TILES.index(3891) :])
    reduced, mod_all, cond_grad = reduce_slots(
        grad_buffer, mod_sent, own_low, info, slot_count, data_count, seq_count
    )
    (grad_conditions,) = silu_cond_back(cond_grad.reshape(1, SEGS, COND_STRIDE * LANES)[:, :, :D])
    new_master, new_first, new_second = update(
        reduced, cond_own, mod_all, own_first, master, first_moment, second_moment
    )
    return (
        result.astype(jnp.bfloat16),
        grad_tokens,
        grad_conditions,
        new_master,
        new_first,
        new_second,
    )


def solution(mesh):
    return jax.shard_map(
        shards,
        mesh=mesh,
        in_specs=(
            P("dp", "seq", None),
            P("dp", None, None),
            P("dp", None),
            P("dp", None),
            P("dp", "seq", None),
            P("dp", "seq", None),
            P(),
            P(("dp", "seq"), None),
            P(("dp", "seq"), None),
            P(("dp", "seq"), None),
        ),
        out_specs=(
            P("dp", "seq", None),
            P("dp", "seq", None),
            P("dp", None, None),
            P(("dp", "seq"), None),
            P(("dp", "seq"), None),
            P(("dp", "seq"), None),
        ),
        check_vma=False,
    )
```
